32 devices in a mesh: fsdp: 32 (over z, y, x, core).
Axes of the slice: x: 2, y: 2, z: 4, core: 2. Of those that a mesh axis runs over, the one named last changes fastest.
Arguments:
- inputs: bfloat16 [2, 4096, 1280], P(None, 'fsdp'), may hold values from -6 to 6
- cotangent: bfloat16 [2, 4096, 1280], P(None, 'fsdp'), may hold values from -6 to 6
- lengths: int32 [2, 4], replicated, may hold values from 512 to 1024, as said below
- first_gain: float32 [1280], P('fsdp'), may hold values from 0.25 to 1.75
- first_shift: float32 [1280], P('fsdp'), may hold values from -3 to 3
- query_weight: float32 [1280, 1280], P('fsdp'), may hold values from -0.15625 to 0.15625
- query_bias: float32 [1280], P('fsdp'), may hold values from -3 to 3
- key_weight: float32 [1280, 1280], P('fsdp'), may hold values from -0.15625 to 0.15625
- value_weight: float32 [1280, 1280], P('fsdp'), may hold values from -0.15625 to 0.15625
- value_bias: float32 [1280], P('fsdp'), may hold values from -3 to 3
- output_weight: float32 [1280, 1280], P('fsdp'), may hold values from -1.25 to 1.25
- output_bias: float32 [1280], P('fsdp'), may hold values from -3 to 3
- second_gain: float32 [1280], P('fsdp'), may hold values from 0.25 to 1.75
- second_shift: float32 [1280], P('fsdp'), may hold values from -3 to 3
- expand_weight: float32 [1280, 5120], P('fsdp'), may hold values from -0.15625 to 0.15625
- expand_bias: float32 [5120], P('fsdp'), may hold values from -3 to 3
- shrink_weight: float32 [5120, 1280], P('fsdp'), may hold values from -0.078125 to 0.078125
- shrink_bias: float32 [1280], P('fsdp'), may hold values from -3 to 3
Outputs:
- block_out: bfloat16 [2, 4096, 1280], P(None, 'fsdp')
- input_grad: bfloat16 [2, 4096, 1280], P(None, 'fsdp')
- grad_first_gain: float32 [1280], P('fsdp')
- grad_first_shift: float32 [1280], P('fsdp')
- grad_query_weight: float32 [1280, 1280], P('fsdp')
- grad_query_bias: float32 [1280], P('fsdp')
- grad_key_weight: float32 [1280, 1280], P('fsdp')
- grad_value_weight: float32 [1280, 1280], P('fsdp')
- grad_value_bias: float32 [1280], P('fsdp')
- grad_output_weight: float32 [1280, 1280], P('fsdp')
- grad_output_bias: float32 [1280], P('fsdp')
- grad_second_gain: float32 [1280], P('fsdp')
- grad_second_shift: float32 [1280], P('fsdp')
- grad_expand_weight: float32 [1280, 5120], P('fsdp')
- grad_expand_bias: float32 [5120], P('fsdp')
- grad_shrink_weight: float32 [5120, 1280], P('fsdp')
- grad_shrink_bias: float32 [1280], P('fsdp')
The draws below stay inside these ranges and needn't reach their ends.
Inputs may be any that keep to these rules, and one draw needn't show every extreme that they name: `lengths`: in every micro-batch some clip has all 1024 positions valid.
All inputs are finite; a program needn't handle non-finite values.
Results may differ from the reference program's by a relative error of at most 0.014.
Values may be sent and summed in bfloat16 or wider, within the bound.
A program may use at most 512 MiB of HBM per device.

```python
import jax
import jax.numpy as jnp
from jax import lax

D = 1280
H = 16
HD = 80
FF = 5120
MB = 2
SLOT = 1024
CLIPS = 4
TOKENS = 4096


def draw_lengths(key, part):
    base = jax.random.randint(jax.random.fold_in(key, 11), (MB, CLIPS), SLOT // 2, SLOT + 1)
    chosen = jax.random.randint(jax.random.fold_in(key, 12), (MB, 1), 0, CLIPS)
    columns = jnp.arange(CLIPS)[None, :]
    return jnp.where(columns == chosen, SLOT, base).astype(jnp.int32)


def shard_levels(own_key, dims, cuts, low, high):
    loudness, own = 1.0, jax.random.fold_in(own_key, 6)
    for dim, parts in cuts:
        steps = jnp.exp(jax.random.uniform(jax.random.fold_in(own, dim), (parts,), jnp.float32, low / len(cuts), high / len(cuts)))
        loudness = loudness * jnp.repeat(steps, dims[dim] // parts).reshape([-1 if axis == dim else 1 for axis in range(len(dims))])
    return loudness


def scatter_about(own_key, shape, spread, limit, shards=(), dtype=jnp.bfloat16):
    entries = spread * jax.random.normal(own_key, shape, jnp.float32)
    if shards:
        entries = entries * shard_levels(own_key, shape, shards, -0.22, 0.18)
    return jnp.clip(entries, -limit, limit).astype(dtype)


def setup_inputs(seed: int = 0) -> dict:
    key_of = jax.random.split(jax.random.key(seed), 19)
    inputs = scatter_about(key_of[0], (MB, TOKENS, D), 1.0, 6.0, ((1, 32),))
    cotangent = scatter_about(key_of[1], (MB, TOKENS, D), 1.0, 6.0, ((1, 32),))
    lengths = draw_lengths(jax.random.fold_in(key_of[18], 71), 0)
    first_gain = jnp.clip(1.0 + 0.15 * jax.random.normal(key_of[3], (D,), jnp.float32), 0.25, 1.75)
    first_shift = scatter_about(key_of[4], (D,), 0.5, 3.0, ((0, 32),), jnp.float32)
    query_weight = scatter_about(key_of[5], (D, D), D ** -0.5, 0.15625, ((0, 32),), jnp.float32)
    query_bias = scatter_about(key_of[6], (D,), 0.5, 3.0, ((0, 32),), jnp.float32)
    key_weight = scatter_about(key_of[7], (D, D), D ** -0.5, 0.15625, ((0, 32),), jnp.float32)
    value_weight = scatter_about(key_of[8], (D, D), D ** -0.5, 0.15625, ((0, 32),), jnp.float32)
    value_bias = scatter_about(key_of[9], (D,), 0.5, 3.0, ((0, 32),), jnp.float32)
    output_weight = scatter_about(key_of[10], (D, D), (D // 64) ** -0.5, 1.25, ((0, 32),), jnp.float32)
    output_bias = scatter_about(key_of[11], (D,), 0.5, 3.0, ((0, 32),), jnp.float32)
    second_gain = jnp.clip(1.0 + 0.15 * jax.random.normal(key_of[12], (D,), jnp.float32), 0.25, 1.75)
    second_shift = scatter_about(key_of[13], (D,), 0.5, 3.0, ((0, 32),), jnp.float32)
    expand_weight = scatter_about(key_of[14], (D, FF), D ** -0.5, 0.15625, ((0, 32),), jnp.float32)
    expand_bias = scatter_about(key_of[15], (FF,), 0.5, 3.0, ((0, 32),), jnp.float32)
    shrink_weight = scatter_about(key_of[16], (FF, D), FF ** -0.5, 0.078125, ((0, 32),), jnp.float32)
    shrink_bias = scatter_about(key_of[17], (D,), 0.5, 3.0, ((0, 32),), jnp.float32)
    return {"inputs": inputs, "cotangent": cotangent, "lengths": lengths, "first_gain": first_gain, "first_shift": first_shift, "query_weight": query_weight, "query_bias": query_bias, "key_weight": key_weight, "value_weight": value_weight, "value_bias": value_bias, "output_weight": output_weight, "output_bias": output_bias, "second_gain": second_gain, "second_shift": second_shift, "expand_weight": expand_weight, "expand_bias": expand_bias, "shrink_weight": shrink_weight, "shrink_bias": shrink_bias}


EPS = 1e-05
NEG = -1000000000.0
HIGH = lax.Precision.HIGHEST

@jax.custom_vjp
def low(v):
    return lax.optimization_barrier(v.astype(jnp.bfloat16)).astype(jnp.float32)

@jax.custom_vjp
def low_back(v):
    return v

def low_keep(v):
    return (low(v), None)

def low_pass(kept, grad):
    return (grad,)

def back_keep(v):
    return (v, None)

def back_low(kept, grad):
    return (low(grad),)
low.defvjp(low_keep, low_pass)
low_back.defvjp(back_keep, back_low)

def layer_norm(row_block, gain_vec, shift_vec):
    row_mean = lax.optimization_barrier(jnp.mean(row_block, -1, keepdims=True))
    centered = row_block - row_mean
    variance = lax.optimization_barrier(jnp.mean(centered * centered, -1, keepdims=True))
    return centered * lax.rsqrt(variance + EPS) * gain_vec + shift_vec

def product(left_rows, right_rows):
    return jnp.dot(left_rows, right_rows, precision=HIGH)

def block(row_block, key_valid, first_gain, first_shift, query_weight, query_bias, key_weight, value_weight, value_bias, output_weight, output_bias, second_gain, second_shift, expand_weight, expand_bias, shrink_weight, shrink_bias):
    row_count = row_block.shape[0]
    first_low = low(layer_norm(row_block, first_gain, first_shift))
    queries = low(low_back(product(first_low, low(query_weight)) + query_bias))
    key_rows = low(low_back(product(first_low, low(key_weight))))
    values = low(low_back(product(first_low, low(value_weight)) + value_bias))
    query_heads = queries.reshape(row_count, H, HD)
    key_heads = key_rows.reshape(row_count, H, HD)
    value_heads = values.reshape(row_count, H, HD)
    scores = low_back(jnp.einsum('qhd,khd->hqk', query_heads, key_heads, precision=HIGH) * HD ** (-0.5))
    scores = jnp.where(key_valid[None, None, :], scores, NEG)
    row_peak = lax.optimization_barrier(jnp.max(scores, -1, keepdims=True))
    exponent = jnp.exp(scores - row_peak)
    soft_probs = exponent / lax.optimization_barrier(jnp.sum(exponent, -1, keepdims=True))
    mixed_rows = jnp.einsum('hqk,khd->qhd', low(soft_probs), value_heads, precision=HIGH).reshape(row_count, H * HD)
    mixed_rows = low(low_back(mixed_rows))
    residual = row_block + low_back(product(mixed_rows, low(output_weight))) + output_bias
    second_low = low(layer_norm(residual, second_gain, second_shift))
    hidden = low_back(product(second_low, low(expand_weight)) + expand_bias)
    active = low(low_back(jax.nn.gelu(hidden, approximate=False)))
    return residual + product(active, low(shrink_weight)) + shrink_bias

def reference(inputs, cotangent, lengths, first_gain, first_shift, query_weight, query_bias, key_weight, value_weight, value_bias, output_weight, output_bias, second_gain, second_shift, expand_weight, expand_bias, shrink_weight, shrink_bias):
    params = (first_gain, first_shift, query_weight, query_bias, key_weight, value_weight, value_bias, output_weight, output_bias, second_gain, second_shift, expand_weight, expand_bias, shrink_weight, shrink_bias)
    clip_count = lengths.shape[0] * lengths.shape[1]
    slot_rows = inputs.shape[1] // lengths.shape[1]
    width = inputs.shape[2]
    clip_inputs = inputs.reshape(clip_count, slot_rows, width)
    clip_cotangents = cotangent.reshape(clip_count, slot_rows, width)
    clip_lengths = lengths.reshape(clip_count)

    def one_clip(carry, packed):
        clip_in, clip_cot, clip_len = packed
        key_valid = jnp.arange(slot_rows) < clip_len

        def forward(row_block, *weights):
            return block(row_block, key_valid, *weights)
        result, pullback = jax.vjp(forward, clip_in.astype(jnp.float32), *params)
        grads = pullback(clip_cot.astype(jnp.float32))
        carry = tuple((running + extra for running, extra in zip(carry, grads[1:])))
        return (carry, (result.astype(jnp.bfloat16), grads[0].astype(jnp.bfloat16)))
    start = tuple((jnp.zeros_like(weight_arr) for weight_arr in params))
    totals, (outs_all, grads_all) = lax.scan(one_clip, start, (clip_inputs, clip_cotangents, clip_lengths))
    block_out = outs_all.reshape(inputs.shape)
    input_grad = grads_all.reshape(inputs.shape)
    return (block_out, input_grad, totals[0], totals[1], totals[2], totals[3], totals[4], totals[5], totals[6], totals[7], totals[8], totals[9], totals[10], totals[11], totals[12], totals[13], totals[14])
```

```python
from functools import partial

import jax
import jax.numpy as jnp
from jax import lax
from jax.experimental import pallas as pl
from jax.experimental.pallas import tpu as pltpu
from jax.sharding import PartitionSpec as P

H = 16
HD = 80
CHIPS = 4
CORES = 2
DEV_CLIP = CHIPS * CORES
OWN_HEADS = H // CHIPS
OWN_FEATURES = OWN_HEADS * HD
QKV_WIDTH = 1024
TILE = 256
VEC_ROWS = 16
ROW_GAIN_ONE, ROW_SHIFT_ONE, ROW_GAIN_TWO, ROW_SHIFT_TWO, ROW_BIAS_OUT, ROW_BIAS_SHRINK = range(6)
ROW_EXPAND = 8
ROW_QKV = 12

EPS = 1e-05
NEG = -1000000000.0
SCALE = HD ** (-0.5)
BF = jnp.bfloat16
F32 = jnp.float32


def dot_nn(left, right):
    return lax.dot_general(left, right, (((1,), (0,)), ((), ())), preferred_element_type=F32)


def dot_nt(left, right):
    return lax.dot_general(left, right, (((1,), (1,)), ((), ())), preferred_element_type=F32)


def dot_tn(left, right):
    return lax.dot_general(left, right, (((0,), (0,)), ((), ())), preferred_element_type=F32)


def norm_parts(rows):
    mean = jnp.mean(rows, -1, keepdims=True)
    centered = rows - mean
    inverse = lax.rsqrt(jnp.mean(centered * centered, -1, keepdims=True) + EPS)
    return centered * inverse, inverse


def norm_backward(gradient, normed, inverse, gain):
    scaled = gradient * gain
    return inverse * (
        scaled
        - jnp.mean(scaled, -1, keepdims=True)
        - normed * jnp.mean(scaled * normed, -1, keepdims=True)
    )


def place(device):
    return device // DEV_CLIP, (device % DEV_CLIP) // CORES, device % CORES


def flipped(number, by):
    low, high = number % 2, number // 2
    if by & 1:
        low = 1 - low
    if by & 2:
        high = 1 - high
    return high * 2 + low


SEMS = 160
LOCAL_SEMS = 40


def block_kernel(fused, planes, micro, tok, width, ff_own, share, ff_share, *refs):
    names = ["x", "dy", "lengths", "vec", "wq", "we", "wo", "ws"]
    names += ["bo", "ig", "vo", "gq", "ge", "go", "gs"]
    if fused:
        names += ["Lq", "Le", "Lo", "Ls", "Zq", "Ze", "Zo", "Zs"]
    names += ["Wq", "We", "Wo", "Ws", "xg", "dyg", "a2g", "drg", "act", "dhid"]
    names += ["q", "kv", "mixed", "lse", "dmix", "dq", "dl"]
    names += ["sb", "sbo", "rb", "rbo", "resid", "dresid", "vfin", "be", "bq", "vexp", "vqkv", "vrow"]
    if fused:
        names += ["so", "oo", "ao", "aq", "ae", "alq", "ale", "v1", "v2", "vz", "vp", "vs", "u0", "u1", "u2", "uz", "up", "us"]
    names += ["ssem", "rsem", "lsem"]
    r = dict(zip(names, refs, strict=True))
    r["dqkv"] = r["dhid"].at[:, :, 0:QKV_WIDTH]
    me = lax.axis_index("fsdp")
    c, k, e = place(me)
    rows = CHIPS * tok

    def chip_peer(by):
        return c * DEV_CLIP + flipped(k, by) * CORES + e

    sibling = c * DEV_CLIP + k * CORES + (1 - e)

    def plane_peer(by):
        return flipped(c, by) * DEV_CLIP + k * CORES + e

    counters = {"remote": 0, "local": 0}
    pending = []

    def send(src, dst, device):
        i = counters["remote"]
        counters["remote"] += 1
        copy = pltpu.make_async_remote_copy(
            src_ref=src, dst_ref=dst, send_sem=r["ssem"].at[i], recv_sem=r["rsem"].at[i],
            device_id=(device,), device_id_type=pl.DeviceIdType.MESH,
        )
        copy.start()
        state = {"sent": False}

        def wait_send():
            if not state["sent"]:
                state["sent"] = True
                copy.wait_send()

        copy_handle = (copy.wait_recv, wait_send)
        pending.append(wait_send)
        return copy_handle

    def local(src, dst):
        i = counters["local"]
        counters["local"] += 1
        copy = pltpu.make_async_copy(src, dst, r["lsem"].at[i])
        copy.start()
        return copy.wait

    def recv_all(handles):
        for handle in handles:
            handle[0]()

    def sent_all(handles):
        for handle in handles:
            handle[1]()

    peers = [chip_peer(by) for by in (1, 2, 3)] + [sibling]
    if fused:
        peers += [plane_peer(by) for by in range(1, planes)]
    barrier = pltpu.get_barrier_semaphore()
    for peer in peers:
        pl.semaphore_signal(barrier, inc=1, device_id=(peer,), device_id_type=pl.DeviceIdType.MESH)
    pl.semaphore_wait(barrier, len(peers))

    Wq, We, Wo, Ws = r["Wq"], r["We"], r["Wo"], r["Ws"]
    Ws2 = Ws.reshape(ff_own, width)
    flat = {name: r[name].reshape(micro * rows, width) for name in ("act", "dhid", "drg", "a2g", "dyg", "xg", "sbo")}
    chip_rows = CHIPS * share
    plane_rows = CORES * chip_rows

    def stacked(name, count, lanes):
        return flat[name].at[0:count * chip_rows].reshape(count, chip_rows, width).at[:, :, 0:lanes]

    def by_core(own, other):
        return jnp.where(e == 0, own, other), jnp.where(e == 0, other, own)

    def join_rows(own, other, count):
        first, second = by_core(own, other)
        pieces = []
        for j in range(count):
            pieces += [first[j * share:(j + 1) * share], second[j * share:(j + 1) * share]]
        return jnp.concatenate(pieces, 0)

    def split_rows(block, count):
        pieces = [block[j * share:(j + 1) * share] for j in range(2 * count)]
        return by_core(jnp.concatenate(pieces[0::2], 0), jnp.concatenate(pieces[1::2], 0))

    def join_planes(own, other, out):
        @pl.loop(0, planes)
        def _(i):
            block = join_rows(own[i].astype(F32), other[i].astype(F32), CHIPS)
            out[pl.ds(pl.multiple_of(i * plane_rows, plane_rows), plane_rows), :] = block.astype(BF)

    def split_planes(grads, own, other):
        @pl.loop(0, planes)
        def _(i):
            block = grads[pl.ds(pl.multiple_of(i * plane_rows, plane_rows), plane_rows), :].astype(F32)
            mine, theirs = split_rows(block, CHIPS)
            own[i] = mine.astype(BF)
            other[i] = theirs.astype(BF)

    def gather_start(src, dst, b):
        return [send(src, dst.at[b, k], chip_peer(by)) for by in (3, 1, 2)]

    x_local = [local(r["x"].at[b], r["xg"].at[b, k]) for b in range(micro)]
    dy_local = [local(r["dy"].at[b], r["dyg"].at[b, k]) for b in range(micro)]
    x_gather = [None] * micro
    dy_gather = [None] * micro
    if fused:
        wq_own = local(r["wq"].at[k], r["alq"].at[k])
        we_own = local(r["we"].at[k], r["ale"].at[k])
        wo_own = local(r["wo"], r["so"].at[c])
        ws_own = local(r["ws"], Ws.at[c, e])
        wq_plane = [send(r["wq"].at[flipped(k, by)], r["alq"].at[k], chip_peer(by)) for by in (3, 1, 2)]
        vec_z = [send(r["vec"], r["vz"].at[by - 1], plane_peer(by)) for by in range(1, planes)]
        x_gather[0] = gather_start(r["x"].at[0], r["xg"], 0)
        recv_all(wq_plane)
        wq_own()
        wq_mine, wq_other = stacked("drg", planes, QKV_WIDTH), stacked("a2g", planes, QKV_WIDTH)
        we_mine, we_other = stacked("act", planes, ff_own), stacked("dhid", planes, ff_own)

        def pack_plane(blocks, out):
            out[c] = jnp.concatenate([blocks[j].astype(F32) for j in range(CHIPS)], 0).astype(BF)

        pack_plane(r["alq"], wq_mine)
        wq_z = [send(wq_mine.at[c], wq_mine.at[c], plane_peer(by)) for by in range(1, planes)]
        wo_z = [send(r["wo"], r["so"].at[c], plane_peer(by)) for by in range(1, planes)]
        we_plane = [send(r["we"].at[flipped(k, by)], r["ale"].at[k], chip_peer(by)) for by in (3, 1, 2)]
        recv_all(vec_z)
        total = r["vec"][...]
        for by in range(1, planes):
            total = total + r["vz"][by - 1]
        r["v1"][...] = total
        vec_p = [send(r["v1"], r["vp"].at[by - 1], chip_peer(by)) for by in (1, 2, 3)]
        for b in range(1, micro):
            x_gather[b] = gather_start(r["x"].at[b], r["xg"], b)
        recv_all(vec_p)
        total = r["v1"][...]
        for by in (1, 2, 3):
            total = total + r["vp"][by - 1]
        r["v2"][...] = total
        vec_s = [send(r["v2"], r["vs"], sibling)]
        recv_all(we_plane)
        we_own()
        wo_own()
        ws_own()
        pack_plane(r["ale"], we_mine)
        we_z = [send(we_mine.at[c], we_mine.at[c], plane_peer(by)) for by in range(1, planes)]
        ws_z = [send(r["ws"], Ws.at[c, e], plane_peer(by)) for by in range(1, planes)]
        recv_all(vec_s)
        r["vfin"][...] = r["v2"][...] + r["vs"][...]
    else:
        loads = [local(r["wq"], Wq), local(r["we"], We), local(r["wo"], Wo), local(r["ws"], Ws2)]
        for b in range(micro):
            x_gather[b] = gather_start(r["x"].at[b], r["xg"], b)
        r["vfin"][...] = r["vec"][...]
        for load in loads:
            load()
    for b in range(micro):
        dy_gather[b] = gather_start(r["dy"].at[b], r["dyg"], b)

    vfin = r["vfin"]
    own_row = lax.broadcasted_iota(jnp.int32, (CHIPS, width), 0) == k
    r["be"][...] = jnp.sum(jnp.where(own_row, vfin[ROW_EXPAND:ROW_EXPAND + CHIPS, :], 0.0), 0, keepdims=True)
    r["bq"][...] = jnp.sum(jnp.where(own_row, vfin[ROW_QKV:ROW_QKV + CHIPS, :], 0.0), 0, keepdims=True)[:, :QKV_WIDTH]
    r["vrow"][...] = jnp.zeros_like(r["vrow"])
    r["vexp"][...] = jnp.zeros_like(r["vexp"])
    r["vqkv"][...] = jnp.zeros_like(r["vqkv"])

    def vec_row(index):
        return vfin[index:index + 1, :]

    def add_row(index, value):
        r["vrow"][index:index + 1, :] += value

    for b in range(micro):
        x_local[b]()
        recv_all(x_gather[b])

        @pl.loop(0, CHIPS)
        def _(i):
            normed, _inverse = norm_parts(r["xg"][b, i].astype(F32))
            r["xg"][b, i] = (normed * vec_row(ROW_GAIN_ONE) + vec_row(ROW_SHIFT_ONE)).astype(BF)

    if fused:
        recv_all(wq_z)
        wq_s = [send(wq_mine, wq_other, sibling)]
        recv_all(wo_z)
        wo_s = [send(r["so"], r["oo"], sibling)]
        recv_all(wq_s)
        join_planes(wq_mine, wq_other, Wq)

    kv_swap = [None] * micro
    half = rows // 2
    for b in range(micro):

        @pl.loop(0, 2)
        def _(i):
            lines = r["xg"].reshape(micro, rows, width)[b, pl.ds(pl.multiple_of(i * half, half), half), :]
            out = (dot_nn(lines, Wq[...]) + r["bq"][...]).astype(BF)
            at = pl.ds(pl.multiple_of(i * half, half), half)
            for h in range(OWN_HEADS):
                r["q"][b, h, at, :] = out[:, h * HD:(h + 1) * HD]
                for part in range(2):
                    low = (part + 1) * OWN_FEATURES + h * HD
                    r["kv"][b, part, h, e, at, :] = out[:, low:low + HD]

        kv_swap[b] = [send(r["kv"].at[b, :, :, e], r["kv"].at[b, :, :, e], sibling)]

    keys = CORES * rows
    chunk_places = [(2 * (i % CHIPS) + i // CHIPS) * tok for i in range(DEV_CLIP)]

    def masked_scores(b, key_rows, query_rows):
        raw = dot_nt(key_rows, query_rows)
        index = lax.broadcasted_iota(jnp.int32, (tok, raw.shape[1]), 0)
        length = r["lengths"][b, c]
        return jnp.concatenate(
            [
                jnp.where(index < length - first, raw[i * tok:(i + 1) * tok] * SCALE, NEG)
                for i, first in enumerate(chunk_places)
            ],
            0,
        )

    def attend(b):
        @pl.loop(0, OWN_HEADS * 2)
        def _(step):
            h, part = step // 2, step % 2
            at = pl.ds(pl.multiple_of(part * half, half), half)
            key_rows = r["kv"][b, 0, h].reshape(keys, HD)
            value_rows = r["kv"][b, 1, h].reshape(keys, HD)
            scores = masked_scores(b, key_rows, r["q"][b, h, at, :])
            peak = jnp.max(scores, 0, keepdims=True)
            exponent = jnp.exp(scores - peak)
            sums = jnp.sum(exponent, 0, keepdims=True)
            probs = (exponent * (1.0 / sums)).astype(BF)
            r["lse"][b, h, :, at] = peak + jnp.log(sums)
            r["mixed"][b, h, :, at] = dot_tn(value_rows, probs).astype(BF)

    def reduce_start(slots, landing, b):
        return [send(slots.at[b, flipped(k, by)], landing.at[b, by - 1], chip_peer(by)) for by in (3, 1, 2)]

    def reduced(slots, landing, b):
        total = slots[b, k].astype(F32)
        for by in (1, 2, 3):
            total = total + landing[b, by - 1].astype(F32)
        return total

    def tiles(count, body):
        @pl.loop(0, count)
        def _(i):
            body(pl.ds(pl.multiple_of(i * TILE, TILE), TILE))

    def partial_sum(slots, b, product):
        view = slots.reshape(micro, rows, width)

        def body(at):
            view[b, :, at] = product(at).astype(BF)

        tiles(width // TILE, body)

    sb, sbo, rb, rbo = r["sb"], r["sbo"], r["rb"], r["rbo"]
    first_reduce = [None] * micro
    for b in range(micro):
        recv_all(kv_swap[b])
        attend(b)
        if fused and b == 0:
            recv_all(wo_s)
            for i in range(planes):
                pair = join_rows(r["so"][i].astype(F32), r["oo"][i].astype(F32), 1)
                Wo[i * HD:(i + 1) * HD, :] = pair.astype(BF)
        lines = r["mixed"].reshape(micro, OWN_FEATURES, rows)
        partial_sum(sb, b, lambda at: dot_tn(lines[b], Wo[:, at]))
        first_reduce[b] = reduce_start(sb, rb, b)

    second_gather = [None] * micro
    for b in range(micro):
        recv_all(first_reduce[b])
        residual = r["x"][b].astype(F32) + reduced(sb, rb, b) + vec_row(ROW_BIAS_OUT)
        r["resid"][b] = residual
        normed, _inverse = norm_parts(residual)
        r["a2g"][b, k] = (normed * vec_row(ROW_GAIN_TWO) + vec_row(ROW_SHIFT_TWO)).astype(BF)
        second_gather[b] = gather_start(r["a2g"].at[b, k], r["a2g"], b)

    if fused:
        recv_all(we_z)
        we_s = [send(we_mine, we_other, sibling)]
        recv_all(ws_z)
        ws_s = [send(Ws.at[:, e], Ws.at[:, e], sibling)]
        recv_all(we_s)
        sent_all(we_s + we_z + wq_s + wq_z)
        join_planes(we_mine, we_other, We)
        recv_all(ws_s)

    a2_rows = r["a2g"].reshape(micro, rows, width)
    dy_rows = r["dyg"].reshape(micro, rows, width)
    dr_rows = r["drg"].reshape(micro, rows, width)
    a1_rows = r["xg"].reshape(micro, rows, width)
    hidden_reduce = [None] * micro
    for b in range(micro):
        recv_all(second_gather[b])
        dy_local[b]()
        recv_all(dy_gather[b])

        def feed(at):
            hidden = dot_nn(a2_rows[b], We[:, at]) + r["be"][:, at]
            grad_active = dot_nt(dy_rows[b], Ws2[at, :]).astype(BF).astype(F32)
            normal = 0.5 * (1.0 + lax.erf(hidden * 0.7071067811865476))
            r["act"][b, :, at] = (hidden * normal).astype(BF)
            density = jnp.exp(-0.5 * hidden * hidden) * 0.3989422804014327
            grad_hidden = (grad_active * (normal + hidden * density)).astype(BF)
            r["dhid"][b, :, at] = grad_hidden
            r["vexp"][:, at] += jnp.sum(grad_hidden.astype(F32), 0, keepdims=True)

        tiles(ff_own // TILE, feed)
        sent_all(first_reduce[b])
        partial_sum(sb, b, lambda at: dot_nt(r["dhid"][b], We[at, :]))
        hidden_reduce[b] = reduce_start(sb, rb, b)

    def finish_hidden(b):
        recv_all(hidden_reduce[b])
        gradient = reduced(sb, rb, b)
        normed, inverse = norm_parts(r["resid"][b])
        dy_own = r["dy"][b].astype(F32)
        total = dy_own + norm_backward(gradient, normed, inverse, vec_row(ROW_GAIN_TWO))
        r["dresid"][b] = total
        r["drg"][b, k] = total.astype(BF)
        gathers = gather_start(r["drg"].at[b, k], r["drg"], b)
        add_row(ROW_GAIN_TWO, jnp.sum(gradient * normed, 0, keepdims=True))
        add_row(ROW_SHIFT_TWO, jnp.sum(gradient, 0, keepdims=True))
        add_row(ROW_BIAS_OUT, jnp.sum(total, 0, keepdims=True))
        add_row(ROW_BIAS_SHRINK, jnp.sum(dy_own, 0, keepdims=True))
        return gathers

    resid_gather = [None] * micro
    out_reduce = [None] * micro
    for b in range(micro):
        partial_sum(sbo, b, lambda at: dot_nn(r["act"][b], Ws2[:, at]))
        resid_gather[b] = finish_hidden(b)
        out_reduce[b] = reduce_start(sbo, rbo, b)

    def weight_gradient(count, lefts, rights, out):
        def body(at):
            total = dot_tn(lefts[0, :, at], rights[0])
            for b in range(1, micro):
                total = total + dot_tn(lefts[b, :, at], rights[b])
            out[at, :] = total.astype(BF)

        tiles(count // TILE, body)

    if fused:
        sent_all(ws_z + ws_s + wo_z + wo_s + wq_plane + we_plane)

    def sibling_add(handles, landing, fetched, out, mine):
        recv_all(handles)
        sent_all(handles)
        local(landing, fetched)()

        @pl.loop(0, planes)
        def _(i):
            out[i] = (mine(i).astype(F32) + fetched[i].astype(F32)).astype(BF)

    def plane_start(space, landing):
        return [send(space.at[flipped(c, by)], landing.at[by - 1], plane_peer(by)) for by in range(1, planes)]

    def plane_sum(handles, space, landing, arrived):
        recv_all(handles)
        local(landing, arrived)()
        total = space[c].astype(F32)
        for by in range(1, planes):
            total = total + arrived[by - 1].astype(F32)
        return total

    weight_gradient(ff_own, r["act"], dy_rows, Ws2)
    if fused:
        gs_s = [send(Ws.at[:, 1 - e], r["Ls"], sibling)]
    weight_gradient(width, a2_rows, r["dhid"], We)
    if fused:
        space_e, other_e = stacked("act", planes, ff_own), stacked("dhid", planes, ff_own)
        split_planes(We, space_e, other_e)
        ge_s = [send(other_e, r["Le"], sibling)]
        sent_all(second_gather[0] + second_gather[1] + dy_gather[0] + dy_gather[1])
        space_s = flat["dyg"].at[0:planes * ff_share].reshape(planes, ff_share, width)
        arrived_s = flat["a2g"].at[0:(planes - 1) * ff_share].reshape(planes - 1, ff_share, width)
        arrived_e = flat["a2g"].at[512:512 + (planes - 1) * chip_rows].reshape(planes - 1, chip_rows, width)
        sibling_add(gs_s, r["Ls"], space_s, space_s, lambda i: Ws[i, e])
        gs_z = plane_start(space_s, r["Zs"])
        sibling_add(ge_s, r["Le"], other_e, space_e, lambda i: space_e[i])
        ge_z = plane_start(space_e, r["Ze"])

    def mixed_gradient(b):
        recv_all(resid_gather[b])

        @pl.loop(0, 2)
        def _(i):
            at = pl.ds(pl.multiple_of(i * half, half), half)
            out = dot_nt(dr_rows[b, at, :], Wo[...]).astype(BF)
            for h in range(OWN_HEADS):
                r["dmix"][h, at, :] = out[:, h * HD:(h + 1) * HD]

    def attend_back(b):
        sent_all(kv_swap[b])

        @pl.loop(0, OWN_HEADS)
        def _(h):
            key_rows = r["kv"][b, 0, h].reshape(keys, HD)
            value_rows = r["kv"][b, 1, h].reshape(keys, HD)
            grad_keys = None
            grad_values = None
            for part in range(2):
                at = pl.ds(part * half, half)
                query_rows = r["q"][b, h, at, :]
                mix_rows = r["dmix"][h, at, :]
                probs = jnp.exp(masked_scores(b, key_rows, query_rows) - r["lse"][b, h, :, at])
                grad_probs = dot_nt(value_rows, mix_rows)
                inner = jnp.sum(probs * grad_probs, 0, keepdims=True)
                grad_scores = (probs * (grad_probs - inner)).astype(BF)
                grad_query = dot_tn(key_rows, grad_scores) * SCALE
                r["dq"][h, at, :] = grad_query.T.astype(BF)
                key_term = dot_nn(grad_scores, query_rows)
                value_term = dot_nn(probs.astype(BF), mix_rows)
                grad_keys = key_term if grad_keys is None else grad_keys + key_term
                grad_values = value_term if grad_values is None else grad_values + value_term
            r["kv"][b, 0, h] = (grad_keys * SCALE).astype(BF).reshape(CORES, rows, HD)
            r["kv"][b, 1, h] = grad_values.astype(BF).reshape(CORES, rows, HD)

        return [send(r["kv"].at[b, :, :, 1 - e], r["dl"].at[b], sibling)]

    def join_gradients(b, handles):
        recv_all(handles)

        @pl.loop(0, CHIPS)
        def _(i):
            at = pl.ds(pl.multiple_of(i * tok, tok), tok)
            pieces = [r["dq"][h, at, :] for h in range(OWN_HEADS)]
            for part in range(2):
                for h in range(OWN_HEADS):
                    pair = r["kv"][b, part, h, e, at, :].astype(F32) + r["dl"][b, part, h, at, :].astype(F32)
                    pieces.append(pair.astype(BF))
            pieces.append(jnp.zeros((tok, QKV_WIDTH - 3 * OWN_FEATURES), BF))
            line = jnp.concatenate(pieces, 1)
            r["dqkv"][b, at, :] = line
            r["vqkv"][...] += jnp.sum(line.astype(F32), 0, keepdims=True)

    def input_start(b):
        sent_all(hidden_reduce[b])
        partial_sum(sb, b, lambda at: dot_nt(r["dqkv"][b], Wq[at, :]))
        return reduce_start(sb, rb, b)

    def finish_input(b, handles):
        recv_all(handles)
        gradient = reduced(sb, rb, b)
        normed, inverse = norm_parts(r["x"][b].astype(F32))
        back = norm_backward(gradient, normed, inverse, vec_row(ROW_GAIN_ONE))
        r["ig"][b] = (r["dresid"][b] + back).astype(BF)
        add_row(ROW_GAIN_ONE, jnp.sum(gradient * normed, 0, keepdims=True))
        add_row(ROW_SHIFT_ONE, jnp.sum(gradient, 0, keepdims=True))

    def finish_out(b):
        recv_all(out_reduce[b])
        total = r["resid"][b] + reduced(sbo, rbo, b) + vec_row(ROW_BIAS_SHRINK)
        r["bo"][b] = total.astype(BF)

    input_reduce = [None] * micro
    swap = None
    for b in range(micro):
        mixed_gradient(b)
        if b == micro - 1:
            mixed2 = r["mixed"].reshape(micro, OWN_FEATURES, rows)
            lead = dot_nn(mixed2[0], dr_rows[0])
            for other in range(1, micro):
                lead = lead + dot_nn(mixed2[other], dr_rows[other])
            if fused:
                space_o, other_o, arrived_o = r["so"], r["oo"], r["ao"]
                for i in range(planes):
                    mine, theirs = split_rows(lead[i * HD:(i + 1) * HD], 1)
                    space_o[i] = mine.astype(BF)
                    other_o[i] = theirs.astype(BF)
                go_s = [send(other_o, r["Lo"], sibling)]
            else:
                Wo[...] = lead.astype(BF)
        if b > 0:
            join_gradients(b - 1, swap)
            input_reduce[b - 1] = input_start(b - 1)
        swap = attend_back(b)
    last = micro - 1
    join_gradients(last, swap)
    input_reduce[last] = input_start(last)
    weight_gradient(width, a1_rows, r["dqkv"], Wq)
    if fused:
        sent_all(resid_gather[0] + resid_gather[1])
        space_q, other_q = stacked("drg", planes, QKV_WIDTH), stacked("xg", planes, QKV_WIDTH)
        arrived_q = stacked("sbo", planes - 1, QKV_WIDTH)
        split_planes(Wq, space_q, other_q)
        gq_s = [send(other_q, r["Lq"], sibling)]
        sibling_add(go_s, r["Lo"], other_o, space_o, lambda i: space_o[i])
        go_z = plane_start(space_o, r["Zo"])
        sibling_add(gq_s, r["Lq"], other_q, space_q, lambda i: space_q[i])
        gq_z = plane_start(space_q, r["Zq"])
        sent_all(out_reduce[0] + out_reduce[1])
    for b in range(micro):
        finish_out(b)
    for b in range(micro):
        finish_input(b, input_reduce[b])

    mine_e = lax.broadcasted_iota(jnp.int32, (VEC_ROWS, width), 0) == ROW_EXPAND + k
    mine_q = lax.broadcasted_iota(jnp.int32, (VEC_ROWS, width), 0) == ROW_QKV + k
    padded = jnp.concatenate([r["vqkv"][...], jnp.zeros((1, width - QKV_WIDTH), F32)], 1)
    sums = r["vrow"][...] + jnp.where(mine_e, r["vexp"][...], 0.0) + jnp.where(mine_q, padded, 0.0)
    if fused:
        r["u0"][...] = sums

        def unpack_plane(total, blocks):
            for j in range(CHIPS):
                blocks[j] = total[j * share:(j + 1) * share].astype(BF)

        sum_z = [send(r["u0"], r["uz"].at[by - 1], plane_peer(by)) for by in range(1, planes)]
        r["gs"][...] = plane_sum(gs_z, space_s, r["Zs"], arrived_s)
        recv_all(sum_z)
        total = r["u0"][...]
        for by in range(1, planes):
            total = total + r["uz"][by - 1]
        r["u1"][...] = total
        sum_p = [send(r["u1"], r["up"].at[by - 1], chip_peer(by)) for by in (1, 2, 3)]
        unpack_plane(plane_sum(ge_z, space_e, r["Ze"], arrived_e), r["ae"])
        ge_p = [send(r["ae"].at[flipped(k, by)], r["ale"].at[k], chip_peer(by)) for by in (3, 1, 2)]
        recv_all(sum_p)
        total = r["u1"][...]
        for by in (1, 2, 3):
            total = total + r["up"][by - 1]
        r["u2"][...] = total
        sum_s = [send(r["u2"], r["us"], sibling)]
        unpack_plane(plane_sum(gq_z, space_q, r["Zq"], arrived_q), r["aq"])
        gq_p = [send(r["aq"].at[flipped(k, by)], r["alq"].at[k], chip_peer(by)) for by in (3, 1, 2)]
        r["go"][...] = plane_sum(go_z, space_o, r["Zo"], arrived_o)
        recv_all(sum_s)
        r["vo"][...] = r["u2"][...] + r["us"][...]
        recv_all(ge_p)
        r["ge"][k] = r["ae"][k].astype(F32)
        for by in (1, 2, 3):
            r["ge"][flipped(k, by)] = r["ale"][flipped(k, by)].astype(F32)
        recv_all(gq_p)
        r["gq"][k] = r["aq"][k].astype(F32)
        for by in (1, 2, 3):
            r["gq"][flipped(k, by)] = r["alq"][flipped(k, by)].astype(F32)
    else:
        r["vo"][...] = sums
        stores = [local(Wq, r["gq"]), local(We, r["ge"]), local(Wo, r["go"]), local(Ws2, r["gs"])]
        for store in stores:
            store()
    for wait in pending:
        wait()


def run_block(fused, planes, x, dy, lengths, vec, wq, we, wo, ws, share, ff_share):
    micro, tok, width = x.shape
    ff_own = width
    rows = CHIPS * tok
    vmem = pl.BlockSpec(memory_space=pltpu.VMEM)
    anywhere = pl.BlockSpec(memory_space=pl.ANY)
    smem = pl.BlockSpec(memory_space=pltpu.SMEM)

    def shape(*dims, dtype=BF):
        return jax.ShapeDtypeStruct(dims, dtype)

    outs = [
        (shape(micro, tok, width), vmem),
        (shape(micro, tok, width), vmem),
        (shape(VEC_ROWS, width, dtype=F32), vmem),
    ]
    if fused:
        outs += [
            (shape(CHIPS, share, QKV_WIDTH, dtype=F32), vmem),
            (shape(CHIPS, share, ff_own, dtype=F32), vmem),
            (shape(share, width, dtype=F32), vmem),
            (shape(ff_share, width, dtype=F32), vmem),
        ]
        for count in (planes, planes - 1):
            outs += [
                (shape(count, CHIPS * share, QKV_WIDTH), anywhere),
                (shape(count, CHIPS * share, ff_own), anywhere),
                (shape(count, share, width), anywhere),
                (shape(count, ff_share, width), anywhere),
            ]
    else:
        outs += [
            (shape(width, QKV_WIDTH), anywhere),
            (shape(width, ff_own), anywhere),
            (shape(OWN_FEATURES, width), anywhere),
            (shape(ff_own, width), anywhere),
        ]
    if fused:
        weights = [
            pltpu.VMEM((width, QKV_WIDTH), BF),
            pltpu.VMEM((width, ff_own), BF),
            pltpu.VMEM((OWN_FEATURES, width), BF),
            pltpu.VMEM((planes, CORES, ff_share, width), BF),
        ]
    else:
        weights = [
            pltpu.VMEM((width, QKV_WIDTH), BF),
            pltpu.VMEM((width, ff_own), BF),
            pltpu.VMEM((OWN_FEATURES, width), BF),
            pltpu.VMEM((ff_own, width), BF),
        ]
    scratch = weights + [
        pltpu.VMEM((micro, CHIPS, tok, width), BF),
        pltpu.VMEM((micro, CHIPS, tok, width), BF),
        pltpu.VMEM((micro, CHIPS, tok, width), BF),
        pltpu.VMEM((micro, CHIPS, tok, width), BF),
        pltpu.VMEM((micro, rows, ff_own), BF),
        pltpu.VMEM((micro, rows, ff_own), BF),
        pltpu.VMEM((micro, OWN_HEADS, rows, HD), BF),
        pltpu.VMEM((micro, 2, OWN_HEADS, CORES, rows, HD), BF),
        pltpu.VMEM((micro, OWN_HEADS, HD, rows), BF),
        pltpu.VMEM((micro, OWN_HEADS, 1, rows), F32),
        pltpu.VMEM((OWN_HEADS, rows, HD), BF),
        pltpu.VMEM((OWN_HEADS, rows, HD), BF),
        pltpu.VMEM((micro, 2, OWN_HEADS, rows, HD), BF),
        pltpu.VMEM((micro, CHIPS, tok, width), BF),
        pltpu.VMEM((micro, CHIPS, tok, width), BF),
        pltpu.VMEM((micro, CHIPS - 1, tok, width), BF),
        pltpu.VMEM((micro, CHIPS - 1, tok, width), BF),
        pltpu.VMEM((micro, tok, width), F32),
        pltpu.VMEM((micro, tok, width), F32),
        pltpu.VMEM((VEC_ROWS, width), F32),
        pltpu.VMEM((1, ff_own), F32),
        pltpu.VMEM((1, QKV_WIDTH), F32),
        pltpu.VMEM((1, ff_own), F32),
        pltpu.VMEM((1, QKV_WIDTH), F32),
        pltpu.VMEM((VEC_ROWS, width), F32),
    ]
    if fused:
        scratch += [
            pltpu.VMEM((planes, share, width), BF),
            pltpu.VMEM((planes, share, width), BF),
            pltpu.VMEM((planes - 1, share, width), BF),
            pltpu.VMEM((CHIPS, share, QKV_WIDTH), BF),
            pltpu.VMEM((CHIPS, share, ff_own), BF),
            pltpu.VMEM((CHIPS, share, QKV_WIDTH), BF),
            pltpu.VMEM((CHIPS, share, ff_own), BF),
        ]
        for _ in range(2):
            if _ == 1:
                scratch.append(pltpu.VMEM((VEC_ROWS, width), F32))
            scratch += [
                pltpu.VMEM((VEC_ROWS, width), F32),
                pltpu.VMEM((VEC_ROWS, width), F32),
                pltpu.VMEM((planes - 1, VEC_ROWS, width), F32),
                pltpu.VMEM((CHIPS - 1, VEC_ROWS, width), F32),
                pltpu.VMEM((VEC_ROWS, width), F32),
            ]
    scratch += [
        pltpu.SemaphoreType.DMA((SEMS,)),
        pltpu.SemaphoreType.DMA((SEMS,)),
        pltpu.SemaphoreType.DMA((LOCAL_SEMS,)),
    ]
    return pl.pallas_call(
        partial(block_kernel, fused, planes, micro, tok, width, ff_own, share, ff_share),
        out_shape=[out for out, _ in outs],
        in_specs=[vmem, vmem, smem, vmem, anywhere, anywhere, anywhere, anywhere],
        out_specs=[spec for _, spec in outs],
        scratch_shapes=scratch,
        compiler_params=pltpu.CompilerParams(
            collective_id=0, has_side_effects=True, vmem_limit_bytes=63 * 1000 * 1000
        ),
    )(x, dy, lengths, vec, wq, we, wo, ws)


def by_chip(matrix, part):
    rows = matrix.shape[0]
    return matrix.reshape(rows, -1, CHIPS, part).transpose(2, 0, 1, 3).reshape(CHIPS, rows, -1)


def from_chips(blocks, part):
    rows = blocks.shape[1]
    return blocks.reshape(CHIPS, rows, -1, part).transpose(1, 2, 0, 3).reshape(rows, -1)


def body(
    inputs, cotangent, lengths, first_gain, first_shift, query_weight, query_bias, key_weight,
    value_weight, value_bias, output_weight, output_bias, second_gain, second_shift,
    expand_weight, expand_bias, shrink_weight, shrink_bias,
):
    device = lax.axis_index("fsdp")
    count = lax.axis_size("fsdp")
    c, k, e = place(device)
    planes = count // DEV_CLIP
    width = inputs.shape[2]
    share = query_weight.shape[0]
    ff_share = shrink_weight.shape[0]
    ff_part = width // 4
    fused = planes == 4 and share * 2 == HD and ff_share * 2 == ff_part
    plain = (first_gain, first_shift, second_gain, second_shift, output_bias, shrink_bias)
    low = [w.astype(BF) for w in (query_weight, key_weight, value_weight, expand_weight, output_weight, shrink_weight)]
    if fused:
        vec = jnp.zeros((VEC_ROWS, width), F32)
        vec = lax.dynamic_update_slice(vec, jnp.stack(plain), (0, device * share))
        vec = lax.dynamic_update_slice(vec, expand_bias[None], (ROW_EXPAND + k, (2 * c + e) * ff_share))
        at = (2 * c + e) * share
        vec = lax.dynamic_update_slice(vec, query_bias[None], (ROW_QKV + k, at))
        vec = lax.dynamic_update_slice(vec, value_bias[None], (ROW_QKV + k, 2 * OWN_FEATURES + at))
        wide = [by_chip(w, HD) for w in low[:3]]
        wide.append(jnp.zeros((CHIPS, share, QKV_WIDTH - 3 * OWN_FEATURES), BF))
        wq = jnp.concatenate(wide, 2)
        we = by_chip(low[3], ff_part)
        got = run_block(True, planes, inputs, cotangent, lengths, vec, wq, we, low[4], low[5], share, ff_share)
        block_out, input_grad, sums, gq, ge, grad_output_w, grad_shrink_w = got[:7]
        grad_query_w, grad_key_w, grad_value_w = (
            from_chips(gq[:, :, i * OWN_FEATURES:(i + 1) * OWN_FEATURES], HD) for i in range(3)
        )
        grad_expand_w = from_chips(ge, ff_part)
        own = lax.dynamic_slice(sums, (0, device * share), (len(plain), share))
        owned = [own[i] for i in range(len(plain))]
        grad_expand_b = lax.dynamic_slice(sums, (ROW_EXPAND + k, (2 * c + e) * ff_share), (1, ff_share))[0]
        grad_query_b = lax.dynamic_slice(sums, (ROW_QKV + k, at), (1, share))[0]
        grad_value_b = lax.dynamic_slice(sums, (ROW_QKV + k, 2 * OWN_FEATURES + at), (1, share))[0]
    else:

        def whole(array):
            return lax.all_gather(array, "fsdp", axis=0, tiled=True)

        def mine(blocks):
            return lax.dynamic_index_in_dim(blocks, k, 0, keepdims=False)

        full = [whole(w) for w in low]
        pieces = [mine(by_chip(w, HD)) for w in full[:3]]
        pieces.append(jnp.zeros((width, QKV_WIDTH - 3 * OWN_FEATURES), BF))
        wq = jnp.concatenate(pieces, 1)
        we = mine(by_chip(full[3], ff_part))
        wo = mine(by_chip(full[4].T, HD)).T
        ws = mine(by_chip(full[5].T, ff_part)).T
        blank = jnp.zeros((2, width), F32)
        bias_e = by_chip(whole(expand_bias)[None], ff_part)[:, 0]
        bias_q = by_chip(whole(query_bias)[None], HD)[:, 0]
        bias_v = by_chip(whole(value_bias)[None], HD)[:, 0]
        bias_rows = jnp.concatenate(
            [bias_q, jnp.zeros_like(bias_q), bias_v, jnp.zeros((CHIPS, width - 3 * OWN_FEATURES), F32)], 1
        )
        vec = jnp.concatenate([jnp.stack([whole(v) for v in plain]), blank, bias_e, bias_rows])
        got = run_block(False, planes, inputs, cotangent, lengths, vec, wq, we, wo, ws, share, ff_share)
        block_out, input_grad, sums, gq, ge, go, gs = got[:7]

        def spread(block, part):
            places = lax.broadcasted_iota(jnp.int32, (CHIPS, 1, 1), 0) == k
            return from_chips(jnp.where(places, block.astype(F32)[None], 0.0), part)

        def owned_sum(array):
            return lax.psum_scatter(array, "fsdp", scatter_dimension=0, tiled=True)

        grad_query_w, grad_key_w, grad_value_w = (
            owned_sum(spread(gq[:, i * OWN_FEATURES:(i + 1) * OWN_FEATURES], HD)) for i in range(3)
        )
        grad_expand_w = owned_sum(spread(ge, ff_part))
        grad_output_w = owned_sum(spread(go.T, HD).T)
        grad_shrink_w = owned_sum(spread(gs.T, ff_part).T)
        owned = [owned_sum(sums[i]) for i in range(len(plain))]
        sums_q = sums[ROW_QKV:ROW_QKV + CHIPS, None]
        grad_expand_b = owned_sum(from_chips(sums[ROW_EXPAND:ROW_EXPAND + CHIPS, None], ff_part)[0])
        grad_query_b = owned_sum(from_chips(sums_q[:, :, :OWN_FEATURES], HD)[0])
        grad_value_b = owned_sum(from_chips(sums_q[:, :, 2 * OWN_FEATURES:3 * OWN_FEATURES], HD)[0])
    return (
        block_out,
        input_grad,
        owned[0],
        owned[1],
        grad_query_w,
        grad_query_b,
        grad_key_w,
        grad_value_w,
        grad_value_b,
        grad_output_w,
        owned[4],
        owned[2],
        owned[3],
        grad_expand_w,
        grad_expand_b,
        grad_shrink_w,
        owned[5],
    )


def solution(mesh):
    rows, matrix, vector = P(None, "fsdp", None), P("fsdp", None), P("fsdp")
    in_specs = (
        rows, rows, P(), vector, vector, matrix, vector, matrix, matrix, vector, matrix, vector,
        vector, vector, matrix, vector, matrix, vector,
    )
    out_specs = (
        rows, rows, vector, vector, matrix, vector, matrix, matrix, vector, matrix, vector,
        vector, vector, matrix, vector, matrix, vector,
    )
    return jax.shard_map(body, mesh=mesh, in_specs=in_specs, out_specs=out_specs, check_vma=False)
```

```python
from functools import partial

import jax
import jax.numpy as jnp
from jax import lax
from jax.experimental import pallas as pl
from jax.experimental.pallas import tpu as pltpu
from jax.sharding import PartitionSpec as P

H = 16
HD = 80
CHIPS = 4
CORES = 2
DEV_CLIP = CHIPS * CORES
OWN_HEADS = H // CHIPS
OWN_FEATURES = OWN_HEADS * HD
QKV_WIDTH = 1024
TILE = 256
VEC_ROWS = 16
ROW_GAIN_ONE, ROW_SHIFT_ONE, ROW_GAIN_TWO, ROW_SHIFT_TWO, ROW_BIAS_OUT, ROW_BIAS_SHRINK = range(6)
ROW_EXPAND = 8
ROW_QKV = 12

EPS = 1e-05
NEG = -1000000000.0
SCALE = HD ** (-0.5)
BF = jnp.bfloat16
F32 = jnp.float32


def dot_nn(left, right):
    return lax.dot_general(left, right, (((1,), (0,)), ((), ())), preferred_element_type=F32)


def dot_nt(left, right):
    return lax.dot_general(left, right, (((1,), (1,)), ((), ())), preferred_element_type=F32)


def dot_tn(left, right):
    return lax.dot_general(left, right, (((0,), (0,)), ((), ())), preferred_element_type=F32)


def norm_parts(rows):
    mean = jnp.mean(rows, -1, keepdims=True)
    centered = rows - mean
    inverse = lax.rsqrt(jnp.mean(centered * centered, -1, keepdims=True) + EPS)
    return centered * inverse, inverse


def norm_backward(gradient, normed, inverse, gain):
    scaled = gradient * gain
    return inverse * (
        scaled
        - jnp.mean(scaled, -1, keepdims=True)
        - normed * jnp.mean(scaled * normed, -1, keepdims=True)
    )


def place(device):
    return device // DEV_CLIP, (device % DEV_CLIP) // CORES, device % CORES


def flipped(number, by):
    low, high = number % 2, number // 2
    if by & 1:
        low = 1 - low
    if by & 2:
        high = 1 - high
    return high * 2 + low


SEMS = 240
LOCAL_SEMS = 40


def block_kernel(fused, planes, micro, tok, width, ff_own, share, ff_share, *refs):
    names = ["x", "dy", "lengths", "vec", "wq", "we", "wo", "ws"]
    names += ["bo", "ig", "vo", "gq", "ge", "go", "gs"]
    if fused:
        names += ["Lq", "Le", "Lo", "Ls"]
    names += ["Wq", "We", "Wo", "Ws", "xg", "dyg", "a2g", "drg", "act", "dhid"]
    names += ["q", "kv", "mixed", "lse", "dmix", "dq", "dl"]
    names += ["sb", "sbo", "rb", "rbo", "resid", "dresid", "vfin", "be", "bq", "vexp", "vqkv", "vrow"]
    if fused:
        names += ["so", "oo", "ao", "aq", "ae", "alq", "ale", "v1", "v2", "vz", "vp", "vs", "u0", "u1", "u2", "uz", "up", "us"]
        names += ["ready", "ready_q"]
    names += ["ssem", "rsem", "lsem"]
    r = dict(zip(names, refs, strict=True))
    r["dqkv"] = r["dhid"].at[:, :, 0:QKV_WIDTH]
    me = lax.axis_index("fsdp")
    c, k, e = place(me)
    rows = CHIPS * tok

    def chip_peer(by):
        return c * DEV_CLIP + flipped(k, by) * CORES + e

    sibling = c * DEV_CLIP + k * CORES + (1 - e)

    def plane_peer(by):
        return flipped(c, by) * DEV_CLIP + k * CORES + e

    counters = {"remote": 0, "local": 0}
    pending = []

    def send(src, dst, device):
        i = counters["remote"]
        counters["remote"] += 1
        copy = pltpu.make_async_remote_copy(
            src_ref=src, dst_ref=dst, send_sem=r["ssem"].at[i], recv_sem=r["rsem"].at[i],
            device_id=(device,), device_id_type=pl.DeviceIdType.MESH,
        )
        copy.start()
        state = {"sent": False}

        def wait_send():
            if not state["sent"]:
                state["sent"] = True
                copy.wait_send()

        copy_handle = (copy.wait_recv, wait_send)
        pending.append(wait_send)
        return copy_handle

    def send_if(held, src, dst, device, due, arriving):
        i = counters["remote"]
        counters["remote"] += 1

        def copy(source, target, to):
            return pltpu.make_async_remote_copy(
                src_ref=source, dst_ref=target, send_sem=r["ssem"].at[i], recv_sem=r["rsem"].at[i],
                device_id=(to,), device_id_type=pl.DeviceIdType.MESH,
            )

        @pl.when(held)
        def _():
            copy(src(), dst(), device).start()

        state = {"sent": False}

        def wait_send():
            if not state["sent"]:
                state["sent"] = True

                @pl.when(held)
                def _():
                    copy(src(), dst(), device).wait_send()

        def wait_recv():
            @pl.when(due)
            def _():
                copy(arriving(), arriving(), sibling).wait_recv()

        copy_handle = (wait_recv, wait_send)
        pending.append(wait_send)
        return copy_handle

    def line_group(mine, theirs):
        return {"mine": mine, "theirs": theirs, "steps": [], "swaps": []}

    def forward(group, step):
        mine, theirs = group["mine"], group["theirs"]
        if step > 0:
            recv_all(group["steps"][step - 1])
        if step < planes - 1:
            n = step + 1
            group["steps"].append([
                send_if(
                    (c >= n - 1) & (c < planes - 1), lambda: mine(c - n + 1), lambda: mine(c - n + 1),
                    me + DEV_CLIP, c >= n, lambda: mine(c - n),
                ),
                send_if(
                    (c + n - 1 < planes) & (c >= 1), lambda: mine(c + n - 1), lambda: mine(c + n - 1),
                    me - DEV_CLIP, c + n < planes, lambda: mine(c + n),
                ),
            ])
        if step == 0:
            group["swaps"].append(send(mine(c), theirs(c), sibling))
        else:
            for held, i in ((c >= step, c - step), (c + step < planes, c + step)):
                group["swaps"].append(
                    send_if(
                        held, lambda i=i: mine(i), lambda i=i: theirs(i), sibling, held, lambda i=i: theirs(i)
                    )
                )

    def group_sent(group):
        sent_all(sum(group["steps"], []) + group["swaps"])

    def local(src, dst):
        i = counters["local"]
        counters["local"] += 1
        copy = pltpu.make_async_copy(src, dst, r["lsem"].at[i])
        copy.start()
        return copy.wait

    def recv_all(handles):
        for handle in handles:
            handle[0]()

    def sent_all(handles):
        for handle in handles:
            handle[1]()

    peers = [chip_peer(by) for by in (1, 2, 3)] + [sibling]
    if fused:
        peers += [plane_peer(by) for by in range(1, planes)]
    barrier = pltpu.get_barrier_semaphore()
    for peer in peers:
        pl.semaphore_signal(barrier, inc=1, device_id=(peer,), device_id_type=pl.DeviceIdType.MESH)
    pl.semaphore_wait(barrier, len(peers))

    Wq, We, Wo, Ws = r["Wq"], r["We"], r["Wo"], r["Ws"]
    Ws2 = Ws.reshape(ff_own, width)
    flat = {name: r[name].reshape(micro * rows, width) for name in ("act", "dhid", "drg", "a2g", "dyg", "xg", "sbo")}
    chip_rows = CHIPS * share
    plane_rows = CORES * chip_rows

    def stacked(name, count, lanes):
        return flat[name].at[0:count * chip_rows].reshape(count, chip_rows, width).at[:, :, 0:lanes]

    def by_core(own, other):
        return jnp.where(e == 0, own, other), jnp.where(e == 0, other, own)

    def join_rows(own, other, count):
        first, second = by_core(own, other)
        pieces = []
        for j in range(count):
            pieces += [first[j * share:(j + 1) * share], second[j * share:(j + 1) * share]]
        return jnp.concatenate(pieces, 0)

    def split_rows(block, count):
        pieces = [block[j * share:(j + 1) * share] for j in range(2 * count)]
        return by_core(jnp.concatenate(pieces[0::2], 0), jnp.concatenate(pieces[1::2], 0))

    def join_planes(own, other, out):
        @pl.loop(0, planes)
        def _(i):
            block = join_rows(own[i].astype(F32), other[i].astype(F32), CHIPS)
            out[pl.ds(pl.multiple_of(i * plane_rows, plane_rows), plane_rows), :] = block.astype(BF)

    def split_planes(grads, own, other):
        @pl.loop(0, planes)
        def _(i):
            block = grads[pl.ds(pl.multiple_of(i * plane_rows, plane_rows), plane_rows), :].astype(F32)
            mine, theirs = split_rows(block, CHIPS)
            own[i] = mine.astype(BF)
            other[i] = theirs.astype(BF)

    k_x, k_y, k_far = flipped(k, 1), flipped(k, 2), flipped(k, 3)
    x_peer, y_peer, far_peer = chip_peer(1), chip_peer(2), chip_peer(3)
    top, low = slice(0, tok // 2), slice(tok // 2, tok)

    def gather_start(src, dst, b):
        return [dst.at[b], [send(src, dst.at[b, k], x_peer), send(src, dst.at[b, k], y_peer)]]

    def gather_relay(gather):
        dst, handles = gather
        handles[0][0]()
        handles.append(send(dst.at[k_x, top], dst.at[k_x, top], y_peer))
        handles[1][0]()
        handles.append(send(dst.at[k_y, low], dst.at[k_y, low], x_peer))

    def gather_finish(gather):
        recv_all(gather[1][2:])

    def reduce_start(slots, landing, b):
        slots, landing = slots.at[b], landing.at[b]
        return [slots, landing, [
            send(slots.at[k_far, top], landing.at[2, top], x_peer),
            send(slots.at[k_far, low], landing.at[2, low], y_peer),
            send(slots.at[k_x, top], landing.at[0, top], x_peer),
            send(slots.at[k_y, low], landing.at[1, low], y_peer),
        ]]

    def reduce_relay(reduction):
        slots, landing, handles = reduction
        handles[0][0]()
        slots[k_y, top] = (slots[k_y, top].astype(F32) + landing[2, top].astype(F32)).astype(BF)
        handles.append(send(slots.at[k_y, top], landing.at[1, top], y_peer))
        handles[1][0]()
        slots[k_x, low] = (slots[k_x, low].astype(F32) + landing[2, low].astype(F32)).astype(BF)
        handles.append(send(slots.at[k_x, low], landing.at[0, low], x_peer))

    def reduce_finish(reduction):
        slots, landing, handles = reduction
        recv_all(handles[2:])
        return slots[k].astype(F32) + landing[0].astype(F32) + landing[1].astype(F32)

    sb, sbo, rb, rbo = r["sb"], r["sbo"], r["rb"], r["rbo"]
    vfin = r["vfin"]

    def vec_row(index):
        return vfin[index:index + 1, :]

    def add_row(index, value):
        r["vrow"][index:index + 1, :] += value

    def split_vectors():
        own_row = lax.broadcasted_iota(jnp.int32, (CHIPS, width), 0) == k
        expand = jnp.where(own_row, vfin[ROW_EXPAND:ROW_EXPAND + CHIPS, :], 0.0)
        r["be"][...] = jnp.sum(expand, 0, keepdims=True)
        joint = jnp.where(own_row, vfin[ROW_QKV:ROW_QKV + CHIPS, :], 0.0)
        r["bq"][...] = jnp.sum(joint, 0, keepdims=True)[:, :QKV_WIDTH]
        r["vrow"][...] = jnp.zeros_like(r["vrow"])
        r["vexp"][...] = jnp.zeros_like(r["vexp"])
        r["vqkv"][...] = jnp.zeros_like(r["vqkv"])

    def norm_one(b):
        x_local[b]()
        gather_finish(x_gather[b])
        sent_all(x_gather[b][1])

        @pl.loop(0, CHIPS)
        def _(i):
            normed, _inverse = norm_parts(r["xg"][b, i].astype(F32))
            r["xg"][b, i] = (normed * vec_row(ROW_GAIN_ONE) + vec_row(ROW_SHIFT_ONE)).astype(BF)

    a1_rows = r["xg"].reshape(micro, rows, width)
    a2_rows = r["a2g"].reshape(micro, rows, width)
    dy_rows = r["dyg"].reshape(micro, rows, width)
    dr_rows = r["drg"].reshape(micro, rows, width)
    half = rows // 2

    def project(b):
        @pl.loop(0, 2)
        def _(i):
            at = pl.ds(pl.multiple_of(i * half, half), half)
            out = (dot_nn(a1_rows[b, at, :], Wq[...]) + r["bq"][...]).astype(BF)
            for h in range(OWN_HEADS):
                r["q"][b, h, at, :] = out[:, h * HD:(h + 1) * HD]
                for part in range(2):
                    low = (part + 1) * OWN_FEATURES + h * HD
                    r["kv"][b, part, h, e, at, :] = out[:, low:low + HD]

        return [send(r["kv"].at[b, :, :, e], r["kv"].at[b, :, :, e], sibling)]

    keys = CORES * rows
    chunk_places = [(2 * (i % CHIPS) + i // CHIPS) * tok for i in range(DEV_CLIP)]

    def masked_scores(b, key_rows, query_rows):
        raw = dot_nt(key_rows, query_rows)
        index = lax.broadcasted_iota(jnp.int32, (tok, raw.shape[1]), 0)
        length = r["lengths"][b, c]
        return jnp.concatenate(
            [
                jnp.where(index < length - first, raw[i * tok:(i + 1) * tok] * SCALE, NEG)
                for i, first in enumerate(chunk_places)
            ],
            0,
        )

    def attend(b, start, stop):
        @pl.loop(start, stop)
        def _(step):
            h, part = step // 2, step % 2
            at = pl.ds(pl.multiple_of(part * half, half), half)
            key_rows = r["kv"][b, 0, h].reshape(keys, HD)
            value_rows = r["kv"][b, 1, h].reshape(keys, HD)
            scores = masked_scores(b, key_rows, r["q"][b, h, at, :])
            peak = jnp.max(scores, 0, keepdims=True)
            exponent = jnp.exp(scores - peak)
            sums = jnp.sum(exponent, 0, keepdims=True)
            probs = (exponent * (1.0 / sums)).astype(BF)
            r["lse"][b, h, :, at] = peak + jnp.log(sums)
            r["mixed"][b, h, :, at] = dot_tn(value_rows, probs).astype(BF)

    def tiles(start, stop, body):
        @pl.loop(start, stop)
        def _(i):
            body(pl.ds(pl.multiple_of(i * TILE, TILE), TILE))

    def partial_sum(slots, b, product):
        view = slots.reshape(micro, rows, width)

        def body(at):
            view[b, :, at] = product(at).astype(BF)

        tiles(0, width // TILE, body)

    mixed = r["mixed"].reshape(micro, OWN_FEATURES, rows)

    def mix_out(b):
        partial_sum(sb, b, lambda at: dot_tn(mixed[b], Wo[:, at]))
        return reduce_start(sb, rb, b)

    def norm_two(b, reduction):
        residual = r["x"][b].astype(F32) + reduce_finish(reduction) + vec_row(ROW_BIAS_OUT)
        r["resid"][b] = residual
        normed, _inverse = norm_parts(residual)
        r["a2g"][b, k] = (normed * vec_row(ROW_GAIN_TWO) + vec_row(ROW_SHIFT_TWO)).astype(BF)
        return gather_start(r["a2g"].at[b, k], r["a2g"], b)

    def feed(b, start, stop):
        def body(at):
            hidden = dot_nn(a2_rows[b], We[:, at]) + r["be"][:, at]
            grad_active = dot_nt(dy_rows[b], Ws2[at, :]).astype(BF).astype(F32)
            normal = 0.5 * (1.0 + lax.erf(hidden * 0.7071067811865476))
            r["act"][b, :, at] = (hidden * normal).astype(BF)
            density = jnp.exp(-0.5 * hidden * hidden) * 0.3989422804014327
            grad_hidden = (grad_active * (normal + hidden * density)).astype(BF)
            r["dhid"][b, :, at] = grad_hidden
            r["vexp"][:, at] += jnp.sum(grad_hidden.astype(F32), 0, keepdims=True)

        tiles(start, stop, body)

    def hidden_back(b, earlier):
        sent_all(earlier[2])
        partial_sum(sb, b, lambda at: dot_nt(r["dhid"][b], We[at, :]))
        return reduce_start(sb, rb, b)

    def finish_hidden(b, reduction):
        gradient = reduce_finish(reduction)
        normed, inverse = norm_parts(r["resid"][b])
        dy_own = r["dy"][b].astype(F32)
        total = dy_own + norm_backward(gradient, normed, inverse, vec_row(ROW_GAIN_TWO))
        r["dresid"][b] = total
        r["drg"][b, k] = total.astype(BF)
        gather = gather_start(r["drg"].at[b, k], r["drg"], b)
        add_row(ROW_GAIN_TWO, jnp.sum(gradient * normed, 0, keepdims=True))
        add_row(ROW_SHIFT_TWO, jnp.sum(gradient, 0, keepdims=True))
        add_row(ROW_BIAS_OUT, jnp.sum(total, 0, keepdims=True))
        add_row(ROW_BIAS_SHRINK, jnp.sum(dy_own, 0, keepdims=True))
        return gather

    def weight_gradient(count, lefts, rights, out):
        def body(at):
            total = dot_tn(lefts[0, :, at], rights[0])
            for b in range(1, micro):
                total = total + dot_tn(lefts[b, :, at], rights[b])
            out[at, :] = total.astype(BF)

        tiles(0, count // TILE, body)

    def mixed_gradient(b):
        @pl.loop(0, 2)
        def _(i):
            at = pl.ds(pl.multiple_of(i * half, half), half)
            out = dot_nt(dr_rows[b, at, :], Wo[...]).astype(BF)
            for h in range(OWN_HEADS):
                r["dmix"][h, at, :] = out[:, h * HD:(h + 1) * HD]

    def attend_back(b, start, stop):
        @pl.loop(start, stop)
        def _(h):
            key_rows = r["kv"][b, 0, h].reshape(keys, HD)
            value_rows = r["kv"][b, 1, h].reshape(keys, HD)
            grad_keys = None
            grad_values = None
            for part in range(2):
                at = pl.ds(part * half, half)
                query_rows = r["q"][b, h, at, :]
                mix_rows = r["dmix"][h, at, :]
                probs = jnp.exp(masked_scores(b, key_rows, query_rows) - r["lse"][b, h, :, at])
                grad_probs = dot_nt(value_rows, mix_rows)
                inner = jnp.sum(probs * grad_probs, 0, keepdims=True)
                grad_scores = (probs * (grad_probs - inner)).astype(BF)
                grad_query = dot_tn(key_rows, grad_scores) * SCALE
                r["dq"][h, at, :] = grad_query.T.astype(BF)
                key_term = dot_nn(grad_scores, query_rows)
                value_term = dot_nn(probs.astype(BF), mix_rows)
                grad_keys = key_term if grad_keys is None else grad_keys + key_term
                grad_values = value_term if grad_values is None else grad_values + value_term
            r["kv"][b, 0, h] = (grad_keys * SCALE).astype(BF).reshape(CORES, rows, HD)
            r["kv"][b, 1, h] = grad_values.astype(BF).reshape(CORES, rows, HD)

    def swap_back(b):
        return [send(r["kv"].at[b, :, :, 1 - e], r["dl"].at[b], sibling)]

    def join_gradients(b, handles):
        recv_all(handles)

        @pl.loop(0, CHIPS)
        def _(i):
            at = pl.ds(pl.multiple_of(i * tok, tok), tok)
            pieces = [r["dq"][h, at, :] for h in range(OWN_HEADS)]
            for part in range(2):
                for h in range(OWN_HEADS):
                    pair = r["kv"][b, part, h, e, at, :].astype(F32) + r["dl"][b, part, h, at, :].astype(F32)
                    pieces.append(pair.astype(BF))
            pieces.append(jnp.zeros((tok, QKV_WIDTH - 3 * OWN_FEATURES), BF))
            line = jnp.concatenate(pieces, 1)
            r["dqkv"][b, at, :] = line
            r["vqkv"][...] += jnp.sum(line.astype(F32), 0, keepdims=True)

    def input_start(b, earlier):
        sent_all(earlier[2])
        partial_sum(sb, b, lambda at: dot_nt(r["dqkv"][b], Wq[at, :]))
        return reduce_start(sb, rb, b)

    def finish_input(b, reduction):
        gradient = reduce_finish(reduction)
        normed, inverse = norm_parts(r["x"][b].astype(F32))
        back = norm_backward(gradient, normed, inverse, vec_row(ROW_GAIN_ONE))
        r["ig"][b] = (r["dresid"][b] + back).astype(BF)
        add_row(ROW_GAIN_ONE, jnp.sum(gradient * normed, 0, keepdims=True))
        add_row(ROW_SHIFT_ONE, jnp.sum(gradient, 0, keepdims=True))

    def finish_out(b, reduction):
        total = r["resid"][b] + reduce_finish(reduction) + vec_row(ROW_BIAS_SHRINK)
        r["bo"][b] = total.astype(BF)

    def sum_group(space, slots):
        return {"space": space, "slots": slots, "right": {}, "left": {}}

    def add_passing(group, hops):
        space, slots = group["space"], group["slots"]
        for side, held, i, slot in (
            ("right", (c >= 1) & (c - 1 + hops < planes), c - 1 + hops, hops - 1),
            ("left", (c <= planes - 2) & (c + 1 - hops >= 0), c + 1 - hops, 5 - hops),
        ):
            group[side][hops][0]()

            @pl.when(held)
            def _():
                space[i] = (space[i].astype(F32) + slots[slot][...].astype(F32)).astype(BF)

    def sum_step(group, hops):
        space, slots = group["space"], group["slots"]
        if hops < planes - 1:
            add_passing(group, hops + 1)
        group["right"][hops] = send_if(
            c + hops < planes, lambda: space.at[c + hops], lambda: slots[hops - 1], me + DEV_CLIP,
            (c >= 1) & (c - 1 + hops < planes), lambda: slots[hops - 1],
        )
        group["left"][hops] = send_if(
            c - hops >= 0, lambda: space.at[c - hops], lambda: slots[5 - hops], me - DEV_CLIP,
            (c <= planes - 2) & (c + 1 - hops >= 0), lambda: slots[5 - hops],
        )

    def sum_finish(group, out):
        space, slots = group["space"], group["slots"]
        out(space[c].astype(F32), False)
        for side, held, slot in (("right", c >= 1, 0), ("left", c <= planes - 2, 4)):
            group[side][1][0]()

            @pl.when(held)
            def _():
                out(slots[slot][...].astype(F32), True)

    def to_blocks(ref):
        def put(total, more):
            for j in range(CHIPS):
                piece = total[j * share:(j + 1) * share]
                ref[j] = ref[j] + piece if more else piece

        return put

    def to_rows(ref):
        def put(total, more):
            ref[...] = ref[...] + total if more else total

        return put

    def sibling_add(handles, landing, fetched, out, mine):
        recv_all(handles)
        sent_all(handles)
        local(landing, fetched)()

        @pl.loop(0, planes)
        def _(i):
            out[i] = (mine(i).astype(F32) + fetched[i].astype(F32)).astype(BF)

    def free_slots(ready):
        for side, held, device in ((0, c >= 1, me - DEV_CLIP), (1, c <= planes - 2, me + DEV_CLIP)):

            @pl.when(held)
            def _():
                pl.semaphore_signal(
                    ready.at[1 - side], inc=1, device_id=(device,), device_id_type=pl.DeviceIdType.MESH
                )

    def await_slots(ready):
        for side, held in ((0, c >= 1), (1, c <= planes - 2)):

            @pl.when(held)
            def _():
                pl.semaphore_wait(ready.at[side], 1)

    x_local = [local(r["x"].at[b], r["xg"].at[b, k]) for b in range(micro)]
    dy_local = [local(r["dy"].at[b], r["dyg"].at[b, k]) for b in range(micro)]
    x_gather = [None] * micro
    dy_gather = [None] * micro
    if fused:
        wq_mine, wq_other = stacked("drg", planes, QKV_WIDTH), stacked("a2g", planes, QKV_WIDTH)
        we_mine, we_other = stacked("act", planes, ff_own), stacked("dhid", planes, ff_own)
        line_q = line_group(lambda i: wq_mine.at[i], lambda i: wq_other.at[i])
        line_e = line_group(lambda i: we_mine.at[i], lambda i: we_other.at[i])
        line_o = line_group(lambda i: r["so"].at[i], lambda i: r["oo"].at[i])
        line_s = line_group(lambda i: Ws.at[i, e], lambda i: Ws.at[i, e])

        def pack_plane(blocks, out):
            out[c] = jnp.concatenate([blocks[j].astype(F32) for j in range(CHIPS)], 0).astype(BF)

        wq_own = local(r["wq"].at[k], r["alq"].at[k])
        wo_own = local(r["wo"], r["so"].at[c])
        we_own = local(r["we"].at[k], r["ale"].at[k])
        ws_own = local(r["ws"], Ws.at[c, e])
        wq_plane = [send(r["wq"].at[flipped(k, by)], r["alq"].at[k], chip_peer(by)) for by in (3, 1, 2)]
        vec_z = [send(r["vec"], r["vz"].at[by - 1], plane_peer(by)) for by in range(1, planes)]
        wo_own()
        forward(line_o, 0)
        x_gather[0] = gather_start(r["x"].at[0], r["xg"], 0)
        recv_all(wq_plane)
        wq_own()
        pack_plane(r["alq"], wq_mine)
        forward(line_q, 0)
        recv_all(vec_z)
        total = r["vec"][...]
        for by in range(1, planes):
            total = total + r["vz"][by - 1]
        r["v1"][...] = total
        vec_p = [send(r["v1"], r["vp"].at[by - 1], chip_peer(by)) for by in (1, 2, 3)]
        we_plane = [send(r["we"].at[flipped(k, by)], r["ale"].at[k], chip_peer(by)) for by in (3, 1, 2)]
        x_gather[1] = gather_start(r["x"].at[1], r["xg"], 1)
        gather_relay(x_gather[0])
        forward(line_o, 1)
        forward(line_q, 1)
        recv_all(vec_p)
        total = r["v1"][...]
        for by in (1, 2, 3):
            total = total + r["vp"][by - 1]
        r["v2"][...] = total
        vec_s = [send(r["v2"], r["vs"], sibling)]
        recv_all(we_plane)
        we_own()
        pack_plane(r["ale"], we_mine)
        recv_all(vec_s)
        vfin[...] = r["v2"][...] + r["vs"][...]
        ws_own()
    else:
        loads = [local(r["wq"], Wq), local(r["we"], We), local(r["wo"], Wo), local(r["ws"], Ws2)]
        for b in range(micro):
            x_gather[b] = gather_start(r["x"].at[b], r["xg"], b)
        vfin[...] = r["vec"][...]
        gather_relay(x_gather[0])
        for load in loads:
            load()
    split_vectors()
    norm_one(0)
    if fused:
        forward(line_o, 2)
        forward(line_q, 2)
        forward(line_e, 0)
        forward(line_s, 0)
    gather_relay(x_gather[1])
    dy_gather[0] = gather_start(r["dy"].at[0], r["dyg"], 0)
    norm_one(1)
    if fused:
        forward(line_o, 3)
        forward(line_q, 3)
        recv_all(line_q["swaps"])
        join_planes(wq_mine, wq_other, Wq)
    kv_swap = [None] * micro
    kv_swap[0] = project(0)
    gather_relay(dy_gather[0])
    dy_gather[1] = gather_start(r["dy"].at[1], r["dyg"], 1)
    kv_swap[1] = project(1)
    recv_all(kv_swap[0])
    attend(0, 0, OWN_HEADS)
    if fused:
        forward(line_e, 1)
    attend(0, OWN_HEADS, 2 * OWN_HEADS)
    if fused:
        recv_all(line_o["swaps"])
        for i in range(planes):
            pair = join_rows(r["so"][i].astype(F32), r["oo"][i].astype(F32), 1)
            Wo[i * HD:(i + 1) * HD, :] = pair.astype(BF)
    mix_reduce = [mix_out(0), None]
    gather_relay(dy_gather[1])
    if fused:
        forward(line_s, 1)
    recv_all(kv_swap[1])
    attend(1, 0, OWN_HEADS)
    reduce_relay(mix_reduce[0])
    if fused:
        forward(line_e, 2)
    attend(1, OWN_HEADS, 2 * OWN_HEADS)
    mix_reduce[1] = mix_out(1)
    second_gather = [norm_two(0, mix_reduce[0]), None]
    if fused:
        forward(line_s, 2)
    reduce_relay(mix_reduce[1])
    second_gather[1] = norm_two(1, mix_reduce[1])
    gather_relay(second_gather[0])
    if fused:
        forward(line_e, 3)
        recv_all(line_e["swaps"])
        group_sent(line_e)
        group_sent(line_q)
        join_planes(we_mine, we_other, We)
    gather_relay(second_gather[1])
    if fused:
        forward(line_s, 3)
        recv_all(line_s["swaps"])
    gather_finish(second_gather[0])
    dy_local[0]()
    gather_finish(dy_gather[0])
    feed(0, 0, ff_own // TILE)
    hidden_reduce = [hidden_back(0, mix_reduce[0]), None]
    gather_finish(second_gather[1])
    dy_local[1]()
    gather_finish(dy_gather[1])
    feed(1, 0, 3)
    reduce_relay(hidden_reduce[0])
    feed(1, 3, ff_own // TILE)
    hidden_reduce[1] = hidden_back(1, mix_reduce[1])
    resid_gather = [finish_hidden(0, hidden_reduce[0]), None]
    for b in range(micro):
        partial_sum(sbo, b, lambda at: dot_nn(r["act"][b], Ws2[:, at]))
    reduce_relay(hidden_reduce[1])
    if fused:
        sent_all(wq_plane + we_plane)
        group_sent(line_o)
        group_sent(line_s)
    weight_gradient(ff_own, r["act"], dy_rows, Ws2)
    if fused:
        gs_s = [send(Ws.at[:, 1 - e], r["Ls"], sibling)]
    resid_gather[1] = finish_hidden(1, hidden_reduce[1])
    out_reduce = [reduce_start(sbo, rbo, 0), None]
    weight_gradient(width, a2_rows, r["dhid"], We)
    gather_relay(resid_gather[0])
    if fused:
        space_e, other_e = stacked("act", planes, ff_own), stacked("dhid", planes, ff_own)
        space_s = flat["dyg"].at[0:planes * ff_share].reshape(planes, ff_share, width)
        split_planes(We, space_e, other_e)
        ge_s = [send(other_e, r["Le"], sibling)]
        sent_all(second_gather[0][1] + second_gather[1][1] + dy_gather[0][1] + dy_gather[1][1])
        free_slots(r["ready"])
        slots_s = [flat["a2g"].at[i * ff_share:(i + 1) * ff_share] for i in range(5)]
        slots_e = [flat["a2g"].at[5 * chip_rows:6 * chip_rows]]
        for name in ("dyg", "act"):
            slots_e += [flat[name].at[i * chip_rows:(i + 1) * chip_rows] for i in (4, 5)]
        sum_s, sum_e = sum_group(space_s, slots_s), sum_group(space_e, slots_e)
        sibling_add(gs_s, r["Ls"], space_s, space_s, lambda i: Ws[i, e])
        await_slots(r["ready"])
        sum_step(sum_s, 3)
        sibling_add(ge_s, r["Le"], other_e, space_e, lambda i: space_e[i])
        sum_step(sum_e, 3)
    gather_finish(resid_gather[0])
    mixed_gradient(0)
    sent_all(kv_swap[0] + kv_swap[1])
    attend_back(0, 0, 2)
    gather_relay(resid_gather[1])
    if fused:
        sum_step(sum_s, 2)
    attend_back(0, 2, OWN_HEADS)
    swap = swap_back(0)
    reduce_relay(out_reduce[0])
    out_reduce[1] = reduce_start(sbo, rbo, 1)
    gather_finish(resid_gather[1])
    mixed_gradient(1)
    lead = dot_nn(mixed[0], dr_rows[0])
    for other in range(1, micro):
        lead = lead + dot_nn(mixed[other], dr_rows[other])
    if fused:
        space_o, other_o = r["so"], r["oo"]
        for i in range(planes):
            mine, theirs = split_rows(lead[i * HD:(i + 1) * HD], 1)
            space_o[i] = mine.astype(BF)
            other_o[i] = theirs.astype(BF)
        go_s = [send(other_o, r["Lo"], sibling)]
        sum_step(sum_e, 2)
    else:
        Wo[...] = lead.astype(BF)
    join_gradients(0, swap)
    input_reduce = [input_start(0, hidden_reduce[0]), None]
    if fused:
        sum_step(sum_s, 1)
    attend_back(1, 0, 2)
    reduce_relay(out_reduce[1])
    reduce_relay(input_reduce[0])
    if fused:
        sum_step(sum_e, 1)
        sum_o = sum_group(space_o, [r["ao"].at[i] for i in range(5)])
        sibling_add(go_s, r["Lo"], other_o, space_o, lambda i: space_o[i])
        sum_step(sum_o, 3)
    attend_back(1, 2, OWN_HEADS)
    swap = swap_back(1)
    finish_input(0, input_reduce[0])
    join_gradients(1, swap)
    input_reduce[1] = input_start(1, hidden_reduce[1])
    weight_gradient(width, a1_rows, r["dqkv"], Wq)
    if fused:
        free_slots(r["ready_q"])
        sent_all(resid_gather[0][1] + resid_gather[1][1])
        space_q, other_q = stacked("drg", planes, QKV_WIDTH), stacked("xg", planes, QKV_WIDTH)
        split_planes(Wq, space_q, other_q)
        gq_s = [send(other_q, r["Lq"], sibling)]
        sum_step(sum_o, 2)
        five = stacked("dhid", 5, QKV_WIDTH)
        sum_q = sum_group(space_q, [five.at[i] for i in range(5)])
        sibling_add(gq_s, r["Lq"], other_q, space_q, lambda i: space_q[i])
        await_slots(r["ready_q"])
        sum_step(sum_q, 3)
    for b in range(micro):
        finish_out(b, out_reduce[b])
    if fused:
        sum_finish(sum_s, to_rows(r["gs"]))
        sum_finish(sum_e, to_blocks(r["ge"]))
        for j in range(CHIPS):
            r["ae"][j] = r["ge"][j].astype(BF)
        sum_step(sum_o, 1)
    reduce_relay(input_reduce[1])
    if fused:
        ge_p = [send(r["ae"].at[flipped(k, by)], r["ale"].at[k], chip_peer(by)) for by in (3, 1, 2)]
        sum_step(sum_q, 2)
    finish_input(1, input_reduce[1])

    mine_e = lax.broadcasted_iota(jnp.int32, (VEC_ROWS, width), 0) == ROW_EXPAND + k
    mine_q = lax.broadcasted_iota(jnp.int32, (VEC_ROWS, width), 0) == ROW_QKV + k
    padded = jnp.concatenate([r["vqkv"][...], jnp.zeros((1, width - QKV_WIDTH), F32)], 1)
    sums = r["vrow"][...] + jnp.where(mine_e, r["vexp"][...], 0.0) + jnp.where(mine_q, padded, 0.0)
    if fused:
        r["u0"][...] = sums
        sum_z = [send(r["u0"], r["uz"].at[by - 1], plane_peer(by)) for by in range(1, planes)]
        sum_step(sum_q, 1)
        recv_all(sum_z)
        total = r["u0"][...]
        for by in range(1, planes):
            total = total + r["uz"][by - 1]
        r["u1"][...] = total
        sum_p = [send(r["u1"], r["up"].at[by - 1], chip_peer(by)) for by in (1, 2, 3)]
        sum_finish(sum_o, to_rows(r["go"]))
        recv_all(ge_p)
        for by in (1, 2, 3):
            r["ge"][flipped(k, by)] = r["ale"][flipped(k, by)].astype(F32)
        recv_all(sum_p)
        total = r["u1"][...]
        for by in (1, 2, 3):
            total = total + r["up"][by - 1]
        r["u2"][...] = total
        sum_s = [send(r["u2"], r["us"], sibling)]
        sum_finish(sum_q, to_blocks(r["gq"]))
        for j in range(CHIPS):
            r["aq"][j] = r["gq"][j].astype(BF)
        gq_p = [send(r["aq"].at[flipped(k, by)], r["alq"].at[k], chip_peer(by)) for by in (3, 1, 2)]
        recv_all(sum_s)
        r["vo"][...] = r["u2"][...] + r["us"][...]
        recv_all(gq_p)
        for by in (1, 2, 3):
            r["gq"][flipped(k, by)] = r["alq"][flipped(k, by)].astype(F32)
    else:
        r["vo"][...] = sums
        stores = [local(Wq, r["gq"]), local(We, r["ge"]), local(Wo, r["go"]), local(Ws2, r["gs"])]
        for store in stores:
            store()
    for wait in pending:
        wait()


def run_block(fused, planes, x, dy, lengths, vec, wq, we, wo, ws, share, ff_share):
    micro, tok, width = x.shape
    ff_own = width
    rows = CHIPS * tok
    vmem = pl.BlockSpec(memory_space=pltpu.VMEM)
    anywhere = pl.BlockSpec(memory_space=pl.ANY)
    smem = pl.BlockSpec(memory_space=pltpu.SMEM)

    def shape(*dims, dtype=BF):
        return jax.ShapeDtypeStruct(dims, dtype)

    outs = [
        (shape(micro, tok, width), vmem),
        (shape(micro, tok, width), vmem),
        (shape(VEC_ROWS, width, dtype=F32), vmem),
    ]
    if fused:
        outs += [
            (shape(CHIPS, share, QKV_WIDTH, dtype=F32), vmem),
            (shape(CHIPS, share, ff_own, dtype=F32), vmem),
            (shape(share, width, dtype=F32), vmem),
            (shape(ff_share, width, dtype=F32), vmem),
        ]
        outs += [
            (shape(planes, CHIPS * share, QKV_WIDTH), anywhere),
            (shape(planes, CHIPS * share, ff_own), anywhere),
            (shape(planes, share, width), anywhere),
            (shape(planes, ff_share, width), anywhere),
        ]
    else:
        outs += [
            (shape(width, QKV_WIDTH), anywhere),
            (shape(width, ff_own), anywhere),
            (shape(OWN_FEATURES, width), anywhere),
            (shape(ff_own, width), anywhere),
        ]
    if fused:
        weights = [
            pltpu.VMEM((width, QKV_WIDTH), BF),
            pltpu.VMEM((width, ff_own), BF),
            pltpu.VMEM((OWN_FEATURES, width), BF),
            pltpu.VMEM((planes, CORES, ff_share, width), BF),
        ]
    else:
        weights = [
            pltpu.VMEM((width, QKV_WIDTH), BF),
            pltpu.VMEM((width, ff_own), BF),
            pltpu.VMEM((OWN_FEATURES, width), BF),
            pltpu.VMEM((ff_own, width), BF),
        ]
    scratch = weights + [
        pltpu.VMEM((micro, CHIPS, tok, width), BF),
        pltpu.VMEM((micro, CHIPS, tok, width), BF),
        pltpu.VMEM((micro, CHIPS, tok, width), BF),
        pltpu.VMEM((micro, CHIPS, tok, width), BF),
        pltpu.VMEM((micro, rows, ff_own), BF),
        pltpu.VMEM((micro, rows, ff_own), BF),
        pltpu.VMEM((micro, OWN_HEADS, rows, HD), BF),
        pltpu.VMEM((micro, 2, OWN_HEADS, CORES, rows, HD), BF),
        pltpu.VMEM((micro, OWN_HEADS, HD, rows), BF),
        pltpu.VMEM((micro, OWN_HEADS, 1, rows), F32),
        pltpu.VMEM((OWN_HEADS, rows, HD), BF),
        pltpu.VMEM((OWN_HEADS, rows, HD), BF),
        pltpu.VMEM((micro, 2, OWN_HEADS, rows, HD), BF),
        pltpu.VMEM((micro, CHIPS, tok, width), BF),
        pltpu.VMEM((micro, CHIPS, tok, width), BF),
        pltpu.VMEM((micro, CHIPS - 1, tok, width), BF),
        pltpu.VMEM((micro, CHIPS - 1, tok, width), BF),
        pltpu.VMEM((micro, tok, width), F32),
        pltpu.VMEM((micro, tok, width), F32),
        pltpu.VMEM((VEC_ROWS, width), F32),
        pltpu.VMEM((1, ff_own), F32),
        pltpu.VMEM((1, QKV_WIDTH), F32),
        pltpu.VMEM((1, ff_own), F32),
        pltpu.VMEM((1, QKV_WIDTH), F32),
        pltpu.VMEM((VEC_ROWS, width), F32),
    ]
    if fused:
        scratch += [
            pltpu.VMEM((planes, share, width), BF),
            pltpu.VMEM((planes, share, width), BF),
            pltpu.VMEM((5, share, width), BF),
            pltpu.VMEM((CHIPS, share, QKV_WIDTH), BF),
            pltpu.VMEM((CHIPS, share, ff_own), BF),
            pltpu.VMEM((CHIPS, share, QKV_WIDTH), BF),
            pltpu.VMEM((CHIPS, share, ff_own), BF),
        ]
        for _ in range(2):
            if _ == 1:
                scratch.append(pltpu.VMEM((VEC_ROWS, width), F32))
            scratch += [
                pltpu.VMEM((VEC_ROWS, width), F32),
                pltpu.VMEM((VEC_ROWS, width), F32),
                pltpu.VMEM((planes - 1, VEC_ROWS, width), F32),
                pltpu.VMEM((CHIPS - 1, VEC_ROWS, width), F32),
                pltpu.VMEM((VEC_ROWS, width), F32),
            ]
        scratch += [pltpu.SemaphoreType.REGULAR((2,)), pltpu.SemaphoreType.REGULAR((2,))]
    scratch += [
        pltpu.SemaphoreType.DMA((SEMS,)),
        pltpu.SemaphoreType.DMA((SEMS,)),
        pltpu.SemaphoreType.DMA((LOCAL_SEMS,)),
    ]
    return pl.pallas_call(
        partial(block_kernel, fused, planes, micro, tok, width, ff_own, share, ff_share),
        out_shape=[out for out, _ in outs],
        in_specs=[vmem, vmem, smem, vmem, anywhere, anywhere, anywhere, anywhere],
        out_specs=[spec for _, spec in outs],
        scratch_shapes=scratch,
        compiler_params=pltpu.CompilerParams(
            collective_id=0, has_side_effects=True, vmem_limit_bytes=63 * 1000 * 1000
        ),
    )(x, dy, lengths, vec, wq, we, wo, ws)


def by_chip(matrix, part):
    rows = matrix.shape[0]
    return matrix.reshape(rows, -1, CHIPS, part).transpose(2, 0, 1, 3).reshape(CHIPS, rows, -1)


def from_chips(blocks, part):
    rows = blocks.shape[1]
    return blocks.reshape(CHIPS, rows, -1, part).transpose(1, 2, 0, 3).reshape(rows, -1)


def body(
    inputs, cotangent, lengths, first_gain, first_shift, query_weight, query_bias, key_weight,
    value_weight, value_bias, output_weight, output_bias, second_gain, second_shift,
    expand_weight, expand_bias, shrink_weight, shrink_bias,
):
    device = lax.axis_index("fsdp")
    count = lax.axis_size("fsdp")
    c, k, e = place(device)
    planes = count // DEV_CLIP
    width = inputs.shape[2]
    share = query_weight.shape[0]
    ff_share = shrink_weight.shape[0]
    ff_part = width // 4
    fused = planes == 4 and share * 2 == HD and ff_share * 2 == ff_part
    plain = (first_gain, first_shift, second_gain, second_shift, output_bias, shrink_bias)
    low = [w.astype(BF) for w in (query_weight, key_weight, value_weight, expand_weight, output_weight, shrink_weight)]
    if fused:
        vec = jnp.zeros((VEC_ROWS, width), F32)
        vec = lax.dynamic_update_slice(vec, jnp.stack(plain), (0, device * share))
        vec = lax.dynamic_update_slice(vec, expand_bias[None], (ROW_EXPAND + k, (2 * c + e) * ff_share))
        at = (2 * c + e) * share
        vec = lax.dynamic_update_slice(vec, query_bias[None], (ROW_QKV + k, at))
        vec = lax.dynamic_update_slice(vec, value_bias[None], (ROW_QKV + k, 2 * OWN_FEATURES + at))
        wide = [by_chip(w, HD) for w in low[:3]]
        wide.append(jnp.zeros((CHIPS, share, QKV_WIDTH - 3 * OWN_FEATURES), BF))
        wq = jnp.concatenate(wide, 2)
        we = by_chip(low[3], ff_part)
        got = run_block(True, planes, inputs, cotangent, lengths, vec, wq, we, low[4], low[5], share, ff_share)
        block_out, input_grad, sums, gq, ge, grad_output_w, grad_shrink_w = got[:7]
        grad_query_w, grad_key_w, grad_value_w = (
            from_chips(gq[:, :, i * OWN_FEATURES:(i + 1) * OWN_FEATURES], HD) for i in range(3)
        )
        grad_expand_w = from_chips(ge, ff_part)
        own = lax.dynamic_slice(sums, (0, device * share), (len(plain), share))
        owned = [own[i] for i in range(len(plain))]
        grad_expand_b = lax.dynamic_slice(sums, (ROW_EXPAND + k, (2 * c + e) * ff_share), (1, ff_share))[0]
        grad_query_b = lax.dynamic_slice(sums, (ROW_QKV + k, at), (1, share))[0]
        grad_value_b = lax.dynamic_slice(sums, (ROW_QKV + k, 2 * OWN_FEATURES + at), (1, share))[0]
    else:

        def whole(array):
            return lax.all_gather(array, "fsdp", axis=0, tiled=True)

        def mine(blocks):
            return lax.dynamic_index_in_dim(blocks, k, 0, keepdims=False)

        full = [whole(w) for w in low]
        pieces = [mine(by_chip(w, HD)) for w in full[:3]]
        pieces.append(jnp.zeros((width, QKV_WIDTH - 3 * OWN_FEATURES), BF))
        wq = jnp.concatenate(pieces, 1)
        we = mine(by_chip(full[3], ff_part))
        wo = mine(by_chip(full[4].T, HD)).T
        ws = mine(by_chip(full[5].T, ff_part)).T
        blank = jnp.zeros((2, width), F32)
        bias_e = by_chip(whole(expand_bias)[None], ff_part)[:, 0]
        bias_q = by_chip(whole(query_bias)[None], HD)[:, 0]
        bias_v = by_chip(whole(value_bias)[None], HD)[:, 0]
        bias_rows = jnp.concatenate(
            [bias_q, jnp.zeros_like(bias_q), bias_v, jnp.zeros((CHIPS, width - 3 * OWN_FEATURES), F32)], 1
        )
        vec = jnp.concatenate([jnp.stack([whole(v) for v in plain]), blank, bias_e, bias_rows])
        got = run_block(False, planes, inputs, cotangent, lengths, vec, wq, we, wo, ws, share, ff_share)
        block_out, input_grad, sums, gq, ge, go, gs = got[:7]

        def spread(block, part):
            places = lax.broadcasted_iota(jnp.int32, (CHIPS, 1, 1), 0) == k
            return from_chips(jnp.where(places, block.astype(F32)[None], 0.0), part)

        def owned_sum(array):
            return lax.psum_scatter(array, "fsdp", scatter_dimension=0, tiled=True)

        grad_query_w, grad_key_w, grad_value_w = (
            owned_sum(spread(gq[:, i * OWN_FEATURES:(i + 1) * OWN_FEATURES], HD)) for i in range(3)
        )
        grad_expand_w = owned_sum(spread(ge, ff_part))
        grad_output_w = owned_sum(spread(go.T, HD).T)
        grad_shrink_w = owned_sum(spread(gs.T, ff_part).T)
        owned = [owned_sum(sums[i]) for i in range(len(plain))]
        sums_q = sums[ROW_QKV:ROW_QKV + CHIPS, None]
        grad_expand_b = owned_sum(from_chips(sums[ROW_EXPAND:ROW_EXPAND + CHIPS, None], ff_part)[0])
        grad_query_b = owned_sum(from_chips(sums_q[:, :, :OWN_FEATURES], HD)[0])
        grad_value_b = owned_sum(from_chips(sums_q[:, :, 2 * OWN_FEATURES:3 * OWN_FEATURES], HD)[0])
    return (
        block_out,
        input_grad,
        owned[0],
        owned[1],
        grad_query_w,
        grad_query_b,
        grad_key_w,
        grad_value_w,
        grad_value_b,
        grad_output_w,
        owned[4],
        owned[2],
        owned[3],
        grad_expand_w,
        grad_expand_b,
        grad_shrink_w,
        owned[5],
    )


def solution(mesh):
    rows, matrix, vector = P(None, "fsdp", None), P("fsdp", None), P("fsdp")
    in_specs = (
        rows, rows, P(), vector, vector, matrix, vector, matrix, matrix, vector, matrix, vector,
        vector, vector, matrix, vector, matrix, vector,
    )
    out_specs = (
        rows, rows, vector, vector, matrix, vector, matrix, matrix, vector, matrix, vector,
        vector, vector, matrix, vector, matrix, vector,
    )
    return jax.shard_map(body, mesh=mesh, in_specs=in_specs, out_specs=out_specs, check_vma=False)
```

```python
from functools import partial
from types import SimpleNamespace

import jax
import jax.numpy as jnp
from jax import lax
from jax.experimental import pallas as pl
from jax.experimental.pallas import tpu as pltpu
from jax.sharding import PartitionSpec as P

H = 16
HD = 80
CHIPS = 4
CORES = 2
DEV_CLIP = CHIPS * CORES
OWN_HEADS = H // CHIPS
OWN_FEATURES = OWN_HEADS * HD
QKV_WIDTH = 1024
TILE = 256
ROW_GAIN_ONE, ROW_SHIFT_ONE, ROW_GAIN_TWO, ROW_SHIFT_TWO, ROW_BIAS_OUT, ROW_BIAS_SHRINK = range(6)

EPS = 1e-05
NEG = -1000000000.0
SCALE = HD ** (-0.5)
BF = jnp.bfloat16
F32 = jnp.float32


def dot_nn(left, right):
    return lax.dot_general(left, right, (((1,), (0,)), ((), ())), preferred_element_type=F32)


def dot_nt(left, right):
    return lax.dot_general(left, right, (((1,), (1,)), ((), ())), preferred_element_type=F32)


def dot_tn(left, right):
    return lax.dot_general(left, right, (((0,), (0,)), ((), ())), preferred_element_type=F32)


def norm_parts(rows):
    mean = jnp.mean(rows, -1, keepdims=True)
    centered = rows - mean
    inverse = lax.rsqrt(jnp.mean(centered * centered, -1, keepdims=True) + EPS)
    return centered * inverse, inverse


def norm_backward(gradient, normed, inverse, gain):
    scaled = gradient * gain
    return inverse * (
        scaled
        - jnp.mean(scaled, -1, keepdims=True)
        - normed * jnp.mean(scaled * normed, -1, keepdims=True)
    )


def place(device):
    return device // DEV_CLIP, (device % DEV_CLIP) // CORES, device % CORES


def flipped(number, by):
    low, high = number % 2, number // 2
    if by & 1:
        low = 1 - low
    if by & 2:
        high = 1 - high
    return high * 2 + low


SEMS = 240
LOCAL_SEMS = 40


def block_kernel(fused, planes, micro, tok, width, ff_own, share, ff_share, *refs):
    names = ["x", "dy", "lengths"]
    if fused:
        names += ["av", "bv", "cv_", "dv", "ev", "fv"] + ["expand_bias", "query_bias", "value_bias", "wq", "wk", "wv", "we", "wo", "ws"]
    else:
        names += ["vec", "wq", "we", "wo", "ws"]
    names += ["bo", "ig", "vo", "vt", "gq", "ge", "go", "gs"]
    if fused:
        names += ["Lq", "Le", "Lo", "Ls"]
    names += ["Wq", "We", "Wo", "Ws", "xg", "dyg", "a2g", "drg", "act", "dhid"]
    names += ["q", "kv", "mixed", "lse", "dmix", "dq", "dl"]
    names += ["sb", "sbo", "rb", "rbo", "resid", "dresid", "vfin", "be", "bq", "vexp", "vqkv", "vrow"]
    if fused:
        names += ["so", "oo", "ao", "aq", "ae", "alq", "ale", "cv", "cp"]
        names += [letter + end for letter in "ut" for end in ("0", "1", "2", "z", "p", "s")]
        names += ["ready_e", "ready_s", "ready_q"]
    names += ["ssem", "rsem", "lsem"]
    r = SimpleNamespace(**dict(zip(names, refs, strict=True)))
    if fused:
        r.vectors = (r.av, r.bv, r.cv_, r.dv, r.ev, r.fv)
    r.dqkv = r.dhid.at[:, :, 0:QKV_WIDTH]
    me = lax.axis_index("fsdp")
    c, k, e = place(me)
    rows = CHIPS * tok

    def chip_peer(by):
        return c * DEV_CLIP + flipped(k, by) * CORES + e

    sibling = c * DEV_CLIP + k * CORES + (1 - e)

    def plane_peer(by):
        return flipped(c, by) * DEV_CLIP + k * CORES + e

    counters = SimpleNamespace(remote=0, local=0)
    pending = []

    def send(src, dst, device):
        i = counters.remote
        counters.remote += 1
        copy = pltpu.make_async_remote_copy(
            src_ref=src, dst_ref=dst, send_sem=r.ssem.at[i], recv_sem=r.rsem.at[i],
            device_id=(device,), device_id_type=pl.DeviceIdType.MESH,
        )
        copy.start()
        state = SimpleNamespace(sent=False)

        def wait_send():
            if not state.sent:
                state.sent = True
                copy.wait_send()

        copy_handle = (copy.wait_recv, wait_send)
        pending.append(wait_send)
        return copy_handle

    def send_if(held, src, dst, device, due, arriving):
        i = counters.remote
        counters.remote += 1

        def copy(source, target, to):
            return pltpu.make_async_remote_copy(
                src_ref=source, dst_ref=target, send_sem=r.ssem.at[i], recv_sem=r.rsem.at[i],
                device_id=(to,), device_id_type=pl.DeviceIdType.MESH,
            )

        @pl.when(held)
        def _():
            copy(src(), dst(), device).start()

        state = SimpleNamespace(sent=False)

        def wait_send():
            if not state.sent:
                state.sent = True

                @pl.when(held)
                def _():
                    copy(src(), dst(), device).wait_send()

        def wait_recv():
            @pl.when(due)
            def _():
                copy(arriving(), arriving(), sibling).wait_recv()

        copy_handle = (wait_recv, wait_send)
        pending.append(wait_send)
        return copy_handle

    def line_group(mine, theirs):
        return SimpleNamespace(mine=mine, theirs=theirs, steps=[], swaps=[])

    def forward(group, step):
        mine, theirs = group.mine, group.theirs
        if step > 0:
            recv_all(group.steps[step - 1])
        if step < planes - 1:
            n = step + 1
            group.steps.append([
                send_if(
                    (c >= n - 1) & (c < planes - 1), lambda: mine(c - n + 1), lambda: mine(c - n + 1),
                    me + DEV_CLIP, c >= n, lambda: mine(c - n),
                ),
                send_if(
                    (c + n - 1 < planes) & (c >= 1), lambda: mine(c + n - 1), lambda: mine(c + n - 1),
                    me - DEV_CLIP, c + n < planes, lambda: mine(c + n),
                ),
            ])
        if step == 0:
            group.swaps.append(send(mine(c), theirs(c), sibling))
        else:
            for held, i in ((c >= step, c - step), (c + step < planes, c + step)):
                group.swaps.append(
                    send_if(
                        held, lambda i=i: mine(i), lambda i=i: theirs(i), sibling, held, lambda i=i: theirs(i)
                    )
                )

    def group_sent(group):
        sent_all(sum(group.steps, []) + group.swaps)

    def local(src, dst):
        i = counters.local
        counters.local += 1
        copy = pltpu.make_async_copy(src, dst, r.lsem.at[i])
        copy.start()
        return copy.wait

    def recv_all(handles):
        for handle in handles:
            handle[0]()

    def sent_all(handles):
        for handle in handles:
            handle[1]()

    Wq, We, Wo, Ws = r.Wq, r.We, r.Wo, r.Ws
    Ws2 = Ws.reshape(ff_own, width)

    def flat(ref):
        return ref.reshape(micro * rows, width)

    chip_rows = CHIPS * share
    plane_rows = CORES * chip_rows

    def stacked(ref, count, lanes):
        return flat(ref).at[0:count * chip_rows].reshape(count, chip_rows, width).at[:, :, 0:lanes]

    def by_core(own, other):
        return jnp.where(e == 0, own, other), jnp.where(e == 0, other, own)

    def join_rows(own, other, count):
        first, second = by_core(own, other)
        pieces = []
        for j in range(count):
            pieces += [first[j * share:(j + 1) * share], second[j * share:(j + 1) * share]]
        return jnp.concatenate(pieces, 0)

    def split_rows(block, count):
        pieces = [block[j * share:(j + 1) * share] for j in range(2 * count)]
        return by_core(jnp.concatenate(pieces[0::2], 0), jnp.concatenate(pieces[1::2], 0))

    def join_planes(own, other, out):
        @pl.loop(0, planes)
        def _(i):
            block = join_rows(own[i].astype(F32), other[i].astype(F32), CHIPS)
            out[pl.ds(pl.multiple_of(i * plane_rows, plane_rows), plane_rows), :] = block.astype(BF)

    def split_planes(grads, own, other):
        @pl.loop(0, planes)
        def _(i):
            block = grads[pl.ds(pl.multiple_of(i * plane_rows, plane_rows), plane_rows), :].astype(F32)
            mine, theirs = split_rows(block, CHIPS)
            own[i] = mine.astype(BF)
            other[i] = theirs.astype(BF)

    k_x, k_y, k_far = flipped(k, 1), flipped(k, 2), flipped(k, 3)
    x_peer, y_peer, far_peer = chip_peer(1), chip_peer(2), chip_peer(3)
    top, low = slice(0, tok // 2), slice(tok // 2, tok)

    def gather_start(src, dst, b):
        return [dst.at[b], [send(src, dst.at[b, k], x_peer), send(src, dst.at[b, k], y_peer)]]

    def gather_relay(gather):
        dst, handles = gather
        handles[0][0]()
        handles.append(send(dst.at[k_x, top], dst.at[k_x, top], y_peer))
        handles[1][0]()
        handles.append(send(dst.at[k_y, low], dst.at[k_y, low], x_peer))

    def gather_finish(gather):
        recv_all(gather[1][2:])

    def reduce_start(slots, landing, b):
        slots, landing = slots.at[b], landing.at[b]
        return [slots, landing, [
            send(slots.at[k_far, top], landing.at[2, top], x_peer),
            send(slots.at[k_far, low], landing.at[2, low], y_peer),
            send(slots.at[k_x, top], landing.at[0, top], x_peer),
            send(slots.at[k_y, low], landing.at[1, low], y_peer),
        ]]

    def reduce_relay(reduction):
        slots, landing, handles = reduction
        handles[0][0]()
        slots[k_y, top] = (slots[k_y, top].astype(F32) + landing[2, top].astype(F32)).astype(BF)
        handles.append(send(slots.at[k_y, top], landing.at[1, top], y_peer))
        handles[1][0]()
        slots[k_x, low] = (slots[k_x, low].astype(F32) + landing[2, low].astype(F32)).astype(BF)
        handles.append(send(slots.at[k_x, low], landing.at[0, low], x_peer))

    def reduce_finish(reduction):
        slots, landing, handles = reduction
        recv_all(handles[2:])
        return slots[k].astype(F32) + landing[0].astype(F32) + landing[1].astype(F32)

    sb, sbo, rb, rbo = r.sb, r.sbo, r.rb, r.rbo
    vfin = r.vfin

    def vec_row(index):
        return vfin[index:index + 1, :]

    def add_row(index, value):
        r.vrow[index:index + 1, :] += value

    def norm_one(b):
        x_local[b]()
        gather_finish(x_gather[b])
        sent_all(x_gather[b][1])

        @pl.loop(0, CHIPS)
        def _(i):
            normed, _inverse = norm_parts(r.xg[b, i].astype(F32))
            r.xg[b, i] = (normed * vec_row(ROW_GAIN_ONE) + vec_row(ROW_SHIFT_ONE)).astype(BF)

    a1_rows = r.xg.reshape(micro, rows, width)
    a2_rows = r.a2g.reshape(micro, rows, width)
    dy_rows = r.dyg.reshape(micro, rows, width)
    dr_rows = r.drg.reshape(micro, rows, width)
    half = rows // 2

    def project(b):
        @pl.loop(0, 2)
        def _(i):
            at = pl.ds(pl.multiple_of(i * half, half), half)
            out = (dot_nn(a1_rows[b, at, :], Wq[...]) + r.bq[...]).astype(BF)
            for h in range(OWN_HEADS):
                r.q[b, h, at, :] = out[:, h * HD:(h + 1) * HD]
                for part in range(2):
                    low = (part + 1) * OWN_FEATURES + h * HD
                    r.kv[b, part, h, e, at, :] = out[:, low:low + HD]

        return [send(r.kv.at[b, :, :, e], r.kv.at[b, :, :, e], sibling)]

    keys = CORES * rows
    chunk_places = [(2 * (i % CHIPS) + i // CHIPS) * tok for i in range(DEV_CLIP)]

    def masked_scores(b, key_rows, query_rows):
        raw = dot_nt(key_rows, query_rows)
        index = lax.broadcasted_iota(jnp.int32, (tok, raw.shape[1]), 0)
        length = r.lengths[b, c]
        return jnp.concatenate(
            [
                jnp.where(index < length - first, raw[i * tok:(i + 1) * tok] * SCALE, NEG)
                for i, first in enumerate(chunk_places)
            ],
            0,
        )

    def attend(b, start, stop):
        @pl.loop(start, stop)
        def _(step):
            h, part = step // 2, step % 2
            at = pl.ds(pl.multiple_of(part * half, half), half)
            key_rows = r.kv[b, 0, h].reshape(keys, HD)
            value_rows = r.kv[b, 1, h].reshape(keys, HD)
            scores = masked_scores(b, key_rows, r.q[b, h, at, :])
            peak = jnp.max(scores, 0, keepdims=True)
            exponent = jnp.exp(scores - peak)
            sums = jnp.sum(exponent, 0, keepdims=True)
            probs = (exponent * (1.0 / sums)).astype(BF)
            r.lse[b, h, :, at] = peak + jnp.log(sums)
            r.mixed[b, h, :, at] = dot_tn(value_rows, probs).astype(BF)

    def tiles(start, stop, body):
        @pl.loop(start, stop)
        def _(i):
            body(pl.ds(pl.multiple_of(i * TILE, TILE), TILE))

    def partial_sum(slots, b, product):
        view = slots.reshape(micro, rows, width)

        def body(at):
            view[b, :, at] = product(at).astype(BF)

        tiles(0, width // TILE, body)

    mixed = r.mixed.reshape(micro, OWN_FEATURES, rows)

    def mix_out(b):
        partial_sum(sb, b, lambda at: dot_tn(mixed[b], Wo[:, at]))
        return reduce_start(sb, rb, b)

    def norm_two(b, reduction):
        residual = r.x[b].astype(F32) + reduce_finish(reduction) + vec_row(ROW_BIAS_OUT)
        r.resid[b] = residual
        normed, _inverse = norm_parts(residual)
        r.a2g[b, k] = (normed * vec_row(ROW_GAIN_TWO) + vec_row(ROW_SHIFT_TWO)).astype(BF)
        return gather_start(r.a2g.at[b, k], r.a2g, b)

    def feed(b, start, stop):
        def body(at):
            hidden = dot_nn(a2_rows[b], We[:, at]) + r.be[:, at]
            grad_active = dot_nt(dy_rows[b], Ws2[at, :]).astype(BF).astype(F32)
            normal = 0.5 * (1.0 + lax.erf(hidden * 0.7071067811865476))
            r.act[b, :, at] = (hidden * normal).astype(BF)
            density = jnp.exp(-0.5 * hidden * hidden) * 0.3989422804014327
            grad_hidden = (grad_active * (normal + hidden * density)).astype(BF)
            r.dhid[b, :, at] = grad_hidden
            r.vexp[:, at] += jnp.sum(grad_hidden.astype(F32), 0, keepdims=True)

        tiles(start, stop, body)

    def hidden_back(b, earlier):
        sent_all(earlier[2])
        partial_sum(sb, b, lambda at: dot_nt(r.dhid[b], We[at, :]))
        return reduce_start(sb, rb, b)

    def finish_hidden(b, reduction):
        gradient = reduce_finish(reduction)
        normed, inverse = norm_parts(r.resid[b])
        dy_own = r.dy[b].astype(F32)
        total = dy_own + norm_backward(gradient, normed, inverse, vec_row(ROW_GAIN_TWO))
        r.dresid[b] = total
        r.drg[b, k] = total.astype(BF)
        gather = gather_start(r.drg.at[b, k], r.drg, b)
        add_row(ROW_GAIN_TWO, jnp.sum(gradient * normed, 0, keepdims=True))
        add_row(ROW_SHIFT_TWO, jnp.sum(gradient, 0, keepdims=True))
        add_row(ROW_BIAS_OUT, jnp.sum(total, 0, keepdims=True))
        add_row(ROW_BIAS_SHRINK, jnp.sum(dy_own, 0, keepdims=True))
        return gather

    def weight_gradient(count, lefts, rights, out):
        def body(at):
            total = dot_tn(lefts[0, :, at], rights[0])
            for b in range(1, micro):
                total = total + dot_tn(lefts[b, :, at], rights[b])
            out[at, :] = total.astype(BF)

        tiles(0, count // TILE, body)

    def mixed_gradient(b):
        @pl.loop(0, 2)
        def _(i):
            at = pl.ds(pl.multiple_of(i * half, half), half)
            out = dot_nt(dr_rows[b, at, :], Wo[...]).astype(BF)
            for h in range(OWN_HEADS):
                r.dmix[h, at, :] = out[:, h * HD:(h + 1) * HD]

    def attend_back(b, start, stop):
        @pl.loop(start, stop)
        def _(h):
            key_rows = r.kv[b, 0, h].reshape(keys, HD)
            value_rows = r.kv[b, 1, h].reshape(keys, HD)
            grad_keys = None
            grad_values = None
            for part in range(2):
                at = pl.ds(part * half, half)
                query_rows = r.q[b, h, at, :]
                mix_rows = r.dmix[h, at, :]
                probs = jnp.exp(masked_scores(b, key_rows, query_rows) - r.lse[b, h, :, at])
                grad_probs = dot_nt(value_rows, mix_rows)
                inner = jnp.sum(probs * grad_probs, 0, keepdims=True)
                grad_scores = (probs * (grad_probs - inner)).astype(BF)
                grad_query = dot_tn(key_rows, grad_scores) * SCALE
                r.dq[h, at, :] = grad_query.T.astype(BF)
                key_term = dot_nn(grad_scores, query_rows)
                value_term = dot_nn(probs.astype(BF), mix_rows)
                grad_keys = key_term if grad_keys is None else grad_keys + key_term
                grad_values = value_term if grad_values is None else grad_values + value_term
            r.kv[b, 0, h] = (grad_keys * SCALE).astype(BF).reshape(CORES, rows, HD)
            r.kv[b, 1, h] = grad_values.astype(BF).reshape(CORES, rows, HD)

    def swap_back(b):
        return [send(r.kv.at[b, :, :, 1 - e], r.dl.at[b], sibling)]

    def join_gradients(b, handles):
        recv_all(handles)

        @pl.loop(0, CHIPS)
        def _(i):
            at = pl.ds(pl.multiple_of(i * tok, tok), tok)
            pieces = [r.dq[h, at, :] for h in range(OWN_HEADS)]
            for part in range(2):
                for h in range(OWN_HEADS):
                    pair = r.kv[b, part, h, e, at, :].astype(F32) + r.dl[b, part, h, at, :].astype(F32)
                    pieces.append(pair.astype(BF))
            pieces.append(jnp.zeros((tok, QKV_WIDTH - 3 * OWN_FEATURES), BF))
            line = jnp.concatenate(pieces, 1)
            r.dqkv[b, at, :] = line
            r.vqkv[...] += jnp.sum(line.astype(F32), 0, keepdims=True)

    def input_start(b, earlier):
        sent_all(earlier[2])
        partial_sum(sb, b, lambda at: dot_nt(r.dqkv[b], Wq[at, :]))
        return reduce_start(sb, rb, b)

    def finish_input(b, reduction):
        gradient = reduce_finish(reduction)
        normed, inverse = norm_parts(r.x[b].astype(F32))
        back = norm_backward(gradient, normed, inverse, vec_row(ROW_GAIN_ONE))
        r.ig[b] = (r.dresid[b] + back).astype(BF)
        add_row(ROW_GAIN_ONE, jnp.sum(gradient * normed, 0, keepdims=True))
        add_row(ROW_SHIFT_ONE, jnp.sum(gradient, 0, keepdims=True))

    def finish_out(b, reduction):
        total = r.resid[b] + reduce_finish(reduction) + vec_row(ROW_BIAS_SHRINK)
        r.bo[b] = total.astype(BF)

    def sum_group(space, slots):
        return SimpleNamespace(space=space, slots=slots, right={}, left={})

    def add_passing(group, hops):
        space, slots = group.space, group.slots
        for side, held, i, slot in (
            (group.right, (c >= 1) & (c - 1 + hops < planes), c - 1 + hops, hops - 1),
            (group.left, (c <= planes - 2) & (c + 1 - hops >= 0), c + 1 - hops, 5 - hops),
        ):
            side[hops][0]()

            @pl.when(held)
            def _():
                space[i] = (space[i].astype(F32) + slots[slot][...].astype(F32)).astype(BF)

    def sum_step(group, hops):
        space, slots = group.space, group.slots
        if hops < planes - 1:
            add_passing(group, hops + 1)
        group.right[hops] = send_if(
            c + hops < planes, lambda: space.at[c + hops], lambda: slots[hops - 1], me + DEV_CLIP,
            (c >= 1) & (c - 1 + hops < planes), lambda: slots[hops - 1],
        )
        group.left[hops] = send_if(
            c - hops >= 0, lambda: space.at[c - hops], lambda: slots[5 - hops], me - DEV_CLIP,
            (c <= planes - 2) & (c + 1 - hops >= 0), lambda: slots[5 - hops],
        )

    def sum_finish(group, out):
        space, slots = group.space, group.slots
        out(space[c].astype(F32), False)
        for side, held, slot in ((group.right, c >= 1, 0), (group.left, c <= planes - 2, 4)):
            side[1][0]()

            @pl.when(held)
            def _():
                out(slots[slot][...].astype(F32), True)

    def to_blocks(ref):
        def put(total, more):
            for j in range(CHIPS):
                piece = total[j * share:(j + 1) * share]
                ref[j] = ref[j] + piece if more else piece

        return put

    def to_rows(ref):
        def put(total, more):
            ref[...] = ref[...] + total if more else total

        return put

    def sibling_add(handles, landing, fetched, out, mine):
        recv_all(handles)
        sent_all(handles)
        local(landing, fetched)()

        @pl.loop(0, planes)
        def _(i):
            out[i] = (mine(i).astype(F32) + fetched[i].astype(F32)).astype(BF)

    def free_slots(ready):
        for side, held, device in ((0, c >= 1, me - DEV_CLIP), (1, c <= planes - 2, me + DEV_CLIP)):

            @pl.when(held)
            def _():
                pl.semaphore_signal(
                    ready.at[1 - side], inc=1, device_id=(device,), device_id_type=pl.DeviceIdType.MESH
                )

    def await_slots(ready):
        for side, held in ((0, c >= 1), (1, c <= planes - 2)):

            @pl.when(held)
            def _():
                pl.semaphore_wait(ready.at[side], 1)

    resid, dresid = r.resid, r.dresid
    x_local = [local(r.x.at[b], r.xg.at[b, k]) for b in range(micro)]
    dy_local = [local(r.dy.at[b], r.dyg.at[b, k]) for b in range(micro)]
    x_gather = [None] * micro
    dy_gather = [None] * micro
    if fused:
        expand = [dresid.at[0, 0:share], dresid.at[0, share:2 * share], dresid.at[0, 2 * share:3 * share], dresid.at[1, 0:share]]
        first_rows = tok - share
        loads = [local(ref, resid.at[0, i * share:(i + 1) * share]) for i, ref in enumerate((r.wq, r.wk, r.wv))]
        loads.append(local(r.wo, resid.at[1, 0:share]))
        expand_loads = [local(r.we.at[:, i * width:(i + 1) * width], expand[i]) for i in range(planes)]
        expand_loads.append(local(r.ws.at[0:first_rows], resid.at[1, share:tok]))
        expand_loads.append(local(r.ws.at[first_rows:ff_share], dresid.at[1, share:ff_share - first_rows + share]))
        peers = [chip_peer(by) for by in (1, 2, 3)] + [sibling]
        if fused:
            peers += [plane_peer(by) for by in range(1, planes)]
        barrier = pltpu.get_barrier_semaphore()
        for peer in peers:
            pl.semaphore_signal(barrier, inc=1, device_id=(peer,), device_id_type=pl.DeviceIdType.MESH)
        for load in loads:
            load()
        matrices = [resid[0, i * share:(i + 1) * share] for i in range(3)]
        for j in range(CHIPS):
            pieces = [
                matrix[:, (i * CHIPS + j) * HD:(i * CHIPS + j + 1) * HD] for matrix in matrices for i in range(planes)
            ]
            pieces.append(jnp.zeros((share, QKV_WIDTH - 3 * OWN_FEATURES), F32))
            r.aq[j] = jnp.concatenate(pieces, 1).astype(BF)
        r.so[c] = resid[1, 0:share].astype(BF)
        compact = jnp.concatenate([jnp.pad(ref[...], ((0, 0), (0, 256 - share))) for ref in r.vectors], 0)
        tail = jnp.pad(r.expand_bias[...], ((0, 0), (0, 256 - ff_share)))
        pair = [jnp.pad(ref[...], ((0, 0), (0, 128 - share))) for ref in (r.query_bias, r.value_bias)]
        r.cv[c] = jnp.concatenate([compact, tail, jnp.concatenate(pair, 1)], 0)
        pl.semaphore_wait(barrier, len(peers))
        wq_mine, wq_other = stacked(r.drg, planes, QKV_WIDTH), stacked(r.a2g, planes, QKV_WIDTH)
        we_mine, we_other = stacked(r.act, planes, ff_own), stacked(r.dhid, planes, ff_own)
        line_q = line_group(lambda i: wq_mine.at[i], lambda i: wq_other.at[i])
        line_e = line_group(lambda i: we_mine.at[i], lambda i: we_other.at[i])
        line_o = line_group(lambda i: r.so.at[i], lambda i: r.oo.at[i])
        line_s = line_group(lambda i: Ws.at[i, e], lambda i: Ws.at[i, e])

        def pack_plane(blocks, out):
            out[c] = jnp.concatenate([blocks[j].astype(F32) for j in range(CHIPS)], 0).astype(BF)

        wq_plane = [send(r.aq.at[flipped(k, by)], r.alq.at[k], chip_peer(by)) for by in (3, 1, 2)]
        vec_z = [send(r.cv.at[c], r.cv.at[c], plane_peer(by)) for by in range(1, planes)]
        forward(line_o, 0)
        r.alq[k] = r.aq[k]
        recv_all(vec_z)
        r.cp[e, k] = r.cv[...]
        vec_p = [send(r.cv, r.cp.at[e, k], chip_peer(by)) for by in (1, 2, 3)]
        x_gather[0] = gather_start(r.x.at[0], r.xg, 0)
        recv_all(wq_plane)
        pack_plane(r.alq, wq_mine)
        forward(line_q, 0)
        for load in expand_loads:
            load()
        ff_part = width // planes
        for j in range(CHIPS):
            pieces = [block[:, j * ff_part:(j + 1) * ff_part] for block in expand]
            r.ae[j] = jnp.concatenate(pieces, 1).astype(BF)
        we_plane = [send(r.ae.at[flipped(k, by)], r.ale.at[k], chip_peer(by)) for by in (3, 1, 2)]
        r.ale[k] = r.ae[k]
        rows_s = [resid[1, share:tok], dresid[1, share:ff_share - first_rows + share]]
        Ws[c, e] = jnp.concatenate(rows_s, 0).astype(BF)
        recv_all(vec_p)
        vec_s = [send(r.cp.at[e], r.cp.at[e], sibling)]
        recv_all(vec_s)
        places = [(i, f) for i in range(planes) for f in range(CORES)]
        vfin[...] = jnp.concatenate(
            [r.cp[f, j, i][:, 0:share] for i in range(planes) for j in range(CHIPS) for f in range(CORES)], 1
        )
        r.be[...] = jnp.concatenate([r.cp[f, k, i][6:7, 0:ff_share] for i, f in places], 1)
        bias = [jnp.concatenate([r.cp[f, k, i][7:8, at:at + share] for i, f in places], 1) for at in (0, 128)]
        blank = jnp.zeros((1, OWN_FEATURES), F32)
        r.bq[...] = jnp.concatenate([bias[0], blank, bias[1], blank[:, :QKV_WIDTH - 3 * OWN_FEATURES]], 1)
        gather_relay(x_gather[0])
        x_gather[1] = gather_start(r.x.at[1], r.xg, 1)
        forward(line_o, 1)
        forward(line_q, 1)
        recv_all(we_plane)
        pack_plane(r.ale, we_mine)
    else:
        peers = [chip_peer(by) for by in (1, 2, 3)] + [sibling]
        if fused:
            peers += [plane_peer(by) for by in range(1, planes)]
        barrier = pltpu.get_barrier_semaphore()
        for peer in peers:
            pl.semaphore_signal(barrier, inc=1, device_id=(peer,), device_id_type=pl.DeviceIdType.MESH)
        pl.semaphore_wait(barrier, len(peers))
        loads = [local(r.wq, Wq), local(r.we, We), local(r.wo, Wo), local(r.ws, Ws2)]
        for b in range(micro):
            x_gather[b] = gather_start(r.x.at[b], r.xg, b)
        vfin[...] = r.vec[...]
        r.be[...] = r.vec[6:7, :]
        r.bq[...] = r.vec[7:8, :QKV_WIDTH]
        gather_relay(x_gather[0])
        for load in loads:
            load()
    for ref in (r.vrow, r.vexp, r.vqkv):
        ref[...] = jnp.zeros_like(ref)
    norm_one(0)
    if fused:
        forward(line_o, 2)
        forward(line_q, 2)
        forward(line_e, 0)
        forward(line_s, 0)
    gather_relay(x_gather[1])
    dy_gather[0] = gather_start(r.dy.at[0], r.dyg, 0)
    norm_one(1)
    if fused:
        forward(line_o, 3)
        forward(line_q, 3)
        recv_all(line_q.swaps)
        join_planes(wq_mine, wq_other, Wq)
    kv_swap = [None] * micro
    kv_swap[0] = project(0)
    gather_relay(dy_gather[0])
    dy_gather[1] = gather_start(r.dy.at[1], r.dyg, 1)
    kv_swap[1] = project(1)
    recv_all(kv_swap[0])
    attend(0, 0, OWN_HEADS)
    if fused:
        forward(line_e, 1)
    attend(0, OWN_HEADS, 2 * OWN_HEADS)
    if fused:
        recv_all(line_o.swaps)
        for i in range(planes):
            pair = join_rows(r.so[i].astype(F32), r.oo[i].astype(F32), 1)
            Wo[i * HD:(i + 1) * HD, :] = pair.astype(BF)
    mix_reduce = [mix_out(0), None]
    gather_relay(dy_gather[1])
    recv_all(kv_swap[1])
    attend(1, 0, OWN_HEADS)
    if fused:
        forward(line_s, 1)
    attend(1, OWN_HEADS, 2 * OWN_HEADS - 1)
    reduce_relay(mix_reduce[0])
    attend(1, 2 * OWN_HEADS - 1, 2 * OWN_HEADS)
    mix_reduce[1] = mix_out(1)
    if fused:
        forward(line_e, 2)
    second_gather = [norm_two(0, mix_reduce[0]), None]
    if fused:
        forward(line_s, 2)
    reduce_relay(mix_reduce[1])
    gather_relay(second_gather[0])
    second_gather[1] = norm_two(1, mix_reduce[1])
    if fused:
        forward(line_e, 3)
        recv_all(line_e.swaps)
        group_sent(line_e)
        group_sent(line_q)
        join_planes(we_mine, we_other, We)
    gather_finish(second_gather[0])
    dy_local[0]()
    gather_finish(dy_gather[0])
    if fused:
        forward(line_s, 3)
        recv_all(line_s.swaps)
    gather_relay(second_gather[1])
    feed(0, 0, ff_own // TILE)
    hidden_reduce = [hidden_back(0, mix_reduce[0]), None]
    gather_finish(second_gather[1])
    dy_local[1]()
    gather_finish(dy_gather[1])
    feed(1, 0, ff_own // TILE)
    reduce_relay(hidden_reduce[0])
    hidden_reduce[1] = hidden_back(1, mix_reduce[1])
    weight_gradient(width, a2_rows, r.dhid, We)
    if fused:
        sent_all(wq_plane + we_plane)
        group_sent(line_o)
        group_sent(line_s)
        sent_all(second_gather[0][1] + second_gather[1][1])
        free_slots(r.ready_e)
        parts_e = We.reshape(planes, 2, chip_rows, ff_own)
        split_planes(We, parts_e.at[:, 0], parts_e.at[:, 1])
        ge_s = [send(parts_e.at[:, 1], r.Le, sibling)]
    resid_gather = [finish_hidden(0, hidden_reduce[0]), None]
    if fused:
        sum_e = sum_group(parts_e.at[:, 0], [flat(r.a2g).at[i * chip_rows:(i + 1) * chip_rows] for i in range(5)])
        sibling_add(ge_s, r.Le, parts_e.at[:, 1], parts_e.at[:, 0], lambda i: parts_e[i, 0])
        await_slots(r.ready_e)
        sum_step(sum_e, 3)
    for b in range(micro):
        partial_sum(sbo, b, lambda at: dot_nn(r.act[b], Ws2[:, at]))
    reduce_relay(hidden_reduce[1])
    weight_gradient(ff_own, r.act, dy_rows, Ws2)
    if fused:
        sent_all(dy_gather[0][1] + dy_gather[1][1])
        free_slots(r.ready_s)
        gs_s = [send(Ws.at[:, 1 - e], r.Ls, sibling)]
    resid_gather[1] = finish_hidden(1, hidden_reduce[1])
    out_reduce = [reduce_start(sbo, rbo, 0), None]
    gather_relay(resid_gather[0])
    if fused:
        places_s = [flat(r.a2g).at[5 * ff_share:6 * ff_share]]
        for ref in (r.dyg, r.act):
            places_s += [flat(ref).at[i * ff_share:(i + 1) * ff_share] for i in (4, 5)]
        sum_s = sum_group(Ws.at[:, e], places_s)
        sibling_add(gs_s, r.Ls, Ws.at[:, 1 - e], Ws.at[:, e], lambda i: Ws[i, e])
        await_slots(r.ready_s)
        sum_step(sum_s, 3)
        sum_step(sum_e, 2)
    gather_finish(resid_gather[0])
    mixed_gradient(0)
    sent_all(kv_swap[0] + kv_swap[1])
    attend_back(0, 0, 2)
    gather_relay(resid_gather[1])
    reduce_relay(out_reduce[0])
    if fused:
        sum_step(sum_s, 2)
    attend_back(0, 2, OWN_HEADS)
    swap = swap_back(0)
    gather_finish(resid_gather[1])
    mixed_gradient(1)
    lead = dot_nn(mixed[0], dr_rows[0])
    for other in range(1, micro):
        lead = lead + dot_nn(mixed[other], dr_rows[other])
    if fused:
        space_o, other_o = r.so, r.oo
        for i in range(planes):
            mine, theirs = split_rows(lead[i * HD:(i + 1) * HD], 1)
            space_o[i] = mine.astype(BF)
            other_o[i] = theirs.astype(BF)
        go_s = [send(other_o, r.Lo, sibling)]
    else:
        Wo[...] = lead.astype(BF)
    join_gradients(0, swap)
    input_reduce = [input_start(0, hidden_reduce[0]), None]
    if fused:
        sum_step(sum_e, 1)
    attend_back(1, 0, 2)
    out_reduce[1] = reduce_start(sbo, rbo, 1)
    reduce_relay(input_reduce[0])
    if fused:
        sum_o = sum_group(space_o, [r.ao.at[i] for i in range(5)])
        sibling_add(go_s, r.Lo, other_o, space_o, lambda i: space_o[i])
        sum_step(sum_s, 1)
        sum_step(sum_o, 3)
    attend_back(1, 2, OWN_HEADS)
    swap = swap_back(1)
    reduce_relay(out_reduce[1])
    join_gradients(1, swap)
    input_reduce[1] = input_start(1, hidden_reduce[1])
    weight_gradient(width, a1_rows, r.dqkv, Wq)
    if fused:
        free_slots(r.ready_q)
        parts_q = Wq.reshape(planes, 2, chip_rows, QKV_WIDTH)
        split_planes(Wq, parts_q.at[:, 0], parts_q.at[:, 1])
        gq_s = [send(parts_q.at[:, 1], r.Lq, sibling)]
        sum_step(sum_o, 2)
        five = stacked(r.dhid, 5, QKV_WIDTH)
        sum_q = sum_group(parts_q.at[:, 0], [five.at[i] for i in range(5)])
    finish_input(0, input_reduce[0])
    if fused:
        sibling_add(gq_s, r.Lq, parts_q.at[:, 1], parts_q.at[:, 0], lambda i: parts_q[i, 0])
        await_slots(r.ready_q)
        sum_step(sum_q, 3)
    def vector_step(group, step, last):
        zero, one, two, from_z, from_plane, from_core = group
        if step == 0:
            return [send(zero, from_core, sibling)]
        if step == 1:
            one[...] = zero[...] + from_core[...]
            return [send(one, from_z.at[by - 1], plane_peer(by)) for by in range(1, planes)]
        if step == 2:
            total = one[...]
            for by in range(1, planes):
                total = total + from_z[by - 1]
            two[...] = total
            return [send(two, from_plane.at[by - 1], chip_peer(by)) for by in (1, 2, 3)]
        others = from_plane[0] + from_plane[1] + from_plane[2]
        shared = lax.broadcasted_iota(jnp.int32, others.shape, 0) < 6
        last[...] = two[...] + jnp.where(shared, others, 0.0)

    if fused:
        group_u = (r.u0, r.u1, r.u2, r.uz, r.up, r.us)
        group_t = (r.t0, r.t1, r.t2, r.tz, r.tp, r.ts)
    padded = jnp.concatenate([r.vqkv[...], jnp.zeros((1, width - QKV_WIDTH), F32)], 1)
    early = jnp.concatenate([r.vrow[0:6, :], r.vexp[...], padded], 0)
    if fused:
        r.u0[...] = early
        moved = vector_step(group_u, 0, None)
    for b in range(micro):
        finish_out(b, out_reduce[b])
    if fused:
        recv_all(moved)
        moved = vector_step(group_u, 1, None)
        sum_finish(sum_s, to_rows(r.gs))
        sum_finish(sum_e, to_blocks(r.ge))
        for j in range(CHIPS):
            r.ae[j] = r.ge[j].astype(BF)
        sum_step(sum_o, 1)
    reduce_relay(input_reduce[1])
    if fused:
        ge_p = [send(r.ae.at[flipped(k, by)], r.ale.at[k], chip_peer(by)) for by in (3, 1, 2)]
        recv_all(moved)
        moved = vector_step(group_u, 2, None)
        sum_step(sum_q, 2)
    finish_input(1, input_reduce[1])
    late = r.vrow[0:2, :]
    if fused:
        r.t0[...] = late
        moved_late = vector_step(group_t, 0, None)
        recv_all(moved)
        vector_step(group_u, 3, r.vo)
        recv_all(ge_p)
        for by in (1, 2, 3):
            r.ge[flipped(k, by)] = r.ale[flipped(k, by)].astype(F32)
        recv_all(moved_late)
        moved_late = vector_step(group_t, 1, None)
        sum_step(sum_q, 1)
        recv_all(moved_late)
        moved_late = vector_step(group_t, 2, None)
        sum_finish(sum_o, to_rows(r.go))
        recv_all(moved_late)
        vector_step(group_t, 3, r.vt)
        sum_finish(sum_q, to_blocks(r.gq))
        for j in range(CHIPS):
            r.aq[j] = r.gq[j].astype(BF)
        gq_p = [send(r.aq.at[flipped(k, by)], r.alq.at[k], chip_peer(by)) for by in (3, 1, 2)]
        recv_all(gq_p)
        for by in (1, 2, 3):
            r.gq[flipped(k, by)] = r.alq[flipped(k, by)].astype(F32)
    else:
        r.vo[...] = early
        r.vt[...] = late
        stores = [local(Wq, r.gq), local(We, r.ge), local(Wo, r.go), local(Ws2, r.gs)]
        for store in stores:
            store()
    for wait in pending:
        wait()


def run_block(fused, planes, x, dy, lengths, vectors, weights_in, share, ff_share):
    micro, tok, width = x.shape
    ff_own = width
    rows = CHIPS * tok
    vmem = pl.BlockSpec(memory_space=pltpu.VMEM)
    anywhere = pl.BlockSpec(memory_space=pl.ANY)
    smem = pl.BlockSpec(memory_space=pltpu.SMEM)

    def shape(*dims, dtype=BF):
        return jax.ShapeDtypeStruct(dims, dtype)

    outs = [
        (shape(micro, tok, width), vmem),
        (shape(micro, tok, width), vmem),
        (shape(8, width, dtype=F32), vmem),
        (shape(2, width, dtype=F32), vmem),
    ]
    if fused:
        outs += [
            (shape(CHIPS, share, QKV_WIDTH, dtype=F32), vmem),
            (shape(CHIPS, share, ff_own, dtype=F32), vmem),
            (shape(share, width, dtype=F32), vmem),
            (shape(ff_share, width, dtype=F32), vmem),
        ]
        outs += [
            (shape(planes, CHIPS * share, QKV_WIDTH), anywhere),
            (shape(planes, CHIPS * share, ff_own), anywhere),
            (shape(planes, share, width), anywhere),
            (shape(planes, ff_share, width), anywhere),
        ]
    else:
        outs += [
            (shape(width, QKV_WIDTH), anywhere),
            (shape(width, ff_own), anywhere),
            (shape(OWN_FEATURES, width), anywhere),
            (shape(ff_own, width), anywhere),
        ]
    if fused:
        weights = [
            pltpu.VMEM((width, QKV_WIDTH), BF),
            pltpu.VMEM((width, ff_own), BF),
            pltpu.VMEM((OWN_FEATURES, width), BF),
            pltpu.VMEM((planes, CORES, ff_share, width), BF),
        ]
    else:
        weights = [
            pltpu.VMEM((width, QKV_WIDTH), BF),
            pltpu.VMEM((width, ff_own), BF),
            pltpu.VMEM((OWN_FEATURES, width), BF),
            pltpu.VMEM((ff_own, width), BF),
        ]
    scratch = weights + [
        pltpu.VMEM((micro, CHIPS, tok, width), BF),
        pltpu.VMEM((micro, CHIPS, tok, width), BF),
        pltpu.VMEM((micro, CHIPS, tok, width), BF),
        pltpu.VMEM((micro, CHIPS, tok, width), BF),
        pltpu.VMEM((micro, rows, ff_own), BF),
        pltpu.VMEM((micro, rows, ff_own), BF),
        pltpu.VMEM((micro, OWN_HEADS, rows, HD), BF),
        pltpu.VMEM((micro, 2, OWN_HEADS, CORES, rows, HD), BF),
        pltpu.VMEM((micro, OWN_HEADS, HD, rows), BF),
        pltpu.VMEM((micro, OWN_HEADS, 1, rows), F32),
        pltpu.VMEM((OWN_HEADS, rows, HD), BF),
        pltpu.VMEM((OWN_HEADS, rows, HD), BF),
        pltpu.VMEM((micro, 2, OWN_HEADS, rows, HD), BF),
        pltpu.VMEM((micro, CHIPS, tok, width), BF),
        pltpu.VMEM((micro, CHIPS, tok, width), BF),
        pltpu.VMEM((micro, CHIPS - 1, tok, width), BF),
        pltpu.VMEM((micro, CHIPS - 1, tok, width), BF),
        pltpu.VMEM((micro, tok, width), F32),
        pltpu.VMEM((micro, tok, width), F32),
        pltpu.VMEM((8, width), F32),
        pltpu.VMEM((1, ff_own), F32),
        pltpu.VMEM((1, QKV_WIDTH), F32),
        pltpu.VMEM((1, ff_own), F32),
        pltpu.VMEM((1, QKV_WIDTH), F32),
        pltpu.VMEM((8, width), F32),
    ]
    if fused:
        scratch += [
            pltpu.VMEM((planes, share, width), BF),
            pltpu.VMEM((planes, share, width), BF),
            pltpu.VMEM((5, share, width), BF),
            pltpu.VMEM((CHIPS, share, QKV_WIDTH), BF),
            pltpu.VMEM((CHIPS, share, ff_own), BF),
            pltpu.VMEM((CHIPS, share, QKV_WIDTH), BF),
            pltpu.VMEM((CHIPS, share, ff_own), BF),
        ]
        scratch += [
            pltpu.VMEM((planes, 8, 256), F32),
            pltpu.VMEM((CORES, CHIPS, planes, 8, 256), F32),
        ]
        for lines in (8, 2):
            scratch += [pltpu.VMEM((lines, width), F32) for _ in range(3)]
            scratch += [pltpu.VMEM((planes - 1, lines, width), F32), pltpu.VMEM((CHIPS - 1, lines, width), F32)]
            scratch.append(pltpu.VMEM((lines, width), F32))
        scratch += [pltpu.SemaphoreType.REGULAR((2,)) for _ in range(3)]
    scratch += [
        pltpu.SemaphoreType.DMA((SEMS,)),
        pltpu.SemaphoreType.DMA((SEMS,)),
        pltpu.SemaphoreType.DMA((LOCAL_SEMS,)),
    ]
    return pl.pallas_call(
        partial(block_kernel, fused, planes, micro, tok, width, ff_own, share, ff_share),
        out_shape=[out for out, _ in outs],
        in_specs=[vmem, vmem, smem] + [vmem] * len(vectors) + [anywhere] * len(weights_in),
        out_specs=[spec for _, spec in outs],
        scratch_shapes=scratch,
        compiler_params=pltpu.CompilerParams(
            collective_id=0, has_side_effects=True, vmem_limit_bytes=63 * 1000 * 1000
        ),
    )(x, dy, lengths, *vectors, *weights_in)


def finish_kernel(planes, share, ff_share, bo, ig, vo, vt, gq, ge, go, gs, *refs):
    device = lax.axis_index("fsdp")
    c, _, e = place(device)
    outs, (blocks_q, blocks_e, lines, last_lines, sems) = refs[:17], refs[17:]
    moves = [(vo, lines), (vt, last_lines), (gq, blocks_q), (ge, blocks_e)]
    moves += [(bo, outs[0]), (ig, outs[1]), (go, outs[6]), (gs, outs[7])]
    copies = [pltpu.make_async_copy(src, dst, sems.at[i]) for i, (src, dst) in enumerate(moves)]
    for copy in copies:
        copy.start()
    for copy in copies[:4]:
        copy.wait()
    part = ge.shape[2] // planes
    for n in range(planes):
        for j in range(CHIPS):
            at = (n * CHIPS + j) * part
            outs[5][:, at:at + part] = blocks_e[j][:, n * part:(n + 1) * part]
    for i, out in enumerate(outs[2:5]):
        first = i * OWN_FEATURES
        out[...] = jnp.concatenate(
            [blocks_q[j][:, first + n * HD:first + (n + 1) * HD] for n in range(planes) for j in range(CHIPS)], 1
        )
    vo, vt = lines, last_lines
    width = vo.shape[1]

    def own(lines, start, size):
        lane = lax.broadcasted_iota(jnp.int32, (width, size), 0)
        pick = (lane == start + lax.broadcasted_iota(jnp.int32, (width, size), 1)).astype(F32)
        return lax.dot_general(
            lines, pick, (((1,), (0,)), ((), ())), precision=lax.Precision.HIGHEST, preferred_element_type=F32
        )

    early, late = own(vo[...], device * share, share), own(vt[...], device * share, share)
    expand = own(vo[...], (2 * c + e) * ff_share, ff_share)
    query = own(vo[...], (2 * c + e) * share, share)
    value = own(vo[...], 2 * OWN_FEATURES + (2 * c + e) * share, share)
    for out, line in zip(
        outs[8:],
        [late[0:1], late[1:2]] + [early[i:i + 1] for i in range(2, 6)] + [expand[6:7], query[7:8], value[7:8]],
        strict=True,
    ):
        out[...] = line
    for copy in copies[4:]:
        copy.wait()


def finish_block(planes, share, ff_share, results):
    shapes = [results[0], results[1]] + [jax.ShapeDtypeStruct((share, results[2].shape[1]), F32)] * 3
    shapes += [jax.ShapeDtypeStruct((share, CHIPS * results[5].shape[2]), F32), results[6], results[7]]
    shapes = [jax.ShapeDtypeStruct(s.shape, s.dtype) for s in shapes]
    shapes += [jax.ShapeDtypeStruct((1, share), F32)] * 6
    shapes += [jax.ShapeDtypeStruct((1, size), F32) for size in (ff_share, share, share)]
    vmem = pl.BlockSpec(memory_space=pltpu.VMEM)
    anywhere = pl.BlockSpec(memory_space=pl.ANY)
    held = [results[4], results[5], results[2], results[3]]
    return pl.pallas_call(
        partial(finish_kernel, planes, share, ff_share),
        out_shape=shapes,
        in_specs=[anywhere] * 8,
        out_specs=[vmem] * 17,
        scratch_shapes=[pltpu.VMEM(a.shape, a.dtype) for a in held] + [pltpu.SemaphoreType.DMA((8,))],
        compiler_params=pltpu.CompilerParams(vmem_limit_bytes=60 * 1000 * 1000),
    )(*results)


def by_chip(matrix, part):
    rows = matrix.shape[0]
    return matrix.reshape(rows, -1, CHIPS, part).transpose(2, 0, 1, 3).reshape(CHIPS, rows, -1)


def from_chips(blocks, part):
    rows = blocks.shape[1]
    return blocks.reshape(CHIPS, rows, -1, part).transpose(1, 2, 0, 3).reshape(rows, -1)


def body(
    inputs, cotangent, lengths, first_gain, first_shift, query_weight, query_bias, key_weight,
    value_weight, value_bias, output_weight, output_bias, second_gain, second_shift,
    expand_weight, expand_bias, shrink_weight, shrink_bias,
):
    device = lax.axis_index("fsdp")
    count = lax.axis_size("fsdp")
    c, k, e = place(device)
    planes = count // DEV_CLIP
    width = inputs.shape[2]
    share = query_weight.shape[0]
    ff_share = shrink_weight.shape[0]
    ff_part = width // 4
    fused = planes == 4 and share * 2 == HD and ff_share * 2 == ff_part
    plain = (first_gain, first_shift, second_gain, second_shift, output_bias, shrink_bias)
    matrices = (query_weight, key_weight, value_weight, expand_weight, output_weight, shrink_weight)
    if fused:
        vectors = [v.reshape(1, -1) for v in plain + (expand_bias, query_bias, value_bias)]
        got = run_block(True, planes, inputs, cotangent, lengths, vectors, matrices, share, ff_share)
        done = finish_block(planes, share, ff_share, got[:8])
        block_out, input_grad, grad_query_w, grad_key_w, grad_value_w, grad_expand_w, grad_output_w, grad_shrink_w = done[:8]
        owned = [line[0] for line in done[8:14]]
        grad_expand_b, grad_query_b, grad_value_b = (line[0] for line in done[14:])
    else:

        def whole(array):
            return lax.all_gather(array, "fsdp", axis=0, tiled=True)

        def mine(blocks):
            return lax.dynamic_index_in_dim(blocks, k, 0, keepdims=False)

        full = [whole(w.astype(BF)) for w in matrices]
        pieces = [mine(by_chip(w, HD)) for w in full[:3]]
        pieces.append(jnp.zeros((width, QKV_WIDTH - 3 * OWN_FEATURES), BF))
        wq = jnp.concatenate(pieces, 1)
        we = mine(by_chip(full[3], ff_part))
        wo = mine(by_chip(full[4].T, HD)).T
        ws = mine(by_chip(full[5].T, ff_part)).T
        bias_e = mine(by_chip(whole(expand_bias)[None], ff_part))
        bias_q = mine(by_chip(whole(query_bias)[None], HD))
        bias_v = mine(by_chip(whole(value_bias)[None], HD))
        blank = jnp.zeros((1, width - 3 * OWN_FEATURES), F32)
        bias_row = jnp.concatenate([bias_q, jnp.zeros_like(bias_q), bias_v, blank], 1)
        vec = jnp.concatenate([jnp.stack([whole(v) for v in plain]), bias_e, bias_row])
        got = run_block(False, planes, inputs, cotangent, lengths, (vec,), (wq, we, wo, ws), share, ff_share)
        block_out, input_grad, sums, late, gq, ge, go, gs = got[:8]

        def spread(block, part):
            places = lax.broadcasted_iota(jnp.int32, (CHIPS, 1, 1), 0) == k
            return from_chips(jnp.where(places, block.astype(F32)[None], 0.0), part)

        def owned_sum(array):
            return lax.psum_scatter(array, "fsdp", scatter_dimension=0, tiled=True)

        grad_query_w, grad_key_w, grad_value_w = (
            owned_sum(spread(gq[:, i * OWN_FEATURES:(i + 1) * OWN_FEATURES], HD)) for i in range(3)
        )
        grad_expand_w = owned_sum(spread(ge, ff_part))
        grad_output_w = owned_sum(spread(go.T, HD).T)
        grad_shrink_w = owned_sum(spread(gs.T, ff_part).T)
        owned = [owned_sum(late[i]) for i in range(2)] + [owned_sum(sums[i]) for i in range(2, len(plain))]
        line_q, line_v = sums[7:8, :OWN_FEATURES], sums[7:8, 2 * OWN_FEATURES:3 * OWN_FEATURES]
        grad_expand_b = owned_sum(spread(sums[6:7], ff_part)[0])
        grad_query_b = owned_sum(spread(line_q, HD)[0])
        grad_value_b = owned_sum(spread(line_v, HD)[0])
    return (
        block_out,
        input_grad,
        owned[0],
        owned[1],
        grad_query_w,
        grad_query_b,
        grad_key_w,
        grad_value_w,
        grad_value_b,
        grad_output_w,
        owned[4],
        owned[2],
        owned[3],
        grad_expand_w,
        grad_expand_b,
        grad_shrink_w,
        owned[5],
    )


def solution(mesh):
    rows, matrix, vector = P(None, "fsdp", None), P("fsdp", None), P("fsdp")
    in_specs = (
        rows, rows, P(), vector, vector, matrix, vector, matrix, matrix, vector, matrix, vector,
        vector, vector, matrix, vector, matrix, vector,
    )
    out_specs = (
        rows, rows, vector, vector, matrix, vector, matrix, matrix, vector, matrix, vector,
        vector, vector, matrix, vector, matrix, vector,
    )
    return jax.shard_map(body, mesh=mesh, in_specs=in_specs, out_specs=out_specs, check_vma=False)
```

```python
from functools import partial
from types import SimpleNamespace

import jax
import jax.numpy as jnp
from jax import lax
from jax.experimental import pallas as pl
from jax.experimental.pallas import tpu as pltpu
from jax.sharding import PartitionSpec as P

H = 16
HD = 80
CHIPS = 4
CORES = 2
DEV_CLIP = CHIPS * CORES
OWN_HEADS = H // CHIPS
OWN_FEATURES = OWN_HEADS * HD
QKV_WIDTH = 1024
TILE = 256
ROW_GAIN_ONE, ROW_SHIFT_ONE, ROW_GAIN_TWO, ROW_SHIFT_TWO, ROW_BIAS_OUT, ROW_BIAS_SHRINK = range(6)

EPS = 1e-05
NEG = -1000000000.0
SCALE = HD ** (-0.5)
BF = jnp.bfloat16
F32 = jnp.float32


def dot_nn(left, right):
    return lax.dot_general(left, right, (((1,), (0,)), ((), ())), preferred_element_type=F32)


def dot_nt(left, right):
    return lax.dot_general(left, right, (((1,), (1,)), ((), ())), preferred_element_type=F32)


def dot_tn(left, right):
    return lax.dot_general(left, right, (((0,), (0,)), ((), ())), preferred_element_type=F32)


def norm_parts(rows):
    mean = jnp.mean(rows, -1, keepdims=True)
    centered = rows - mean
    inverse = lax.rsqrt(jnp.mean(centered * centered, -1, keepdims=True) + EPS)
    return centered * inverse, inverse


def norm_backward(gradient, normed, inverse, gain):
    scaled = gradient * gain
    return inverse * (
        scaled
        - jnp.mean(scaled, -1, keepdims=True)
        - normed * jnp.mean(scaled * normed, -1, keepdims=True)
    )


def place(device):
    return device // DEV_CLIP, (device % DEV_CLIP) // CORES, device % CORES


def flipped(number, by):
    low, high = number % 2, number // 2
    if by & 1:
        low = 1 - low
    if by & 2:
        high = 1 - high
    return high * 2 + low


SEMS = 240
LOCAL_SEMS = 40


def block_kernel(fused, planes, micro, tok, width, ff_own, share, ff_share, *refs):
    names = ["x", "dy", "lengths"]
    if fused:
        names += ["av", "bv", "cv_", "dv", "ev", "fv"] + ["expand_bias", "query_bias", "value_bias", "wq", "wk", "wv", "we", "wo", "ws"]
    else:
        names += ["vec", "wq", "we", "wo", "ws"]
    names += ["bo", "ig", "vo", "vt", "gq", "ge", "go", "gs"]
    if fused:
        names += ["Lq", "Le", "Lo", "Ls"]
    names += ["Wq", "We", "Wo", "Ws", "xg", "dyg", "a2g", "drg", "act", "dhid"]
    names += ["q", "kv", "mixed", "lse", "dmix", "dq", "dl"]
    names += ["sb", "sbo", "rb", "rbo", "resid", "dresid", "vfin", "be", "bq", "vexp", "vqkv", "vrow"]
    if fused:
        names += ["so", "oo", "ao", "aq", "ae", "alq", "ale", "cv", "cp"]
        names += [letter + end for letter in "ut" for end in ("0", "1", "2", "z", "p", "s")]
        names += ["ready_e", "ready_s", "ready_q"]
    names += ["ssem", "rsem", "lsem"]
    r = SimpleNamespace(**dict(zip(names, refs, strict=True)))
    if fused:
        r.vectors = (r.av, r.bv, r.cv_, r.dv, r.ev, r.fv)
    r.dqkv = r.dhid.at[:, :, 0:QKV_WIDTH]
    me = lax.axis_index("fsdp")
    c, k, e = place(me)
    rows = CHIPS * tok

    def chip_peer(by):
        return c * DEV_CLIP + flipped(k, by) * CORES + e

    sibling = c * DEV_CLIP + k * CORES + (1 - e)

    def plane_peer(by):
        return flipped(c, by) * DEV_CLIP + k * CORES + e

    counters = SimpleNamespace(remote=0, local=0)
    pending = []

    def send(src, dst, device):
        i = counters.remote
        counters.remote += 1
        copy = pltpu.make_async_remote_copy(
            src_ref=src, dst_ref=dst, send_sem=r.ssem.at[i], recv_sem=r.rsem.at[i],
            device_id=(device,), device_id_type=pl.DeviceIdType.MESH,
        )
        copy.start()
        state = SimpleNamespace(sent=False)

        def wait_send():
            if not state.sent:
                state.sent = True
                copy.wait_send()

        copy_handle = (copy.wait_recv, wait_send)
        pending.append(wait_send)
        return copy_handle

    def send_if(held, src, dst, device, due, arriving):
        i = counters.remote
        counters.remote += 1

        def copy(source, target, to):
            return pltpu.make_async_remote_copy(
                src_ref=source, dst_ref=target, send_sem=r.ssem.at[i], recv_sem=r.rsem.at[i],
                device_id=(to,), device_id_type=pl.DeviceIdType.MESH,
            )

        @pl.when(held)
        def _():
            copy(src(), dst(), device).start()

        state = SimpleNamespace(sent=False)

        def wait_send():
            if not state.sent:
                state.sent = True

                @pl.when(held)
                def _():
                    copy(src(), dst(), device).wait_send()

        def wait_recv():
            @pl.when(due)
            def _():
                copy(arriving(), arriving(), sibling).wait_recv()

        copy_handle = (wait_recv, wait_send)
        pending.append(wait_send)
        return copy_handle

    def line_group(mine, theirs):
        return SimpleNamespace(mine=mine, theirs=theirs, steps=[], swaps=[])

    def forward(group, step):
        mine, theirs = group.mine, group.theirs
        if step > 0:
            recv_all(group.steps[step - 1])
        if step < planes - 1:
            n = step + 1
            group.steps.append([
                send_if(
                    (c >= n - 1) & (c < planes - 1), lambda: mine(c - n + 1), lambda: mine(c - n + 1),
                    me + DEV_CLIP, c >= n, lambda: mine(c - n),
                ),
                send_if(
                    (c + n - 1 < planes) & (c >= 1), lambda: mine(c + n - 1), lambda: mine(c + n - 1),
                    me - DEV_CLIP, c + n < planes, lambda: mine(c + n),
                ),
            ])
        if step == 0:
            group.swaps.append(send(mine(c), theirs(c), sibling))
        else:
            for held, i in ((c >= step, c - step), (c + step < planes, c + step)):
                group.swaps.append(
                    send_if(
                        held, lambda i=i: mine(i), lambda i=i: theirs(i), sibling, held, lambda i=i: theirs(i)
                    )
                )

    def group_sent(group):
        sent_all(sum(group.steps, []) + group.swaps)

    def local(src, dst):
        i = counters.local
        counters.local += 1
        copy = pltpu.make_async_copy(src, dst, r.lsem.at[i])
        copy.start()
        return copy.wait

    def recv_all(handles):
        for handle in handles:
            handle[0]()

    def sent_all(handles):
        for handle in handles:
            handle[1]()

    Wq, We, Wo, Ws = r.Wq, r.We, r.Wo, r.Ws
    Ws2 = Ws.reshape(ff_own, width)

    def flat(ref):
        return ref.reshape(micro * rows, width)

    chip_rows = CHIPS * share
    plane_rows = CORES * chip_rows

    def stacked(ref, count, lanes):
        return flat(ref).at[0:count * chip_rows].reshape(count, chip_rows, width).at[:, :, 0:lanes]

    def by_core(own, other):
        return jnp.where(e == 0, own, other), jnp.where(e == 0, other, own)

    def join_rows(own, other, count):
        first, second = by_core(own, other)
        pieces = []
        for j in range(count):
            pieces += [first[j * share:(j + 1) * share], second[j * share:(j + 1) * share]]
        return jnp.concatenate(pieces, 0)

    def split_rows(block, count):
        pieces = [block[j * share:(j + 1) * share] for j in range(2 * count)]
        return by_core(jnp.concatenate(pieces[0::2], 0), jnp.concatenate(pieces[1::2], 0))

    def join_planes(own, other, out):
        @pl.loop(0, planes)
        def _(i):
            block = join_rows(own[i].astype(F32), other[i].astype(F32), CHIPS)
            out[pl.ds(pl.multiple_of(i * plane_rows, plane_rows), plane_rows), :] = block.astype(BF)

    def split_planes(grads, own, other):
        @pl.loop(0, planes)
        def _(i):
            block = grads[pl.ds(pl.multiple_of(i * plane_rows, plane_rows), plane_rows), :].astype(F32)
            mine, theirs = split_rows(block, CHIPS)
            own[i] = mine.astype(BF)
            other[i] = theirs.astype(BF)

    k_x, k_y, k_far = flipped(k, 1), flipped(k, 2), flipped(k, 3)
    x_peer, y_peer, far_peer = chip_peer(1), chip_peer(2), chip_peer(3)
    top, low = slice(0, tok // 2), slice(tok // 2, tok)

    def gather_start(src, dst, b):
        return [dst.at[b], [send(src, dst.at[b, k], x_peer), send(src, dst.at[b, k], y_peer)]]

    def gather_relay(gather):
        dst, handles = gather
        handles[0][0]()
        handles.append(send(dst.at[k_x, top], dst.at[k_x, top], y_peer))
        handles[1][0]()
        handles.append(send(dst.at[k_y, low], dst.at[k_y, low], x_peer))

    def gather_finish(gather):
        recv_all(gather[1][2:])

    def reduce_start(slots, landing, b):
        slots, landing = slots.at[b], landing.at[b]
        return [slots, landing, [
            send(slots.at[k_far, top], landing.at[2, top], x_peer),
            send(slots.at[k_far, low], landing.at[2, low], y_peer),
            send(slots.at[k_x, top], landing.at[0, top], x_peer),
            send(slots.at[k_y, low], landing.at[1, low], y_peer),
        ]]

    def reduce_relay(reduction):
        slots, landing, handles = reduction
        handles[0][0]()
        slots[k_y, top] = (slots[k_y, top].astype(F32) + landing[2, top].astype(F32)).astype(BF)
        handles.append(send(slots.at[k_y, top], landing.at[1, top], y_peer))
        handles[1][0]()
        slots[k_x, low] = (slots[k_x, low].astype(F32) + landing[2, low].astype(F32)).astype(BF)
        handles.append(send(slots.at[k_x, low], landing.at[0, low], x_peer))

    def reduce_finish(reduction):
        slots, landing, handles = reduction
        recv_all(handles[2:])
        return slots[k].astype(F32) + landing[0].astype(F32) + landing[1].astype(F32)

    sb, sbo, rb, rbo = r.sb, r.sbo, r.rb, r.rbo
    vfin = r.vfin

    def vec_row(index):
        return vfin[index:index + 1, :]

    def add_row(index, value):
        r.vrow[index:index + 1, :] += value

    def norm_one(b):
        x_local[b]()
        gather_finish(x_gather[b])
        sent_all(x_gather[b][1])

        @pl.loop(0, CHIPS)
        def _(i):
            normed, _inverse = norm_parts(r.xg[b, i].astype(F32))
            r.xg[b, i] = (normed * vec_row(ROW_GAIN_ONE) + vec_row(ROW_SHIFT_ONE)).astype(BF)

    a1_rows = r.xg.reshape(micro, rows, width)
    a2_rows = r.a2g.reshape(micro, rows, width)
    dy_rows = r.dyg.reshape(micro, rows, width)
    dr_rows = r.drg.reshape(micro, rows, width)
    half = rows // 2

    def project(b):
        @pl.loop(0, 2)
        def _(i):
            at = pl.ds(pl.multiple_of(i * half, half), half)
            out = (dot_nn(a1_rows[b, at, :], Wq[...]) + r.bq[...]).astype(BF)
            for h in range(OWN_HEADS):
                r.q[b, h, at, :] = out[:, h * HD:(h + 1) * HD]
                for part in range(2):
                    low = (part + 1) * OWN_FEATURES + h * HD
                    r.kv[b, part, h, e, at, :] = out[:, low:low + HD]

        return [send(r.kv.at[b, :, :, e], r.kv.at[b, :, :, e], sibling)]

    keys = CORES * rows
    chunk_places = [(2 * (i % CHIPS) + i // CHIPS) * tok for i in range(DEV_CLIP)]

    def masked_scores(b, key_rows, query_rows):
        raw = dot_nt(key_rows, query_rows)
        index = lax.broadcasted_iota(jnp.int32, (tok, raw.shape[1]), 0)
        length = r.lengths[b, c]
        return jnp.concatenate(
            [
                jnp.where(index < length - first, raw[i * tok:(i + 1) * tok] * SCALE, NEG)
                for i, first in enumerate(chunk_places)
            ],
            0,
        )

    def attend(b, start, stop):
        @pl.loop(start, stop)
        def _(step):
            h, part = step // 2, step % 2
            at = pl.ds(pl.multiple_of(part * half, half), half)
            key_rows = r.kv[b, 0, h].reshape(keys, HD)
            value_rows = r.kv[b, 1, h].reshape(keys, HD)
            scores = masked_scores(b, key_rows, r.q[b, h, at, :])
            peak = jnp.max(scores, 0, keepdims=True)
            exponent = jnp.exp(scores - peak)
            sums = jnp.sum(exponent, 0, keepdims=True)
            probs = (exponent * (1.0 / sums)).astype(BF)
            r.lse[b, h, :, at] = peak + jnp.log(sums)
            r.mixed[b, h, :, at] = dot_tn(value_rows, probs).astype(BF)

    def tiles(start, stop, body):
        for i in range(start, stop):
            body(pl.ds(i * TILE, TILE))

    def partial_sum(slots, b, product):
        view = slots.reshape(micro, rows, width)

        def body(at):
            view[b, :, at] = product(at).astype(BF)

        tiles(0, width // TILE, body)

    mixed = r.mixed.reshape(micro, OWN_FEATURES, rows)

    def mix_out(b):
        partial_sum(sb, b, lambda at: dot_tn(mixed[b], Wo[:, at]))
        return reduce_start(sb, rb, b)

    def norm_two(b, reduction):
        residual = r.x[b].astype(F32) + reduce_finish(reduction) + vec_row(ROW_BIAS_OUT)
        r.resid[b] = residual
        normed, _inverse = norm_parts(residual)
        r.a2g[b, k] = (normed * vec_row(ROW_GAIN_TWO) + vec_row(ROW_SHIFT_TWO)).astype(BF)
        return gather_start(r.a2g.at[b, k], r.a2g, b)

    def feed(b, start, stop):
        def body(at):
            hidden = dot_nn(a2_rows[b], We[:, at]) + r.be[:, at]
            grad_active = dot_nt(dy_rows[b], Ws2[at, :]).astype(BF).astype(F32)
            normal = 0.5 * (1.0 + lax.erf(hidden * 0.7071067811865476))
            r.act[b, :, at] = (hidden * normal).astype(BF)
            density = jnp.exp(-0.5 * hidden * hidden) * 0.3989422804014327
            grad_hidden = (grad_active * (normal + hidden * density)).astype(BF)
            r.dhid[b, :, at] = grad_hidden
            r.vexp[:, at] += jnp.sum(grad_hidden.astype(F32), 0, keepdims=True)

        tiles(start, stop, body)

    def hidden_back(b, earlier):
        sent_all(earlier[2])
        partial_sum(sb, b, lambda at: dot_nt(r.dhid[b], We[at, :]))
        return reduce_start(sb, rb, b)

    def finish_hidden(b, reduction):
        gradient = reduce_finish(reduction)
        normed, inverse = norm_parts(r.resid[b])
        dy_own = r.dy[b].astype(F32)
        total = dy_own + norm_backward(gradient, normed, inverse, vec_row(ROW_GAIN_TWO))
        r.dresid[b] = total
        r.drg[b, k] = total.astype(BF)
        gather = gather_start(r.drg.at[b, k], r.drg, b)
        add_row(ROW_GAIN_TWO, jnp.sum(gradient * normed, 0, keepdims=True))
        add_row(ROW_SHIFT_TWO, jnp.sum(gradient, 0, keepdims=True))
        add_row(ROW_BIAS_OUT, jnp.sum(total, 0, keepdims=True))
        add_row(ROW_BIAS_SHRINK, jnp.sum(dy_own, 0, keepdims=True))
        return gather

    def weight_gradient(count, lefts, rights, out):
        def body(at):
            total = dot_tn(lefts[0, :, at], rights[0])
            for b in range(1, micro):
                total = total + dot_tn(lefts[b, :, at], rights[b])
            out[at, :] = total.astype(BF)

        tiles(0, count // TILE, body)

    def mixed_gradient(b):
        @pl.loop(0, 2)
        def _(i):
            at = pl.ds(pl.multiple_of(i * half, half), half)
            out = dot_nt(dr_rows[b, at, :], Wo[...]).astype(BF)
            for h in range(OWN_HEADS):
                r.dmix[h, at, :] = out[:, h * HD:(h + 1) * HD]

    def attend_back(b, start, stop):
        @pl.loop(start, stop)
        def _(h):
            key_rows = r.kv[b, 0, h].reshape(keys, HD)
            value_rows = r.kv[b, 1, h].reshape(keys, HD)
            grad_keys = None
            grad_values = None
            for part in range(2):
                at = pl.ds(part * half, half)
                query_rows = r.q[b, h, at, :]
                mix_rows = r.dmix[h, at, :]
                probs = jnp.exp(masked_scores(b, key_rows, query_rows) - r.lse[b, h, :, at])
                grad_probs = dot_nt(value_rows, mix_rows)
                inner = jnp.sum(probs * grad_probs, 0, keepdims=True)
                grad_scores = (probs * (grad_probs - inner)).astype(BF)
                grad_query = dot_tn(key_rows, grad_scores) * SCALE
                r.dq[h, at, :] = grad_query.T.astype(BF)
                key_term = dot_nn(grad_scores, query_rows)
                value_term = dot_nn(probs.astype(BF), mix_rows)
                grad_keys = key_term if grad_keys is None else grad_keys + key_term
                grad_values = value_term if grad_values is None else grad_values + value_term
            r.kv[b, 0, h] = (grad_keys * SCALE).astype(BF).reshape(CORES, rows, HD)
            r.kv[b, 1, h] = grad_values.astype(BF).reshape(CORES, rows, HD)

    def swap_back(b):
        return [send(r.kv.at[b, :, :, 1 - e], r.dl.at[b], sibling)]

    def join_gradients(b, handles):
        recv_all(handles)

        @pl.loop(0, CHIPS)
        def _(i):
            at = pl.ds(pl.multiple_of(i * tok, tok), tok)
            pieces = [r.dq[h, at, :] for h in range(OWN_HEADS)]
            for part in range(2):
                for h in range(OWN_HEADS):
                    pair = r.kv[b, part, h, e, at, :].astype(F32) + r.dl[b, part, h, at, :].astype(F32)
                    pieces.append(pair.astype(BF))
            pieces.append(jnp.zeros((tok, QKV_WIDTH - 3 * OWN_FEATURES), BF))
            line = jnp.concatenate(pieces, 1)
            r.dqkv[b, at, :] = line
            r.vqkv[...] += jnp.sum(line.astype(F32), 0, keepdims=True)

    def input_start(b, earlier):
        sent_all(earlier[2])
        partial_sum(sb, b, lambda at: dot_nt(r.dqkv[b], Wq[at, :]))
        return reduce_start(sb, rb, b)

    def finish_input(b, reduction):
        gradient = reduce_finish(reduction)
        normed, inverse = norm_parts(r.x[b].astype(F32))
        back = norm_backward(gradient, normed, inverse, vec_row(ROW_GAIN_ONE))
        r.ig[b] = (r.dresid[b] + back).astype(BF)
        add_row(ROW_GAIN_ONE, jnp.sum(gradient * normed, 0, keepdims=True))
        add_row(ROW_SHIFT_ONE, jnp.sum(gradient, 0, keepdims=True))

    def finish_out(b, reduction):
        total = r.resid[b] + reduce_finish(reduction) + vec_row(ROW_BIAS_SHRINK)
        r.bo[b] = total.astype(BF)

    def sum_group(space, slots):
        return SimpleNamespace(space=space, slots=slots, right={}, left={})

    def add_passing(group, hops):
        space, slots = group.space, group.slots
        for side, held, i, slot in (
            (group.right, (c >= 1) & (c - 1 + hops < planes), c - 1 + hops, hops - 1),
            (group.left, (c <= planes - 2) & (c + 1 - hops >= 0), c + 1 - hops, 5 - hops),
        ):
            side[hops][0]()

            @pl.when(held)
            def _():
                space[i] = (space[i].astype(F32) + slots[slot][...].astype(F32)).astype(BF)

    def sum_step(group, hops):
        space, slots = group.space, group.slots
        if hops < planes - 1:
            add_passing(group, hops + 1)
        group.right[hops] = send_if(
            c + hops < planes, lambda: space.at[c + hops], lambda: slots[hops - 1], me + DEV_CLIP,
            (c >= 1) & (c - 1 + hops < planes), lambda: slots[hops - 1],
        )
        group.left[hops] = send_if(
            c - hops >= 0, lambda: space.at[c - hops], lambda: slots[5 - hops], me - DEV_CLIP,
            (c <= planes - 2) & (c + 1 - hops >= 0), lambda: slots[5 - hops],
        )

    def sum_finish(group, out):
        space, slots = group.space, group.slots
        out(space[c].astype(F32), False)
        for side, held, slot in ((group.right, c >= 1, 0), (group.left, c <= planes - 2, 4)):
            side[1][0]()

            @pl.when(held)
            def _():
                out(slots[slot][...].astype(F32), True)

    def to_blocks(ref):
        def put(total, more):
            for j in range(CHIPS):
                piece = total[j * share:(j + 1) * share]
                ref[j] = ref[j] + piece if more else piece

        return put

    def to_rows(ref):
        def put(total, more):
            ref[...] = ref[...] + total if more else total

        return put

    def sibling_add(handles, landing, fetched, out, mine):
        recv_all(handles)
        sent_all(handles)
        local(landing, fetched)()

        @pl.loop(0, planes)
        def _(i):
            out[i] = (mine(i).astype(F32) + fetched[i].astype(F32)).astype(BF)

    def free_slots(ready):
        for side, held, device in ((0, c >= 1, me - DEV_CLIP), (1, c <= planes - 2, me + DEV_CLIP)):

            @pl.when(held)
            def _():
                pl.semaphore_signal(
                    ready.at[1 - side], inc=1, device_id=(device,), device_id_type=pl.DeviceIdType.MESH
                )

    def await_slots(ready):
        for side, held in ((0, c >= 1), (1, c <= planes - 2)):

            @pl.when(held)
            def _():
                pl.semaphore_wait(ready.at[side], 1)

    resid, dresid = r.resid, r.dresid
    x_local = [local(r.x.at[b], r.xg.at[b, k]) for b in range(micro)]
    dy_local = [local(r.dy.at[b], r.dyg.at[b, k]) for b in range(micro)]
    x_gather = [None] * micro
    dy_gather = [None] * micro
    if fused:
        expand = [dresid.at[0, 0:share], dresid.at[0, share:2 * share], dresid.at[0, 2 * share:3 * share], dresid.at[1, 0:share]]
        first_rows = tok - share
        loads = [local(ref, resid.at[0, i * share:(i + 1) * share]) for i, ref in enumerate((r.wq, r.wk, r.wv))]
        loads.append(local(r.wo, resid.at[1, 0:share]))
        expand_loads = [local(r.we.at[:, i * width:(i + 1) * width], expand[i]) for i in range(planes)]
        expand_loads.append(local(r.ws.at[0:first_rows], resid.at[1, share:tok]))
        expand_loads.append(local(r.ws.at[first_rows:ff_share], dresid.at[1, share:ff_share - first_rows + share]))
        peers = [chip_peer(by) for by in (1, 2, 3)] + [sibling]
        if fused:
            peers += [plane_peer(by) for by in range(1, planes)]
        barrier = pltpu.get_barrier_semaphore()
        for peer in peers:
            pl.semaphore_signal(barrier, inc=1, device_id=(peer,), device_id_type=pl.DeviceIdType.MESH)
        for load in loads:
            load()
        matrices = [resid[0, i * share:(i + 1) * share] for i in range(3)]
        for j in range(CHIPS):
            pieces = [
                matrix[:, (i * CHIPS + j) * HD:(i * CHIPS + j + 1) * HD] for matrix in matrices for i in range(planes)
            ]
            pieces.append(jnp.zeros((share, QKV_WIDTH - 3 * OWN_FEATURES), F32))
            r.aq[j] = jnp.concatenate(pieces, 1).astype(BF)
        r.so[c] = resid[1, 0:share].astype(BF)
        compact = jnp.concatenate([jnp.pad(ref[...], ((0, 0), (0, 256 - share))) for ref in r.vectors], 0)
        tail = jnp.pad(r.expand_bias[...], ((0, 0), (0, 256 - ff_share)))
        pair = [jnp.pad(ref[...], ((0, 0), (0, 128 - share))) for ref in (r.query_bias, r.value_bias)]
        r.cv[c] = jnp.concatenate([compact, tail, jnp.concatenate(pair, 1)], 0)
        pl.semaphore_wait(barrier, len(peers))
        wq_mine, wq_other = stacked(r.drg, planes, QKV_WIDTH), stacked(r.a2g, planes, QKV_WIDTH)
        we_mine, we_other = stacked(r.act, planes, ff_own), stacked(r.dhid, planes, ff_own)
        line_q = line_group(lambda i: wq_mine.at[i], lambda i: wq_other.at[i])
        line_e = line_group(lambda i: we_mine.at[i], lambda i: we_other.at[i])
        line_o = line_group(lambda i: r.so.at[i], lambda i: r.oo.at[i])
        line_s = line_group(lambda i: Ws.at[i, e], lambda i: Ws.at[i, e])

        def pack_plane(blocks, out):
            out[c] = jnp.concatenate([blocks[j].astype(F32) for j in range(CHIPS)], 0).astype(BF)

        wq_plane = [send(r.aq.at[flipped(k, by)], r.alq.at[k], chip_peer(by)) for by in (3, 1, 2)]
        vec_z = [send(r.cv.at[c], r.cv.at[c], plane_peer(by)) for by in range(1, planes)]
        forward(line_o, 0)
        r.alq[k] = r.aq[k]
        recv_all(vec_z)
        r.cp[e, k] = r.cv[...]
        vec_p = [send(r.cv, r.cp.at[e, k], chip_peer(by)) for by in (1, 2, 3)]
        x_gather[0] = gather_start(r.x.at[0], r.xg, 0)
        recv_all(wq_plane)
        pack_plane(r.alq, wq_mine)
        forward(line_q, 0)
        for load in expand_loads:
            load()
        ff_part = width // planes
        for j in range(CHIPS):
            pieces = [block[:, j * ff_part:(j + 1) * ff_part] for block in expand]
            r.ae[j] = jnp.concatenate(pieces, 1).astype(BF)
        we_plane = [send(r.ae.at[flipped(k, by)], r.ale.at[k], chip_peer(by)) for by in (3, 1, 2)]
        r.ale[k] = r.ae[k]
        rows_s = [resid[1, share:tok], dresid[1, share:ff_share - first_rows + share]]
        Ws[c, e] = jnp.concatenate(rows_s, 0).astype(BF)
        recv_all(vec_p)
        vec_s = [send(r.cp.at[e], r.cp.at[e], sibling)]
        recv_all(vec_s)
        places = [(i, f) for i in range(planes) for f in range(CORES)]
        vfin[...] = jnp.concatenate(
            [r.cp[f, j, i][:, 0:share] for i in range(planes) for j in range(CHIPS) for f in range(CORES)], 1
        )
        r.be[...] = jnp.concatenate([r.cp[f, k, i][6:7, 0:ff_share] for i, f in places], 1)
        bias = [jnp.concatenate([r.cp[f, k, i][7:8, at:at + share] for i, f in places], 1) for at in (0, 128)]
        blank = jnp.zeros((1, OWN_FEATURES), F32)
        r.bq[...] = jnp.concatenate([bias[0], blank, bias[1], blank[:, :QKV_WIDTH - 3 * OWN_FEATURES]], 1)
        gather_relay(x_gather[0])
        x_gather[1] = gather_start(r.x.at[1], r.xg, 1)
        forward(line_o, 1)
        forward(line_q, 1)
        recv_all(we_plane)
        pack_plane(r.ale, we_mine)
    else:
        peers = [chip_peer(by) for by in (1, 2, 3)] + [sibling]
        if fused:
            peers += [plane_peer(by) for by in range(1, planes)]
        barrier = pltpu.get_barrier_semaphore()
        for peer in peers:
            pl.semaphore_signal(barrier, inc=1, device_id=(peer,), device_id_type=pl.DeviceIdType.MESH)
        pl.semaphore_wait(barrier, len(peers))
        loads = [local(r.wq, Wq), local(r.we, We), local(r.wo, Wo), local(r.ws, Ws2)]
        for b in range(micro):
            x_gather[b] = gather_start(r.x.at[b], r.xg, b)
        vfin[...] = r.vec[...]
        r.be[...] = r.vec[6:7, :]
        r.bq[...] = r.vec[7:8, :QKV_WIDTH]
        gather_relay(x_gather[0])
        for load in loads:
            load()
    for ref in (r.vrow, r.vexp, r.vqkv):
        ref[...] = jnp.zeros_like(ref)
    norm_one(0)
    if fused:
        forward(line_o, 2)
        forward(line_q, 2)
        forward(line_e, 0)
        forward(line_s, 0)
    gather_relay(x_gather[1])
    dy_gather[0] = gather_start(r.dy.at[0], r.dyg, 0)
    norm_one(1)
    if fused:
        forward(line_o, 3)
        forward(line_q, 3)
        recv_all(line_q.swaps)
        join_planes(wq_mine, wq_other, Wq)
    kv_swap = [None] * micro
    kv_swap[0] = project(0)
    gather_relay(dy_gather[0])
    dy_gather[1] = gather_start(r.dy.at[1], r.dyg, 1)
    kv_swap[1] = project(1)
    recv_all(kv_swap[0])
    attend(0, 0, OWN_HEADS)
    if fused:
        forward(line_e, 1)
    attend(0, OWN_HEADS, 2 * OWN_HEADS)
    if fused:
        recv_all(line_o.swaps)
        for i in range(planes):
            pair = join_rows(r.so[i].astype(F32), r.oo[i].astype(F32), 1)
            Wo[i * HD:(i + 1) * HD, :] = pair.astype(BF)
    mix_reduce = [mix_out(0), None]
    gather_relay(dy_gather[1])
    recv_all(kv_swap[1])
    attend(1, 0, OWN_HEADS)
    if fused:
        forward(line_s, 1)
    attend(1, OWN_HEADS, 2 * OWN_HEADS - 1)
    reduce_relay(mix_reduce[0])
    attend(1, 2 * OWN_HEADS - 1, 2 * OWN_HEADS)
    mix_reduce[1] = mix_out(1)
    if fused:
        forward(line_e, 2)
    second_gather = [norm_two(0, mix_reduce[0]), None]
    if fused:
        forward(line_s, 2)
    reduce_relay(mix_reduce[1])
    gather_relay(second_gather[0])
    second_gather[1] = norm_two(1, mix_reduce[1])
    if fused:
        forward(line_e, 3)
        recv_all(line_e.swaps)
        group_sent(line_e)
        group_sent(line_q)
        join_planes(we_mine, we_other, We)
    gather_finish(second_gather[0])
    dy_local[0]()
    gather_finish(dy_gather[0])
    if fused:
        forward(line_s, 3)
        recv_all(line_s.swaps)
    gather_relay(second_gather[1])
    feed(0, 0, ff_own // TILE)
    hidden_reduce = [hidden_back(0, mix_reduce[0]), None]
    gather_finish(second_gather[1])
    dy_local[1]()
    gather_finish(dy_gather[1])
    feed(1, 0, ff_own // TILE)
    reduce_relay(hidden_reduce[0])
    hidden_reduce[1] = hidden_back(1, mix_reduce[1])
    weight_gradient(width, a2_rows, r.dhid, We)
    resid_gather = [finish_hidden(0, hidden_reduce[0]), None]
    if fused:
        sent_all(wq_plane + we_plane)
        group_sent(line_o)
        group_sent(line_s)
        sent_all(second_gather[0][1] + second_gather[1][1])
        free_slots(r.ready_e)
        parts_e = We.reshape(planes, 2, chip_rows, ff_own)
        split_planes(We, parts_e.at[:, 0], parts_e.at[:, 1])
        ge_s = [send(parts_e.at[:, 1], r.Le, sibling)]
    partial_sum(sbo, 0, lambda at: dot_nn(r.act[0], Ws2[:, at]))
    if fused:
        sum_e = sum_group(parts_e.at[:, 0], [flat(r.a2g).at[i * chip_rows:(i + 1) * chip_rows] for i in range(5)])
        sibling_add(ge_s, r.Le, parts_e.at[:, 1], parts_e.at[:, 0], lambda i: parts_e[i, 0])
        await_slots(r.ready_e)
        sum_step(sum_e, 3)
    partial_sum(sbo, 1, lambda at: dot_nn(r.act[1], Ws2[:, at]))
    reduce_relay(hidden_reduce[1])
    weight_gradient(ff_own, r.act, dy_rows, Ws2)
    if fused:
        sent_all(dy_gather[0][1] + dy_gather[1][1])
        free_slots(r.ready_s)
        gs_s = [send(Ws.at[:, 1 - e], r.Ls, sibling)]
    gather_relay(resid_gather[0])
    if fused:
        places_s = [flat(r.a2g).at[5 * ff_share:6 * ff_share]]
        for ref in (r.dyg, r.act):
            places_s += [flat(ref).at[i * ff_share:(i + 1) * ff_share] for i in (4, 5)]
        sum_s = sum_group(Ws.at[:, e], places_s)
        sibling_add(gs_s, r.Ls, Ws.at[:, 1 - e], Ws.at[:, e], lambda i: Ws[i, e])
        await_slots(r.ready_s)
        sum_step(sum_s, 3)
    resid_gather[1] = finish_hidden(1, hidden_reduce[1])
    if fused:
        sum_step(sum_e, 2)
    gather_finish(resid_gather[0])
    mixed_gradient(0)
    sent_all(kv_swap[0] + kv_swap[1])
    attend_back(0, 0, 2)
    gather_relay(resid_gather[1])
    out_reduce = [reduce_start(sbo, rbo, 0), None]
    if fused:
        sum_step(sum_s, 2)
    attend_back(0, 2, OWN_HEADS)
    swap = swap_back(0)
    gather_finish(resid_gather[1])
    mixed_gradient(1)
    lead = dot_nn(mixed[0], dr_rows[0])
    for other in range(1, micro):
        lead = lead + dot_nn(mixed[other], dr_rows[other])
    if fused:
        space_o, other_o = r.so, r.oo
        for i in range(planes):
            mine, theirs = split_rows(lead[i * HD:(i + 1) * HD], 1)
            space_o[i] = mine.astype(BF)
            other_o[i] = theirs.astype(BF)
        go_s = [send(other_o, r.Lo, sibling)]
    else:
        Wo[...] = lead.astype(BF)
    join_gradients(0, swap)
    input_reduce = [input_start(0, hidden_reduce[0]), None]
    if fused:
        sum_step(sum_e, 1)
    attend_back(1, 0, 2)
    reduce_relay(out_reduce[0])
    if fused:
        sum_o = sum_group(space_o, [r.ao.at[i] for i in range(5)])
        sibling_add(go_s, r.Lo, other_o, space_o, lambda i: space_o[i])
        sum_step(sum_s, 1)
        sum_step(sum_o, 3)
    attend_back(1, 2, OWN_HEADS)
    swap = swap_back(1)
    reduce_relay(input_reduce[0])
    join_gradients(1, swap)
    input_reduce[1] = input_start(1, hidden_reduce[1])
    out_reduce[1] = reduce_start(sbo, rbo, 1)
    weight_gradient(width, a1_rows, r.dqkv, Wq)
    if fused:
        free_slots(r.ready_q)
        parts_q = Wq.reshape(planes, 2, chip_rows, QKV_WIDTH)
        split_planes(Wq, parts_q.at[:, 0], parts_q.at[:, 1])
        gq_s = [send(parts_q.at[:, 1], r.Lq, sibling)]
        sum_step(sum_o, 2)
        five = stacked(r.dhid, 5, QKV_WIDTH)
        sum_q = sum_group(parts_q.at[:, 0], [five.at[i] for i in range(5)])
    finish_input(0, input_reduce[0])
    if fused:
        sibling_add(gq_s, r.Lq, parts_q.at[:, 1], parts_q.at[:, 0], lambda i: parts_q[i, 0])
        await_slots(r.ready_q)
        sum_step(sum_q, 3)
    def vector_step(group, step, last):
        zero, one, two, from_z, from_plane, from_core = group
        if step == 0:
            return [send(zero, from_core, sibling)]
        if step == 1:
            one[...] = zero[...] + from_core[...]
            return [send(one, from_z.at[by - 1], plane_peer(by)) for by in range(1, planes)]
        if step == 2:
            total = one[...]
            for by in range(1, planes):
                total = total + from_z[by - 1]
            two[...] = total
            return [send(two, from_plane.at[by - 1], chip_peer(by)) for by in (1, 2, 3)]
        others = from_plane[0] + from_plane[1] + from_plane[2]
        shared = lax.broadcasted_iota(jnp.int32, others.shape, 0) < 6
        last[...] = two[...] + jnp.where(shared, others, 0.0)

    if fused:
        group_u = (r.u0, r.u1, r.u2, r.uz, r.up, r.us)
        group_t = (r.t0, r.t1, r.t2, r.tz, r.tp, r.ts)
    padded = jnp.concatenate([r.vqkv[...], jnp.zeros((1, width - QKV_WIDTH), F32)], 1)
    early = jnp.concatenate([r.vrow[0:6, :], r.vexp[...], padded], 0)
    if fused:
        r.u0[...] = early
        moved = vector_step(group_u, 0, None)
    finish_out(0, out_reduce[0])
    reduce_relay(input_reduce[1])
    if fused:
        recv_all(moved)
        moved = vector_step(group_u, 1, None)
        sum_finish(sum_s, to_rows(r.gs))
        sum_finish(sum_e, to_blocks(r.ge))
        for j in range(CHIPS):
            r.ae[j] = r.ge[j].astype(BF)
        sum_step(sum_o, 1)
    reduce_relay(out_reduce[1])
    if fused:
        ge_p = [send(r.ae.at[flipped(k, by)], r.ale.at[k], chip_peer(by)) for by in (3, 1, 2)]
        recv_all(moved)
        moved = vector_step(group_u, 2, None)
        sum_step(sum_q, 2)
    finish_input(1, input_reduce[1])
    finish_out(1, out_reduce[1])
    late = r.vrow[0:2, :]
    if fused:
        r.t0[...] = late
        moved_late = vector_step(group_t, 0, None)
        recv_all(moved)
        vector_step(group_u, 3, r.vo)
        recv_all(ge_p)
        for by in (1, 2, 3):
            r.ge[flipped(k, by)] = r.ale[flipped(k, by)].astype(F32)
        recv_all(moved_late)
        moved_late = vector_step(group_t, 1, None)
        sum_step(sum_q, 1)
        recv_all(moved_late)
        moved_late = vector_step(group_t, 2, None)
        sum_finish(sum_o, to_rows(r.go))
        recv_all(moved_late)
        vector_step(group_t, 3, r.vt)
        sum_finish(sum_q, to_blocks(r.gq))
        for j in range(CHIPS):
            r.aq[j] = r.gq[j].astype(BF)
        gq_p = [send(r.aq.at[flipped(k, by)], r.alq.at[k], chip_peer(by)) for by in (3, 1, 2)]
        recv_all(gq_p)
        for by in (1, 2, 3):
            r.gq[flipped(k, by)] = r.alq[flipped(k, by)].astype(F32)
    else:
        r.vo[...] = early
        r.vt[...] = late
        stores = [local(Wq, r.gq), local(We, r.ge), local(Wo, r.go), local(Ws2, r.gs)]
        for store in stores:
            store()
    for wait in pending:
        wait()


def run_block(fused, planes, x, dy, lengths, vectors, weights_in, share, ff_share):
    micro, tok, width = x.shape
    ff_own = width
    rows = CHIPS * tok
    vmem = pl.BlockSpec(memory_space=pltpu.VMEM)
    anywhere = pl.BlockSpec(memory_space=pl.ANY)
    smem = pl.BlockSpec(memory_space=pltpu.SMEM)

    def shape(*dims, dtype=BF):
        return jax.ShapeDtypeStruct(dims, dtype)

    outs = [
        (shape(micro, tok, width), vmem),
        (shape(micro, tok, width), vmem),
        (shape(8, width, dtype=F32), vmem),
        (shape(2, width, dtype=F32), vmem),
    ]
    if fused:
        outs += [
            (shape(CHIPS, share, QKV_WIDTH, dtype=F32), vmem),
            (shape(CHIPS, share, ff_own, dtype=F32), vmem),
            (shape(share, width, dtype=F32), vmem),
            (shape(ff_share, width, dtype=F32), vmem),
        ]
        outs += [
            (shape(planes, CHIPS * share, QKV_WIDTH), anywhere),
            (shape(planes, CHIPS * share, ff_own), anywhere),
            (shape(planes, share, width), anywhere),
            (shape(planes, ff_share, width), anywhere),
        ]
    else:
        outs += [
            (shape(width, QKV_WIDTH), anywhere),
            (shape(width, ff_own), anywhere),
            (shape(OWN_FEATURES, width), anywhere),
            (shape(ff_own, width), anywhere),
        ]
    if fused:
        weights = [
            pltpu.VMEM((width, QKV_WIDTH), BF),
            pltpu.VMEM((width, ff_own), BF),
            pltpu.VMEM((OWN_FEATURES, width), BF),
            pltpu.VMEM((planes, CORES, ff_share, width), BF),
        ]
    else:
        weights = [
            pltpu.VMEM((width, QKV_WIDTH), BF),
            pltpu.VMEM((width, ff_own), BF),
            pltpu.VMEM((OWN_FEATURES, width), BF),
            pltpu.VMEM((ff_own, width), BF),
        ]
    scratch = weights + [
        pltpu.VMEM((micro, CHIPS, tok, width), BF),
        pltpu.VMEM((micro, CHIPS, tok, width), BF),
        pltpu.VMEM((micro, CHIPS, tok, width), BF),
        pltpu.VMEM((micro, CHIPS, tok, width), BF),
        pltpu.VMEM((micro, rows, ff_own), BF),
        pltpu.VMEM((micro, rows, ff_own), BF),
        pltpu.VMEM((micro, OWN_HEADS, rows, HD), BF),
        pltpu.VMEM((micro, 2, OWN_HEADS, CORES, rows, HD), BF),
        pltpu.VMEM((micro, OWN_HEADS, HD, rows), BF),
        pltpu.VMEM((micro, OWN_HEADS, 1, rows), F32),
        pltpu.VMEM((OWN_HEADS, rows, HD), BF),
        pltpu.VMEM((OWN_HEADS, rows, HD), BF),
        pltpu.VMEM((micro, 2, OWN_HEADS, rows, HD), BF),
        pltpu.VMEM((micro, CHIPS, tok, width), BF),
        pltpu.VMEM((micro, CHIPS, tok, width), BF),
        pltpu.VMEM((micro, CHIPS - 1, tok, width), BF),
        pltpu.VMEM((micro, CHIPS - 1, tok, width), BF),
        pltpu.VMEM((micro, tok, width), F32),
        pltpu.VMEM((micro, tok, width), F32),
        pltpu.VMEM((8, width), F32),
        pltpu.VMEM((1, ff_own), F32),
        pltpu.VMEM((1, QKV_WIDTH), F32),
        pltpu.VMEM((1, ff_own), F32),
        pltpu.VMEM((1, QKV_WIDTH), F32),
        pltpu.VMEM((8, width), F32),
    ]
    if fused:
        scratch += [
            pltpu.VMEM((planes, share, width), BF),
            pltpu.VMEM((planes, share, width), BF),
            pltpu.VMEM((5, share, width), BF),
            pltpu.VMEM((CHIPS, share, QKV_WIDTH), BF),
            pltpu.VMEM((CHIPS, share, ff_own), BF),
            pltpu.VMEM((CHIPS, share, QKV_WIDTH), BF),
            pltpu.VMEM((CHIPS, share, ff_own), BF),
        ]
        scratch += [
            pltpu.VMEM((planes, 8, 256), F32),
            pltpu.VMEM((CORES, CHIPS, planes, 8, 256), F32),
        ]
        for lines in (8, 2):
            scratch += [pltpu.VMEM((lines, width), F32) for _ in range(3)]
            scratch += [pltpu.VMEM((planes - 1, lines, width), F32), pltpu.VMEM((CHIPS - 1, lines, width), F32)]
            scratch.append(pltpu.VMEM((lines, width), F32))
        scratch += [pltpu.SemaphoreType.REGULAR((2,)) for _ in range(3)]
    scratch += [
        pltpu.SemaphoreType.DMA((SEMS,)),
        pltpu.SemaphoreType.DMA((SEMS,)),
        pltpu.SemaphoreType.DMA((LOCAL_SEMS,)),
    ]
    return pl.pallas_call(
        partial(block_kernel, fused, planes, micro, tok, width, ff_own, share, ff_share),
        out_shape=[out for out, _ in outs],
        in_specs=[vmem, vmem, smem] + [vmem] * len(vectors) + [anywhere] * len(weights_in),
        out_specs=[spec for _, spec in outs],
        scratch_shapes=scratch,
        compiler_params=pltpu.CompilerParams(
            collective_id=0, has_side_effects=True, vmem_limit_bytes=63 * 1000 * 1000
        ),
    )(x, dy, lengths, *vectors, *weights_in)


def finish_kernel(planes, share, ff_share, bo, ig, vo, vt, gq, ge, go, gs, *refs):
    device = lax.axis_index("fsdp")
    c, _, e = place(device)
    outs, (blocks_q, blocks_e, lines, last_lines, sems) = refs[:17], refs[17:]
    moves = [(vo, lines), (vt, last_lines), (gq, blocks_q), (ge, blocks_e)]
    moves += [(bo, outs[0]), (ig, outs[1]), (go, outs[6]), (gs, outs[7])]
    copies = [pltpu.make_async_copy(src, dst, sems.at[i]) for i, (src, dst) in enumerate(moves)]
    for copy in copies:
        copy.start()
    for copy in copies[:4]:
        copy.wait()
    part = ge.shape[2] // planes
    for n in range(planes):
        for j in range(CHIPS):
            at = (n * CHIPS + j) * part
            outs[5][:, at:at + part] = blocks_e[j][:, n * part:(n + 1) * part]
    for i, out in enumerate(outs[2:5]):
        first = i * OWN_FEATURES
        out[...] = jnp.concatenate(
            [blocks_q[j][:, first + n * HD:first + (n + 1) * HD] for n in range(planes) for j in range(CHIPS)], 1
        )
    vo, vt = lines, last_lines
    width = vo.shape[1]

    def own(lines, start, size):
        lane = lax.broadcasted_iota(jnp.int32, (width, size), 0)
        pick = (lane == start + lax.broadcasted_iota(jnp.int32, (width, size), 1)).astype(F32)
        return lax.dot_general(
            lines, pick, (((1,), (0,)), ((), ())), precision=lax.Precision.HIGHEST, preferred_element_type=F32
        )

    early, late = own(vo[...], device * share, share), own(vt[...], device * share, share)
    expand = own(vo[...], (2 * c + e) * ff_share, ff_share)
    query = own(vo[...], (2 * c + e) * share, share)
    value = own(vo[...], 2 * OWN_FEATURES + (2 * c + e) * share, share)
    for out, line in zip(
        outs[8:],
        [late[0:1], late[1:2]] + [early[i:i + 1] for i in range(2, 6)] + [expand[6:7], query[7:8], value[7:8]],
        strict=True,
    ):
        out[...] = line
    for copy in copies[4:]:
        copy.wait()


def finish_block(planes, share, ff_share, results):
    shapes = [results[0], results[1]] + [jax.ShapeDtypeStruct((share, results[2].shape[1]), F32)] * 3
    shapes += [jax.ShapeDtypeStruct((share, CHIPS * results[5].shape[2]), F32), results[6], results[7]]
    shapes = [jax.ShapeDtypeStruct(s.shape, s.dtype) for s in shapes]
    shapes += [jax.ShapeDtypeStruct((1, share), F32)] * 6
    shapes += [jax.ShapeDtypeStruct((1, size), F32) for size in (ff_share, share, share)]
    vmem = pl.BlockSpec(memory_space=pltpu.VMEM)
    anywhere = pl.BlockSpec(memory_space=pl.ANY)
    held = [results[4], results[5], results[2], results[3]]
    return pl.pallas_call(
        partial(finish_kernel, planes, share, ff_share),
        out_shape=shapes,
        in_specs=[anywhere] * 8,
        out_specs=[vmem] * 17,
        scratch_shapes=[pltpu.VMEM(a.shape, a.dtype) for a in held] + [pltpu.SemaphoreType.DMA((8,))],
        compiler_params=pltpu.CompilerParams(vmem_limit_bytes=60 * 1000 * 1000),
    )(*results)


def by_chip(matrix, part):
    rows = matrix.shape[0]
    return matrix.reshape(rows, -1, CHIPS, part).transpose(2, 0, 1, 3).reshape(CHIPS, rows, -1)


def from_chips(blocks, part):
    rows = blocks.shape[1]
    return blocks.reshape(CHIPS, rows, -1, part).transpose(1, 2, 0, 3).reshape(rows, -1)


def body(
    inputs, cotangent, lengths, first_gain, first_shift, query_weight, query_bias, key_weight,
    value_weight, value_bias, output_weight, output_bias, second_gain, second_shift,
    expand_weight, expand_bias, shrink_weight, shrink_bias,
):
    device = lax.axis_index("fsdp")
    count = lax.axis_size("fsdp")
    c, k, e = place(device)
    planes = count // DEV_CLIP
    width = inputs.shape[2]
    share = query_weight.shape[0]
    ff_share = shrink_weight.shape[0]
    ff_part = width // 4
    fused = planes == 4 and share * 2 == HD and ff_share * 2 == ff_part
    plain = (first_gain, first_shift, second_gain, second_shift, output_bias, shrink_bias)
    matrices = (query_weight, key_weight, value_weight, expand_weight, output_weight, shrink_weight)
    if fused:
        vectors = [v.reshape(1, -1) for v in plain + (expand_bias, query_bias, value_bias)]
        got = run_block(True, planes, inputs, cotangent, lengths, vectors, matrices, share, ff_share)
        done = finish_block(planes, share, ff_share, got[:8])
        block_out, input_grad, grad_query_w, grad_key_w, grad_value_w, grad_expand_w, grad_output_w, grad_shrink_w = done[:8]
        owned = [line[0] for line in done[8:14]]
        grad_expand_b, grad_query_b, grad_value_b = (line[0] for line in done[14:])
    else:

        def whole(array):
            return lax.all_gather(array, "fsdp", axis=0, tiled=True)

        def mine(blocks):
            return lax.dynamic_index_in_dim(blocks, k, 0, keepdims=False)

        full = [whole(w.astype(BF)) for w in matrices]
        pieces = [mine(by_chip(w, HD)) for w in full[:3]]
        pieces.append(jnp.zeros((width, QKV_WIDTH - 3 * OWN_FEATURES), BF))
        wq = jnp.concatenate(pieces, 1)
        we = mine(by_chip(full[3], ff_part))
        wo = mine(by_chip(full[4].T, HD)).T
        ws = mine(by_chip(full[5].T, ff_part)).T
        bias_e = mine(by_chip(whole(expand_bias)[None], ff_part))
        bias_q = mine(by_chip(whole(query_bias)[None], HD))
        bias_v = mine(by_chip(whole(value_bias)[None], HD))
        blank = jnp.zeros((1, width - 3 * OWN_FEATURES), F32)
        bias_row = jnp.concatenate([bias_q, jnp.zeros_like(bias_q), bias_v, blank], 1)
        vec = jnp.concatenate([jnp.stack([whole(v) for v in plain]), bias_e, bias_row])
        got = run_block(False, planes, inputs, cotangent, lengths, (vec,), (wq, we, wo, ws), share, ff_share)
        block_out, input_grad, sums, late, gq, ge, go, gs = got[:8]

        def spread(block, part):
            places = lax.broadcasted_iota(jnp.int32, (CHIPS, 1, 1), 0) == k
            return from_chips(jnp.where(places, block.astype(F32)[None], 0.0), part)

        def owned_sum(array):
            return lax.psum_scatter(array, "fsdp", scatter_dimension=0, tiled=True)

        grad_query_w, grad_key_w, grad_value_w = (
            owned_sum(spread(gq[:, i * OWN_FEATURES:(i + 1) * OWN_FEATURES], HD)) for i in range(3)
        )
        grad_expand_w = owned_sum(spread(ge, ff_part))
        grad_output_w = owned_sum(spread(go.T, HD).T)
        grad_shrink_w = owned_sum(spread(gs.T, ff_part).T)
        owned = [owned_sum(late[i]) for i in range(2)] + [owned_sum(sums[i]) for i in range(2, len(plain))]
        line_q, line_v = sums[7:8, :OWN_FEATURES], sums[7:8, 2 * OWN_FEATURES:3 * OWN_FEATURES]
        grad_expand_b = owned_sum(spread(sums[6:7], ff_part)[0])
        grad_query_b = owned_sum(spread(line_q, HD)[0])
        grad_value_b = owned_sum(spread(line_v, HD)[0])
    return (
        block_out,
        input_grad,
        owned[0],
        owned[1],
        grad_query_w,
        grad_query_b,
        grad_key_w,
        grad_value_w,
        grad_value_b,
        grad_output_w,
        owned[4],
        owned[2],
        owned[3],
        grad_expand_w,
        grad_expand_b,
        grad_shrink_w,
        owned[5],
    )


def solution(mesh):
    rows, matrix, vector = P(None, "fsdp", None), P("fsdp", None), P("fsdp")
    in_specs = (
        rows, rows, P(), vector, vector, matrix, vector, matrix, matrix, vector, matrix, vector,
        vector, vector, matrix, vector, matrix, vector,
    )
    out_specs = (
        rows, rows, vector, vector, matrix, vector, matrix, matrix, vector, matrix, vector,
        vector, vector, matrix, vector, matrix, vector,
    )
    return jax.shard_map(body, mesh=mesh, in_specs=in_specs, out_specs=out_specs, check_vma=False)
```

```python
from functools import partial
from types import SimpleNamespace

import jax
import jax.numpy as jnp
from jax import lax
from jax.experimental import pallas as pl
from jax.experimental.pallas import tpu as pltpu
from jax.sharding import PartitionSpec as P

H = 16
HD = 80
CHIPS = 4
CORES = 2
DEV_CLIP = CHIPS * CORES
OWN_HEADS = H // CHIPS
OWN_FEATURES = OWN_HEADS * HD
QKV_WIDTH = 1024
TILE = 256
ROW_GAIN_ONE, ROW_SHIFT_ONE, ROW_GAIN_TWO, ROW_SHIFT_TWO, ROW_BIAS_OUT, ROW_BIAS_SHRINK = range(6)

EPS = 1e-05
NEG = -1000000000.0
SCALE = HD ** (-0.5)
BF = jnp.bfloat16
F32 = jnp.float32


def dot_nn(left, right):
    return lax.dot_general(left, right, (((1,), (0,)), ((), ())), preferred_element_type=F32)


def dot_nt(left, right):
    return lax.dot_general(left, right, (((1,), (1,)), ((), ())), preferred_element_type=F32)


def dot_tn(left, right):
    return lax.dot_general(left, right, (((0,), (0,)), ((), ())), preferred_element_type=F32)


def norm_parts(rows):
    mean = jnp.mean(rows, -1, keepdims=True)
    centered = rows - mean
    inverse = lax.rsqrt(jnp.mean(centered * centered, -1, keepdims=True) + EPS)
    return centered * inverse, inverse


def norm_backward(gradient, normed, inverse, gain):
    scaled = gradient * gain
    return inverse * (
        scaled
        - jnp.mean(scaled, -1, keepdims=True)
        - normed * jnp.mean(scaled * normed, -1, keepdims=True)
    )


def place(device):
    return device // DEV_CLIP, (device % DEV_CLIP) // CORES, device % CORES


def flipped(number, by):
    low, high = number % 2, number // 2
    if by & 1:
        low = 1 - low
    if by & 2:
        high = 1 - high
    return high * 2 + low


SEND_SEMS, RECV_SEMS, LOCAL_SEMS = 104, 217, 18


def block_kernel(fused, planes, micro, tok, width, ff_own, share, ff_share, *refs):
    names = ["x", "dy", "lengths"]
    if fused:
        names += ["av", "bv", "cv_", "dv", "ev", "fv"] + ["expand_bias", "query_bias", "value_bias", "wq", "wk", "wv", "we", "wo", "ws"]
    else:
        names += ["vec", "wq", "we", "wo", "ws"]
    names += ["bo", "ig", "vo", "vt", "gq", "ge", "go", "gs"]
    if fused:
        names += ["Lq", "Le", "Lo", "Ls"]
    names += ["Wq", "We", "Wo", "Ws", "xg", "dyg", "a2g", "drg", "act", "dhid"]
    names += ["q", "kv", "mixed", "lse", "dmix", "dq", "dl"]
    names += ["sb", "sbo", "rb", "rbo", "resid", "dresid", "vfin", "be", "bq", "vexp", "vqkv", "vrow"]
    if fused:
        names += ["so", "oo", "ao", "aq", "ae", "alq", "ale", "cv", "cp"]
        names += [letter + end for letter in "ut" for end in ("0", "1", "2", "z", "p", "s")]
        names += ["ready_e", "ready_s", "ready_q"]
    names += ["ssem", "rsem", "lsem"]
    r = SimpleNamespace(**dict(zip(names, refs, strict=True)))
    if fused:
        r.vectors = (r.av, r.bv, r.cv_, r.dv, r.ev, r.fv)
    r.dqkv = r.dhid.at[:, :, 0:QKV_WIDTH]
    me = lax.axis_index("fsdp")
    c, k, e = place(me)
    rows = CHIPS * tok

    def chip_peer(by):
        return c * DEV_CLIP + flipped(k, by) * CORES + e

    sibling = c * DEV_CLIP + k * CORES + (1 - e)

    def plane_peer(by):
        return flipped(c, by) * DEV_CLIP + k * CORES + e

    counters = SimpleNamespace(remote=0, local=0, sends=0, free=[])
    pending = []

    def send_semaphore():
        if counters.free:
            return counters.free.pop()
        counters.sends += 1
        return counters.sends - 1

    def flush(count=None):
        for wait in pending[:len(pending) - (count or 0)]:
            wait()

    def send(src, dst, device):
        i = counters.remote
        counters.remote += 1
        out = send_semaphore()
        copy = pltpu.make_async_remote_copy(
            src_ref=src, dst_ref=dst, send_sem=r.ssem.at[out], recv_sem=r.rsem.at[i],
            device_id=(device,), device_id_type=pl.DeviceIdType.MESH,
        )
        copy.start()
        state = SimpleNamespace(sent=False)

        def wait_send():
            if not state.sent:
                state.sent = True
                counters.free.append(out)
                copy.wait_send()

        copy_handle = (copy.wait_recv, wait_send)
        pending.append(wait_send)
        return copy_handle

    def send_if(held, src, dst, device, due, arriving):
        i = counters.remote
        counters.remote += 1
        out = send_semaphore()

        def copy(source, target, to):
            return pltpu.make_async_remote_copy(
                src_ref=source, dst_ref=target, send_sem=r.ssem.at[out], recv_sem=r.rsem.at[i],
                device_id=(to,), device_id_type=pl.DeviceIdType.MESH,
            )

        @pl.when(held)
        def _():
            copy(src(), dst(), device).start()

        state = SimpleNamespace(sent=False)

        def wait_send():
            if not state.sent:
                state.sent = True
                counters.free.append(out)

                @pl.when(held)
                def _():
                    copy(src(), dst(), device).wait_send()

        def wait_recv():
            @pl.when(due)
            def _():
                copy(arriving(), arriving(), sibling).wait_recv()

        copy_handle = (wait_recv, wait_send)
        pending.append(wait_send)
        return copy_handle

    def line_group(mine, theirs):
        return SimpleNamespace(mine=mine, theirs=theirs, steps=[], swaps=[])

    def forward(group, step):
        mine, theirs = group.mine, group.theirs
        if step > 0:
            recv_all(group.steps[step - 1])
        if step < planes - 1:
            n = step + 1
            group.steps.append([
                send_if(
                    (c >= n - 1) & (c < planes - 1), lambda: mine(c - n + 1), lambda: mine(c - n + 1),
                    me + DEV_CLIP, c >= n, lambda: mine(c - n),
                ),
                send_if(
                    (c + n - 1 < planes) & (c >= 1), lambda: mine(c + n - 1), lambda: mine(c + n - 1),
                    me - DEV_CLIP, c + n < planes, lambda: mine(c + n),
                ),
            ])
        if step == 0:
            group.swaps.append(send(mine(c), theirs(c), sibling))
        else:
            for held, i in ((c >= step, c - step), (c + step < planes, c + step)):
                group.swaps.append(
                    send_if(
                        held, lambda i=i: mine(i), lambda i=i: theirs(i), sibling, held, lambda i=i: theirs(i)
                    )
                )

    def group_sent(group):
        sent_all(sum(group.steps, []) + group.swaps)

    def local(src, dst):
        i = counters.local
        counters.local += 1
        copy = pltpu.make_async_copy(src, dst, r.lsem.at[i])
        copy.start()
        return copy.wait

    def recv_all(handles):
        for handle in handles:
            handle[0]()

    def sent_all(handles):
        for handle in handles:
            handle[1]()

    Wq, We, Wo, Ws = r.Wq, r.We, r.Wo, r.Ws
    Ws2 = Ws.reshape(ff_own, width)

    def flat(ref):
        return ref.reshape(micro * rows, width)

    chip_rows = CHIPS * share
    plane_rows = CORES * chip_rows
    chip_halves = (slice(0, chip_rows // 2), slice(chip_rows // 2, chip_rows))

    def stacked(ref, count, lanes):
        return flat(ref).at[0:count * chip_rows].reshape(count, chip_rows, width).at[:, :, 0:lanes]

    def by_core(own, other):
        return jnp.where(e == 0, own, other), jnp.where(e == 0, other, own)

    def join_rows(own, other, count):
        first, second = by_core(own, other)
        pieces = []
        for j in range(count):
            pieces += [first[j * share:(j + 1) * share], second[j * share:(j + 1) * share]]
        return jnp.concatenate(pieces, 0)

    def split_rows(block, count):
        pieces = [block[j * share:(j + 1) * share] for j in range(2 * count)]
        return by_core(jnp.concatenate(pieces[0::2], 0), jnp.concatenate(pieces[1::2], 0))

    def join_planes(own, other, out):
        @pl.loop(0, planes)
        def _(i):
            block = join_rows(own[i].astype(F32), other[i].astype(F32), CHIPS)
            out[pl.ds(pl.multiple_of(i * plane_rows, plane_rows), plane_rows), :] = block.astype(BF)

    def split_planes(grads, own, other):
        @pl.loop(0, planes)
        def _(i):
            block = grads[pl.ds(pl.multiple_of(i * plane_rows, plane_rows), plane_rows), :].astype(F32)
            mine, theirs = split_rows(block, CHIPS)
            own[i] = mine.astype(BF)
            other[i] = theirs.astype(BF)

    k_x, k_y, k_far = flipped(k, 1), flipped(k, 2), flipped(k, 3)
    x_peer, y_peer, far_peer = chip_peer(1), chip_peer(2), chip_peer(3)
    top, low = slice(0, tok // 2), slice(tok // 2, tok)

    def gather_start(src, dst, b):
        return [dst.at[b], [send(src, dst.at[b, k], x_peer), send(src, dst.at[b, k], y_peer)]]

    def gather_relay(gather):
        dst, handles = gather
        handles[0][0]()
        handles.append(send(dst.at[k_x, top], dst.at[k_x, top], y_peer))
        handles[1][0]()
        handles.append(send(dst.at[k_y, low], dst.at[k_y, low], x_peer))

    def gather_finish(gather):
        recv_all(gather[1][2:])

    def reduce_start(slots, landing, b):
        slots, landing = slots.at[b], landing.at[b]
        return [slots, landing, [
            send(slots.at[k_far, top], landing.at[2, top], x_peer),
            send(slots.at[k_far, low], landing.at[2, low], y_peer),
            send(slots.at[k_x, top], landing.at[0, top], x_peer),
            send(slots.at[k_y, low], landing.at[1, low], y_peer),
        ]]

    def reduce_relay(reduction):
        slots, landing, handles = reduction
        handles[0][0]()
        slots[k_y, top] = (slots[k_y, top].astype(F32) + landing[2, top].astype(F32)).astype(BF)
        handles.append(send(slots.at[k_y, top], landing.at[1, top], y_peer))
        handles[1][0]()
        slots[k_x, low] = (slots[k_x, low].astype(F32) + landing[2, low].astype(F32)).astype(BF)
        handles.append(send(slots.at[k_x, low], landing.at[0, low], x_peer))

    def reduce_finish(reduction):
        slots, landing, handles = reduction
        recv_all(handles[2:])
        return slots[k].astype(F32) + landing[0].astype(F32) + landing[1].astype(F32)

    sb, sbo, rb, rbo = r.sb, r.sbo, r.rb, r.rbo
    vfin = r.vfin

    def vec_row(index):
        return vfin[index:index + 1, :]

    def add_row(index, value):
        r.vrow[index:index + 1, :] += value

    def norm_one(b):
        x_local[b]()
        gather_finish(x_gather[b])
        sent_all(x_gather[b][1])

        @pl.loop(0, CHIPS)
        def _(i):
            normed, _inverse = norm_parts(r.xg[b, i].astype(F32))
            r.xg[b, i] = (normed * vec_row(ROW_GAIN_ONE) + vec_row(ROW_SHIFT_ONE)).astype(BF)

    a1_rows = r.xg.reshape(micro, rows, width)
    a2_rows = r.a2g.reshape(micro, rows, width)
    dy_rows = r.dyg.reshape(micro, rows, width)
    dr_rows = r.drg.reshape(micro, rows, width)
    half = rows // 2

    def project(b):
        @pl.loop(0, 2)
        def _(i):
            at = pl.ds(pl.multiple_of(i * half, half), half)
            out = (dot_nn(a1_rows[b, at, :], Wq[...]) + r.bq[...]).astype(BF)
            for h in range(OWN_HEADS):
                r.q[b, h, at, :] = out[:, h * HD:(h + 1) * HD]
                for part in range(2):
                    low = (part + 1) * OWN_FEATURES + h * HD
                    r.kv[b, part, h, e, at, :] = out[:, low:low + HD]

        return [send(r.kv.at[b, :, :, e], r.kv.at[b, :, :, e], sibling)]

    keys = CORES * rows
    chunk_places = [(2 * (i % CHIPS) + i // CHIPS) * tok for i in range(DEV_CLIP)]

    def masked_scores(b, key_rows, query_rows):
        raw = dot_nt(key_rows, query_rows)
        index = lax.broadcasted_iota(jnp.int32, (tok, raw.shape[1]), 0)
        length = r.lengths[b, c]
        return jnp.concatenate(
            [
                raw[i * tok:(i + 1) * tok] * SCALE
                if first + tok <= keys // 2
                else jnp.where(index < length - first, raw[i * tok:(i + 1) * tok] * SCALE, NEG)
                for i, first in enumerate(chunk_places)
            ],
            0,
        )

    def attend(b, start, stop):
        @pl.loop(start, stop)
        def _(step):
            h, part = step // 2, step % 2
            at = pl.ds(pl.multiple_of(part * half, half), half)
            key_rows = r.kv[b, 0, h].reshape(keys, HD)
            value_rows = r.kv[b, 1, h].reshape(keys, HD)
            scores = masked_scores(b, key_rows, r.q[b, h, at, :])
            peak = jnp.max(scores, 0, keepdims=True)
            exponent = jnp.exp(scores - peak)
            sums = jnp.sum(exponent, 0, keepdims=True)
            probs = (exponent * (1.0 / sums)).astype(BF)
            r.lse[b, h, :, at] = peak + jnp.log(sums)
            r.mixed[b, h, :, at] = dot_tn(value_rows, probs).astype(BF)

    def tiles(start, stop, body):
        for i in range(start, stop):
            body(pl.ds(i * TILE, TILE))

    def partial_sum(slots, b, product):
        view = slots.reshape(micro, rows, width)

        def body(at):
            view[b, :, at] = product(at).astype(BF)

        tiles(0, width // TILE, body)

    mixed = r.mixed.reshape(micro, OWN_FEATURES, rows)

    def mix_out(b):
        partial_sum(sb, b, lambda at: dot_tn(mixed[b], Wo[:, at]))
        return reduce_start(sb, rb, b)

    def norm_two(b, reduction):
        residual = r.x[b].astype(F32) + reduce_finish(reduction) + vec_row(ROW_BIAS_OUT)
        r.resid[b] = residual
        normed, _inverse = norm_parts(residual)
        r.a2g[b, k] = (normed * vec_row(ROW_GAIN_TWO) + vec_row(ROW_SHIFT_TWO)).astype(BF)
        return gather_start(r.a2g.at[b, k], r.a2g, b)

    def feed(b, start, stop):
        def body(at):
            hidden = dot_nn(a2_rows[b], We[:, at]) + r.be[:, at]
            grad_active = dot_nt(dy_rows[b], Ws2[at, :]).astype(BF).astype(F32)
            normal = 0.5 * (1.0 + lax.erf(hidden * 0.7071067811865476))
            r.act[b, :, at] = (hidden * normal).astype(BF)
            density = jnp.exp(-0.5 * hidden * hidden) * 0.3989422804014327
            grad_hidden = (grad_active * (normal + hidden * density)).astype(BF)
            r.dhid[b, :, at] = grad_hidden
            r.vexp[:, at] += jnp.sum(grad_hidden.astype(F32), 0, keepdims=True)

        tiles(start, stop, body)

    def hidden_back(b, earlier):
        sent_all(earlier[2])
        partial_sum(sb, b, lambda at: dot_nt(r.dhid[b], We[at, :]))
        return reduce_start(sb, rb, b)

    def finish_hidden(b, reduction):
        gradient = reduce_finish(reduction)
        normed, inverse = norm_parts(r.resid[b])
        dy_own = r.dy[b].astype(F32)
        total = dy_own + norm_backward(gradient, normed, inverse, vec_row(ROW_GAIN_TWO))
        r.dresid[b] = total
        r.drg[b, k] = total.astype(BF)
        gather = gather_start(r.drg.at[b, k], r.drg, b)
        add_row(ROW_GAIN_TWO, jnp.sum(gradient * normed, 0, keepdims=True))
        add_row(ROW_SHIFT_TWO, jnp.sum(gradient, 0, keepdims=True))
        add_row(ROW_BIAS_OUT, jnp.sum(total, 0, keepdims=True))
        add_row(ROW_BIAS_SHRINK, jnp.sum(dy_own, 0, keepdims=True))
        return gather

    def weight_gradient(count, lefts, rights, out):
        def body(at):
            total = dot_tn(lefts[0, :, at], rights[0])
            for b in range(1, micro):
                total = total + dot_tn(lefts[b, :, at], rights[b])
            out[at, :] = total.astype(BF)

        tiles(0, count // TILE, body)

    def mixed_gradient(b):
        @pl.loop(0, 2)
        def _(i):
            at = pl.ds(pl.multiple_of(i * half, half), half)
            out = dot_nt(dr_rows[b, at, :], Wo[...]).astype(BF)
            for h in range(OWN_HEADS):
                r.dmix[h, at, :] = out[:, h * HD:(h + 1) * HD]

    def attend_back(b, start, stop):
        @pl.loop(start, stop)
        def _(h):
            key_rows = r.kv[b, 0, h].reshape(keys, HD)
            value_rows = r.kv[b, 1, h].reshape(keys, HD)
            grad_keys = None
            grad_values = None
            for part in range(2):
                at = pl.ds(part * half, half)
                query_rows = r.q[b, h, at, :]
                mix_rows = r.dmix[h, at, :]
                probs = jnp.exp(masked_scores(b, key_rows, query_rows) - r.lse[b, h, :, at])
                grad_probs = dot_nt(value_rows, mix_rows)
                inner = jnp.sum(probs * grad_probs, 0, keepdims=True)
                grad_scores = (probs * (grad_probs - inner)).astype(BF)
                grad_query = dot_tn(key_rows, grad_scores) * SCALE
                r.dq[h, at, :] = grad_query.T.astype(BF)
                key_term = dot_nn(grad_scores, query_rows)
                value_term = dot_nn(probs.astype(BF), mix_rows)
                grad_keys = key_term if grad_keys is None else grad_keys + key_term
                grad_values = value_term if grad_values is None else grad_values + value_term
            r.kv[b, 0, h] = (grad_keys * SCALE).astype(BF).reshape(CORES, rows, HD)
            r.kv[b, 1, h] = grad_values.astype(BF).reshape(CORES, rows, HD)

    def swap_back(b, start, stop):
        return [send(r.kv.at[b, :, start:stop, 1 - e], r.dl.at[b, :, start:stop], sibling)]

    def join_gradients(b, handles):
        recv_all(handles)

        @pl.loop(0, CHIPS)
        def _(i):
            at = pl.ds(pl.multiple_of(i * tok, tok), tok)
            pieces = [r.dq[h, at, :] for h in range(OWN_HEADS)]
            for part in range(2):
                for h in range(OWN_HEADS):
                    pair = r.kv[b, part, h, e, at, :].astype(F32) + r.dl[b, part, h, at, :].astype(F32)
                    pieces.append(pair.astype(BF))
            pieces.append(jnp.zeros((tok, QKV_WIDTH - 3 * OWN_FEATURES), BF))
            line = jnp.concatenate(pieces, 1)
            r.dqkv[b, at, :] = line
            r.vqkv[...] += jnp.sum(line.astype(F32), 0, keepdims=True)

    def input_start(b, earlier):
        sent_all(earlier[2])
        partial_sum(sb, b, lambda at: dot_nt(r.dqkv[b], Wq[at, :]))
        return reduce_start(sb, rb, b)

    def finish_input(b, reduction):
        gradient = reduce_finish(reduction)
        normed, inverse = norm_parts(r.x[b].astype(F32))
        back = norm_backward(gradient, normed, inverse, vec_row(ROW_GAIN_ONE))
        r.ig[b] = (r.dresid[b] + back).astype(BF)
        add_row(ROW_GAIN_ONE, jnp.sum(gradient * normed, 0, keepdims=True))
        add_row(ROW_SHIFT_ONE, jnp.sum(gradient, 0, keepdims=True))

    def finish_out(b, reduction):
        total = r.resid[b] + reduce_finish(reduction) + vec_row(ROW_BIAS_SHRINK)
        r.bo[b] = total.astype(BF)

    def sum_group(space, slots):
        return SimpleNamespace(space=space, slots=slots, right={}, left={})

    def add_passing(group, hops):
        space, slots = group.space, group.slots
        for side, held, i, slot in (
            (group.right, (c >= 1) & (c - 1 + hops < planes), c - 1 + hops, hops - 1),
            (group.left, (c <= planes - 2) & (c + 1 - hops >= 0), c + 1 - hops, 5 - hops),
        ):
            side[hops][0]()

            @pl.when(held)
            def _():
                space[i] = (space[i].astype(F32) + slots[slot][...].astype(F32)).astype(BF)

    def sum_step(group, hops):
        space, slots = group.space, group.slots
        if hops < planes - 1:
            add_passing(group, hops + 1)
        group.right[hops] = send_if(
            c + hops < planes, lambda: space.at[c + hops], lambda: slots[hops - 1], me + DEV_CLIP,
            (c >= 1) & (c - 1 + hops < planes), lambda: slots[hops - 1],
        )
        group.left[hops] = send_if(
            c - hops >= 0, lambda: space.at[c - hops], lambda: slots[5 - hops], me - DEV_CLIP,
            (c <= planes - 2) & (c + 1 - hops >= 0), lambda: slots[5 - hops],
        )

    def sum_finish(group, out):
        space, slots = group.space, group.slots
        out(space[c].astype(F32), False)
        for side, held, slot in ((group.right, c >= 1, 0), (group.left, c <= planes - 2, 4)):
            side[1][0]()

            @pl.when(held)
            def _():
                out(slots[slot][...].astype(F32), True)

    def to_blocks(ref, first):
        def put(total, more):
            for j in range(total.shape[0] // share):
                piece = total[j * share:(j + 1) * share]
                ref[first + j] = ref[first + j] + piece if more else piece

        return put

    def to_rows(ref):
        def put(total, more):
            ref[...] = ref[...] + total if more else total

        return put

    def sibling_add(handles, landing, fetched, out, mine):
        recv_all(handles)
        sent_all(handles)
        local(landing, fetched)()

        @pl.loop(0, planes)
        def _(i):
            out[i] = (mine(i).astype(F32) + fetched[i].astype(F32)).astype(BF)

    def free_slots(ready):
        for side, held, device in ((0, c >= 1, me - DEV_CLIP), (1, c <= planes - 2, me + DEV_CLIP)):

            @pl.when(held)
            def _():
                pl.semaphore_signal(
                    ready.at[1 - side], inc=1, device_id=(device,), device_id_type=pl.DeviceIdType.MESH
                )

    def await_slots(ready):
        for side, held in ((0, c >= 1), (1, c <= planes - 2)):

            @pl.when(held)
            def _():
                pl.semaphore_wait(ready.at[side], 1)

    resid, dresid = r.resid, r.dresid
    x_local = [local(r.x.at[b], r.xg.at[b, k]) for b in range(micro)]
    dy_local = [local(r.dy.at[b], r.dyg.at[b, k]) for b in range(micro)]
    x_gather = [None] * micro
    dy_gather = [None] * micro
    if fused:
        expand = [dresid.at[0, 0:share], dresid.at[0, share:2 * share], dresid.at[0, 2 * share:3 * share], dresid.at[1, 0:share]]
        first_rows = tok - share
        loads = [local(ref, resid.at[0, i * share:(i + 1) * share]) for i, ref in enumerate((r.wq, r.wk, r.wv))]
        loads.append(local(r.wo, resid.at[1, 0:share]))
        expand_loads = [local(r.we.at[:, i * width:(i + 1) * width], expand[i]) for i in range(planes)]
        expand_loads.append(local(r.ws.at[0:first_rows], resid.at[1, share:tok]))
        expand_loads.append(local(r.ws.at[first_rows:ff_share], dresid.at[1, share:ff_share - first_rows + share]))
        peers = [chip_peer(by) for by in (1, 2, 3)] + [sibling]
        if fused:
            peers += [plane_peer(by) for by in range(1, planes)]
        barrier = pltpu.get_barrier_semaphore()
        for peer in peers:
            pl.semaphore_signal(barrier, inc=1, device_id=(peer,), device_id_type=pl.DeviceIdType.MESH)
        for load in loads:
            load()
        matrices = [resid[0, i * share:(i + 1) * share] for i in range(3)]
        for j in range(CHIPS):
            pieces = [
                matrix[:, (i * CHIPS + j) * HD:(i * CHIPS + j + 1) * HD] for matrix in matrices for i in range(planes)
            ]
            pieces.append(jnp.zeros((share, QKV_WIDTH - 3 * OWN_FEATURES), F32))
            r.aq[j] = jnp.concatenate(pieces, 1).astype(BF)
        r.so[c] = resid[1, 0:share].astype(BF)
        compact = jnp.concatenate([jnp.pad(ref[...], ((0, 0), (0, 256 - share))) for ref in r.vectors], 0)
        tail = jnp.pad(r.expand_bias[...], ((0, 0), (0, 256 - ff_share)))
        pair = [jnp.pad(ref[...], ((0, 0), (0, 128 - share))) for ref in (r.query_bias, r.value_bias)]
        r.cv[c] = jnp.concatenate([compact, tail, jnp.concatenate(pair, 1)], 0)
        pl.semaphore_wait(barrier, len(peers))
        wq_mine, wq_other = stacked(r.drg, planes, QKV_WIDTH), stacked(r.a2g, planes, QKV_WIDTH)
        we_mine, we_other = stacked(r.act, planes, ff_own), stacked(r.dhid, planes, ff_own)
        lines_q = [
            line_group(lambda i, at=at: wq_mine.at[i, at], lambda i, at=at: wq_other.at[i, at]) for at in chip_halves
        ]
        line_e = line_group(lambda i: we_mine.at[i], lambda i: we_other.at[i])
        line_o = line_group(lambda i: r.so.at[i], lambda i: r.oo.at[i])
        line_s = line_group(lambda i: Ws.at[i, e], lambda i: Ws.at[i, e])

        def pack_plane(blocks, out):
            out[c] = jnp.concatenate([blocks[j].astype(F32) for j in range(CHIPS)], 0).astype(BF)

        wq_plane = [send(r.aq.at[flipped(k, by)], r.alq.at[k], chip_peer(by)) for by in (3, 1, 2)]
        vec_z = [send(r.cv.at[c], r.cv.at[c], plane_peer(by)) for by in range(1, planes)]
        forward(line_o, 0)
        r.alq[k] = r.aq[k]
        recv_all(vec_z)
        r.cp[e, k] = r.cv[...]
        vec_p = [send(r.cv, r.cp.at[e, k], chip_peer(by)) for by in (1, 2, 3)]
        x_gather[0] = gather_start(r.x.at[0], r.xg, 0)
        recv_all(wq_plane)
        pack_plane(r.alq, wq_mine)
        for line in lines_q:
            forward(line, 0)
        for load in expand_loads:
            load()
        ff_part = width // planes
        for j in range(CHIPS):
            pieces = [block[:, j * ff_part:(j + 1) * ff_part] for block in expand]
            r.ae[j] = jnp.concatenate(pieces, 1).astype(BF)
        we_plane = [send(r.ae.at[flipped(k, by)], r.ale.at[k], chip_peer(by)) for by in (3, 1, 2)]
        r.ale[k] = r.ae[k]
        rows_s = [resid[1, share:tok], dresid[1, share:ff_share - first_rows + share]]
        Ws[c, e] = jnp.concatenate(rows_s, 0).astype(BF)
        recv_all(vec_p)
        vec_s = [send(r.cp.at[e], r.cp.at[e], sibling)]
        recv_all(vec_s)
        places = [(i, f) for i in range(planes) for f in range(CORES)]
        vfin[...] = jnp.concatenate(
            [r.cp[f, j, i][:, 0:share] for i in range(planes) for j in range(CHIPS) for f in range(CORES)], 1
        )
        r.be[...] = jnp.concatenate([r.cp[f, k, i][6:7, 0:ff_share] for i, f in places], 1)
        bias = [jnp.concatenate([r.cp[f, k, i][7:8, at:at + share] for i, f in places], 1) for at in (0, 128)]
        blank = jnp.zeros((1, OWN_FEATURES), F32)
        r.bq[...] = jnp.concatenate([bias[0], blank, bias[1], blank[:, :QKV_WIDTH - 3 * OWN_FEATURES]], 1)
        gather_relay(x_gather[0])
        x_gather[1] = gather_start(r.x.at[1], r.xg, 1)
        forward(line_o, 1)
        for line in lines_q:
            forward(line, 1)
        recv_all(we_plane)
        pack_plane(r.ale, we_mine)
    else:
        peers = [chip_peer(by) for by in (1, 2, 3)] + [sibling]
        if fused:
            peers += [plane_peer(by) for by in range(1, planes)]
        barrier = pltpu.get_barrier_semaphore()
        for peer in peers:
            pl.semaphore_signal(barrier, inc=1, device_id=(peer,), device_id_type=pl.DeviceIdType.MESH)
        pl.semaphore_wait(barrier, len(peers))
        loads = [local(r.wq, Wq), local(r.we, We), local(r.wo, Wo), local(r.ws, Ws2)]
        for b in range(micro):
            x_gather[b] = gather_start(r.x.at[b], r.xg, b)
        vfin[...] = r.vec[...]
        r.be[...] = r.vec[6:7, :]
        r.bq[...] = r.vec[7:8, :QKV_WIDTH]
        gather_relay(x_gather[0])
        for load in loads:
            load()
    for ref in (r.vrow, r.vexp, r.vqkv):
        ref[...] = jnp.zeros_like(ref)
    norm_one(0)
    if fused:
        forward(line_o, 2)
        for line in lines_q:
            forward(line, 2)
        forward(line_e, 0)
        forward(line_s, 0)
    gather_relay(x_gather[1])
    dy_gather[0] = gather_start(r.dy.at[0], r.dyg, 0)
    norm_one(1)
    if fused:
        forward(line_o, 3)
        for line in lines_q:
            forward(line, 3)
        for line in lines_q:
            recv_all(line.swaps)
        join_planes(wq_mine, wq_other, Wq)
    kv_swap = [None] * micro
    kv_swap[0] = project(0)
    gather_relay(dy_gather[0])
    dy_gather[1] = gather_start(r.dy.at[1], r.dyg, 1)
    kv_swap[1] = project(1)
    recv_all(kv_swap[0])
    attend(0, 0, OWN_HEADS)
    if fused:
        forward(line_e, 1)
    attend(0, OWN_HEADS, 2 * OWN_HEADS)
    if fused:
        recv_all(line_o.swaps)
        for i in range(planes):
            pair = join_rows(r.so[i].astype(F32), r.oo[i].astype(F32), 1)
            Wo[i * HD:(i + 1) * HD, :] = pair.astype(BF)
    mix_reduce = [mix_out(0), None]
    gather_relay(dy_gather[1])
    recv_all(kv_swap[1])
    attend(1, 0, OWN_HEADS)
    if fused:
        forward(line_s, 1)
    attend(1, OWN_HEADS, 2 * OWN_HEADS - 1)
    reduce_relay(mix_reduce[0])
    attend(1, 2 * OWN_HEADS - 1, 2 * OWN_HEADS)
    mix_reduce[1] = mix_out(1)
    if fused:
        forward(line_e, 2)
    second_gather = [norm_two(0, mix_reduce[0]), None]
    if fused:
        forward(line_s, 2)
    reduce_relay(mix_reduce[1])
    gather_relay(second_gather[0])
    second_gather[1] = norm_two(1, mix_reduce[1])
    if fused:
        forward(line_e, 3)
        recv_all(line_e.swaps)
        group_sent(line_e)
        for line in lines_q:
            group_sent(line)
        join_planes(we_mine, we_other, We)
    gather_finish(second_gather[0])
    dy_local[0]()
    gather_finish(dy_gather[0])
    if fused:
        forward(line_s, 3)
        recv_all(line_s.swaps)
    flush(20)
    feed(0, 0, 3)
    gather_relay(second_gather[1])
    feed(0, 3, ff_own // TILE)
    hidden_reduce = [hidden_back(0, mix_reduce[0]), None]
    gather_finish(second_gather[1])
    dy_local[1]()
    gather_finish(dy_gather[1])
    feed(1, 0, ff_own // TILE)
    reduce_relay(hidden_reduce[0])
    hidden_reduce[1] = hidden_back(1, mix_reduce[1])
    weight_gradient(width, a2_rows, r.dhid, We)
    resid_gather = [finish_hidden(0, hidden_reduce[0]), None]
    if fused:
        sent_all(wq_plane + we_plane)
        group_sent(line_o)
        group_sent(line_s)
        sent_all(second_gather[0][1] + second_gather[1][1])
        free_slots(r.ready_e)
        parts_e = We.reshape(planes, 2, chip_rows, ff_own)
        split_planes(We, parts_e.at[:, 0], parts_e.at[:, 1])
        ge_s = [send(parts_e.at[:, 1], r.Le, sibling)]
    partial_sum(sbo, 0, lambda at: dot_nn(r.act[0], Ws2[:, at]))
    if fused:
        sum_e = sum_group(parts_e.at[:, 0], [flat(r.a2g).at[i * chip_rows:(i + 1) * chip_rows] for i in range(5)])
        sibling_add(ge_s, r.Le, parts_e.at[:, 1], parts_e.at[:, 0], lambda i: parts_e[i, 0])
        await_slots(r.ready_e)
        sum_step(sum_e, 3)
    partial_sum(sbo, 1, lambda at: dot_nn(r.act[1], Ws2[:, at]))
    reduce_relay(hidden_reduce[1])
    weight_gradient(ff_own, r.act, dy_rows, Ws2)
    if fused:
        sent_all(dy_gather[0][1] + dy_gather[1][1])
        free_slots(r.ready_s)
        gs_s = [send(Ws.at[:, 1 - e], r.Ls, sibling)]
    gather_relay(resid_gather[0])
    if fused:
        places_s = [flat(r.a2g).at[5 * ff_share:6 * ff_share]]
        for ref in (r.dyg, r.act):
            places_s += [flat(ref).at[i * ff_share:(i + 1) * ff_share] for i in (4, 5)]
        sum_s = sum_group(Ws.at[:, e], places_s)
        sibling_add(gs_s, r.Ls, Ws.at[:, 1 - e], Ws.at[:, e], lambda i: Ws[i, e])
        await_slots(r.ready_s)
        sum_step(sum_s, 3)
    resid_gather[1] = finish_hidden(1, hidden_reduce[1])
    if fused:
        sum_step(sum_e, 2)
    flush(20)
    gather_finish(resid_gather[0])
    mixed_gradient(0)
    sent_all(kv_swap[0] + kv_swap[1])
    attend_back(0, 0, 2)
    gather_relay(resid_gather[1])
    out_reduce = [reduce_start(sbo, rbo, 0), None]
    if fused:
        sum_step(sum_s, 2)
    attend_back(0, 2, OWN_HEADS)
    swap = swap_back(0, 0, OWN_HEADS)
    gather_finish(resid_gather[1])
    mixed_gradient(1)
    lead = dot_nn(mixed[0], dr_rows[0])
    for other in range(1, micro):
        lead = lead + dot_nn(mixed[other], dr_rows[other])
    if fused:
        space_o, other_o = r.so, r.oo
        for i in range(planes):
            mine, theirs = split_rows(lead[i * HD:(i + 1) * HD], 1)
            space_o[i] = mine.astype(BF)
            other_o[i] = theirs.astype(BF)
        go_s = [send(other_o, r.Lo, sibling)]
    else:
        Wo[...] = lead.astype(BF)
    join_gradients(0, swap)
    input_reduce = [input_start(0, hidden_reduce[0]), None]
    if fused:
        sum_step(sum_e, 1)
    attend_back(1, 0, 2)
    last_swap = swap_back(1, 0, 2)
    reduce_relay(out_reduce[0])
    if fused:
        sum_o = sum_group(space_o, [r.ao.at[i] for i in range(5)])
        sibling_add(go_s, r.Lo, other_o, space_o, lambda i: space_o[i])
        sum_step(sum_s, 1)
        sum_step(sum_o, 3)
    attend_back(1, 2, OWN_HEADS)
    last_swap += swap_back(1, 2, OWN_HEADS)
    reduce_relay(input_reduce[0])
    join_gradients(1, last_swap)
    input_reduce[1] = input_start(1, hidden_reduce[1])
    weight_gradient(width, a1_rows, r.dqkv, Wq)
    flush(20)
    if fused:
        free_slots(r.ready_q)
        parts_q = Wq.reshape(planes, 2, chip_rows, QKV_WIDTH)
        split_planes(Wq, parts_q.at[:, 0], parts_q.at[:, 1])
        gq_s = [send(parts_q.at[:, 1], r.Lq, sibling)]
        sum_step(sum_o, 2)
        five = stacked(r.dhid, 5, QKV_WIDTH)
        sums_q = [sum_group(parts_q.at[:, 0, at], [five.at[i, at] for i in range(5)]) for at in chip_halves]
    finish_input(0, input_reduce[0])
    if fused:
        sibling_add(gq_s, r.Lq, parts_q.at[:, 1], parts_q.at[:, 0], lambda i: parts_q[i, 0])
        await_slots(r.ready_q)
        for group in sums_q:
            sum_step(group, 3)
    def vector_step(group, step, last):
        zero, one, two, from_z, from_plane, from_core = group
        if step == 0:
            return [send(zero, from_core, sibling)]
        if step == 1:
            one[...] = zero[...] + from_core[...]
            return [send(one, from_z.at[by - 1], plane_peer(by)) for by in range(1, planes)]
        if step == 2:
            total = one[...]
            for by in range(1, planes):
                total = total + from_z[by - 1]
            two[...] = total
            return [send(two, from_plane.at[by - 1], chip_peer(by)) for by in (1, 2, 3)]
        others = from_plane[0] + from_plane[1] + from_plane[2]
        shared = lax.broadcasted_iota(jnp.int32, others.shape, 0) < 6
        last[...] = two[...] + jnp.where(shared, others, 0.0)

    if fused:
        group_u = (r.u0, r.u1, r.u2, r.uz, r.up, r.us)
        group_t = (r.t0, r.t1, r.t2, r.tz, r.tp, r.ts)
    padded = jnp.concatenate([r.vqkv[...], jnp.zeros((1, width - QKV_WIDTH), F32)], 1)
    early = jnp.concatenate([r.vrow[0:6, :], r.vexp[...], padded], 0)
    if fused:
        r.u0[...] = early
        moved = vector_step(group_u, 0, None)
    reduce_relay(input_reduce[1])
    out_reduce[1] = reduce_start(sbo, rbo, 1)
    finish_out(0, out_reduce[0])
    if fused:
        recv_all(moved)
        moved = vector_step(group_u, 1, None)
        sum_finish(sum_s, to_rows(r.gs))
        sum_finish(sum_e, to_blocks(r.ge, 0))
        for j in range(CHIPS):
            r.ae[j] = r.ge[j].astype(BF)
        sum_step(sum_o, 1)
    if fused:
        ge_p = [send(r.ae.at[flipped(k, by)], r.ale.at[k], chip_peer(by)) for by in (3, 1, 2)]
        recv_all(moved)
        moved = vector_step(group_u, 2, None)
        for group in sums_q:
            sum_step(group, 2)
    finish_input(1, input_reduce[1])
    late = r.vrow[0:2, :]
    if fused:
        r.t0[...] = late
        moved_late = vector_step(group_t, 0, None)
    reduce_relay(out_reduce[1])
    if fused:
        recv_all(moved)
        vector_step(group_u, 3, r.vo)
        recv_all(ge_p)
        for by in (1, 2, 3):
            r.ge[flipped(k, by)] = r.ale[flipped(k, by)].astype(F32)
        recv_all(moved_late)
        moved_late = vector_step(group_t, 1, None)
        for group in sums_q:
            sum_step(group, 1)
        recv_all(moved_late)
        moved_late = vector_step(group_t, 2, None)
        sum_finish(sum_o, to_rows(r.go))
        recv_all(moved_late)
        vector_step(group_t, 3, r.vt)
    finish_out(1, out_reduce[1])
    if fused:
        for i, group in enumerate(sums_q):
            sum_finish(group, to_blocks(r.gq, i * CHIPS // 2))
        for j in range(CHIPS):
            r.aq[j] = r.gq[j].astype(BF)
        gq_p = [send(r.aq.at[flipped(k, by)], r.alq.at[k], chip_peer(by)) for by in (3, 1, 2)]
        recv_all(gq_p)
        for by in (1, 2, 3):
            r.gq[flipped(k, by)] = r.alq[flipped(k, by)].astype(F32)
    else:
        r.vo[...] = early
        r.vt[...] = late
        stores = [local(Wq, r.gq), local(We, r.ge), local(Wo, r.go), local(Ws2, r.gs)]
        for store in stores:
            store()
    flush()


def run_block(fused, planes, x, dy, lengths, vectors, weights_in, share, ff_share):
    micro, tok, width = x.shape
    ff_own = width
    rows = CHIPS * tok
    vmem = pl.BlockSpec(memory_space=pltpu.VMEM)
    anywhere = pl.BlockSpec(memory_space=pl.ANY)
    smem = pl.BlockSpec(memory_space=pltpu.SMEM)

    def shape(*dims, dtype=BF):
        return jax.ShapeDtypeStruct(dims, dtype)

    outs = [
        (shape(micro, tok, width), vmem),
        (shape(micro, tok, width), vmem),
        (shape(8, width, dtype=F32), vmem),
        (shape(2, width, dtype=F32), vmem),
    ]
    if fused:
        outs += [
            (shape(CHIPS, share, QKV_WIDTH, dtype=F32), vmem),
            (shape(CHIPS, share, ff_own, dtype=F32), vmem),
            (shape(share, width, dtype=F32), vmem),
            (shape(ff_share, width, dtype=F32), vmem),
        ]
        outs += [
            (shape(planes, CHIPS * share, QKV_WIDTH), anywhere),
            (shape(planes, CHIPS * share, ff_own), anywhere),
            (shape(planes, share, width), anywhere),
            (shape(planes, ff_share, width), anywhere),
        ]
    else:
        outs += [
            (shape(width, QKV_WIDTH), anywhere),
            (shape(width, ff_own), anywhere),
            (shape(OWN_FEATURES, width), anywhere),
            (shape(ff_own, width), anywhere),
        ]
    if fused:
        weights = [
            pltpu.VMEM((width, QKV_WIDTH), BF),
            pltpu.VMEM((width, ff_own), BF),
            pltpu.VMEM((OWN_FEATURES, width), BF),
            pltpu.VMEM((planes, CORES, ff_share, width), BF),
        ]
    else:
        weights = [
            pltpu.VMEM((width, QKV_WIDTH), BF),
            pltpu.VMEM((width, ff_own), BF),
            pltpu.VMEM((OWN_FEATURES, width), BF),
            pltpu.VMEM((ff_own, width), BF),
        ]
    scratch = weights + [
        pltpu.VMEM((micro, CHIPS, tok, width), BF),
        pltpu.VMEM((micro, CHIPS, tok, width), BF),
        pltpu.VMEM((micro, CHIPS, tok, width), BF),
        pltpu.VMEM((micro, CHIPS, tok, width), BF),
        pltpu.VMEM((micro, rows, ff_own), BF),
        pltpu.VMEM((micro, rows, ff_own), BF),
        pltpu.VMEM((micro, OWN_HEADS, rows, HD), BF),
        pltpu.VMEM((micro, 2, OWN_HEADS, CORES, rows, HD), BF),
        pltpu.VMEM((micro, OWN_HEADS, HD, rows), BF),
        pltpu.VMEM((micro, OWN_HEADS, 1, rows), F32),
        pltpu.VMEM((OWN_HEADS, rows, HD), BF),
        pltpu.VMEM((OWN_HEADS, rows, HD), BF),
        pltpu.VMEM((micro, 2, OWN_HEADS, rows, HD), BF),
        pltpu.VMEM((micro, CHIPS, tok, width), BF),
        pltpu.VMEM((micro, CHIPS, tok, width), BF),
        pltpu.VMEM((micro, CHIPS - 1, tok, width), BF),
        pltpu.VMEM((micro, CHIPS - 1, tok, width), BF),
        pltpu.VMEM((micro, tok, width), F32),
        pltpu.VMEM((micro, tok, width), F32),
        pltpu.VMEM((8, width), F32),
        pltpu.VMEM((1, ff_own), F32),
        pltpu.VMEM((1, QKV_WIDTH), F32),
        pltpu.VMEM((1, ff_own), F32),
        pltpu.VMEM((1, QKV_WIDTH), F32),
        pltpu.VMEM((8, width), F32),
    ]
    if fused:
        scratch += [
            pltpu.VMEM((planes, share, width), BF),
            pltpu.VMEM((planes, share, width), BF),
            pltpu.VMEM((5, share, width), BF),
            pltpu.VMEM((CHIPS, share, QKV_WIDTH), BF),
            pltpu.VMEM((CHIPS, share, ff_own), BF),
            pltpu.VMEM((CHIPS, share, QKV_WIDTH), BF),
            pltpu.VMEM((CHIPS, share, ff_own), BF),
        ]
        scratch += [
            pltpu.VMEM((planes, 8, 256), F32),
            pltpu.VMEM((CORES, CHIPS, planes, 8, 256), F32),
        ]
        for lines in (8, 2):
            scratch += [pltpu.VMEM((lines, width), F32) for _ in range(3)]
            scratch += [pltpu.VMEM((planes - 1, lines, width), F32), pltpu.VMEM((CHIPS - 1, lines, width), F32)]
            scratch.append(pltpu.VMEM((lines, width), F32))
        scratch += [pltpu.SemaphoreType.REGULAR((2,)) for _ in range(3)]
    scratch += [
        pltpu.SemaphoreType.DMA((SEND_SEMS,)),
        pltpu.SemaphoreType.DMA((RECV_SEMS,)),
        pltpu.SemaphoreType.DMA((LOCAL_SEMS,)),
    ]
    return pl.pallas_call(
        partial(block_kernel, fused, planes, micro, tok, width, ff_own, share, ff_share),
        out_shape=[out for out, _ in outs],
        in_specs=[vmem, vmem, smem] + [vmem] * len(vectors) + [anywhere] * len(weights_in),
        out_specs=[spec for _, spec in outs],
        scratch_shapes=scratch,
        compiler_params=pltpu.CompilerParams(
            collective_id=0, has_side_effects=True, vmem_limit_bytes=63 * 1000 * 1000
        ),
    )(x, dy, lengths, *vectors, *weights_in)


def finish_kernel(planes, share, ff_share, bo, ig, vo, vt, gq, ge, go, gs, *refs):
    device = lax.axis_index("fsdp")
    c, _, e = place(device)
    outs, (blocks_q, blocks_e, lines, last_lines, sems) = refs[:17], refs[17:]
    moves = [(vo, lines), (vt, last_lines), (gq, blocks_q), (ge, blocks_e)]
    moves += [(bo, outs[0]), (ig, outs[1]), (go, outs[6]), (gs, outs[7])]
    copies = [pltpu.make_async_copy(src, dst, sems.at[i]) for i, (src, dst) in enumerate(moves)]
    for copy in copies:
        copy.start()
    for copy in copies[:4]:
        copy.wait()
    part = ge.shape[2] // planes
    for n in range(planes):
        for j in range(CHIPS):
            at = (n * CHIPS + j) * part
            outs[5][:, at:at + part] = blocks_e[j][:, n * part:(n + 1) * part]
    for i, out in enumerate(outs[2:5]):
        first = i * OWN_FEATURES
        out[...] = jnp.concatenate(
            [blocks_q[j][:, first + n * HD:first + (n + 1) * HD] for n in range(planes) for j in range(CHIPS)], 1
        )
    vo, vt = lines, last_lines
    width = vo.shape[1]

    def own(lines, start, size):
        lane = lax.broadcasted_iota(jnp.int32, (width, size), 0)
        pick = (lane == start + lax.broadcasted_iota(jnp.int32, (width, size), 1)).astype(F32)
        return lax.dot_general(
            lines, pick, (((1,), (0,)), ((), ())), precision=lax.Precision.HIGHEST, preferred_element_type=F32
        )

    early, late = own(vo[...], device * share, share), own(vt[...], device * share, share)
    expand = own(vo[...], (2 * c + e) * ff_share, ff_share)
    query = own(vo[...], (2 * c + e) * share, share)
    value = own(vo[...], 2 * OWN_FEATURES + (2 * c + e) * share, share)
    for out, line in zip(
        outs[8:],
        [late[0:1], late[1:2]] + [early[i:i + 1] for i in range(2, 6)] + [expand[6:7], query[7:8], value[7:8]],
        strict=True,
    ):
        out[...] = line
    for copy in copies[4:]:
        copy.wait()


def finish_block(planes, share, ff_share, results):
    shapes = [results[0], results[1]] + [jax.ShapeDtypeStruct((share, results[2].shape[1]), F32)] * 3
    shapes += [jax.ShapeDtypeStruct((share, CHIPS * results[5].shape[2]), F32), results[6], results[7]]
    shapes = [jax.ShapeDtypeStruct(s.shape, s.dtype) for s in shapes]
    shapes += [jax.ShapeDtypeStruct((1, share), F32)] * 6
    shapes += [jax.ShapeDtypeStruct((1, size), F32) for size in (ff_share, share, share)]
    vmem = pl.BlockSpec(memory_space=pltpu.VMEM)
    anywhere = pl.BlockSpec(memory_space=pl.ANY)
    held = [results[4], results[5], results[2], results[3]]
    return pl.pallas_call(
        partial(finish_kernel, planes, share, ff_share),
        out_shape=shapes,
        in_specs=[anywhere] * 8,
        out_specs=[vmem] * 17,
        scratch_shapes=[pltpu.VMEM(a.shape, a.dtype) for a in held] + [pltpu.SemaphoreType.DMA((8,))],
        compiler_params=pltpu.CompilerParams(vmem_limit_bytes=60 * 1000 * 1000),
    )(*results)


def by_chip(matrix, part):
    rows = matrix.shape[0]
    return matrix.reshape(rows, -1, CHIPS, part).transpose(2, 0, 1, 3).reshape(CHIPS, rows, -1)


def from_chips(blocks, part):
    rows = blocks.shape[1]
    return blocks.reshape(CHIPS, rows, -1, part).transpose(1, 2, 0, 3).reshape(rows, -1)


def body(
    inputs, cotangent, lengths, first_gain, first_shift, query_weight, query_bias, key_weight,
    value_weight, value_bias, output_weight, output_bias, second_gain, second_shift,
    expand_weight, expand_bias, shrink_weight, shrink_bias,
):
    device = lax.axis_index("fsdp")
    count = lax.axis_size("fsdp")
    c, k, e = place(device)
    planes = count // DEV_CLIP
    width = inputs.shape[2]
    share = query_weight.shape[0]
    ff_share = shrink_weight.shape[0]
    ff_part = width // 4
    fused = planes == 4 and share * 2 == HD and ff_share * 2 == ff_part
    plain = (first_gain, first_shift, second_gain, second_shift, output_bias, shrink_bias)
    matrices = (query_weight, key_weight, value_weight, expand_weight, output_weight, shrink_weight)
    if fused:
        vectors = [v.reshape(1, -1) for v in plain + (expand_bias, query_bias, value_bias)]
        got = run_block(True, planes, inputs, cotangent, lengths, vectors, matrices, share, ff_share)
        done = finish_block(planes, share, ff_share, got[:8])
        block_out, input_grad, grad_query_w, grad_key_w, grad_value_w, grad_expand_w, grad_output_w, grad_shrink_w = done[:8]
        owned = [line[0] for line in done[8:14]]
        grad_expand_b, grad_query_b, grad_value_b = (line[0] for line in done[14:])
    else:

        def whole(array):
            return lax.all_gather(array, "fsdp", axis=0, tiled=True)

        def mine(blocks):
            return lax.dynamic_index_in_dim(blocks, k, 0, keepdims=False)

        full = [whole(w.astype(BF)) for w in matrices]
        pieces = [mine(by_chip(w, HD)) for w in full[:3]]
        pieces.append(jnp.zeros((width, QKV_WIDTH - 3 * OWN_FEATURES), BF))
        wq = jnp.concatenate(pieces, 1)
        we = mine(by_chip(full[3], ff_part))
        wo = mine(by_chip(full[4].T, HD)).T
        ws = mine(by_chip(full[5].T, ff_part)).T
        bias_e = mine(by_chip(whole(expand_bias)[None], ff_part))
        bias_q = mine(by_chip(whole(query_bias)[None], HD))
        bias_v = mine(by_chip(whole(value_bias)[None], HD))
        blank = jnp.zeros((1, width - 3 * OWN_FEATURES), F32)
        bias_row = jnp.concatenate([bias_q, jnp.zeros_like(bias_q), bias_v, blank], 1)
        vec = jnp.concatenate([jnp.stack([whole(v) for v in plain]), bias_e, bias_row])
        got = run_block(False, planes, inputs, cotangent, lengths, (vec,), (wq, we, wo, ws), share, ff_share)
        block_out, input_grad, sums, late, gq, ge, go, gs = got[:8]

        def spread(block, part):
            places = lax.broadcasted_iota(jnp.int32, (CHIPS, 1, 1), 0) == k
            return from_chips(jnp.where(places, block.astype(F32)[None], 0.0), part)

        def owned_sum(array):
            return lax.psum_scatter(array, "fsdp", scatter_dimension=0, tiled=True)

        grad_query_w, grad_key_w, grad_value_w = (
            owned_sum(spread(gq[:, i * OWN_FEATURES:(i + 1) * OWN_FEATURES], HD)) for i in range(3)
        )
        grad_expand_w = owned_sum(spread(ge, ff_part))
        grad_output_w = owned_sum(spread(go.T, HD).T)
        grad_shrink_w = owned_sum(spread(gs.T, ff_part).T)
        owned = [owned_sum(late[i]) for i in range(2)] + [owned_sum(sums[i]) for i in range(2, len(plain))]
        line_q, line_v = sums[7:8, :OWN_FEATURES], sums[7:8, 2 * OWN_FEATURES:3 * OWN_FEATURES]
        grad_expand_b = owned_sum(spread(sums[6:7], ff_part)[0])
        grad_query_b = owned_sum(spread(line_q, HD)[0])
        grad_value_b = owned_sum(spread(line_v, HD)[0])
    return (
        block_out,
        input_grad,
        owned[0],
        owned[1],
        grad_query_w,
        grad_query_b,
        grad_key_w,
        grad_value_w,
        grad_value_b,
        grad_output_w,
        owned[4],
        owned[2],
        owned[3],
        grad_expand_w,
        grad_expand_b,
        grad_shrink_w,
        owned[5],
    )


def solution(mesh):
    rows, matrix, vector = P(None, "fsdp", None), P("fsdp", None), P("fsdp")
    in_specs = (
        rows, rows, P(), vector, vector, matrix, vector, matrix, matrix, vector, matrix, vector,
        vector, vector, matrix, vector, matrix, vector,
    )
    out_specs = (
        rows, rows, vector, vector, matrix, vector, matrix, matrix, vector, matrix, vector,
        vector, vector, matrix, vector, matrix, vector,
    )
    return jax.shard_map(body, mesh=mesh, in_specs=in_specs, out_specs=out_specs, check_vma=False)
```

```python
from functools import partial
from types import SimpleNamespace

import jax
import jax.numpy as jnp
from jax import lax
from jax.experimental import pallas as pl
from jax.experimental.pallas import tpu as pltpu
from jax.sharding import PartitionSpec as P

H = 16
HD = 80
CHIPS = 4
CORES = 2
DEV_CLIP = CHIPS * CORES
OWN_HEADS = H // CHIPS
OWN_FEATURES = OWN_HEADS * HD
QKV_WIDTH = 1024
TILE = 256
ROW_GAIN_ONE, ROW_SHIFT_ONE, ROW_GAIN_TWO, ROW_SHIFT_TWO, ROW_BIAS_OUT, ROW_BIAS_SHRINK = range(6)

EPS = 1e-05
NEG = -1000000000.0
SCALE = HD ** (-0.5)
BF = jnp.bfloat16
F32 = jnp.float32


def dot_nn(left, right):
    return lax.dot_general(left, right, (((1,), (0,)), ((), ())), preferred_element_type=F32)


def dot_nt(left, right):
    return lax.dot_general(left, right, (((1,), (1,)), ((), ())), preferred_element_type=F32)


def dot_tn(left, right):
    return lax.dot_general(left, right, (((0,), (0,)), ((), ())), preferred_element_type=F32)


def norm_parts(rows):
    mean = jnp.mean(rows, -1, keepdims=True)
    centered = rows - mean
    inverse = lax.rsqrt(jnp.mean(centered * centered, -1, keepdims=True) + EPS)
    return centered * inverse, inverse


def norm_backward(gradient, normed, inverse, gain):
    scaled = gradient * gain
    return inverse * (
        scaled
        - jnp.mean(scaled, -1, keepdims=True)
        - normed * jnp.mean(scaled * normed, -1, keepdims=True)
    )


def place(device):
    return device // DEV_CLIP, (device % DEV_CLIP) // CORES, device % CORES


def flipped(number, by):
    low, high = number % 2, number // 2
    if by & 1:
        low = 1 - low
    if by & 2:
        high = 1 - high
    return high * 2 + low


SEND_SEMS, RECV_SEMS, LOCAL_SEMS = 104, 217, 18


def block_kernel(fused, planes, micro, tok, width, ff_own, share, ff_share, *refs):
    names = ["x", "dy", "lengths"]
    if fused:
        names += ["av", "bv", "cv_", "dv", "ev", "fv"] + ["expand_bias", "query_bias", "value_bias", "wq", "wk", "wv", "we", "wo", "ws"]
    else:
        names += ["vec", "wq", "we", "wo", "ws"]
    names += ["bo", "ig", "vo", "vt", "gq", "ge", "go", "gs"]
    if fused:
        names += ["Lq", "Le", "Lo", "Ls"]
    names += ["Wq", "We", "Wo", "Ws", "xg", "dyg", "a2g", "drg", "act", "dhid"]
    names += ["q", "kv", "mixed", "lse", "dmix", "dq", "dl"]
    names += ["sb", "sbo", "rb", "rbo", "resid", "dresid", "vfin", "be", "bq", "vexp", "vqkv", "vrow"]
    if fused:
        names += ["so", "oo", "ao", "aq", "ae", "alq", "ale", "cv", "cp"]
        names += [letter + end for letter in "ut" for end in ("0", "1", "2", "z", "p", "s")]
        names += ["ready_e", "ready_s", "ready_q"]
    names += ["ssem", "rsem", "lsem"]
    r = SimpleNamespace(**dict(zip(names, refs, strict=True)))
    if fused:
        r.vectors = (r.av, r.bv, r.cv_, r.dv, r.ev, r.fv)
    r.dqkv = r.dhid.at[:, :, 0:QKV_WIDTH]
    me = lax.axis_index("fsdp")
    c, k, e = place(me)
    rows = CHIPS * tok

    def chip_peer(by):
        return c * DEV_CLIP + flipped(k, by) * CORES + e

    sibling = c * DEV_CLIP + k * CORES + (1 - e)

    def plane_peer(by):
        return flipped(c, by) * DEV_CLIP + k * CORES + e

    counters = SimpleNamespace(remote=0, local=0, sends=0, free=[])
    pending = []

    def send_semaphore():
        if counters.free:
            return counters.free.pop()
        counters.sends += 1
        return counters.sends - 1

    def flush(count=None):
        for wait in pending[:len(pending) - (count or 0)]:
            wait()

    def send(src, dst, device):
        i = counters.remote
        counters.remote += 1
        out = send_semaphore()
        copy = pltpu.make_async_remote_copy(
            src_ref=src, dst_ref=dst, send_sem=r.ssem.at[out], recv_sem=r.rsem.at[i],
            device_id=(device,), device_id_type=pl.DeviceIdType.MESH,
        )
        copy.start()
        state = SimpleNamespace(sent=False)

        def wait_send():
            if not state.sent:
                state.sent = True
                counters.free.append(out)
                copy.wait_send()

        copy_handle = (copy.wait_recv, wait_send)
        pending.append(wait_send)
        return copy_handle

    def send_if(held, src, dst, device, due, arriving):
        i = counters.remote
        counters.remote += 1
        out = send_semaphore()

        def copy(source, target, to):
            return pltpu.make_async_remote_copy(
                src_ref=source, dst_ref=target, send_sem=r.ssem.at[out], recv_sem=r.rsem.at[i],
                device_id=(to,), device_id_type=pl.DeviceIdType.MESH,
            )

        @pl.when(held)
        def _():
            copy(src(), dst(), device).start()

        state = SimpleNamespace(sent=False)

        def wait_send():
            if not state.sent:
                state.sent = True
                counters.free.append(out)

                @pl.when(held)
                def _():
                    copy(src(), dst(), device).wait_send()

        def wait_recv():
            @pl.when(due)
            def _():
                copy(arriving(), arriving(), sibling).wait_recv()

        copy_handle = (wait_recv, wait_send)
        pending.append(wait_send)
        return copy_handle

    def line_group(mine, theirs):
        return SimpleNamespace(mine=mine, theirs=theirs, steps=[], swaps=[])

    def forward(group, step):
        mine, theirs = group.mine, group.theirs
        if step > 0:
            recv_all(group.steps[step - 1])
        if step < planes - 1:
            n = step + 1
            group.steps.append([
                send_if(
                    (c >= n - 1) & (c < planes - 1), lambda: mine(c - n + 1), lambda: mine(c - n + 1),
                    me + DEV_CLIP, c >= n, lambda: mine(c - n),
                ),
                send_if(
                    (c + n - 1 < planes) & (c >= 1), lambda: mine(c + n - 1), lambda: mine(c + n - 1),
                    me - DEV_CLIP, c + n < planes, lambda: mine(c + n),
                ),
            ])
        if step == 0:
            group.swaps.append(send(mine(c), theirs(c), sibling))
        else:
            for held, i in ((c >= step, c - step), (c + step < planes, c + step)):
                group.swaps.append(
                    send_if(
                        held, lambda i=i: mine(i), lambda i=i: theirs(i), sibling, held, lambda i=i: theirs(i)
                    )
                )

    def group_sent(group):
        sent_all(sum(group.steps, []) + group.swaps)

    def local(src, dst):
        i = counters.local
        counters.local += 1
        copy = pltpu.make_async_copy(src, dst, r.lsem.at[i])
        copy.start()
        return copy.wait

    def recv_all(handles):
        for handle in handles:
            handle[0]()

    def sent_all(handles):
        for handle in handles:
            handle[1]()

    Wq, We, Wo, Ws = r.Wq, r.We, r.Wo, r.Ws
    Ws2 = Ws.reshape(ff_own, width)

    def flat(ref):
        return ref.reshape(micro * rows, width)

    chip_rows = CHIPS * share
    plane_rows = CORES * chip_rows
    chip_halves = (slice(0, chip_rows // 2), slice(chip_rows // 2, chip_rows))

    def stacked(ref, count, lanes):
        return flat(ref).at[0:count * chip_rows].reshape(count, chip_rows, width).at[:, :, 0:lanes]

    def by_core(own, other):
        return jnp.where(e == 0, own, other), jnp.where(e == 0, other, own)

    def join_rows(own, other, count):
        first, second = by_core(own, other)
        pieces = []
        for j in range(count):
            pieces += [first[j * share:(j + 1) * share], second[j * share:(j + 1) * share]]
        return jnp.concatenate(pieces, 0)

    def split_rows(block, count):
        pieces = [block[j * share:(j + 1) * share] for j in range(2 * count)]
        return by_core(jnp.concatenate(pieces[0::2], 0), jnp.concatenate(pieces[1::2], 0))

    def join_planes(own, other, out):
        @pl.loop(0, planes)
        def _(i):
            block = join_rows(own[i].astype(F32), other[i].astype(F32), CHIPS)
            out[pl.ds(pl.multiple_of(i * plane_rows, plane_rows), plane_rows), :] = block.astype(BF)

    def split_planes(grads, own, other):
        @pl.loop(0, planes)
        def _(i):
            block = grads[pl.ds(pl.multiple_of(i * plane_rows, plane_rows), plane_rows), :].astype(F32)
            mine, theirs = split_rows(block, CHIPS)
            own[i] = mine.astype(BF)
            other[i] = theirs.astype(BF)

    k_x, k_y, k_far = flipped(k, 1), flipped(k, 2), flipped(k, 3)
    x_peer, y_peer, far_peer = chip_peer(1), chip_peer(2), chip_peer(3)
    top, low = slice(0, tok // 2), slice(tok // 2, tok)

    def gather_start(src, dst, b):
        return [dst.at[b], [send(src, dst.at[b, k], x_peer), send(src, dst.at[b, k], y_peer)]]

    def gather_relay(gather):
        dst, handles = gather
        handles[0][0]()
        handles.append(send(dst.at[k_x, top], dst.at[k_x, top], y_peer))
        handles[1][0]()
        handles.append(send(dst.at[k_y, low], dst.at[k_y, low], x_peer))

    def gather_finish(gather):
        recv_all(gather[1][2:])

    def reduce_start(slots, landing, b):
        slots, landing = slots.at[b], landing.at[b]
        return [slots, landing, [
            send(slots.at[k_far, top], landing.at[2, top], x_peer),
            send(slots.at[k_far, low], landing.at[2, low], y_peer),
            send(slots.at[k_x, top], landing.at[0, top], x_peer),
            send(slots.at[k_y, low], landing.at[1, low], y_peer),
        ]]

    def reduce_relay(reduction):
        slots, landing, handles = reduction
        handles[0][0]()
        slots[k_y, top] = (slots[k_y, top].astype(F32) + landing[2, top].astype(F32)).astype(BF)
        handles.append(send(slots.at[k_y, top], landing.at[1, top], y_peer))
        handles[1][0]()
        slots[k_x, low] = (slots[k_x, low].astype(F32) + landing[2, low].astype(F32)).astype(BF)
        handles.append(send(slots.at[k_x, low], landing.at[0, low], x_peer))

    def reduce_finish(reduction):
        slots, landing, handles = reduction
        recv_all(handles[2:])
        return slots[k].astype(F32) + landing[0].astype(F32) + landing[1].astype(F32)

    sb, sbo, rb, rbo = r.sb, r.sbo, r.rb, r.rbo
    vfin = r.vfin

    def vec_row(index):
        return vfin[index:index + 1, :]

    def add_row(index, value):
        r.vrow[index:index + 1, :] += value

    def norm_one(b):
        x_local[b]()
        gather_finish(x_gather[b])
        sent_all(x_gather[b][1])

        @pl.loop(0, CHIPS)
        def _(i):
            normed, _inverse = norm_parts(r.xg[b, i].astype(F32))
            r.xg[b, i] = (normed * vec_row(ROW_GAIN_ONE) + vec_row(ROW_SHIFT_ONE)).astype(BF)

    a1_rows = r.xg.reshape(micro, rows, width)
    a2_rows = r.a2g.reshape(micro, rows, width)
    dy_rows = r.dyg.reshape(micro, rows, width)
    dr_rows = r.drg.reshape(micro, rows, width)
    half = rows // 2

    def project(b):
        @pl.loop(0, 2)
        def _(i):
            at = pl.ds(pl.multiple_of(i * half, half), half)
            out = (dot_nn(a1_rows[b, at, :], Wq[...]) + r.bq[...]).astype(BF)
            for h in range(OWN_HEADS):
                r.q[b, h, at, :] = out[:, h * HD:(h + 1) * HD]
                for part in range(2):
                    low = (part + 1) * OWN_FEATURES + h * HD
                    r.kv[b, part, h, e, at, :] = out[:, low:low + HD]

        return [send(r.kv.at[b, :, :, e], r.kv.at[b, :, :, e], sibling)]

    keys = CORES * rows
    chunk_places = [(2 * (i % CHIPS) + i // CHIPS) * tok for i in range(DEV_CLIP)]

    def masked_scores(b, key_rows, query_rows):
        raw = dot_nt(key_rows, query_rows)
        index = lax.broadcasted_iota(jnp.int32, (tok, raw.shape[1]), 0)
        length = r.lengths[b, c]
        return jnp.concatenate(
            [
                raw[i * tok:(i + 1) * tok] * SCALE
                if first + tok <= keys // 2
                else jnp.where(index < length - first, raw[i * tok:(i + 1) * tok] * SCALE, NEG)
                for i, first in enumerate(chunk_places)
            ],
            0,
        )

    def attend(b, start, stop):
        @pl.loop(start, stop)
        def _(step):
            h, part = step // 2, step % 2
            at = pl.ds(pl.multiple_of(part * half, half), half)
            key_rows = r.kv[b, 0, h].reshape(keys, HD)
            value_rows = r.kv[b, 1, h].reshape(keys, HD)
            scores = masked_scores(b, key_rows, r.q[b, h, at, :])
            peak = jnp.max(scores, 0, keepdims=True)
            exponent = jnp.exp(scores - peak)
            sums = jnp.sum(exponent, 0, keepdims=True)
            probs = (exponent * (1.0 / sums)).astype(BF)
            r.lse[b, h, :, at] = peak + jnp.log(sums)
            r.mixed[b, h, :, at] = dot_tn(value_rows, probs).astype(BF)

    def tiles(start, stop, body):
        @pl.loop(start, stop)
        def _(i):
            body(pl.ds(pl.multiple_of(i * TILE, TILE), TILE))

    def partial_sum(slots, b, product):
        view = slots.reshape(micro, rows, width)

        def body(at):
            view[b, :, at] = product(at).astype(BF)

        tiles(0, width // TILE, body)

    mixed = r.mixed.reshape(micro, OWN_FEATURES, rows)

    def mix_out(b):
        partial_sum(sb, b, lambda at: dot_tn(mixed[b], Wo[:, at]))
        return reduce_start(sb, rb, b)

    def norm_two(b, reduction):
        residual = r.x[b].astype(F32) + reduce_finish(reduction) + vec_row(ROW_BIAS_OUT)
        r.resid[b] = residual
        normed, _inverse = norm_parts(residual)
        r.a2g[b, k] = (normed * vec_row(ROW_GAIN_TWO) + vec_row(ROW_SHIFT_TWO)).astype(BF)
        return gather_start(r.a2g.at[b, k], r.a2g, b)

    def feed(b, start, stop):
        def body(at):
            hidden = dot_nn(a2_rows[b], We[:, at]) + r.be[:, at]
            grad_active = dot_nt(dy_rows[b], Ws2[at, :]).astype(BF).astype(F32)
            normal = 0.5 * (1.0 + lax.erf(hidden * 0.7071067811865476))
            r.act[b, :, at] = (hidden * normal).astype(BF)
            density = jnp.exp(-0.5 * hidden * hidden) * 0.3989422804014327
            grad_hidden = (grad_active * (normal + hidden * density)).astype(BF)
            r.dhid[b, :, at] = grad_hidden
            r.vexp[:, at] += jnp.sum(grad_hidden.astype(F32), 0, keepdims=True)

        tiles(start, stop, body)

    def hidden_back(b, earlier):
        sent_all(earlier[2])
        partial_sum(sb, b, lambda at: dot_nt(r.dhid[b], We[at, :]))
        return reduce_start(sb, rb, b)

    def finish_hidden(b, reduction):
        gradient = reduce_finish(reduction)
        normed, inverse = norm_parts(r.resid[b])
        dy_own = r.dy[b].astype(F32)
        total = dy_own + norm_backward(gradient, normed, inverse, vec_row(ROW_GAIN_TWO))
        r.dresid[b] = total
        r.drg[b, k] = total.astype(BF)
        gather = gather_start(r.drg.at[b, k], r.drg, b)
        add_row(ROW_GAIN_TWO, jnp.sum(gradient * normed, 0, keepdims=True))
        add_row(ROW_SHIFT_TWO, jnp.sum(gradient, 0, keepdims=True))
        add_row(ROW_BIAS_OUT, jnp.sum(total, 0, keepdims=True))
        add_row(ROW_BIAS_SHRINK, jnp.sum(dy_own, 0, keepdims=True))
        return gather

    def weight_gradient(count, lefts, rights, out):
        def body(at):
            total = dot_tn(lefts[0, :, at], rights[0])
            for b in range(1, micro):
                total = total + dot_tn(lefts[b, :, at], rights[b])
            out[at, :] = total.astype(BF)

        tiles(0, count // TILE, body)

    def mixed_gradient(b):
        @pl.loop(0, 2)
        def _(i):
            at = pl.ds(pl.multiple_of(i * half, half), half)
            out = dot_nt(dr_rows[b, at, :], Wo[...]).astype(BF)
            for h in range(OWN_HEADS):
                r.dmix[h, at, :] = out[:, h * HD:(h + 1) * HD]

    def attend_back(b, start, stop):
        @pl.loop(start, stop)
        def _(h):
            key_rows = r.kv[b, 0, h].reshape(keys, HD)
            value_rows = r.kv[b, 1, h].reshape(keys, HD)
            grad_keys = None
            grad_values = None
            for part in range(2):
                at = pl.ds(part * half, half)
                query_rows = r.q[b, h, at, :]
                mix_rows = r.dmix[h, at, :]
                probs = jnp.exp(masked_scores(b, key_rows, query_rows) - r.lse[b, h, :, at])
                grad_probs = dot_nt(value_rows, mix_rows)
                inner = jnp.sum(probs * grad_probs, 0, keepdims=True)
                grad_scores = (probs * (grad_probs - inner)).astype(BF)
                grad_query = dot_tn(key_rows, grad_scores) * SCALE
                r.dq[h, at, :] = grad_query.T.astype(BF)
                key_term = dot_nn(grad_scores, query_rows)
                value_term = dot_nn(probs.astype(BF), mix_rows)
                grad_keys = key_term if grad_keys is None else grad_keys + key_term
                grad_values = value_term if grad_values is None else grad_values + value_term
            r.kv[b, 0, h] = (grad_keys * SCALE).astype(BF).reshape(CORES, rows, HD)
            r.kv[b, 1, h] = grad_values.astype(BF).reshape(CORES, rows, HD)

    def swap_back(b, start, stop):
        return [send(r.kv.at[b, :, start:stop, 1 - e], r.dl.at[b, :, start:stop], sibling)]

    def join_gradients(b, handles):
        recv_all(handles)

        @pl.loop(0, CHIPS)
        def _(i):
            at = pl.ds(pl.multiple_of(i * tok, tok), tok)
            pieces = [r.dq[h, at, :] for h in range(OWN_HEADS)]
            for part in range(2):
                for h in range(OWN_HEADS):
                    pair = r.kv[b, part, h, e, at, :].astype(F32) + r.dl[b, part, h, at, :].astype(F32)
                    pieces.append(pair.astype(BF))
            pieces.append(jnp.zeros((tok, QKV_WIDTH - 3 * OWN_FEATURES), BF))
            line = jnp.concatenate(pieces, 1)
            r.dqkv[b, at, :] = line
            r.vqkv[...] += jnp.sum(line.astype(F32), 0, keepdims=True)

    def input_start(b, earlier):
        sent_all(earlier[2])
        partial_sum(sb, b, lambda at: dot_nt(r.dqkv[b], Wq[at, :]))
        return reduce_start(sb, rb, b)

    def finish_input(b, reduction):
        gradient = reduce_finish(reduction)
        normed, inverse = norm_parts(r.x[b].astype(F32))
        back = norm_backward(gradient, normed, inverse, vec_row(ROW_GAIN_ONE))
        r.ig[b] = (r.dresid[b] + back).astype(BF)
        add_row(ROW_GAIN_ONE, jnp.sum(gradient * normed, 0, keepdims=True))
        add_row(ROW_SHIFT_ONE, jnp.sum(gradient, 0, keepdims=True))

    def finish_out(b, reduction):
        total = r.resid[b] + reduce_finish(reduction) + vec_row(ROW_BIAS_SHRINK)
        r.bo[b] = total.astype(BF)

    def sum_group(space, slots):
        return SimpleNamespace(space=space, slots=slots, right={}, left={})

    def add_passing(group, hops):
        space, slots = group.space, group.slots
        for side, held, i, slot in (
            (group.right, (c >= 1) & (c - 1 + hops < planes), c - 1 + hops, hops - 1),
            (group.left, (c <= planes - 2) & (c + 1 - hops >= 0), c + 1 - hops, 5 - hops),
        ):
            side[hops][0]()

            @pl.when(held)
            def _():
                space[i] = (space[i].astype(F32) + slots[slot][...].astype(F32)).astype(BF)

    def sum_step(group, hops):
        space, slots = group.space, group.slots
        if hops < planes - 1:
            add_passing(group, hops + 1)
        group.right[hops] = send_if(
            c + hops < planes, lambda: space.at[c + hops], lambda: slots[hops - 1], me + DEV_CLIP,
            (c >= 1) & (c - 1 + hops < planes), lambda: slots[hops - 1],
        )
        group.left[hops] = send_if(
            c - hops >= 0, lambda: space.at[c - hops], lambda: slots[5 - hops], me - DEV_CLIP,
            (c <= planes - 2) & (c + 1 - hops >= 0), lambda: slots[5 - hops],
        )

    def sum_finish(group, out):
        space, slots = group.space, group.slots
        out(space[c].astype(F32), False)
        for side, held, slot in ((group.right, c >= 1, 0), (group.left, c <= planes - 2, 4)):
            side[1][0]()

            @pl.when(held)
            def _():
                out(slots[slot][...].astype(F32), True)

    def to_blocks(ref, first):
        def put(total, more):
            for j in range(total.shape[0] // share):
                piece = total[j * share:(j + 1) * share]
                ref[first + j] = ref[first + j] + piece if more else piece

        return put

    def to_rows(ref):
        def put(total, more):
            ref[...] = ref[...] + total if more else total

        return put

    def sibling_add(handles, landing, fetched, out, mine):
        recv_all(handles)
        sent_all(handles)
        local(landing, fetched)()

        @pl.loop(0, planes)
        def _(i):
            out[i] = (mine(i).astype(F32) + fetched[i].astype(F32)).astype(BF)

    def free_slots(ready):
        for side, held, device in ((0, c >= 1, me - DEV_CLIP), (1, c <= planes - 2, me + DEV_CLIP)):

            @pl.when(held)
            def _():
                pl.semaphore_signal(
                    ready.at[1 - side], inc=1, device_id=(device,), device_id_type=pl.DeviceIdType.MESH
                )

    def await_slots(ready):
        for side, held in ((0, c >= 1), (1, c <= planes - 2)):

            @pl.when(held)
            def _():
                pl.semaphore_wait(ready.at[side], 1)

    resid, dresid = r.resid, r.dresid
    x_local = [local(r.x.at[b], r.xg.at[b, k]) for b in range(micro)]
    dy_local = [local(r.dy.at[b], r.dyg.at[b, k]) for b in range(micro)]
    x_gather = [None] * micro
    dy_gather = [None] * micro
    if fused:
        expand = [dresid.at[0, 0:share], dresid.at[0, share:2 * share], dresid.at[0, 2 * share:3 * share], dresid.at[1, 0:share]]
        first_rows = tok - share
        loads = [local(ref, resid.at[0, i * share:(i + 1) * share]) for i, ref in enumerate((r.wq, r.wk, r.wv))]
        loads.append(local(r.wo, resid.at[1, 0:share]))
        expand_loads = [local(r.we.at[:, i * width:(i + 1) * width], expand[i]) for i in range(planes)]
        expand_loads.append(local(r.ws.at[0:first_rows], resid.at[1, share:tok]))
        expand_loads.append(local(r.ws.at[first_rows:ff_share], dresid.at[1, share:ff_share - first_rows + share]))
        peers = [chip_peer(by) for by in (1, 2, 3)] + [sibling]
        if fused:
            peers += [plane_peer(by) for by in range(1, planes)]
        barrier = pltpu.get_barrier_semaphore()
        for peer in peers:
            pl.semaphore_signal(barrier, inc=1, device_id=(peer,), device_id_type=pl.DeviceIdType.MESH)
        for load in loads:
            load()
        matrices = [resid[0, i * share:(i + 1) * share] for i in range(3)]
        for j in range(CHIPS):
            pieces = [
                matrix[:, (i * CHIPS + j) * HD:(i * CHIPS + j + 1) * HD] for matrix in matrices for i in range(planes)
            ]
            pieces.append(jnp.zeros((share, QKV_WIDTH - 3 * OWN_FEATURES), F32))
            r.aq[j] = jnp.concatenate(pieces, 1).astype(BF)
        r.so[c] = resid[1, 0:share].astype(BF)
        compact = jnp.concatenate([jnp.pad(ref[...], ((0, 0), (0, 256 - share))) for ref in r.vectors], 0)
        tail = jnp.pad(r.expand_bias[...], ((0, 0), (0, 256 - ff_share)))
        pair = [jnp.pad(ref[...], ((0, 0), (0, 128 - share))) for ref in (r.query_bias, r.value_bias)]
        r.cv[c] = jnp.concatenate([compact, tail, jnp.concatenate(pair, 1)], 0)
        pl.semaphore_wait(barrier, len(peers))
        wq_mine, wq_other = stacked(r.drg, planes, QKV_WIDTH), stacked(r.a2g, planes, QKV_WIDTH)
        we_mine, we_other = stacked(r.act, planes, ff_own), stacked(r.dhid, planes, ff_own)
        lines_q = [
            line_group(lambda i, at=at: wq_mine.at[i, at], lambda i, at=at: wq_other.at[i, at]) for at in chip_halves
        ]
        line_e = line_group(lambda i: we_mine.at[i], lambda i: we_other.at[i])
        line_o = line_group(lambda i: r.so.at[i], lambda i: r.oo.at[i])
        line_s = line_group(lambda i: Ws.at[i, e], lambda i: Ws.at[i, e])

        def pack_plane(blocks, out):
            out[c] = jnp.concatenate([blocks[j].astype(F32) for j in range(CHIPS)], 0).astype(BF)

        wq_plane = [send(r.aq.at[flipped(k, by)], r.alq.at[k], chip_peer(by)) for by in (3, 1, 2)]
        vec_z = [send(r.cv.at[c], r.cv.at[c], plane_peer(by)) for by in range(1, planes)]
        forward(line_o, 0)
        r.alq[k] = r.aq[k]
        recv_all(vec_z)
        r.cp[e, k] = r.cv[...]
        vec_p = [send(r.cv, r.cp.at[e, k], chip_peer(by)) for by in (1, 2, 3)]
        x_gather[0] = gather_start(r.x.at[0], r.xg, 0)
        recv_all(wq_plane)
        pack_plane(r.alq, wq_mine)
        for line in lines_q:
            forward(line, 0)
        for load in expand_loads:
            load()
        ff_part = width // planes
        for j in range(CHIPS):
            pieces = [block[:, j * ff_part:(j + 1) * ff_part] for block in expand]
            r.ae[j] = jnp.concatenate(pieces, 1).astype(BF)
        we_plane = [send(r.ae.at[flipped(k, by)], r.ale.at[k], chip_peer(by)) for by in (3, 1, 2)]
        r.ale[k] = r.ae[k]
        rows_s = [resid[1, share:tok], dresid[1, share:ff_share - first_rows + share]]
        Ws[c, e] = jnp.concatenate(rows_s, 0).astype(BF)
        recv_all(vec_p)
        vec_s = [send(r.cp.at[e], r.cp.at[e], sibling)]
        recv_all(vec_s)
        places = [(i, f) for i in range(planes) for f in range(CORES)]
        vfin[...] = jnp.concatenate(
            [r.cp[f, j, i][:, 0:share] for i in range(planes) for j in range(CHIPS) for f in range(CORES)], 1
        )
        r.be[...] = jnp.concatenate([r.cp[f, k, i][6:7, 0:ff_share] for i, f in places], 1)
        bias = [jnp.concatenate([r.cp[f, k, i][7:8, at:at + share] for i, f in places], 1) for at in (0, 128)]
        blank = jnp.zeros((1, OWN_FEATURES), F32)
        r.bq[...] = jnp.concatenate([bias[0], blank, bias[1], blank[:, :QKV_WIDTH - 3 * OWN_FEATURES]], 1)
        gather_relay(x_gather[0])
        x_gather[1] = gather_start(r.x.at[1], r.xg, 1)
        forward(line_o, 1)
        for line in lines_q:
            forward(line, 1)
        recv_all(we_plane)
        pack_plane(r.ale, we_mine)
    else:
        peers = [chip_peer(by) for by in (1, 2, 3)] + [sibling]
        if fused:
            peers += [plane_peer(by) for by in range(1, planes)]
        barrier = pltpu.get_barrier_semaphore()
        for peer in peers:
            pl.semaphore_signal(barrier, inc=1, device_id=(peer,), device_id_type=pl.DeviceIdType.MESH)
        pl.semaphore_wait(barrier, len(peers))
        loads = [local(r.wq, Wq), local(r.we, We), local(r.wo, Wo), local(r.ws, Ws2)]
        for b in range(micro):
            x_gather[b] = gather_start(r.x.at[b], r.xg, b)
        vfin[...] = r.vec[...]
        r.be[...] = r.vec[6:7, :]
        r.bq[...] = r.vec[7:8, :QKV_WIDTH]
        gather_relay(x_gather[0])
        for load in loads:
            load()
    for ref in (r.vrow, r.vexp, r.vqkv):
        ref[...] = jnp.zeros_like(ref)
    norm_one(0)
    if fused:
        forward(line_o, 2)
        for line in lines_q:
            forward(line, 2)
        forward(line_e, 0)
        forward(line_s, 0)
    gather_relay(x_gather[1])
    dy_gather[0] = gather_start(r.dy.at[0], r.dyg, 0)
    norm_one(1)
    if fused:
        forward(line_o, 3)
        for line in lines_q:
            forward(line, 3)
        for line in lines_q:
            recv_all(line.swaps)
        join_planes(wq_mine, wq_other, Wq)
    kv_swap = [None] * micro
    kv_swap[0] = project(0)
    gather_relay(dy_gather[0])
    dy_gather[1] = gather_start(r.dy.at[1], r.dyg, 1)
    kv_swap[1] = project(1)
    recv_all(kv_swap[0])
    attend(0, 0, OWN_HEADS)
    if fused:
        forward(line_e, 1)
    attend(0, OWN_HEADS, 2 * OWN_HEADS)
    if fused:
        recv_all(line_o.swaps)
        for i in range(planes):
            pair = join_rows(r.so[i].astype(F32), r.oo[i].astype(F32), 1)
            Wo[i * HD:(i + 1) * HD, :] = pair.astype(BF)
    mix_reduce = [mix_out(0), None]
    gather_relay(dy_gather[1])
    recv_all(kv_swap[1])
    attend(1, 0, OWN_HEADS)
    if fused:
        forward(line_s, 1)
    attend(1, OWN_HEADS, 2 * OWN_HEADS - 1)
    reduce_relay(mix_reduce[0])
    attend(1, 2 * OWN_HEADS - 1, 2 * OWN_HEADS)
    mix_reduce[1] = mix_out(1)
    if fused:
        forward(line_e, 2)
    second_gather = [norm_two(0, mix_reduce[0]), None]
    if fused:
        forward(line_s, 2)
    reduce_relay(mix_reduce[1])
    gather_relay(second_gather[0])
    second_gather[1] = norm_two(1, mix_reduce[1])
    if fused:
        forward(line_e, 3)
        recv_all(line_e.swaps)
        group_sent(line_e)
        for line in lines_q:
            group_sent(line)
        join_planes(we_mine, we_other, We)
    gather_finish(second_gather[0])
    dy_local[0]()
    gather_finish(dy_gather[0])
    if fused:
        forward(line_s, 3)
        recv_all(line_s.swaps)
    flush(20)
    feed(0, 0, 3)
    gather_relay(second_gather[1])
    feed(0, 3, ff_own // TILE)
    hidden_reduce = [hidden_back(0, mix_reduce[0]), None]
    gather_finish(second_gather[1])
    dy_local[1]()
    gather_finish(dy_gather[1])
    feed(1, 0, ff_own // TILE)
    reduce_relay(hidden_reduce[0])
    hidden_reduce[1] = hidden_back(1, mix_reduce[1])
    weight_gradient(width, a2_rows, r.dhid, We)
    resid_gather = [finish_hidden(0, hidden_reduce[0]), None]
    if fused:
        sent_all(wq_plane + we_plane)
        group_sent(line_o)
        group_sent(line_s)
        sent_all(second_gather[0][1] + second_gather[1][1])
        free_slots(r.ready_e)
        parts_e = We.reshape(planes, 2, chip_rows, ff_own)
        split_planes(We, parts_e.at[:, 0], parts_e.at[:, 1])
        ge_s = [send(parts_e.at[:, 1], r.Le, sibling)]
    partial_sum(sbo, 0, lambda at: dot_nn(r.act[0], Ws2[:, at]))
    if fused:
        sum_e = sum_group(parts_e.at[:, 0], [flat(r.a2g).at[i * chip_rows:(i + 1) * chip_rows] for i in range(5)])
        sibling_add(ge_s, r.Le, parts_e.at[:, 1], parts_e.at[:, 0], lambda i: parts_e[i, 0])
        await_slots(r.ready_e)
        sum_step(sum_e, 3)
    partial_sum(sbo, 1, lambda at: dot_nn(r.act[1], Ws2[:, at]))
    reduce_relay(hidden_reduce[1])
    weight_gradient(ff_own, r.act, dy_rows, Ws2)
    if fused:
        sent_all(dy_gather[0][1] + dy_gather[1][1])
        free_slots(r.ready_s)
        gs_s = [send(Ws.at[:, 1 - e], r.Ls, sibling)]
    gather_relay(resid_gather[0])
    if fused:
        places_s = [flat(r.a2g).at[5 * ff_share:6 * ff_share]]
        for ref in (r.dyg, r.act):
            places_s += [flat(ref).at[i * ff_share:(i + 1) * ff_share] for i in (4, 5)]
        sum_s = sum_group(Ws.at[:, e], places_s)
        sibling_add(gs_s, r.Ls, Ws.at[:, 1 - e], Ws.at[:, e], lambda i: Ws[i, e])
        await_slots(r.ready_s)
        sum_step(sum_s, 3)
    resid_gather[1] = finish_hidden(1, hidden_reduce[1])
    if fused:
        sum_step(sum_e, 2)
    flush(20)
    gather_finish(resid_gather[0])
    mixed_gradient(0)
    sent_all(kv_swap[0] + kv_swap[1])
    attend_back(0, 0, 2)
    gather_relay(resid_gather[1])
    out_reduce = [reduce_start(sbo, rbo, 0), None]
    if fused:
        sum_step(sum_s, 2)
    attend_back(0, 2, OWN_HEADS)
    swap = swap_back(0, 0, OWN_HEADS)
    gather_finish(resid_gather[1])
    mixed_gradient(1)
    lead = dot_nn(mixed[0], dr_rows[0])
    for other in range(1, micro):
        lead = lead + dot_nn(mixed[other], dr_rows[other])
    if fused:
        space_o, other_o = r.so, r.oo
        for i in range(planes):
            mine, theirs = split_rows(lead[i * HD:(i + 1) * HD], 1)
            space_o[i] = mine.astype(BF)
            other_o[i] = theirs.astype(BF)
        go_s = [send(other_o, r.Lo, sibling)]
    else:
        Wo[...] = lead.astype(BF)
    join_gradients(0, swap)
    input_reduce = [input_start(0, hidden_reduce[0]), None]
    if fused:
        sum_step(sum_e, 1)
    attend_back(1, 0, 2)
    last_swap = swap_back(1, 0, 2)
    reduce_relay(out_reduce[0])
    if fused:
        sum_o = sum_group(space_o, [r.ao.at[i] for i in range(5)])
        sibling_add(go_s, r.Lo, other_o, space_o, lambda i: space_o[i])
        sum_step(sum_s, 1)
        sum_step(sum_o, 3)
    attend_back(1, 2, OWN_HEADS)
    last_swap += swap_back(1, 2, OWN_HEADS)
    reduce_relay(input_reduce[0])
    join_gradients(1, last_swap)
    input_reduce[1] = input_start(1, hidden_reduce[1])
    weight_gradient(width, a1_rows, r.dqkv, Wq)
    flush(20)
    if fused:
        free_slots(r.ready_q)
        parts_q = Wq.reshape(planes, 2, chip_rows, QKV_WIDTH)
        split_planes(Wq, parts_q.at[:, 0], parts_q.at[:, 1])
        gq_s = [send(parts_q.at[:, 1], r.Lq, sibling)]
        sum_step(sum_o, 2)
        five = stacked(r.dhid, 5, QKV_WIDTH)
        sums_q = [sum_group(parts_q.at[:, 0, at], [five.at[i, at] for i in range(5)]) for at in chip_halves]
    finish_input(0, input_reduce[0])
    if fused:
        sibling_add(gq_s, r.Lq, parts_q.at[:, 1], parts_q.at[:, 0], lambda i: parts_q[i, 0])
        await_slots(r.ready_q)
        for group in sums_q:
            sum_step(group, 3)
    def vector_step(group, step, last):
        zero, one, two, from_z, from_plane, from_core = group
        if step == 0:
            return [send(zero, from_core, sibling)]
        if step == 1:
            one[...] = zero[...] + from_core[...]
            return [send(one, from_z.at[by - 1], plane_peer(by)) for by in range(1, planes)]
        if step == 2:
            total = one[...]
            for by in range(1, planes):
                total = total + from_z[by - 1]
            two[...] = total
            return [send(two, from_plane.at[by - 1], chip_peer(by)) for by in (1, 2, 3)]
        others = from_plane[0] + from_plane[1] + from_plane[2]
        shared = lax.broadcasted_iota(jnp.int32, others.shape, 0) < 6
        last[...] = two[...] + jnp.where(shared, others, 0.0)

    if fused:
        group_u = (r.u0, r.u1, r.u2, r.uz, r.up, r.us)
        group_t = (r.t0, r.t1, r.t2, r.tz, r.tp, r.ts)
    padded = jnp.concatenate([r.vqkv[...], jnp.zeros((1, width - QKV_WIDTH), F32)], 1)
    early = jnp.concatenate([r.vrow[0:6, :], r.vexp[...], padded], 0)
    if fused:
        r.u0[...] = early
        moved = vector_step(group_u, 0, None)
    reduce_relay(input_reduce[1])
    out_reduce[1] = reduce_start(sbo, rbo, 1)
    finish_out(0, out_reduce[0])
    if fused:
        recv_all(moved)
        moved = vector_step(group_u, 1, None)
        sum_finish(sum_s, to_rows(r.gs))
        sum_finish(sum_e, to_blocks(r.ge, 0))
        for j in range(CHIPS):
            r.ae[j] = r.ge[j].astype(BF)
        sum_step(sum_o, 1)
    if fused:
        ge_p = [send(r.ae.at[flipped(k, by)], r.ale.at[k], chip_peer(by)) for by in (3, 1, 2)]
        recv_all(moved)
        moved = vector_step(group_u, 2, None)
        for group in sums_q:
            sum_step(group, 2)
    finish_input(1, input_reduce[1])
    late = r.vrow[0:2, :]
    if fused:
        r.t0[...] = late
        moved_late = vector_step(group_t, 0, None)
    reduce_relay(out_reduce[1])
    if fused:
        recv_all(moved)
        vector_step(group_u, 3, r.vo)
        recv_all(ge_p)
        for by in (1, 2, 3):
            r.ge[flipped(k, by)] = r.ale[flipped(k, by)].astype(F32)
        recv_all(moved_late)
        moved_late = vector_step(group_t, 1, None)
        for group in sums_q:
            sum_step(group, 1)
        recv_all(moved_late)
        moved_late = vector_step(group_t, 2, None)
        sum_finish(sum_o, to_rows(r.go))
        recv_all(moved_late)
        vector_step(group_t, 3, r.vt)
    finish_out(1, out_reduce[1])
    if fused:
        for i, group in enumerate(sums_q):
            sum_finish(group, to_blocks(r.gq, i * CHIPS // 2))
        for j in range(CHIPS):
            r.aq[j] = r.gq[j].astype(BF)
        gq_p = [send(r.aq.at[flipped(k, by)], r.alq.at[k], chip_peer(by)) for by in (3, 1, 2)]
        recv_all(gq_p)
        for by in (1, 2, 3):
            r.gq[flipped(k, by)] = r.alq[flipped(k, by)].astype(F32)
    else:
        r.vo[...] = early
        r.vt[...] = late
        stores = [local(Wq, r.gq), local(We, r.ge), local(Wo, r.go), local(Ws2, r.gs)]
        for store in stores:
            store()
    flush()


def run_block(fused, planes, x, dy, lengths, vectors, weights_in, share, ff_share):
    micro, tok, width = x.shape
    ff_own = width
    rows = CHIPS * tok
    vmem = pl.BlockSpec(memory_space=pltpu.VMEM)
    anywhere = pl.BlockSpec(memory_space=pl.ANY)
    smem = pl.BlockSpec(memory_space=pltpu.SMEM)

    def shape(*dims, dtype=BF):
        return jax.ShapeDtypeStruct(dims, dtype)

    outs = [
        (shape(micro, tok, width), vmem),
        (shape(micro, tok, width), vmem),
        (shape(8, width, dtype=F32), vmem),
        (shape(2, width, dtype=F32), vmem),
    ]
    if fused:
        outs += [
            (shape(CHIPS, share, QKV_WIDTH, dtype=F32), vmem),
            (shape(CHIPS, share, ff_own, dtype=F32), vmem),
            (shape(share, width, dtype=F32), vmem),
            (shape(ff_share, width, dtype=F32), vmem),
        ]
        outs += [
            (shape(planes, CHIPS * share, QKV_WIDTH), anywhere),
            (shape(planes, CHIPS * share, ff_own), anywhere),
            (shape(planes, share, width), anywhere),
            (shape(planes, ff_share, width), anywhere),
        ]
    else:
        outs += [
            (shape(width, QKV_WIDTH), anywhere),
            (shape(width, ff_own), anywhere),
            (shape(OWN_FEATURES, width), anywhere),
            (shape(ff_own, width), anywhere),
        ]
    if fused:
        weights = [
            pltpu.VMEM((width, QKV_WIDTH), BF),
            pltpu.VMEM((width, ff_own), BF),
            pltpu.VMEM((OWN_FEATURES, width), BF),
            pltpu.VMEM((planes, CORES, ff_share, width), BF),
        ]
    else:
        weights = [
            pltpu.VMEM((width, QKV_WIDTH), BF),
            pltpu.VMEM((width, ff_own), BF),
            pltpu.VMEM((OWN_FEATURES, width), BF),
            pltpu.VMEM((ff_own, width), BF),
        ]
    scratch = weights + [
        pltpu.VMEM((micro, CHIPS, tok, width), BF),
        pltpu.VMEM((micro, CHIPS, tok, width), BF),
        pltpu.VMEM((micro, CHIPS, tok, width), BF),
        pltpu.VMEM((micro, CHIPS, tok, width), BF),
        pltpu.VMEM((micro, rows, ff_own), BF),
        pltpu.VMEM((micro, rows, ff_own), BF),
        pltpu.VMEM((micro, OWN_HEADS, rows, HD), BF),
        pltpu.VMEM((micro, 2, OWN_HEADS, CORES, rows, HD), BF),
        pltpu.VMEM((micro, OWN_HEADS, HD, rows), BF),
        pltpu.VMEM((micro, OWN_HEADS, 1, rows), F32),
        pltpu.VMEM((OWN_HEADS, rows, HD), BF),
        pltpu.VMEM((OWN_HEADS, rows, HD), BF),
        pltpu.VMEM((micro, 2, OWN_HEADS, rows, HD), BF),
        pltpu.VMEM((micro, CHIPS, tok, width), BF),
        pltpu.VMEM((micro, CHIPS, tok, width), BF),
        pltpu.VMEM((micro, CHIPS - 1, tok, width), BF),
        pltpu.VMEM((micro, CHIPS - 1, tok, width), BF),
        pltpu.VMEM((micro, tok, width), F32),
        pltpu.VMEM((micro, tok, width), F32),
        pltpu.VMEM((8, width), F32),
        pltpu.VMEM((1, ff_own), F32),
        pltpu.VMEM((1, QKV_WIDTH), F32),
        pltpu.VMEM((1, ff_own), F32),
        pltpu.VMEM((1, QKV_WIDTH), F32),
        pltpu.VMEM((8, width), F32),
    ]
    if fused:
        scratch += [
            pltpu.VMEM((planes, share, width), BF),
            pltpu.VMEM((planes, share, width), BF),
            pltpu.VMEM((5, share, width), BF),
            pltpu.VMEM((CHIPS, share, QKV_WIDTH), BF),
            pltpu.VMEM((CHIPS, share, ff_own), BF),
            pltpu.VMEM((CHIPS, share, QKV_WIDTH), BF),
            pltpu.VMEM((CHIPS, share, ff_own), BF),
        ]
        scratch += [
            pltpu.VMEM((planes, 8, 256), F32),
            pltpu.VMEM((CORES, CHIPS, planes, 8, 256), F32),
        ]
        for lines in (8, 2):
            scratch += [pltpu.VMEM((lines, width), F32) for _ in range(3)]
            scratch += [pltpu.VMEM((planes - 1, lines, width), F32), pltpu.VMEM((CHIPS - 1, lines, width), F32)]
            scratch.append(pltpu.VMEM((lines, width), F32))
        scratch += [pltpu.SemaphoreType.REGULAR((2,)) for _ in range(3)]
    scratch += [
        pltpu.SemaphoreType.DMA((SEND_SEMS,)),
        pltpu.SemaphoreType.DMA((RECV_SEMS,)),
        pltpu.SemaphoreType.DMA((LOCAL_SEMS,)),
    ]
    return pl.pallas_call(
        partial(block_kernel, fused, planes, micro, tok, width, ff_own, share, ff_share),
        out_shape=[out for out, _ in outs],
        in_specs=[vmem, vmem, smem] + [vmem] * len(vectors) + [anywhere] * len(weights_in),
        out_specs=[spec for _, spec in outs],
        scratch_shapes=scratch,
        compiler_params=pltpu.CompilerParams(
            collective_id=0, has_side_effects=True, vmem_limit_bytes=63 * 1000 * 1000
        ),
    )(x, dy, lengths, *vectors, *weights_in)


def finish_kernel(planes, share, ff_share, bo, ig, vo, vt, gq, ge, go, gs, *refs):
    device = lax.axis_index("fsdp")
    c, _, e = place(device)
    outs, (blocks_q, blocks_e, lines, last_lines, sems) = refs[:17], refs[17:]
    moves = [(vo, lines), (vt, last_lines), (gq, blocks_q), (ge, blocks_e)]
    moves += [(bo, outs[0]), (ig, outs[1]), (go, outs[6]), (gs, outs[7])]
    copies = [pltpu.make_async_copy(src, dst, sems.at[i]) for i, (src, dst) in enumerate(moves)]
    for copy in copies:
        copy.start()
    for copy in copies[:4]:
        copy.wait()
    part = ge.shape[2] // planes
    for n in range(planes):
        for j in range(CHIPS):
            at = (n * CHIPS + j) * part
            outs[5][:, at:at + part] = blocks_e[j][:, n * part:(n + 1) * part]
    for i, out in enumerate(outs[2:5]):
        first = i * OWN_FEATURES
        out[...] = jnp.concatenate(
            [blocks_q[j][:, first + n * HD:first + (n + 1) * HD] for n in range(planes) for j in range(CHIPS)], 1
        )
    vo, vt = lines, last_lines
    width = vo.shape[1]

    def own(lines, start, size):
        lane = lax.broadcasted_iota(jnp.int32, (width, size), 0)
        pick = (lane == start + lax.broadcasted_iota(jnp.int32, (width, size), 1)).astype(F32)
        return lax.dot_general(
            lines, pick, (((1,), (0,)), ((), ())), precision=lax.Precision.HIGHEST, preferred_element_type=F32
        )

    early, late = own(vo[...], device * share, share), own(vt[...], device * share, share)
    expand = own(vo[...], (2 * c + e) * ff_share, ff_share)
    query = own(vo[...], (2 * c + e) * share, share)
    value = own(vo[...], 2 * OWN_FEATURES + (2 * c + e) * share, share)
    for out, line in zip(
        outs[8:],
        [late[0:1], late[1:2]] + [early[i:i + 1] for i in range(2, 6)] + [expand[6:7], query[7:8], value[7:8]],
        strict=True,
    ):
        out[...] = line
    for copy in copies[4:]:
        copy.wait()


def finish_block(planes, share, ff_share, results):
    shapes = [results[0], results[1]] + [jax.ShapeDtypeStruct((share, results[2].shape[1]), F32)] * 3
    shapes += [jax.ShapeDtypeStruct((share, CHIPS * results[5].shape[2]), F32), results[6], results[7]]
    shapes = [jax.ShapeDtypeStruct(s.shape, s.dtype) for s in shapes]
    shapes += [jax.ShapeDtypeStruct((1, share), F32)] * 6
    shapes += [jax.ShapeDtypeStruct((1, size), F32) for size in (ff_share, share, share)]
    vmem = pl.BlockSpec(memory_space=pltpu.VMEM)
    anywhere = pl.BlockSpec(memory_space=pl.ANY)
    held = [results[4], results[5], results[2], results[3]]
    return pl.pallas_call(
        partial(finish_kernel, planes, share, ff_share),
        out_shape=shapes,
        in_specs=[anywhere] * 8,
        out_specs=[vmem] * 17,
        scratch_shapes=[pltpu.VMEM(a.shape, a.dtype) for a in held] + [pltpu.SemaphoreType.DMA((8,))],
        compiler_params=pltpu.CompilerParams(vmem_limit_bytes=60 * 1000 * 1000),
    )(*results)


def by_chip(matrix, part):
    rows = matrix.shape[0]
    return matrix.reshape(rows, -1, CHIPS, part).transpose(2, 0, 1, 3).reshape(CHIPS, rows, -1)


def from_chips(blocks, part):
    rows = blocks.shape[1]
    return blocks.reshape(CHIPS, rows, -1, part).transpose(1, 2, 0, 3).reshape(rows, -1)


def body(
    inputs, cotangent, lengths, first_gain, first_shift, query_weight, query_bias, key_weight,
    value_weight, value_bias, output_weight, output_bias, second_gain, second_shift,
    expand_weight, expand_bias, shrink_weight, shrink_bias,
):
    device = lax.axis_index("fsdp")
    count = lax.axis_size("fsdp")
    c, k, e = place(device)
    planes = count // DEV_CLIP
    width = inputs.shape[2]
    share = query_weight.shape[0]
    ff_share = shrink_weight.shape[0]
    ff_part = width // 4
    fused = planes == 4 and share * 2 == HD and ff_share * 2 == ff_part
    plain = (first_gain, first_shift, second_gain, second_shift, output_bias, shrink_bias)
    matrices = (query_weight, key_weight, value_weight, expand_weight, output_weight, shrink_weight)
    if fused:
        vectors = [v.reshape(1, -1) for v in plain + (expand_bias, query_bias, value_bias)]
        got = run_block(True, planes, inputs, cotangent, lengths, vectors, matrices, share, ff_share)
        done = finish_block(planes, share, ff_share, got[:8])
        block_out, input_grad, grad_query_w, grad_key_w, grad_value_w, grad_expand_w, grad_output_w, grad_shrink_w = done[:8]
        owned = [line[0] for line in done[8:14]]
        grad_expand_b, grad_query_b, grad_value_b = (line[0] for line in done[14:])
    else:

        def whole(array):
            return lax.all_gather(array, "fsdp", axis=0, tiled=True)

        def mine(blocks):
            return lax.dynamic_index_in_dim(blocks, k, 0, keepdims=False)

        full = [whole(w.astype(BF)) for w in matrices]
        pieces = [mine(by_chip(w, HD)) for w in full[:3]]
        pieces.append(jnp.zeros((width, QKV_WIDTH - 3 * OWN_FEATURES), BF))
        wq = jnp.concatenate(pieces, 1)
        we = mine(by_chip(full[3], ff_part))
        wo = mine(by_chip(full[4].T, HD)).T
        ws = mine(by_chip(full[5].T, ff_part)).T
        bias_e = mine(by_chip(whole(expand_bias)[None], ff_part))
        bias_q = mine(by_chip(whole(query_bias)[None], HD))
        bias_v = mine(by_chip(whole(value_bias)[None], HD))
        blank = jnp.zeros((1, width - 3 * OWN_FEATURES), F32)
        bias_row = jnp.concatenate([bias_q, jnp.zeros_like(bias_q), bias_v, blank], 1)
        vec = jnp.concatenate([jnp.stack([whole(v) for v in plain]), bias_e, bias_row])
        got = run_block(False, planes, inputs, cotangent, lengths, (vec,), (wq, we, wo, ws), share, ff_share)
        block_out, input_grad, sums, late, gq, ge, go, gs = got[:8]

        def spread(block, part):
            places = lax.broadcasted_iota(jnp.int32, (CHIPS, 1, 1), 0) == k
            return from_chips(jnp.where(places, block.astype(F32)[None], 0.0), part)

        def owned_sum(array):
            return lax.psum_scatter(array, "fsdp", scatter_dimension=0, tiled=True)

        grad_query_w, grad_key_w, grad_value_w = (
            owned_sum(spread(gq[:, i * OWN_FEATURES:(i + 1) * OWN_FEATURES], HD)) for i in range(3)
        )
        grad_expand_w = owned_sum(spread(ge, ff_part))
        grad_output_w = owned_sum(spread(go.T, HD).T)
        grad_shrink_w = owned_sum(spread(gs.T, ff_part).T)
        owned = [owned_sum(late[i]) for i in range(2)] + [owned_sum(sums[i]) for i in range(2, len(plain))]
        line_q, line_v = sums[7:8, :OWN_FEATURES], sums[7:8, 2 * OWN_FEATURES:3 * OWN_FEATURES]
        grad_expand_b = owned_sum(spread(sums[6:7], ff_part)[0])
        grad_query_b = owned_sum(spread(line_q, HD)[0])
        grad_value_b = owned_sum(spread(line_v, HD)[0])
    return (
        block_out,
        input_grad,
        owned[0],
        owned[1],
        grad_query_w,
        grad_query_b,
        grad_key_w,
        grad_value_w,
        grad_value_b,
        grad_output_w,
        owned[4],
        owned[2],
        owned[3],
        grad_expand_w,
        grad_expand_b,
        grad_shrink_w,
        owned[5],
    )


def solution(mesh):
    rows, matrix, vector = P(None, "fsdp", None), P("fsdp", None), P("fsdp")
    in_specs = (
        rows, rows, P(), vector, vector, matrix, vector, matrix, matrix, vector, matrix, vector,
        vector, vector, matrix, vector, matrix, vector,
    )
    out_specs = (
        rows, rows, vector, vector, matrix, vector, matrix, matrix, vector, matrix, vector,
        vector, vector, matrix, vector, matrix, vector,
    )
    return jax.shard_map(body, mesh=mesh, in_specs=in_specs, out_specs=out_specs, check_vma=False)
```

```python
from functools import partial
from types import SimpleNamespace

import jax
import jax.numpy as jnp
from jax import lax
from jax.experimental import pallas as pl
from jax.experimental.pallas import tpu as pltpu
from jax.sharding import PartitionSpec as P

H = 16
HD = 80
CHIPS = 4
CORES = 2
DEV_CLIP = CHIPS * CORES
OWN_HEADS = H // CHIPS
OWN_FEATURES = OWN_HEADS * HD
QKV_WIDTH = 1024
TILE = 256
ROW_GAIN_ONE, ROW_SHIFT_ONE, ROW_GAIN_TWO, ROW_SHIFT_TWO, ROW_BIAS_OUT, ROW_BIAS_SHRINK = range(6)

EPS = 1e-05
NEG = -1000000000.0
SCALE = HD ** (-0.5)
BF = jnp.bfloat16
F32 = jnp.float32


def dot_nn(left, right):
    return lax.dot_general(left, right, (((1,), (0,)), ((), ())), preferred_element_type=F32)


def dot_nt(left, right):
    return lax.dot_general(left, right, (((1,), (1,)), ((), ())), preferred_element_type=F32)


def dot_tn(left, right):
    return lax.dot_general(left, right, (((0,), (0,)), ((), ())), preferred_element_type=F32)


def norm_parts(rows):
    mean = jnp.mean(rows, -1, keepdims=True)
    centered = rows - mean
    inverse = lax.rsqrt(jnp.mean(centered * centered, -1, keepdims=True) + EPS)
    return centered * inverse, inverse


def norm_backward(gradient, normed, inverse, gain):
    scaled = gradient * gain
    return inverse * (
        scaled
        - jnp.mean(scaled, -1, keepdims=True)
        - normed * jnp.mean(scaled * normed, -1, keepdims=True)
    )


def place(device):
    return device // DEV_CLIP, (device % DEV_CLIP) // CORES, device % CORES


def flipped(number, by):
    low, high = number % 2, number // 2
    if by & 1:
        low = 1 - low
    if by & 2:
        high = 1 - high
    return high * 2 + low


SEND_SEMS, RECV_SEMS, LOCAL_SEMS = 104, 217, 18


def block_kernel(fused, planes, micro, tok, width, ff_own, share, ff_share, *refs):
    names = ["x", "dy", "lengths"]
    if fused:
        names += ["av", "bv", "cv_", "dv", "ev", "fv"] + ["expand_bias", "query_bias", "value_bias", "wq", "wk", "wv", "we", "wo", "ws"]
    else:
        names += ["vec", "wq", "we", "wo", "ws"]
    names += ["bo", "ig", "vo", "vt", "gq", "ge", "go", "gs"]
    if fused:
        names += ["Lq", "Le", "Lo", "Ls"]
    names += ["Wq", "We", "Wo", "Ws", "xg", "dyg", "a2g", "drg", "act", "dhid"]
    names += ["q", "kv", "mixed", "lse", "dmix", "dq", "dl"]
    names += ["sb", "sbo", "rb", "rbo", "resid", "dresid", "vfin", "be", "bq", "vexp", "vqkv", "vrow"]
    if fused:
        names += ["so", "oo", "ao", "aq", "ae", "alq", "ale", "cv", "cp"]
        names += [letter + end for letter in "ut" for end in ("0", "1", "2", "z", "p", "s")]
        names += ["ready_e", "ready_s", "ready_q"]
    names += ["ssem", "rsem", "lsem"]
    r = SimpleNamespace(**dict(zip(names, refs, strict=True)))
    if fused:
        r.vectors = (r.av, r.bv, r.cv_, r.dv, r.ev, r.fv)
    r.dqkv = r.dhid.at[:, :, 0:QKV_WIDTH]
    me = lax.axis_index("fsdp")
    c, k, e = place(me)
    rows = CHIPS * tok

    def chip_peer(by):
        return c * DEV_CLIP + flipped(k, by) * CORES + e

    sibling = c * DEV_CLIP + k * CORES + (1 - e)

    def plane_peer(by):
        return flipped(c, by) * DEV_CLIP + k * CORES + e

    counters = SimpleNamespace(remote=0, local=0, sends=0, free=[])
    pending = []

    def send_semaphore():
        if counters.free:
            return counters.free.pop()
        counters.sends += 1
        return counters.sends - 1

    def flush(count=None):
        for wait in pending[:len(pending) - (count or 0)]:
            wait()

    def send(src, dst, device):
        i = counters.remote
        counters.remote += 1
        out = send_semaphore()
        copy = pltpu.make_async_remote_copy(
            src_ref=src, dst_ref=dst, send_sem=r.ssem.at[out], recv_sem=r.rsem.at[i],
            device_id=(device,), device_id_type=pl.DeviceIdType.MESH,
        )
        copy.start()
        state = SimpleNamespace(sent=False)

        def wait_send():
            if not state.sent:
                state.sent = True
                counters.free.append(out)
                copy.wait_send()

        copy_handle = (copy.wait_recv, wait_send)
        pending.append(wait_send)
        return copy_handle

    def send_if(held, src, dst, device, due, arriving):
        i = counters.remote
        counters.remote += 1
        out = send_semaphore()

        def copy(source, target, to):
            return pltpu.make_async_remote_copy(
                src_ref=source, dst_ref=target, send_sem=r.ssem.at[out], recv_sem=r.rsem.at[i],
                device_id=(to,), device_id_type=pl.DeviceIdType.MESH,
            )

        @pl.when(held)
        def _():
            copy(src(), dst(), device).start()

        state = SimpleNamespace(sent=False)

        def wait_send():
            if not state.sent:
                state.sent = True
                counters.free.append(out)

                @pl.when(held)
                def _():
                    copy(src(), dst(), device).wait_send()

        def wait_recv():
            @pl.when(due)
            def _():
                copy(arriving(), arriving(), sibling).wait_recv()

        copy_handle = (wait_recv, wait_send)
        pending.append(wait_send)
        return copy_handle

    def line_group(mine, theirs):
        return SimpleNamespace(mine=mine, theirs=theirs, steps=[], swaps=[])

    def forward(group, step):
        mine, theirs = group.mine, group.theirs
        if step > 0:
            recv_all(group.steps[step - 1])
        if step < planes - 1:
            n = step + 1
            group.steps.append([
                send_if(
                    (c >= n - 1) & (c < planes - 1), lambda: mine(c - n + 1), lambda: mine(c - n + 1),
                    me + DEV_CLIP, c >= n, lambda: mine(c - n),
                ),
                send_if(
                    (c + n - 1 < planes) & (c >= 1), lambda: mine(c + n - 1), lambda: mine(c + n - 1),
                    me - DEV_CLIP, c + n < planes, lambda: mine(c + n),
                ),
            ])
        if step == 0:
            group.swaps.append(send(mine(c), theirs(c), sibling))
        else:
            for held, i in ((c >= step, c - step), (c + step < planes, c + step)):
                group.swaps.append(
                    send_if(
                        held, lambda i=i: mine(i), lambda i=i: theirs(i), sibling, held, lambda i=i: theirs(i)
                    )
                )

    def group_sent(group):
        sent_all(sum(group.steps, []) + group.swaps)

    def local(src, dst):
        i = counters.local
        counters.local += 1
        copy = pltpu.make_async_copy(src, dst, r.lsem.at[i])
        copy.start()
        return copy.wait

    def recv_all(handles):
        for handle in handles:
            handle[0]()

    def sent_all(handles):
        for handle in handles:
            handle[1]()

    Wq, We, Wo, Ws = r.Wq, r.We, r.Wo, r.Ws
    Ws2 = Ws.reshape(ff_own, width)

    def flat(ref):
        return ref.reshape(micro * rows, width)

    chip_rows = CHIPS * share
    plane_rows = CORES * chip_rows
    chip_halves = (slice(0, chip_rows // 2), slice(chip_rows // 2, chip_rows))

    def stacked(ref, count, lanes):
        return flat(ref).at[0:count * chip_rows].reshape(count, chip_rows, width).at[:, :, 0:lanes]

    def by_core(own, other):
        return jnp.where(e == 0, own, other), jnp.where(e == 0, other, own)

    def join_rows(own, other, count):
        first, second = by_core(own, other)
        pieces = []
        for j in range(count):
            pieces += [first[j * share:(j + 1) * share], second[j * share:(j + 1) * share]]
        return jnp.concatenate(pieces, 0)

    def split_rows(block, count):
        pieces = [block[j * share:(j + 1) * share] for j in range(2 * count)]
        return by_core(jnp.concatenate(pieces[0::2], 0), jnp.concatenate(pieces[1::2], 0))

    def join_planes(own, other, out):
        @pl.loop(0, planes)
        def _(i):
            block = join_rows(own[i].astype(F32), other[i].astype(F32), CHIPS)
            out[pl.ds(pl.multiple_of(i * plane_rows, plane_rows), plane_rows), :] = block.astype(BF)

    def split_planes(grads, own, other):
        @pl.loop(0, planes)
        def _(i):
            block = grads[pl.ds(pl.multiple_of(i * plane_rows, plane_rows), plane_rows), :].astype(F32)
            mine, theirs = split_rows(block, CHIPS)
            own[i] = mine.astype(BF)
            other[i] = theirs.astype(BF)

    k_x, k_y, k_far = flipped(k, 1), flipped(k, 2), flipped(k, 3)
    x_peer, y_peer, far_peer = chip_peer(1), chip_peer(2), chip_peer(3)
    top, low = slice(0, tok // 2), slice(tok // 2, tok)

    def gather_start(src, dst, b):
        return [dst.at[b], [send(src, dst.at[b, k], x_peer), send(src, dst.at[b, k], y_peer)]]

    def gather_relay(gather):
        dst, handles = gather
        handles[0][0]()
        handles.append(send(dst.at[k_x, top], dst.at[k_x, top], y_peer))
        handles[1][0]()
        handles.append(send(dst.at[k_y, low], dst.at[k_y, low], x_peer))

    def gather_finish(gather):
        recv_all(gather[1][2:])

    def reduce_start(slots, landing, b):
        slots, landing = slots.at[b], landing.at[b]
        return [slots, landing, [
            send(slots.at[k_far, top], landing.at[2, top], x_peer),
            send(slots.at[k_far, low], landing.at[2, low], y_peer),
            send(slots.at[k_x, top], landing.at[0, top], x_peer),
            send(slots.at[k_y, low], landing.at[1, low], y_peer),
        ]]

    def reduce_relay(reduction):
        slots, landing, handles = reduction
        handles[0][0]()
        slots[k_y, top] = (slots[k_y, top].astype(F32) + landing[2, top].astype(F32)).astype(BF)
        handles.append(send(slots.at[k_y, top], landing.at[1, top], y_peer))
        handles[1][0]()
        slots[k_x, low] = (slots[k_x, low].astype(F32) + landing[2, low].astype(F32)).astype(BF)
        handles.append(send(slots.at[k_x, low], landing.at[0, low], x_peer))

    def reduce_finish(reduction):
        slots, landing, handles = reduction
        recv_all(handles[2:])
        return slots[k].astype(F32) + landing[0].astype(F32) + landing[1].astype(F32)

    sb, sbo, rb, rbo = r.sb, r.sbo, r.rb, r.rbo
    vfin = r.vfin

    def vec_row(index):
        return vfin[index:index + 1, :]

    def add_row(index, value):
        r.vrow[index:index + 1, :] += value

    def norm_one(b):
        x_local[b]()
        gather_finish(x_gather[b])
        sent_all(x_gather[b][1])

        @pl.loop(0, CHIPS)
        def _(i):
            normed, _inverse = norm_parts(r.xg[b, i].astype(F32))
            r.xg[b, i] = (normed * vec_row(ROW_GAIN_ONE) + vec_row(ROW_SHIFT_ONE)).astype(BF)

    a1_rows = r.xg.reshape(micro, rows, width)
    a2_rows = r.a2g.reshape(micro, rows, width)
    dy_rows = r.dyg.reshape(micro, rows, width)
    dr_rows = r.drg.reshape(micro, rows, width)
    half = rows // 2

    def project(b):
        @pl.loop(0, 2)
        def _(i):
            at = pl.ds(pl.multiple_of(i * half, half), half)
            out = (dot_nn(a1_rows[b, at, :], Wq[...]) + r.bq[...]).astype(BF)
            for h in range(OWN_HEADS):
                r.q[b, h, at, :] = out[:, h * HD:(h + 1) * HD]
                for part in range(2):
                    low = (part + 1) * OWN_FEATURES + h * HD
                    r.kv[b, part, h, e, at, :] = out[:, low:low + HD]

        return [send(r.kv.at[b, :, :, e], r.kv.at[b, :, :, e], sibling)]

    keys = CORES * rows
    chunk_places = [(2 * (i % CHIPS) + i // CHIPS) * tok for i in range(DEV_CLIP)]

    def masked_scores(b, key_rows, query_rows):
        raw = dot_nt(key_rows, query_rows)
        index = lax.broadcasted_iota(jnp.int32, (tok, raw.shape[1]), 0)
        length = r.lengths[b, c]
        return jnp.concatenate(
            [
                raw[i * tok:(i + 1) * tok] * SCALE
                if first + tok <= keys // 2
                else jnp.where(index < length - first, raw[i * tok:(i + 1) * tok] * SCALE, NEG)
                for i, first in enumerate(chunk_places)
            ],
            0,
        )

    def attend(b, start, stop):
        @pl.loop(start, stop)
        def _(step):
            h, part = step // 2, step % 2
            at = pl.ds(pl.multiple_of(part * half, half), half)
            key_rows = r.kv[b, 0, h].reshape(keys, HD)
            value_rows = r.kv[b, 1, h].reshape(keys, HD)
            scores = masked_scores(b, key_rows, r.q[b, h, at, :])
            peak = jnp.max(scores, 0, keepdims=True)
            exponent = jnp.exp(scores - peak)
            sums = jnp.sum(exponent, 0, keepdims=True)
            probs = (exponent * (1.0 / sums)).astype(BF)
            r.lse[b, h, :, at] = peak + jnp.log(sums)
            r.mixed[b, h, :, at] = dot_tn(value_rows, probs).astype(BF)

    def tiles(start, stop, body):
        @pl.loop(start, stop)
        def _(i):
            body(pl.ds(pl.multiple_of(i * TILE, TILE), TILE))

    def partial_sum(slots, b, product):
        view = slots.reshape(micro, rows, width)

        def body(at):
            view[b, :, at] = product(at).astype(BF)

        tiles(0, width // TILE, body)

    mixed = r.mixed.reshape(micro, OWN_FEATURES, rows)

    def mix_out(b):
        partial_sum(sb, b, lambda at: dot_tn(mixed[b], Wo[:, at]))
        return reduce_start(sb, rb, b)

    def norm_two(b, reduction):
        residual = r.x[b].astype(F32) + reduce_finish(reduction) + vec_row(ROW_BIAS_OUT)
        r.resid[b] = residual
        normed, _inverse = norm_parts(residual)
        r.a2g[b, k] = (normed * vec_row(ROW_GAIN_TWO) + vec_row(ROW_SHIFT_TWO)).astype(BF)
        return gather_start(r.a2g.at[b, k], r.a2g, b)

    def feed(b, start, stop):
        def body(at):
            hidden = dot_nn(a2_rows[b], We[:, at]) + r.be[:, at]
            grad_active = dot_nt(dy_rows[b], Ws2[at, :]).astype(BF).astype(F32)
            normal = 0.5 * (1.0 + lax.erf(hidden * 0.7071067811865476))
            r.act[b, :, at] = (hidden * normal).astype(BF)
            density = jnp.exp(-0.5 * hidden * hidden) * 0.3989422804014327
            grad_hidden = (grad_active * (normal + hidden * density)).astype(BF)
            r.dhid[b, :, at] = grad_hidden
            r.vexp[:, at] += jnp.sum(grad_hidden.astype(F32), 0, keepdims=True)

        tiles(start, stop, body)

    def hidden_back(b, earlier):
        sent_all(earlier[2])
        partial_sum(sb, b, lambda at: dot_nt(r.dhid[b], We[at, :]))
        return reduce_start(sb, rb, b)

    def finish_hidden(b, reduction):
        gradient = reduce_finish(reduction)
        normed, inverse = norm_parts(r.resid[b])
        dy_own = r.dy[b].astype(F32)
        total = dy_own + norm_backward(gradient, normed, inverse, vec_row(ROW_GAIN_TWO))
        r.dresid[b] = total
        r.drg[b, k] = total.astype(BF)
        gather = gather_start(r.drg.at[b, k], r.drg, b)
        add_row(ROW_GAIN_TWO, jnp.sum(gradient * normed, 0, keepdims=True))
        add_row(ROW_SHIFT_TWO, jnp.sum(gradient, 0, keepdims=True))
        add_row(ROW_BIAS_OUT, jnp.sum(total, 0, keepdims=True))
        add_row(ROW_BIAS_SHRINK, jnp.sum(dy_own, 0, keepdims=True))
        return gather

    def weight_gradient(count, lefts, rights, out):
        def body(at):
            total = dot_tn(lefts[0, :, at], rights[0])
            for b in range(1, micro):
                total = total + dot_tn(lefts[b, :, at], rights[b])
            out[at, :] = total.astype(BF)

        tiles(0, count // TILE, body)

    def mixed_gradient(b):
        @pl.loop(0, 2)
        def _(i):
            at = pl.ds(pl.multiple_of(i * half, half), half)
            out = dot_nt(dr_rows[b, at, :], Wo[...]).astype(BF)
            for h in range(OWN_HEADS):
                r.dmix[h, at, :] = out[:, h * HD:(h + 1) * HD]

    def attend_back(b, start, stop):
        @pl.loop(start, stop)
        def _(h):
            key_rows = r.kv[b, 0, h].reshape(keys, HD)
            value_rows = r.kv[b, 1, h].reshape(keys, HD)
            grad_keys = None
            grad_values = None
            for part in range(2):
                at = pl.ds(part * half, half)
                query_rows = r.q[b, h, at, :]
                mix_rows = r.dmix[h, at, :]
                probs = jnp.exp(masked_scores(b, key_rows, query_rows) - r.lse[b, h, :, at])
                grad_probs = dot_nt(value_rows, mix_rows)
                inner = jnp.sum(probs * grad_probs, 0, keepdims=True)
                grad_scores = (probs * (grad_probs - inner)).astype(BF)
                grad_query = dot_tn(key_rows, grad_scores) * SCALE
                r.dq[h, at, :] = grad_query.T.astype(BF)
                key_term = dot_nn(grad_scores, query_rows)
                value_term = dot_nn(probs.astype(BF), mix_rows)
                grad_keys = key_term if grad_keys is None else grad_keys + key_term
                grad_values = value_term if grad_values is None else grad_values + value_term
            r.kv[b, 0, h] = (grad_keys * SCALE).astype(BF).reshape(CORES, rows, HD)
            r.kv[b, 1, h] = grad_values.astype(BF).reshape(CORES, rows, HD)

    def swap_back(b, start, stop):
        return [send(r.kv.at[b, :, start:stop, 1 - e], r.dl.at[b, :, start:stop], sibling)]

    def join_gradients(b, handles):
        recv_all(handles)

        @pl.loop(0, CHIPS)
        def _(i):
            at = pl.ds(pl.multiple_of(i * tok, tok), tok)
            pieces = [r.dq[h, at, :] for h in range(OWN_HEADS)]
            for part in range(2):
                for h in range(OWN_HEADS):
                    pair = r.kv[b, part, h, e, at, :].astype(F32) + r.dl[b, part, h, at, :].astype(F32)
                    pieces.append(pair.astype(BF))
            pieces.append(jnp.zeros((tok, QKV_WIDTH - 3 * OWN_FEATURES), BF))
            line = jnp.concatenate(pieces, 1)
            r.dqkv[b, at, :] = line
            r.vqkv[...] += jnp.sum(line.astype(F32), 0, keepdims=True)

    def input_start(b, earlier):
        sent_all(earlier[2])
        partial_sum(sb, b, lambda at: dot_nt(r.dqkv[b], Wq[at, :]))
        return reduce_start(sb, rb, b)

    def finish_input(b, reduction):
        gradient = reduce_finish(reduction)
        normed, inverse = norm_parts(r.x[b].astype(F32))
        back = norm_backward(gradient, normed, inverse, vec_row(ROW_GAIN_ONE))
        r.ig[b] = (r.dresid[b] + back).astype(BF)
        add_row(ROW_GAIN_ONE, jnp.sum(gradient * normed, 0, keepdims=True))
        add_row(ROW_SHIFT_ONE, jnp.sum(gradient, 0, keepdims=True))

    def finish_out(b, reduction):
        total = r.resid[b] + reduce_finish(reduction) + vec_row(ROW_BIAS_SHRINK)
        r.bo[b] = total.astype(BF)

    def sum_group(space, slots):
        return SimpleNamespace(space=space, slots=slots, right={}, left={})

    def add_passing(group, hops):
        space, slots = group.space, group.slots
        for side, held, i, slot in (
            (group.right, (c >= 1) & (c - 1 + hops < planes), c - 1 + hops, hops - 1),
            (group.left, (c <= planes - 2) & (c + 1 - hops >= 0), c + 1 - hops, 5 - hops),
        ):
            side[hops][0]()

            @pl.when(held)
            def _():
                space[i] = (space[i].astype(F32) + slots[slot][...].astype(F32)).astype(BF)

    def sum_step(group, hops):
        space, slots = group.space, group.slots
        if hops < planes - 1:
            add_passing(group, hops + 1)
        group.right[hops] = send_if(
            c + hops < planes, lambda: space.at[c + hops], lambda: slots[hops - 1], me + DEV_CLIP,
            (c >= 1) & (c - 1 + hops < planes), lambda: slots[hops - 1],
        )
        group.left[hops] = send_if(
            c - hops >= 0, lambda: space.at[c - hops], lambda: slots[5 - hops], me - DEV_CLIP,
            (c <= planes - 2) & (c + 1 - hops >= 0), lambda: slots[5 - hops],
        )

    def sum_finish(group, out):
        space, slots = group.space, group.slots
        out(space[c].astype(F32), False)
        for side, held, slot in ((group.right, c >= 1, 0), (group.left, c <= planes - 2, 4)):
            side[1][0]()

            @pl.when(held)
            def _():
                out(slots[slot][...].astype(F32), True)

    def to_blocks(ref, first):
        def put(total, more):
            for j in range(total.shape[0] // share):
                piece = total[j * share:(j + 1) * share]
                ref[first + j] = ref[first + j] + piece if more else piece

        return put

    def to_rows(ref):
        def put(total, more):
            ref[...] = ref[...] + total if more else total

        return put

    def sibling_add(handles, landing, fetched, out, mine):
        recv_all(handles)
        sent_all(handles)
        local(landing, fetched)()

        @pl.loop(0, planes)
        def _(i):
            out[i] = (mine(i).astype(F32) + fetched[i].astype(F32)).astype(BF)

    def free_slots(ready):
        for side, held, device in ((0, c >= 1, me - DEV_CLIP), (1, c <= planes - 2, me + DEV_CLIP)):

            @pl.when(held)
            def _():
                pl.semaphore_signal(
                    ready.at[1 - side], inc=1, device_id=(device,), device_id_type=pl.DeviceIdType.MESH
                )

    def await_slots(ready):
        for side, held in ((0, c >= 1), (1, c <= planes - 2)):

            @pl.when(held)
            def _():
                pl.semaphore_wait(ready.at[side], 1)

    resid, dresid = r.resid, r.dresid
    x_local = [local(r.x.at[b], r.xg.at[b, k]) for b in range(micro)]
    dy_local = [local(r.dy.at[b], r.dyg.at[b, k]) for b in range(micro)]
    x_gather = [None] * micro
    dy_gather = [None] * micro
    if fused:
        expand = [dresid.at[0, 0:share], dresid.at[0, share:2 * share], dresid.at[0, 2 * share:3 * share], dresid.at[1, 0:share]]
        first_rows = tok - share
        loads = [local(ref, resid.at[0, i * share:(i + 1) * share]) for i, ref in enumerate((r.wq, r.wk, r.wv))]
        loads.append(local(r.wo, resid.at[1, 0:share]))
        expand_loads = [local(r.we.at[:, i * width:(i + 1) * width], expand[i]) for i in range(planes)]
        expand_loads.append(local(r.ws.at[0:first_rows], resid.at[1, share:tok]))
        expand_loads.append(local(r.ws.at[first_rows:ff_share], dresid.at[1, share:ff_share - first_rows + share]))
        peers = [chip_peer(by) for by in (1, 2, 3)] + [sibling]
        if fused:
            peers += [plane_peer(by) for by in range(1, planes)]
        barrier = pltpu.get_barrier_semaphore()
        for peer in peers:
            pl.semaphore_signal(barrier, inc=1, device_id=(peer,), device_id_type=pl.DeviceIdType.MESH)
        for load in loads:
            load()
        matrices = [resid[0, i * share:(i + 1) * share] for i in range(3)]
        for j in range(CHIPS):
            pieces = [
                matrix[:, (i * CHIPS + j) * HD:(i * CHIPS + j + 1) * HD] for matrix in matrices for i in range(planes)
            ]
            pieces.append(jnp.zeros((share, QKV_WIDTH - 3 * OWN_FEATURES), F32))
            r.aq[j] = jnp.concatenate(pieces, 1).astype(BF)
        r.so[c] = resid[1, 0:share].astype(BF)
        compact = jnp.concatenate([jnp.pad(ref[...], ((0, 0), (0, 256 - share))) for ref in r.vectors], 0)
        tail = jnp.pad(r.expand_bias[...], ((0, 0), (0, 256 - ff_share)))
        pair = [jnp.pad(ref[...], ((0, 0), (0, 128 - share))) for ref in (r.query_bias, r.value_bias)]
        r.cv[c] = jnp.concatenate([compact, tail, jnp.concatenate(pair, 1)], 0)
        pl.semaphore_wait(barrier, len(peers))
        wq_mine, wq_other = stacked(r.drg, planes, QKV_WIDTH), stacked(r.a2g, planes, QKV_WIDTH)
        we_mine, we_other = stacked(r.act, planes, ff_own), stacked(r.dhid, planes, ff_own)
        lines_q = [
            line_group(lambda i, at=at: wq_mine.at[i, at], lambda i, at=at: wq_other.at[i, at]) for at in chip_halves
        ]
        line_e = line_group(lambda i: we_mine.at[i], lambda i: we_other.at[i])
        line_o = line_group(lambda i: r.so.at[i], lambda i: r.oo.at[i])
        line_s = line_group(lambda i: Ws.at[i, e], lambda i: Ws.at[i, e])

        def pack_plane(blocks, out):
            out[c] = jnp.concatenate([blocks[j].astype(F32) for j in range(CHIPS)], 0).astype(BF)

        wq_plane = [send(r.aq.at[flipped(k, by)], r.alq.at[k], chip_peer(by)) for by in (3, 1, 2)]
        vec_z = [send(r.cv.at[c], r.cv.at[c], plane_peer(by)) for by in range(1, planes)]
        forward(line_o, 0)
        r.alq[k] = r.aq[k]
        recv_all(vec_z)
        r.cp[e, k] = r.cv[...]
        vec_p = [send(r.cv, r.cp.at[e, k], chip_peer(by)) for by in (1, 2, 3)]
        x_gather[0] = gather_start(r.x.at[0], r.xg, 0)
        recv_all(wq_plane)
        pack_plane(r.alq, wq_mine)
        for line in lines_q:
            forward(line, 0)
        for load in expand_loads:
            load()
        ff_part = width // planes
        for j in range(CHIPS):
            pieces = [block[:, j * ff_part:(j + 1) * ff_part] for block in expand]
            r.ae[j] = jnp.concatenate(pieces, 1).astype(BF)
        we_plane = [send(r.ae.at[flipped(k, by)], r.ale.at[k], chip_peer(by)) for by in (3, 1, 2)]
        r.ale[k] = r.ae[k]
        rows_s = [resid[1, share:tok], dresid[1, share:ff_share - first_rows + share]]
        Ws[c, e] = jnp.concatenate(rows_s, 0).astype(BF)
        recv_all(vec_p)
        vec_s = [send(r.cp.at[e], r.cp.at[e], sibling)]
        recv_all(vec_s)
        places = [(i, f) for i in range(planes) for f in range(CORES)]
        vfin[...] = jnp.concatenate(
            [r.cp[f, j, i][:, 0:share] for i in range(planes) for j in range(CHIPS) for f in range(CORES)], 1
        )
        r.be[...] = jnp.concatenate([r.cp[f, k, i][6:7, 0:ff_share] for i, f in places], 1)
        bias = [jnp.concatenate([r.cp[f, k, i][7:8, at:at + share] for i, f in places], 1) for at in (0, 128)]
        blank = jnp.zeros((1, OWN_FEATURES), F32)
        r.bq[...] = jnp.concatenate([bias[0], blank, bias[1], blank[:, :QKV_WIDTH - 3 * OWN_FEATURES]], 1)
        gather_relay(x_gather[0])
        x_gather[1] = gather_start(r.x.at[1], r.xg, 1)
        forward(line_o, 1)
        for line in lines_q:
            forward(line, 1)
        recv_all(we_plane)
        pack_plane(r.ale, we_mine)
    else:
        peers = [chip_peer(by) for by in (1, 2, 3)] + [sibling]
        if fused:
            peers += [plane_peer(by) for by in range(1, planes)]
        barrier = pltpu.get_barrier_semaphore()
        for peer in peers:
            pl.semaphore_signal(barrier, inc=1, device_id=(peer,), device_id_type=pl.DeviceIdType.MESH)
        pl.semaphore_wait(barrier, len(peers))
        loads = [local(r.wq, Wq), local(r.we, We), local(r.wo, Wo), local(r.ws, Ws2)]
        for b in range(micro):
            x_gather[b] = gather_start(r.x.at[b], r.xg, b)
        vfin[...] = r.vec[...]
        r.be[...] = r.vec[6:7, :]
        r.bq[...] = r.vec[7:8, :QKV_WIDTH]
        gather_relay(x_gather[0])
        for load in loads:
            load()
    for ref in (r.vrow, r.vexp, r.vqkv):
        ref[...] = jnp.zeros_like(ref)
    norm_one(0)
    if fused:
        forward(line_o, 2)
        for line in lines_q:
            forward(line, 2)
        forward(line_e, 0)
        forward(line_s, 0)
    gather_relay(x_gather[1])
    dy_gather[0] = gather_start(r.dy.at[0], r.dyg, 0)
    norm_one(1)
    if fused:
        forward(line_o, 3)
        for line in lines_q:
            forward(line, 3)
        for line in lines_q:
            recv_all(line.swaps)
        join_planes(wq_mine, wq_other, Wq)
    kv_swap = [None] * micro
    kv_swap[0] = project(0)
    gather_relay(dy_gather[0])
    dy_gather[1] = gather_start(r.dy.at[1], r.dyg, 1)
    kv_swap[1] = project(1)
    recv_all(kv_swap[0])
    attend(0, 0, OWN_HEADS)
    if fused:
        forward(line_e, 1)
    attend(0, OWN_HEADS, 2 * OWN_HEADS)
    if fused:
        recv_all(line_o.swaps)
        for i in range(planes):
            pair = join_rows(r.so[i].astype(F32), r.oo[i].astype(F32), 1)
            Wo[i * HD:(i + 1) * HD, :] = pair.astype(BF)
    mix_reduce = [mix_out(0), None]
    gather_relay(dy_gather[1])
    recv_all(kv_swap[1])
    attend(1, 0, OWN_HEADS)
    if fused:
        forward(line_s, 1)
    attend(1, OWN_HEADS, 2 * OWN_HEADS - 1)
    reduce_relay(mix_reduce[0])
    attend(1, 2 * OWN_HEADS - 1, 2 * OWN_HEADS)
    mix_reduce[1] = mix_out(1)
    if fused:
        forward(line_e, 2)
    second_gather = [norm_two(0, mix_reduce[0]), None]
    if fused:
        forward(line_s, 2)
    reduce_relay(mix_reduce[1])
    gather_relay(second_gather[0])
    second_gather[1] = norm_two(1, mix_reduce[1])
    if fused:
        forward(line_e, 3)
        recv_all(line_e.swaps)
        group_sent(line_e)
        for line in lines_q:
            group_sent(line)
        join_planes(we_mine, we_other, We)
    gather_finish(second_gather[0])
    dy_local[0]()
    gather_finish(dy_gather[0])
    if fused:
        forward(line_s, 3)
        recv_all(line_s.swaps)
    flush(20)
    feed(0, 0, 3)
    gather_relay(second_gather[1])
    feed(0, 3, ff_own // TILE)
    hidden_reduce = [hidden_back(0, mix_reduce[0]), None]
    gather_finish(second_gather[1])
    dy_local[1]()
    gather_finish(dy_gather[1])
    feed(1, 0, ff_own // TILE)
    reduce_relay(hidden_reduce[0])
    hidden_reduce[1] = hidden_back(1, mix_reduce[1])
    weight_gradient(width, a2_rows, r.dhid, We)
    resid_gather = [finish_hidden(0, hidden_reduce[0]), None]
    if fused:
        sent_all(wq_plane + we_plane)
        group_sent(line_o)
        group_sent(line_s)
        sent_all(second_gather[0][1] + second_gather[1][1])
        free_slots(r.ready_e)
        parts_e = We.reshape(planes, 2, chip_rows, ff_own)
        split_planes(We, parts_e.at[:, 0], parts_e.at[:, 1])
        ge_s = [send(parts_e.at[:, 1], r.Le, sibling)]
    partial_sum(sbo, 0, lambda at: dot_nn(r.act[0], Ws2[:, at]))
    if fused:
        sum_e = sum_group(parts_e.at[:, 0], [flat(r.a2g).at[i * chip_rows:(i + 1) * chip_rows] for i in range(5)])
        sibling_add(ge_s, r.Le, parts_e.at[:, 1], parts_e.at[:, 0], lambda i: parts_e[i, 0])
        await_slots(r.ready_e)
        sum_step(sum_e, 3)
    partial_sum(sbo, 1, lambda at: dot_nn(r.act[1], Ws2[:, at]))
    reduce_relay(hidden_reduce[1])
    weight_gradient(ff_own, r.act, dy_rows, Ws2)
    if fused:
        sent_all(dy_gather[0][1] + dy_gather[1][1])
        free_slots(r.ready_s)
        gs_s = [send(Ws.at[:, 1 - e], r.Ls, sibling)]
    gather_relay(resid_gather[0])
    if fused:
        places_s = [flat(r.a2g).at[5 * ff_share:6 * ff_share]]
        for ref in (r.dyg, r.act):
            places_s += [flat(ref).at[i * ff_share:(i + 1) * ff_share] for i in (4, 5)]
        sum_s = sum_group(Ws.at[:, e], places_s)
        sibling_add(gs_s, r.Ls, Ws.at[:, 1 - e], Ws.at[:, e], lambda i: Ws[i, e])
        await_slots(r.ready_s)
        sum_step(sum_s, 3)
    resid_gather[1] = finish_hidden(1, hidden_reduce[1])
    if fused:
        sum_step(sum_e, 2)
    flush(20)
    gather_finish(resid_gather[0])
    mixed_gradient(0)
    sent_all(kv_swap[0] + kv_swap[1])
    attend_back(0, 0, 2)
    gather_relay(resid_gather[1])
    out_reduce = [reduce_start(sbo, rbo, 0), None]
    if fused:
        sum_step(sum_s, 2)
    attend_back(0, 2, OWN_HEADS)
    swap = swap_back(0, 0, OWN_HEADS)
    gather_finish(resid_gather[1])
    mixed_gradient(1)
    lead = dot_nn(mixed[0], dr_rows[0])
    for other in range(1, micro):
        lead = lead + dot_nn(mixed[other], dr_rows[other])
    if fused:
        space_o, other_o = r.so, r.oo
        for i in range(planes):
            mine, theirs = split_rows(lead[i * HD:(i + 1) * HD], 1)
            space_o[i] = mine.astype(BF)
            other_o[i] = theirs.astype(BF)
        go_s = [send(other_o, r.Lo, sibling)]
    else:
        Wo[...] = lead.astype(BF)
    join_gradients(0, swap)
    input_reduce = [input_start(0, hidden_reduce[0]), None]
    if fused:
        sum_step(sum_e, 1)
    attend_back(1, 0, 2)
    last_swap = swap_back(1, 0, 2)
    reduce_relay(out_reduce[0])
    if fused:
        sum_o = sum_group(space_o, [r.ao.at[i] for i in range(5)])
        sibling_add(go_s, r.Lo, other_o, space_o, lambda i: space_o[i])
        sum_step(sum_s, 1)
        sum_step(sum_o, 3)
    attend_back(1, 2, OWN_HEADS)
    last_swap += swap_back(1, 2, OWN_HEADS)
    reduce_relay(input_reduce[0])
    join_gradients(1, last_swap)
    input_reduce[1] = input_start(1, hidden_reduce[1])
    weight_gradient(width, a1_rows, r.dqkv, Wq)
    flush(20)
    if fused:
        free_slots(r.ready_q)
        parts_q = Wq.reshape(planes, 2, chip_rows, QKV_WIDTH)
        split_planes(Wq, parts_q.at[:, 0], parts_q.at[:, 1])
        gq_s = [send(parts_q.at[:, 1], r.Lq, sibling)]
        sum_step(sum_o, 2)
        five = stacked(r.dhid, 5, QKV_WIDTH)
        sums_q = [sum_group(parts_q.at[:, 0, at], [five.at[i, at] for i in range(5)]) for at in chip_halves]
    finish_input(0, input_reduce[0])
    if fused:
        sibling_add(gq_s, r.Lq, parts_q.at[:, 1], parts_q.at[:, 0], lambda i: parts_q[i, 0])
        await_slots(r.ready_q)
        for group in sums_q:
            sum_step(group, 3)
    def vector_step(group, step, last):
        zero, one, two, from_z, from_plane, from_core = group
        if step == 0:
            return [send(zero, from_core, sibling)]
        if step == 1:
            one[...] = zero[...] + from_core[...]
            return [send(one, from_z.at[by - 1], plane_peer(by)) for by in range(1, planes)]
        if step == 2:
            total = one[...]
            for by in range(1, planes):
                total = total + from_z[by - 1]
            two[...] = total
            return [send(two, from_plane.at[by - 1], chip_peer(by)) for by in (1, 2, 3)]
        others = from_plane[0] + from_plane[1] + from_plane[2]
        shared = lax.broadcasted_iota(jnp.int32, others.shape, 0) < 6
        last[...] = two[...] + jnp.where(shared, others, 0.0)

    if fused:
        group_u = (r.u0, r.u1, r.u2, r.uz, r.up, r.us)
        group_t = (r.t0, r.t1, r.t2, r.tz, r.tp, r.ts)
    padded = jnp.concatenate([r.vqkv[...], jnp.zeros((1, width - QKV_WIDTH), F32)], 1)
    early = jnp.concatenate([r.vrow[0:6, :], r.vexp[...], padded], 0)
    if fused:
        r.u0[...] = early
        moved = vector_step(group_u, 0, None)
    reduce_relay(input_reduce[1])
    out_reduce[1] = reduce_start(sbo, rbo, 1)
    finish_out(0, out_reduce[0])
    if fused:
        recv_all(moved)
        moved = vector_step(group_u, 1, None)
        sum_finish(sum_s, to_rows(r.gs))
        sum_finish(sum_e, to_blocks(r.ge, 0))
        for j in range(CHIPS):
            r.ae[j] = r.ge[j].astype(BF)
        sum_step(sum_o, 1)
    if fused:
        ge_p = [send(r.ae.at[flipped(k, by)], r.ale.at[k], chip_peer(by)) for by in (3, 1, 2)]
        recv_all(moved)
        moved = vector_step(group_u, 2, None)
        for group in sums_q:
            sum_step(group, 2)
    finish_input(1, input_reduce[1])
    late = r.vrow[0:2, :]
    if fused:
        r.t0[...] = late
        moved_late = vector_step(group_t, 0, None)
    reduce_relay(out_reduce[1])
    if fused:
        recv_all(moved)
        vector_step(group_u, 3, r.vo)
        recv_all(ge_p)
        for by in (1, 2, 3):
            r.ge[flipped(k, by)] = r.ale[flipped(k, by)].astype(F32)
        recv_all(moved_late)
        moved_late = vector_step(group_t, 1, None)
        for group in sums_q:
            sum_step(group, 1)
        recv_all(moved_late)
        moved_late = vector_step(group_t, 2, None)
        sum_finish(sum_o, to_rows(r.go))
        recv_all(moved_late)
        vector_step(group_t, 3, r.vt)
    finish_out(1, out_reduce[1])
    if fused:
        for i, group in enumerate(sums_q):
            sum_finish(group, to_blocks(r.gq, i * CHIPS // 2))
        for j in range(CHIPS):
            r.aq[j] = r.gq[j].astype(BF)
        gq_p = [send(r.aq.at[flipped(k, by)], r.alq.at[k], chip_peer(by)) for by in (3, 1, 2)]
        recv_all(gq_p)
        for by in (1, 2, 3):
            r.gq[flipped(k, by)] = r.alq[flipped(k, by)].astype(F32)
    else:
        r.vo[...] = early
        r.vt[...] = late
        stores = [local(Wq, r.gq), local(We, r.ge), local(Wo, r.go), local(Ws2, r.gs)]
        for store in stores:
            store()
    flush()


def run_block(fused, planes, x, dy, lengths, vectors, weights_in, share, ff_share):
    micro, tok, width = x.shape
    ff_own = width
    rows = CHIPS * tok
    vmem = pl.BlockSpec(memory_space=pltpu.VMEM)
    anywhere = pl.BlockSpec(memory_space=pl.ANY)
    smem = pl.BlockSpec(memory_space=pltpu.SMEM)

    def shape(*dims, dtype=BF):
        return jax.ShapeDtypeStruct(dims, dtype)

    outs = [
        (shape(micro, tok, width), vmem),
        (shape(micro, tok, width), vmem),
        (shape(8, width, dtype=F32), vmem),
        (shape(2, width, dtype=F32), vmem),
    ]
    if fused:
        outs += [
            (shape(CHIPS, share, QKV_WIDTH, dtype=F32), vmem),
            (shape(CHIPS, share, ff_own, dtype=F32), vmem),
            (shape(share, width, dtype=F32), vmem),
            (shape(ff_share, width, dtype=F32), vmem),
        ]
        outs += [
            (shape(planes, CHIPS * share, QKV_WIDTH), anywhere),
            (shape(planes, CHIPS * share, ff_own), anywhere),
            (shape(planes, share, width), anywhere),
            (shape(planes, ff_share, width), anywhere),
        ]
    else:
        outs += [
            (shape(width, QKV_WIDTH), anywhere),
            (shape(width, ff_own), anywhere),
            (shape(OWN_FEATURES, width), anywhere),
            (shape(ff_own, width), anywhere),
        ]
    if fused:
        weights = [
            pltpu.VMEM((width, QKV_WIDTH), BF),
            pltpu.VMEM((width, ff_own), BF),
            pltpu.VMEM((OWN_FEATURES, width), BF),
            pltpu.VMEM((planes, CORES, ff_share, width), BF),
        ]
    else:
        weights = [
            pltpu.VMEM((width, QKV_WIDTH), BF),
            pltpu.VMEM((width, ff_own), BF),
            pltpu.VMEM((OWN_FEATURES, width), BF),
            pltpu.VMEM((ff_own, width), BF),
        ]
    scratch = weights + [
        pltpu.VMEM((micro, CHIPS, tok, width), BF),
        pltpu.VMEM((micro, CHIPS, tok, width), BF),
        pltpu.VMEM((micro, CHIPS, tok, width), BF),
        pltpu.VMEM((micro, CHIPS, tok, width), BF),
        pltpu.VMEM((micro, rows, ff_own), BF),
        pltpu.VMEM((micro, rows, ff_own), BF),
        pltpu.VMEM((micro, OWN_HEADS, rows, HD), BF),
        pltpu.VMEM((micro, 2, OWN_HEADS, CORES, rows, HD), BF),
        pltpu.VMEM((micro, OWN_HEADS, HD, rows), BF),
        pltpu.VMEM((micro, OWN_HEADS, 1, rows), F32),
        pltpu.VMEM((OWN_HEADS, rows, HD), BF),
        pltpu.VMEM((OWN_HEADS, rows, HD), BF),
        pltpu.VMEM((micro, 2, OWN_HEADS, rows, HD), BF),
        pltpu.VMEM((micro, CHIPS, tok, width), BF),
        pltpu.VMEM((micro, CHIPS, tok, width), BF),
        pltpu.VMEM((micro, CHIPS - 1, tok, width), BF),
        pltpu.VMEM((micro, CHIPS - 1, tok, width), BF),
        pltpu.VMEM((micro, tok, width), F32),
        pltpu.VMEM((micro, tok, width), F32),
        pltpu.VMEM((8, width), F32),
        pltpu.VMEM((1, ff_own), F32),
        pltpu.VMEM((1, QKV_WIDTH), F32),
        pltpu.VMEM((1, ff_own), F32),
        pltpu.VMEM((1, QKV_WIDTH), F32),
        pltpu.VMEM((8, width), F32),
    ]
    if fused:
        scratch += [
            pltpu.VMEM((planes, share, width), BF),
            pltpu.VMEM((planes, share, width), BF),
            pltpu.VMEM((5, share, width), BF),
            pltpu.VMEM((CHIPS, share, QKV_WIDTH), BF),
            pltpu.VMEM((CHIPS, share, ff_own), BF),
            pltpu.VMEM((CHIPS, share, QKV_WIDTH), BF),
            pltpu.VMEM((CHIPS, share, ff_own), BF),
        ]
        scratch += [
            pltpu.VMEM((planes, 8, 256), F32),
            pltpu.VMEM((CORES, CHIPS, planes, 8, 256), F32),
        ]
        for lines in (8, 2):
            scratch += [pltpu.VMEM((lines, width), F32) for _ in range(3)]
            scratch += [pltpu.VMEM((planes - 1, lines, width), F32), pltpu.VMEM((CHIPS - 1, lines, width), F32)]
            scratch.append(pltpu.VMEM((lines, width), F32))
        scratch += [pltpu.SemaphoreType.REGULAR((2,)) for _ in range(3)]
    scratch += [
        pltpu.SemaphoreType.DMA((SEND_SEMS,)),
        pltpu.SemaphoreType.DMA((RECV_SEMS,)),
        pltpu.SemaphoreType.DMA((LOCAL_SEMS,)),
    ]
    return pl.pallas_call(
        partial(block_kernel, fused, planes, micro, tok, width, ff_own, share, ff_share),
        out_shape=[out for out, _ in outs],
        in_specs=[vmem, vmem, smem] + [vmem] * len(vectors) + [anywhere] * len(weights_in),
        out_specs=[spec for _, spec in outs],
        scratch_shapes=scratch,
        compiler_params=pltpu.CompilerParams(
            collective_id=0, has_side_effects=True, vmem_limit_bytes=63 * 1000 * 1000
        ),
    )(x, dy, lengths, *vectors, *weights_in)


def finish_kernel(planes, share, ff_share, bo, ig, vo, vt, gq, ge, go, gs, *refs):
    device = lax.axis_index("fsdp")
    c, _, e = place(device)
    outs, (blocks_q, blocks_e, lines, last_lines, sems) = refs[:17], refs[17:]
    moves = [(vo, lines), (vt, last_lines), (gq, blocks_q), (ge, blocks_e)]
    moves += [(bo, outs[0]), (ig, outs[1]), (go, outs[6]), (gs, outs[7])]
    copies = [pltpu.make_async_copy(src, dst, sems.at[i]) for i, (src, dst) in enumerate(moves)]
    for copy in copies:
        copy.start()
    for copy in copies[:4]:
        copy.wait()
    part = ge.shape[2] // planes
    for n in range(planes):
        for j in range(CHIPS):
            at = (n * CHIPS + j) * part
            outs[5][:, at:at + part] = blocks_e[j][:, n * part:(n + 1) * part]
    for i, out in enumerate(outs[2:5]):
        first = i * OWN_FEATURES
        out[...] = jnp.concatenate(
            [blocks_q[j][:, first + n * HD:first + (n + 1) * HD] for n in range(planes) for j in range(CHIPS)], 1
        )
    vo, vt = lines, last_lines
    width = vo.shape[1]

    def own(lines, start, size):
        return pltpu.roll(lines, lax.rem(width - start, width), 1)[:, 0:size]

    early = own(vo[...], device * share, share)
    late = own(jnp.concatenate([vt[...], vo[2:8, :]], 0), device * share, share)
    expand = own(vo[...], (2 * c + e) * ff_share, ff_share)
    query = own(vo[...], (2 * c + e) * share, share)
    value = own(vo[...], 2 * OWN_FEATURES + (2 * c + e) * share, share)
    for out, line in zip(
        outs[8:],
        [late[0:1], late[1:2]] + [early[i:i + 1] for i in range(2, 6)] + [expand[6:7], query[7:8], value[7:8]],
        strict=True,
    ):
        out[...] = line
    for copy in copies[4:]:
        copy.wait()


def finish_block(planes, share, ff_share, results):
    shapes = [results[0], results[1]] + [jax.ShapeDtypeStruct((share, results[2].shape[1]), F32)] * 3
    shapes += [jax.ShapeDtypeStruct((share, CHIPS * results[5].shape[2]), F32), results[6], results[7]]
    shapes = [jax.ShapeDtypeStruct(s.shape, s.dtype) for s in shapes]
    shapes += [jax.ShapeDtypeStruct((1, share), F32)] * 6
    shapes += [jax.ShapeDtypeStruct((1, size), F32) for size in (ff_share, share, share)]
    vmem = pl.BlockSpec(memory_space=pltpu.VMEM)
    anywhere = pl.BlockSpec(memory_space=pl.ANY)
    held = [results[4], results[5], results[2], results[3]]
    return pl.pallas_call(
        partial(finish_kernel, planes, share, ff_share),
        out_shape=shapes,
        in_specs=[anywhere] * 8,
        out_specs=[vmem] * 17,
        scratch_shapes=[pltpu.VMEM(a.shape, a.dtype) for a in held] + [pltpu.SemaphoreType.DMA((8,))],
        compiler_params=pltpu.CompilerParams(vmem_limit_bytes=60 * 1000 * 1000),
    )(*results)


def by_chip(matrix, part):
    rows = matrix.shape[0]
    return matrix.reshape(rows, -1, CHIPS, part).transpose(2, 0, 1, 3).reshape(CHIPS, rows, -1)


def from_chips(blocks, part):
    rows = blocks.shape[1]
    return blocks.reshape(CHIPS, rows, -1, part).transpose(1, 2, 0, 3).reshape(rows, -1)


def body(
    inputs, cotangent, lengths, first_gain, first_shift, query_weight, query_bias, key_weight,
    value_weight, value_bias, output_weight, output_bias, second_gain, second_shift,
    expand_weight, expand_bias, shrink_weight, shrink_bias,
):
    device = lax.axis_index("fsdp")
    count = lax.axis_size("fsdp")
    c, k, e = place(device)
    planes = count // DEV_CLIP
    width = inputs.shape[2]
    share = query_weight.shape[0]
    ff_share = shrink_weight.shape[0]
    ff_part = width // 4
    fused = planes == 4 and share * 2 == HD and ff_share * 2 == ff_part
    plain = (first_gain, first_shift, second_gain, second_shift, output_bias, shrink_bias)
    matrices = (query_weight, key_weight, value_weight, expand_weight, output_weight, shrink_weight)
    if fused:
        vectors = [v.reshape(1, -1) for v in plain + (expand_bias, query_bias, value_bias)]
        got = run_block(True, planes, inputs, cotangent, lengths, vectors, matrices, share, ff_share)
        done = finish_block(planes, share, ff_share, got[:8])
        block_out, input_grad, grad_query_w, grad_key_w, grad_value_w, grad_expand_w, grad_output_w, grad_shrink_w = done[:8]
        owned = [line[0] for line in done[8:14]]
        grad_expand_b, grad_query_b, grad_value_b = (line[0] for line in done[14:])
    else:

        def whole(array):
            return lax.all_gather(array, "fsdp", axis=0, tiled=True)

        def mine(blocks):
            return lax.dynamic_index_in_dim(blocks, k, 0, keepdims=False)

        full = [whole(w.astype(BF)) for w in matrices]
        pieces = [mine(by_chip(w, HD)) for w in full[:3]]
        pieces.append(jnp.zeros((width, QKV_WIDTH - 3 * OWN_FEATURES), BF))
        wq = jnp.concatenate(pieces, 1)
        we = mine(by_chip(full[3], ff_part))
        wo = mine(by_chip(full[4].T, HD)).T
        ws = mine(by_chip(full[5].T, ff_part)).T
        bias_e = mine(by_chip(whole(expand_bias)[None], ff_part))
        bias_q = mine(by_chip(whole(query_bias)[None], HD))
        bias_v = mine(by_chip(whole(value_bias)[None], HD))
        blank = jnp.zeros((1, width - 3 * OWN_FEATURES), F32)
        bias_row = jnp.concatenate([bias_q, jnp.zeros_like(bias_q), bias_v, blank], 1)
        vec = jnp.concatenate([jnp.stack([whole(v) for v in plain]), bias_e, bias_row])
        got = run_block(False, planes, inputs, cotangent, lengths, (vec,), (wq, we, wo, ws), share, ff_share)
        block_out, input_grad, sums, late, gq, ge, go, gs = got[:8]

        def spread(block, part):
            places = lax.broadcasted_iota(jnp.int32, (CHIPS, 1, 1), 0) == k
            return from_chips(jnp.where(places, block.astype(F32)[None], 0.0), part)

        def owned_sum(array):
            return lax.psum_scatter(array, "fsdp", scatter_dimension=0, tiled=True)

        grad_query_w, grad_key_w, grad_value_w = (
            owned_sum(spread(gq[:, i * OWN_FEATURES:(i + 1) * OWN_FEATURES], HD)) for i in range(3)
        )
        grad_expand_w = owned_sum(spread(ge, ff_part))
        grad_output_w = owned_sum(spread(go.T, HD).T)
        grad_shrink_w = owned_sum(spread(gs.T, ff_part).T)
        owned = [owned_sum(late[i]) for i in range(2)] + [owned_sum(sums[i]) for i in range(2, len(plain))]
        line_q, line_v = sums[7:8, :OWN_FEATURES], sums[7:8, 2 * OWN_FEATURES:3 * OWN_FEATURES]
        grad_expand_b = owned_sum(spread(sums[6:7], ff_part)[0])
        grad_query_b = owned_sum(spread(line_q, HD)[0])
        grad_value_b = owned_sum(spread(line_v, HD)[0])
    return (
        block_out,
        input_grad,
        owned[0],
        owned[1],
        grad_query_w,
        grad_query_b,
        grad_key_w,
        grad_value_w,
        grad_value_b,
        grad_output_w,
        owned[4],
        owned[2],
        owned[3],
        grad_expand_w,
        grad_expand_b,
        grad_shrink_w,
        owned[5],
    )


def solution(mesh):
    rows, matrix, vector = P(None, "fsdp", None), P("fsdp", None), P("fsdp")
    in_specs = (
        rows, rows, P(), vector, vector, matrix, vector, matrix, matrix, vector, matrix, vector,
        vector, vector, matrix, vector, matrix, vector,
    )
    out_specs = (
        rows, rows, vector, vector, matrix, vector, matrix, matrix, vector, matrix, vector,
        vector, vector, matrix, vector, matrix, vector,
    )
    return jax.shard_map(body, mesh=mesh, in_specs=in_specs, out_specs=out_specs, check_vma=False)
```

```python
from functools import partial
from types import SimpleNamespace

import jax
import jax.numpy as jnp
from jax import lax
from jax.experimental import pallas as pl
from jax.experimental.pallas import tpu as pltpu
from jax.sharding import PartitionSpec as P

H = 16
HD = 80
CHIPS = 4
CORES = 2
DEV_CLIP = CHIPS * CORES
OWN_HEADS = H // CHIPS
OWN_FEATURES = OWN_HEADS * HD
QKV_WIDTH = 1024
TILE = 256
ROW_GAIN_ONE, ROW_SHIFT_ONE, ROW_GAIN_TWO, ROW_SHIFT_TWO, ROW_BIAS_OUT, ROW_BIAS_SHRINK = range(6)

EPS = 1e-05
NEG = -1000000000.0
SCALE = HD ** (-0.5)
BF = jnp.bfloat16
F32 = jnp.float32


def dot_nn(left, right):
    return lax.dot_general(left, right, (((1,), (0,)), ((), ())), preferred_element_type=F32)


def dot_nt(left, right):
    return lax.dot_general(left, right, (((1,), (1,)), ((), ())), preferred_element_type=F32)


def dot_tn(left, right):
    return lax.dot_general(left, right, (((0,), (0,)), ((), ())), preferred_element_type=F32)


def norm_parts(rows):
    mean = jnp.mean(rows, -1, keepdims=True)
    centered = rows - mean
    inverse = lax.rsqrt(jnp.mean(centered * centered, -1, keepdims=True) + EPS)
    return centered * inverse, inverse


def norm_backward(gradient, normed, inverse, gain):
    scaled = gradient * gain
    return inverse * (
        scaled
        - jnp.mean(scaled, -1, keepdims=True)
        - normed * jnp.mean(scaled * normed, -1, keepdims=True)
    )


def place(device):
    return device // DEV_CLIP, (device % DEV_CLIP) // CORES, device % CORES


def flipped(number, by):
    low, high = number % 2, number // 2
    if by & 1:
        low = 1 - low
    if by & 2:
        high = 1 - high
    return high * 2 + low


SEND_SEMS, RECV_SEMS, LOCAL_SEMS = 104, 217, 18


def block_kernel(fused, planes, micro, tok, width, ff_own, share, ff_share, *refs):
    names = ["x", "dy", "lengths"]
    if fused:
        names += ["av", "bv", "cv_", "dv", "ev", "fv"] + ["expand_bias", "query_bias", "value_bias", "wq", "wk", "wv", "we", "wo", "ws"]
    else:
        names += ["vec", "wq", "we", "wo", "ws"]
    names += ["bo", "ig", "vo", "vt", "gq", "ge", "go", "gs"]
    if fused:
        names += ["Lq", "Le", "Lo", "Ls"]
    names += ["Wq", "We", "Wo", "Ws", "xg", "dyg", "a2g", "drg", "act", "dhid"]
    names += ["q", "kv", "mixed", "lse", "dmix", "dq", "dl"]
    names += ["sb", "sbo", "rb", "rbo", "resid", "dresid", "vfin", "be", "bq", "vexp", "vqkv", "vrow"]
    if fused:
        names += ["so", "oo", "ao", "aq", "ae", "alq", "ale", "cv", "cp"]
        names += [letter + end for letter in "ut" for end in ("0", "1", "2", "z", "p", "s")]
        names += ["ready_e", "ready_s", "ready_q"]
    names += ["ssem", "rsem", "lsem"]
    r = SimpleNamespace(**dict(zip(names, refs, strict=True)))
    if fused:
        r.vectors = (r.av, r.bv, r.cv_, r.dv, r.ev, r.fv)
    r.dqkv = r.dhid.at[:, :, 0:QKV_WIDTH]
    me = lax.axis_index("fsdp")
    c, k, e = place(me)
    rows = CHIPS * tok

    def chip_peer(by):
        return c * DEV_CLIP + flipped(k, by) * CORES + e

    sibling = c * DEV_CLIP + k * CORES + (1 - e)

    def plane_peer(by):
        return flipped(c, by) * DEV_CLIP + k * CORES + e

    counters = SimpleNamespace(remote=0, local=0, sends=0, free=[])
    pending = []

    def send_semaphore():
        if counters.free:
            return counters.free.pop()
        counters.sends += 1
        return counters.sends - 1

    def flush(count=None):
        for wait in pending[:len(pending) - (count or 0)]:
            wait()

    def send(src, dst, device):
        i = counters.remote
        counters.remote += 1
        out = send_semaphore()
        copy = pltpu.make_async_remote_copy(
            src_ref=src, dst_ref=dst, send_sem=r.ssem.at[out], recv_sem=r.rsem.at[i],
            device_id=(device,), device_id_type=pl.DeviceIdType.MESH,
        )
        copy.start()
        state = SimpleNamespace(sent=False)

        def wait_send():
            if not state.sent:
                state.sent = True
                counters.free.append(out)
                copy.wait_send()

        copy_handle = (copy.wait_recv, wait_send)
        pending.append(wait_send)
        return copy_handle

    def send_if(held, src, dst, device, due, arriving):
        i = counters.remote
        counters.remote += 1
        out = send_semaphore()

        def copy(source, target, to):
            return pltpu.make_async_remote_copy(
                src_ref=source, dst_ref=target, send_sem=r.ssem.at[out], recv_sem=r.rsem.at[i],
                device_id=(to,), device_id_type=pl.DeviceIdType.MESH,
            )

        @pl.when(held)
        def _():
            copy(src(), dst(), device).start()

        state = SimpleNamespace(sent=False)

        def wait_send():
            if not state.sent:
                state.sent = True
                counters.free.append(out)

                @pl.when(held)
                def _():
                    copy(src(), dst(), device).wait_send()

        def wait_recv():
            @pl.when(due)
            def _():
                copy(arriving(), arriving(), sibling).wait_recv()

        copy_handle = (wait_recv, wait_send)
        pending.append(wait_send)
        return copy_handle

    def line_group(mine, theirs):
        return SimpleNamespace(mine=mine, theirs=theirs, steps=[], swaps=[])

    def forward(group, step):
        mine, theirs = group.mine, group.theirs
        if step > 0:
            recv_all(group.steps[step - 1])
        if step < planes - 1:
            n = step + 1
            group.steps.append([
                send_if(
                    (c >= n - 1) & (c < planes - 1), lambda: mine(c - n + 1), lambda: mine(c - n + 1),
                    me + DEV_CLIP, c >= n, lambda: mine(c - n),
                ),
                send_if(
                    (c + n - 1 < planes) & (c >= 1), lambda: mine(c + n - 1), lambda: mine(c + n - 1),
                    me - DEV_CLIP, c + n < planes, lambda: mine(c + n),
                ),
            ])
        if step == 0:
            group.swaps.append(send(mine(c), theirs(c), sibling))
        else:
            for held, i in ((c >= step, c - step), (c + step < planes, c + step)):
                group.swaps.append(
                    send_if(
                        held, lambda i=i: mine(i), lambda i=i: theirs(i), sibling, held, lambda i=i: theirs(i)
                    )
                )

    def group_sent(group):
        sent_all(sum(group.steps, []) + group.swaps)

    def local(src, dst):
        i = counters.local
        counters.local += 1
        copy = pltpu.make_async_copy(src, dst, r.lsem.at[i])
        copy.start()
        return copy.wait

    def recv_all(handles):
        for handle in handles:
            handle[0]()

    def sent_all(handles):
        for handle in handles:
            handle[1]()

    Wq, We, Wo, Ws = r.Wq, r.We, r.Wo, r.Ws
    Ws2 = Ws.reshape(ff_own, width)

    def flat(ref):
        return ref.reshape(micro * rows, width)

    chip_rows = CHIPS * share
    plane_rows = CORES * chip_rows
    chip_halves = (slice(0, chip_rows // 2), slice(chip_rows // 2, chip_rows))

    def stacked(ref, count, lanes):
        return flat(ref).at[0:count * chip_rows].reshape(count, chip_rows, width).at[:, :, 0:lanes]

    def by_core(own, other):
        return jnp.where(e == 0, own, other), jnp.where(e == 0, other, own)

    def join_rows(own, other, count):
        first, second = by_core(own, other)
        pieces = []
        for j in range(count):
            pieces += [first[j * share:(j + 1) * share], second[j * share:(j + 1) * share]]
        return jnp.concatenate(pieces, 0)

    def split_rows(block, count):
        pieces = [block[j * share:(j + 1) * share] for j in range(2 * count)]
        return by_core(jnp.concatenate(pieces[0::2], 0), jnp.concatenate(pieces[1::2], 0))

    def join_planes(own, other, out):
        @pl.loop(0, planes)
        def _(i):
            block = join_rows(own[i].astype(F32), other[i].astype(F32), CHIPS)
            out[pl.ds(pl.multiple_of(i * plane_rows, plane_rows), plane_rows), :] = block.astype(BF)

    def split_planes(grads, own, other):
        @pl.loop(0, planes)
        def _(i):
            block = grads[pl.ds(pl.multiple_of(i * plane_rows, plane_rows), plane_rows), :].astype(F32)
            mine, theirs = split_rows(block, CHIPS)
            own[i] = mine.astype(BF)
            other[i] = theirs.astype(BF)

    k_x, k_y, k_far = flipped(k, 1), flipped(k, 2), flipped(k, 3)
    x_peer, y_peer, far_peer = chip_peer(1), chip_peer(2), chip_peer(3)
    top, low = slice(0, tok // 2), slice(tok // 2, tok)

    def gather_start(src, dst, b):
        return [dst.at[b], [send(src, dst.at[b, k], x_peer), send(src, dst.at[b, k], y_peer)]]

    def gather_relay(gather):
        dst, handles = gather
        handles[0][0]()
        handles.append(send(dst.at[k_x, top], dst.at[k_x, top], y_peer))
        handles[1][0]()
        handles.append(send(dst.at[k_y, low], dst.at[k_y, low], x_peer))

    def gather_finish(gather):
        recv_all(gather[1][2:])

    def reduce_start(slots, landing, b):
        slots, landing = slots.at[b], landing.at[b]
        return [slots, landing, [
            send(slots.at[k_far, top], landing.at[2, top], x_peer),
            send(slots.at[k_far, low], landing.at[2, low], y_peer),
            send(slots.at[k_x, top], landing.at[0, top], x_peer),
            send(slots.at[k_y, low], landing.at[1, low], y_peer),
        ]]

    def reduce_relay(reduction):
        slots, landing, handles = reduction
        handles[0][0]()
        slots[k_y, top] = (slots[k_y, top].astype(F32) + landing[2, top].astype(F32)).astype(BF)
        handles.append(send(slots.at[k_y, top], landing.at[1, top], y_peer))
        handles[1][0]()
        slots[k_x, low] = (slots[k_x, low].astype(F32) + landing[2, low].astype(F32)).astype(BF)
        handles.append(send(slots.at[k_x, low], landing.at[0, low], x_peer))

    def reduce_finish(reduction):
        slots, landing, handles = reduction
        recv_all(handles[2:])
        return slots[k].astype(F32) + landing[0].astype(F32) + landing[1].astype(F32)

    sb, sbo, rb, rbo = r.sb, r.sbo, r.rb, r.rbo
    vfin = r.vfin

    def vec_row(index):
        return vfin[index:index + 1, :]

    def add_row(index, value):
        r.vrow[index:index + 1, :] += value

    def norm_one(b):
        x_local[b]()
        gather_finish(x_gather[b])
        sent_all(x_gather[b][1])

        @pl.loop(0, CHIPS)
        def _(i):
            normed, _inverse = norm_parts(r.xg[b, i].astype(F32))
            r.xg[b, i] = (normed * vec_row(ROW_GAIN_ONE) + vec_row(ROW_SHIFT_ONE)).astype(BF)

    a1_rows = r.xg.reshape(micro, rows, width)
    a2_rows = r.a2g.reshape(micro, rows, width)
    dy_rows = r.dyg.reshape(micro, rows, width)
    dr_rows = r.drg.reshape(micro, rows, width)
    half = rows // 2

    def project(b):
        @pl.loop(0, 2)
        def _(i):
            at = pl.ds(pl.multiple_of(i * half, half), half)
            out = (dot_nn(a1_rows[b, at, :], Wq[...]) + r.bq[...]).astype(BF)
            for h in range(OWN_HEADS):
                r.q[b, h, at, :] = out[:, h * HD:(h + 1) * HD]
                for part in range(2):
                    low = (part + 1) * OWN_FEATURES + h * HD
                    r.kv[b, part, h, e, at, :] = out[:, low:low + HD]

        return [send(r.kv.at[b, :, :, e], r.kv.at[b, :, :, e], sibling)]

    keys = CORES * rows
    chunk_places = [(2 * (i % CHIPS) + i // CHIPS) * tok for i in range(DEV_CLIP)]

    def masked_scores(b, key_rows, query_rows):
        raw = dot_nt(key_rows, query_rows)
        index = lax.broadcasted_iota(jnp.int32, (tok, raw.shape[1]), 0)
        length = r.lengths[b, c]
        return jnp.concatenate(
            [
                raw[i * tok:(i + 1) * tok] * SCALE
                if first + tok <= keys // 2
                else jnp.where(index < length - first, raw[i * tok:(i + 1) * tok] * SCALE, NEG)
                for i, first in enumerate(chunk_places)
            ],
            0,
        )

    def attend(b, start, stop):
        @pl.loop(start, stop)
        def _(step):
            h, part = step // 2, step % 2
            at = pl.ds(pl.multiple_of(part * half, half), half)
            key_rows = r.kv[b, 0, h].reshape(keys, HD)
            value_rows = r.kv[b, 1, h].reshape(keys, HD)
            scores = masked_scores(b, key_rows, r.q[b, h, at, :])
            peak = jnp.max(scores, 0, keepdims=True)
            exponent = jnp.exp(scores - peak)
            sums = jnp.sum(exponent, 0, keepdims=True)
            probs = (exponent * (1.0 / sums)).astype(BF)
            r.lse[b, h, :, at] = peak + jnp.log(sums)
            r.mixed[b, h, :, at] = dot_tn(value_rows, probs).astype(BF)

    def tiles(start, stop, body):
        @pl.loop(start, stop)
        def _(i):
            body(pl.ds(pl.multiple_of(i * TILE, TILE), TILE))

    def partial_sum(slots, b, product):
        view = slots.reshape(micro, rows, width)

        def body(at):
            view[b, :, at] = product(at).astype(BF)

        tiles(0, width // TILE, body)

    mixed = r.mixed.reshape(micro, OWN_FEATURES, rows)

    def mix_out(b):
        partial_sum(sb, b, lambda at: dot_tn(mixed[b], Wo[:, at]))
        return reduce_start(sb, rb, b)

    def norm_two(b, reduction):
        residual = r.x[b].astype(F32) + reduce_finish(reduction) + vec_row(ROW_BIAS_OUT)
        r.resid[b] = residual
        normed, _inverse = norm_parts(residual)
        r.a2g[b, k] = (normed * vec_row(ROW_GAIN_TWO) + vec_row(ROW_SHIFT_TWO)).astype(BF)
        return gather_start(r.a2g.at[b, k], r.a2g, b)

    def feed(b, start, stop):
        def body(at):
            hidden = dot_nn(a2_rows[b], We[:, at]) + r.be[:, at]
            grad_active = dot_nt(dy_rows[b], Ws2[at, :]).astype(BF).astype(F32)
            normal = 0.5 * (1.0 + lax.erf(hidden * 0.7071067811865476))
            r.act[b, :, at] = (hidden * normal).astype(BF)
            density = jnp.exp(-0.5 * hidden * hidden) * 0.3989422804014327
            grad_hidden = (grad_active * (normal + hidden * density)).astype(BF)
            r.dhid[b, :, at] = grad_hidden
            r.vexp[:, at] += jnp.sum(grad_hidden.astype(F32), 0, keepdims=True)

        tiles(start, stop, body)

    def hidden_back(b, earlier):
        sent_all(earlier[2])
        partial_sum(sb, b, lambda at: dot_nt(r.dhid[b], We[at, :]))
        return reduce_start(sb, rb, b)

    def finish_hidden(b, reduction):
        gradient = reduce_finish(reduction)
        normed, inverse = norm_parts(r.resid[b])
        dy_own = r.dy[b].astype(F32)
        total = dy_own + norm_backward(gradient, normed, inverse, vec_row(ROW_GAIN_TWO))
        r.dresid[b] = total
        r.drg[b, k] = total.astype(BF)
        gather = gather_start(r.drg.at[b, k], r.drg, b)
        add_row(ROW_GAIN_TWO, jnp.sum(gradient * normed, 0, keepdims=True))
        add_row(ROW_SHIFT_TWO, jnp.sum(gradient, 0, keepdims=True))
        add_row(ROW_BIAS_OUT, jnp.sum(total, 0, keepdims=True))
        add_row(ROW_BIAS_SHRINK, jnp.sum(dy_own, 0, keepdims=True))
        return gather

    def weight_gradient(count, lefts, rights, out):
        def body(at):
            total = dot_tn(lefts[0, :, at], rights[0])
            for b in range(1, micro):
                total = total + dot_tn(lefts[b, :, at], rights[b])
            out[at, :] = total.astype(BF)

        tiles(0, count // TILE, body)

    def mixed_gradient(b):
        @pl.loop(0, 2)
        def _(i):
            at = pl.ds(pl.multiple_of(i * half, half), half)
            out = dot_nt(dr_rows[b, at, :], Wo[...]).astype(BF)
            for h in range(OWN_HEADS):
                r.dmix[h, at, :] = out[:, h * HD:(h + 1) * HD]

    def attend_back(b, start, stop):
        @pl.loop(start, stop)
        def _(h):
            key_rows = r.kv[b, 0, h].reshape(keys, HD)
            value_rows = r.kv[b, 1, h].reshape(keys, HD)
            grad_keys = None
            grad_values = None
            for part in range(2):
                at = pl.ds(part * half, half)
                query_rows = r.q[b, h, at, :]
                mix_rows = r.dmix[h, at, :]
                probs = jnp.exp(masked_scores(b, key_rows, query_rows) - r.lse[b, h, :, at])
                grad_probs = dot_nt(value_rows, mix_rows)
                inner = jnp.sum(probs * grad_probs, 0, keepdims=True)
                grad_scores = (probs * (grad_probs - inner)).astype(BF)
                grad_query = dot_tn(key_rows, grad_scores) * SCALE
                r.dq[h, at, :] = grad_query.T.astype(BF)
                key_term = dot_nn(grad_scores, query_rows)
                value_term = dot_nn(probs.astype(BF), mix_rows)
                grad_keys = key_term if grad_keys is None else grad_keys + key_term
                grad_values = value_term if grad_values is None else grad_values + value_term
            r.kv[b, 0, h] = (grad_keys * SCALE).astype(BF).reshape(CORES, rows, HD)
            r.kv[b, 1, h] = grad_values.astype(BF).reshape(CORES, rows, HD)

    def swap_back(b, start, stop):
        return [send(r.kv.at[b, :, start:stop, 1 - e], r.dl.at[b, :, start:stop], sibling)]

    def join_gradients(b, handles):
        recv_all(handles)

        @pl.loop(0, CHIPS)
        def _(i):
            at = pl.ds(pl.multiple_of(i * tok, tok), tok)
            pieces = [r.dq[h, at, :] for h in range(OWN_HEADS)]
            for part in range(2):
                for h in range(OWN_HEADS):
                    pair = r.kv[b, part, h, e, at, :].astype(F32) + r.dl[b, part, h, at, :].astype(F32)
                    pieces.append(pair.astype(BF))
            pieces.append(jnp.zeros((tok, QKV_WIDTH - 3 * OWN_FEATURES), BF))
            line = jnp.concatenate(pieces, 1)
            r.dqkv[b, at, :] = line
            r.vqkv[...] += jnp.sum(line.astype(F32), 0, keepdims=True)

    def input_start(b, earlier):
        sent_all(earlier[2])
        partial_sum(sb, b, lambda at: dot_nt(r.dqkv[b], Wq[at, :]))
        return reduce_start(sb, rb, b)

    def finish_input(b, reduction):
        gradient = reduce_finish(reduction)
        normed, inverse = norm_parts(r.x[b].astype(F32))
        back = norm_backward(gradient, normed, inverse, vec_row(ROW_GAIN_ONE))
        r.ig[b] = (r.dresid[b] + back).astype(BF)
        add_row(ROW_GAIN_ONE, jnp.sum(gradient * normed, 0, keepdims=True))
        add_row(ROW_SHIFT_ONE, jnp.sum(gradient, 0, keepdims=True))

    def finish_out(b, reduction):
        total = r.resid[b] + reduce_finish(reduction) + vec_row(ROW_BIAS_SHRINK)
        r.bo[b] = total.astype(BF)

    def sum_group(space, slots):
        return SimpleNamespace(space=space, slots=slots, right={}, left={})

    def add_passing(group, hops):
        space, slots = group.space, group.slots
        for side, held, i, slot in (
            (group.right, (c >= 1) & (c - 1 + hops < planes), c - 1 + hops, hops - 1),
            (group.left, (c <= planes - 2) & (c + 1 - hops >= 0), c + 1 - hops, 5 - hops),
        ):
            side[hops][0]()

            @pl.when(held)
            def _():
                space[i] = (space[i].astype(F32) + slots[slot][...].astype(F32)).astype(BF)

    def sum_step(group, hops):
        space, slots = group.space, group.slots
        if hops < planes - 1:
            add_passing(group, hops + 1)
        group.right[hops] = send_if(
            c + hops < planes, lambda: space.at[c + hops], lambda: slots[hops - 1], me + DEV_CLIP,
            (c >= 1) & (c - 1 + hops < planes), lambda: slots[hops - 1],
        )
        group.left[hops] = send_if(
            c - hops >= 0, lambda: space.at[c - hops], lambda: slots[5 - hops], me - DEV_CLIP,
            (c <= planes - 2) & (c + 1 - hops >= 0), lambda: slots[5 - hops],
        )

    def sum_finish(group, out):
        space, slots = group.space, group.slots
        out(space[c].astype(F32), False)
        for side, held, slot in ((group.right, c >= 1, 0), (group.left, c <= planes - 2, 4)):
            side[1][0]()

            @pl.when(held)
            def _():
                out(slots[slot][...].astype(F32), True)

    def to_blocks(ref, first):
        def put(total, more):
            for j in range(total.shape[0] // share):
                piece = total[j * share:(j + 1) * share]
                ref[first + j] = ref[first + j] + piece if more else piece

        return put

    def to_rows(ref):
        def put(total, more):
            ref[...] = ref[...] + total if more else total

        return put

    def sibling_add(handles, landing, fetched, out, mine):
        recv_all(handles)
        sent_all(handles)
        local(landing, fetched)()

        @pl.loop(0, planes)
        def _(i):
            out[i] = (mine(i).astype(F32) + fetched[i].astype(F32)).astype(BF)

    def free_slots(ready):
        for side, held, device in ((0, c >= 1, me - DEV_CLIP), (1, c <= planes - 2, me + DEV_CLIP)):

            @pl.when(held)
            def _():
                pl.semaphore_signal(
                    ready.at[1 - side], inc=1, device_id=(device,), device_id_type=pl.DeviceIdType.MESH
                )

    def await_slots(ready):
        for side, held in ((0, c >= 1), (1, c <= planes - 2)):

            @pl.when(held)
            def _():
                pl.semaphore_wait(ready.at[side], 1)

    resid, dresid = r.resid, r.dresid
    x_local = [local(r.x.at[b], r.xg.at[b, k]) for b in range(micro)]
    dy_local = [local(r.dy.at[b], r.dyg.at[b, k]) for b in range(micro)]
    x_gather = [None] * micro
    dy_gather = [None] * micro
    if fused:
        expand = [dresid.at[0, 0:share], dresid.at[0, share:2 * share], dresid.at[0, 2 * share:3 * share], dresid.at[1, 0:share]]
        first_rows = tok - share
        loads = [local(ref, resid.at[0, i * share:(i + 1) * share]) for i, ref in enumerate((r.wq, r.wk, r.wv))]
        loads.append(local(r.wo, resid.at[1, 0:share]))
        expand_loads = [local(r.we.at[:, i * width:(i + 1) * width], expand[i]) for i in range(planes)]
        expand_loads.append(local(r.ws.at[0:first_rows], resid.at[1, share:tok]))
        expand_loads.append(local(r.ws.at[first_rows:ff_share], dresid.at[1, share:ff_share - first_rows + share]))
        peers = [chip_peer(by) for by in (1, 2, 3)] + [sibling]
        if fused:
            peers += [plane_peer(by) for by in range(1, planes)]
        barrier = pltpu.get_barrier_semaphore()
        for peer in peers:
            pl.semaphore_signal(barrier, inc=1, device_id=(peer,), device_id_type=pl.DeviceIdType.MESH)
        for load in loads:
            load()
        matrices = [resid[0, i * share:(i + 1) * share] for i in range(3)]
        for j in range(CHIPS):
            pieces = [
                matrix[:, (i * CHIPS + j) * HD:(i * CHIPS + j + 1) * HD] for matrix in matrices for i in range(planes)
            ]
            pieces.append(jnp.zeros((share, QKV_WIDTH - 3 * OWN_FEATURES), F32))
            r.aq[j] = jnp.concatenate(pieces, 1).astype(BF)
        r.so[c] = resid[1, 0:share].astype(BF)
        compact = jnp.concatenate([jnp.pad(ref[...], ((0, 0), (0, 256 - share))) for ref in r.vectors], 0)
        tail = jnp.pad(r.expand_bias[...], ((0, 0), (0, 256 - ff_share)))
        pair = [jnp.pad(ref[...], ((0, 0), (0, 128 - share))) for ref in (r.query_bias, r.value_bias)]
        r.cv[c] = jnp.concatenate([compact, tail, jnp.concatenate(pair, 1)], 0)
        pl.semaphore_wait(barrier, len(peers))
        wq_mine, wq_other = stacked(r.drg, planes, QKV_WIDTH), stacked(r.a2g, planes, QKV_WIDTH)
        we_mine, we_other = stacked(r.act, planes, ff_own), stacked(r.dhid, planes, ff_own)
        lines_q = [
            line_group(lambda i, at=at: wq_mine.at[i, at], lambda i, at=at: wq_other.at[i, at]) for at in chip_halves
        ]
        line_e = line_group(lambda i: we_mine.at[i], lambda i: we_other.at[i])
        line_o = line_group(lambda i: r.so.at[i], lambda i: r.oo.at[i])
        line_s = line_group(lambda i: Ws.at[i, e], lambda i: Ws.at[i, e])

        def pack_plane(blocks, out):
            out[c] = jnp.concatenate([blocks[j].astype(F32) for j in range(CHIPS)], 0).astype(BF)

        wq_plane = [send(r.aq.at[flipped(k, by)], r.alq.at[k], chip_peer(by)) for by in (3, 1, 2)]
        vec_z = [send(r.cv.at[c], r.cv.at[c], plane_peer(by)) for by in range(1, planes)]
        forward(line_o, 0)
        r.alq[k] = r.aq[k]
        recv_all(vec_z)
        r.cp[e, k] = r.cv[...]
        vec_p = [send(r.cv, r.cp.at[e, k], chip_peer(by)) for by in (1, 2, 3)]
        x_gather[0] = gather_start(r.x.at[0], r.xg, 0)
        recv_all(wq_plane)
        pack_plane(r.alq, wq_mine)
        for line in lines_q:
            forward(line, 0)
        for load in expand_loads:
            load()
        ff_part = width // planes
        for j in range(CHIPS):
            pieces = [block[:, j * ff_part:(j + 1) * ff_part] for block in expand]
            r.ae[j] = jnp.concatenate(pieces, 1).astype(BF)
        we_plane = [send(r.ae.at[flipped(k, by)], r.ale.at[k], chip_peer(by)) for by in (3, 1, 2)]
        r.ale[k] = r.ae[k]
        rows_s = [resid[1, share:tok], dresid[1, share:ff_share - first_rows + share]]
        Ws[c, e] = jnp.concatenate(rows_s, 0).astype(BF)
        recv_all(vec_p)
        vec_s = [send(r.cp.at[e], r.cp.at[e], sibling)]
        recv_all(vec_s)
        places = [(i, f) for i in range(planes) for f in range(CORES)]
        vfin[...] = jnp.concatenate(
            [r.cp[f, j, i][:, 0:share] for i in range(planes) for j in range(CHIPS) for f in range(CORES)], 1
        )
        r.be[...] = jnp.concatenate([r.cp[f, k, i][6:7, 0:ff_share] for i, f in places], 1)
        bias = [jnp.concatenate([r.cp[f, k, i][7:8, at:at + share] for i, f in places], 1) for at in (0, 128)]
        blank = jnp.zeros((1, OWN_FEATURES), F32)
        r.bq[...] = jnp.concatenate([bias[0], blank, bias[1], blank[:, :QKV_WIDTH - 3 * OWN_FEATURES]], 1)
        gather_relay(x_gather[0])
        x_gather[1] = gather_start(r.x.at[1], r.xg, 1)
        forward(line_o, 1)
        for line in lines_q:
            forward(line, 1)
        recv_all(we_plane)
        pack_plane(r.ale, we_mine)
    else:
        peers = [chip_peer(by) for by in (1, 2, 3)] + [sibling]
        if fused:
            peers += [plane_peer(by) for by in range(1, planes)]
        barrier = pltpu.get_barrier_semaphore()
        for peer in peers:
            pl.semaphore_signal(barrier, inc=1, device_id=(peer,), device_id_type=pl.DeviceIdType.MESH)
        pl.semaphore_wait(barrier, len(peers))
        loads = [local(r.wq, Wq), local(r.we, We), local(r.wo, Wo), local(r.ws, Ws2)]
        for b in range(micro):
            x_gather[b] = gather_start(r.x.at[b], r.xg, b)
        vfin[...] = r.vec[...]
        r.be[...] = r.vec[6:7, :]
        r.bq[...] = r.vec[7:8, :QKV_WIDTH]
        gather_relay(x_gather[0])
        for load in loads:
            load()
    for ref in (r.vrow, r.vexp, r.vqkv):
        ref[...] = jnp.zeros_like(ref)
    norm_one(0)
    if fused:
        forward(line_o, 2)
        for line in lines_q:
            forward(line, 2)
        forward(line_e, 0)
        forward(line_s, 0)
    gather_relay(x_gather[1])
    dy_gather[0] = gather_start(r.dy.at[0], r.dyg, 0)
    norm_one(1)
    if fused:
        forward(line_o, 3)
        for line in lines_q:
            forward(line, 3)
        for line in lines_q:
            recv_all(line.swaps)
        join_planes(wq_mine, wq_other, Wq)
    kv_swap = [None] * micro
    kv_swap[0] = project(0)
    gather_relay(dy_gather[0])
    dy_gather[1] = gather_start(r.dy.at[1], r.dyg, 1)
    kv_swap[1] = project(1)
    recv_all(kv_swap[0])
    attend(0, 0, OWN_HEADS)
    if fused:
        forward(line_e, 1)
    attend(0, OWN_HEADS, 2 * OWN_HEADS)
    if fused:
        recv_all(line_o.swaps)
        for i in range(planes):
            pair = join_rows(r.so[i].astype(F32), r.oo[i].astype(F32), 1)
            Wo[i * HD:(i + 1) * HD, :] = pair.astype(BF)
    mix_reduce = [mix_out(0), None]
    gather_relay(dy_gather[1])
    recv_all(kv_swap[1])
    attend(1, 0, OWN_HEADS)
    if fused:
        forward(line_s, 1)
    attend(1, OWN_HEADS, 2 * OWN_HEADS - 1)
    reduce_relay(mix_reduce[0])
    attend(1, 2 * OWN_HEADS - 1, 2 * OWN_HEADS)
    mix_reduce[1] = mix_out(1)
    if fused:
        forward(line_e, 2)
    second_gather = [norm_two(0, mix_reduce[0]), None]
    if fused:
        forward(line_s, 2)
    reduce_relay(mix_reduce[1])
    gather_relay(second_gather[0])
    second_gather[1] = norm_two(1, mix_reduce[1])
    if fused:
        forward(line_e, 3)
        recv_all(line_e.swaps)
        group_sent(line_e)
        for line in lines_q:
            group_sent(line)
        join_planes(we_mine, we_other, We)
    gather_finish(second_gather[0])
    dy_local[0]()
    gather_finish(dy_gather[0])
    if fused:
        forward(line_s, 3)
        recv_all(line_s.swaps)
    flush(20)
    feed(0, 0, 4)
    gather_relay(second_gather[1])
    feed(0, 4, ff_own // TILE)
    hidden_reduce = [hidden_back(0, mix_reduce[0]), None]
    gather_finish(second_gather[1])
    dy_local[1]()
    gather_finish(dy_gather[1])
    feed(1, 0, ff_own // TILE)
    reduce_relay(hidden_reduce[0])
    hidden_reduce[1] = hidden_back(1, mix_reduce[1])
    weight_gradient(width, a2_rows, r.dhid, We)
    resid_gather = [finish_hidden(0, hidden_reduce[0]), None]
    if fused:
        sent_all(wq_plane + we_plane)
        group_sent(line_o)
        group_sent(line_s)
        sent_all(second_gather[0][1] + second_gather[1][1])
        free_slots(r.ready_e)
        parts_e = We.reshape(planes, 2, chip_rows, ff_own)
        split_planes(We, parts_e.at[:, 0], parts_e.at[:, 1])
        ge_s = [send(parts_e.at[:, 1], r.Le, sibling)]
    partial_sum(sbo, 0, lambda at: dot_nn(r.act[0], Ws2[:, at]))
    if fused:
        sum_e = sum_group(parts_e.at[:, 0], [flat(r.a2g).at[i * chip_rows:(i + 1) * chip_rows] for i in range(5)])
        sibling_add(ge_s, r.Le, parts_e.at[:, 1], parts_e.at[:, 0], lambda i: parts_e[i, 0])
        await_slots(r.ready_e)
        sum_step(sum_e, 3)
    partial_sum(sbo, 1, lambda at: dot_nn(r.act[1], Ws2[:, at]))
    reduce_relay(hidden_reduce[1])
    weight_gradient(ff_own, r.act, dy_rows, Ws2)
    if fused:
        sent_all(dy_gather[0][1] + dy_gather[1][1])
        free_slots(r.ready_s)
        gs_s = [send(Ws.at[:, 1 - e], r.Ls, sibling)]
    gather_relay(resid_gather[0])
    if fused:
        places_s = [flat(r.a2g).at[5 * ff_share:6 * ff_share]]
        for ref in (r.dyg, r.act):
            places_s += [flat(ref).at[i * ff_share:(i + 1) * ff_share] for i in (4, 5)]
        sum_s = sum_group(Ws.at[:, e], places_s)
        sibling_add(gs_s, r.Ls, Ws.at[:, 1 - e], Ws.at[:, e], lambda i: Ws[i, e])
        await_slots(r.ready_s)
        sum_step(sum_s, 3)
    resid_gather[1] = finish_hidden(1, hidden_reduce[1])
    if fused:
        sum_step(sum_e, 2)
    flush(20)
    gather_finish(resid_gather[0])
    mixed_gradient(0)
    sent_all(kv_swap[0] + kv_swap[1])
    attend_back(0, 0, 2)
    gather_relay(resid_gather[1])
    out_reduce = [reduce_start(sbo, rbo, 0), None]
    if fused:
        sum_step(sum_s, 2)
    attend_back(0, 2, OWN_HEADS)
    swap = swap_back(0, 0, OWN_HEADS)
    gather_finish(resid_gather[1])
    mixed_gradient(1)
    lead = dot_nn(mixed[0], dr_rows[0])
    for other in range(1, micro):
        lead = lead + dot_nn(mixed[other], dr_rows[other])
    if fused:
        space_o, other_o = r.so, r.oo
        for i in range(planes):
            mine, theirs = split_rows(lead[i * HD:(i + 1) * HD], 1)
            space_o[i] = mine.astype(BF)
            other_o[i] = theirs.astype(BF)
        go_s = [send(other_o, r.Lo, sibling)]
    else:
        Wo[...] = lead.astype(BF)
    join_gradients(0, swap)
    input_reduce = [input_start(0, hidden_reduce[0]), None]
    if fused:
        sum_step(sum_e, 1)
    attend_back(1, 0, 2)
    last_swap = swap_back(1, 0, 2)
    reduce_relay(out_reduce[0])
    if fused:
        sum_o = sum_group(space_o, [r.ao.at[i] for i in range(5)])
        sibling_add(go_s, r.Lo, other_o, space_o, lambda i: space_o[i])
        sum_step(sum_s, 1)
        sum_step(sum_o, 3)
    attend_back(1, 2, OWN_HEADS)
    last_swap += swap_back(1, 2, OWN_HEADS)
    reduce_relay(input_reduce[0])
    join_gradients(1, last_swap)
    input_reduce[1] = input_start(1, hidden_reduce[1])
    weight_gradient(width, a1_rows, r.dqkv, Wq)
    flush(20)
    if fused:
        free_slots(r.ready_q)
        parts_q = Wq.reshape(planes, 2, chip_rows, QKV_WIDTH)
        split_planes(Wq, parts_q.at[:, 0], parts_q.at[:, 1])
        gq_s = [send(parts_q.at[:, 1], r.Lq, sibling)]
        sum_step(sum_o, 2)
        five = stacked(r.dhid, 5, QKV_WIDTH)
        sums_q = [sum_group(parts_q.at[:, 0, at], [five.at[i, at] for i in range(5)]) for at in chip_halves]
    finish_input(0, input_reduce[0])
    if fused:
        sibling_add(gq_s, r.Lq, parts_q.at[:, 1], parts_q.at[:, 0], lambda i: parts_q[i, 0])
        await_slots(r.ready_q)
        for group in sums_q:
            sum_step(group, 3)
    def vector_step(group, step, last):
        zero, one, two, from_z, from_plane, from_core = group
        if step == 0:
            return [send(zero, from_core, sibling)]
        if step == 1:
            one[...] = zero[...] + from_core[...]
            return [send(one, from_z.at[by - 1], plane_peer(by)) for by in range(1, planes)]
        if step == 2:
            total = one[...]
            for by in range(1, planes):
                total = total + from_z[by - 1]
            two[...] = total
            return [send(two, from_plane.at[by - 1], chip_peer(by)) for by in (1, 2, 3)]
        others = from_plane[0] + from_plane[1] + from_plane[2]
        shared = lax.broadcasted_iota(jnp.int32, others.shape, 0) < 6
        last[...] = two[...] + jnp.where(shared, others, 0.0)

    if fused:
        group_u = (r.u0, r.u1, r.u2, r.uz, r.up, r.us)
        group_t = (r.t0, r.t1, r.t2, r.tz, r.tp, r.ts)
    padded = jnp.concatenate([r.vqkv[...], jnp.zeros((1, width - QKV_WIDTH), F32)], 1)
    early = jnp.concatenate([r.vrow[0:6, :], r.vexp[...], padded], 0)
    if fused:
        r.u0[...] = early
        moved = vector_step(group_u, 0, None)
    reduce_relay(input_reduce[1])
    out_reduce[1] = reduce_start(sbo, rbo, 1)
    finish_out(0, out_reduce[0])
    if fused:
        recv_all(moved)
        moved = vector_step(group_u, 1, None)
        sum_finish(sum_s, to_rows(r.gs))
        sum_finish(sum_e, to_blocks(r.ge, 0))
        for j in range(CHIPS):
            r.ae[j] = r.ge[j].astype(BF)
        sum_step(sum_o, 1)
    if fused:
        ge_p = [send(r.ae.at[flipped(k, by)], r.ale.at[k], chip_peer(by)) for by in (3, 1, 2)]
        recv_all(moved)
        moved = vector_step(group_u, 2, None)
        for group in sums_q:
            sum_step(group, 2)
    finish_input(1, input_reduce[1])
    late = r.vrow[0:2, :]
    if fused:
        r.t0[...] = late
        moved_late = vector_step(group_t, 0, None)
    reduce_relay(out_reduce[1])
    if fused:
        recv_all(moved)
        vector_step(group_u, 3, r.vo)
        recv_all(ge_p)
        for by in (1, 2, 3):
            r.ge[flipped(k, by)] = r.ale[flipped(k, by)].astype(F32)
        recv_all(moved_late)
        moved_late = vector_step(group_t, 1, None)
        for group in sums_q:
            sum_step(group, 1)
        recv_all(moved_late)
        moved_late = vector_step(group_t, 2, None)
        sum_finish(sum_o, to_rows(r.go))
        recv_all(moved_late)
        vector_step(group_t, 3, r.vt)
    finish_out(1, out_reduce[1])
    if fused:
        for i, group in enumerate(sums_q):
            sum_finish(group, to_blocks(r.gq, i * CHIPS // 2))
        for j in range(CHIPS):
            r.aq[j] = r.gq[j].astype(BF)
        gq_p = [send(r.aq.at[flipped(k, by)], r.alq.at[k], chip_peer(by)) for by in (3, 1, 2)]
        recv_all(gq_p)
        for by in (1, 2, 3):
            r.gq[flipped(k, by)] = r.alq[flipped(k, by)].astype(F32)
    else:
        r.vo[...] = early
        r.vt[...] = late
        stores = [local(Wq, r.gq), local(We, r.ge), local(Wo, r.go), local(Ws2, r.gs)]
        for store in stores:
            store()
    flush()


def run_block(fused, planes, x, dy, lengths, vectors, weights_in, share, ff_share):
    micro, tok, width = x.shape
    ff_own = width
    rows = CHIPS * tok
    vmem = pl.BlockSpec(memory_space=pltpu.VMEM)
    anywhere = pl.BlockSpec(memory_space=pl.ANY)
    smem = pl.BlockSpec(memory_space=pltpu.SMEM)

    def shape(*dims, dtype=BF):
        return jax.ShapeDtypeStruct(dims, dtype)

    outs = [
        (shape(micro, tok, width), vmem),
        (shape(micro, tok, width), vmem),
        (shape(8, width, dtype=F32), vmem),
        (shape(2, width, dtype=F32), vmem),
    ]
    if fused:
        outs += [
            (shape(CHIPS, share, QKV_WIDTH, dtype=F32), vmem),
            (shape(CHIPS, share, ff_own, dtype=F32), vmem),
            (shape(share, width, dtype=F32), vmem),
            (shape(ff_share, width, dtype=F32), vmem),
        ]
        outs += [
            (shape(planes, CHIPS * share, QKV_WIDTH), anywhere),
            (shape(planes, CHIPS * share, ff_own), anywhere),
            (shape(planes, share, width), anywhere),
            (shape(planes, ff_share, width), anywhere),
        ]
    else:
        outs += [
            (shape(width, QKV_WIDTH), anywhere),
            (shape(width, ff_own), anywhere),
            (shape(OWN_FEATURES, width), anywhere),
            (shape(ff_own, width), anywhere),
        ]
    if fused:
        weights = [
            pltpu.VMEM((width, QKV_WIDTH), BF),
            pltpu.VMEM((width, ff_own), BF),
            pltpu.VMEM((OWN_FEATURES, width), BF),
            pltpu.VMEM((planes, CORES, ff_share, width), BF),
        ]
    else:
        weights = [
            pltpu.VMEM((width, QKV_WIDTH), BF),
            pltpu.VMEM((width, ff_own), BF),
            pltpu.VMEM((OWN_FEATURES, width), BF),
            pltpu.VMEM((ff_own, width), BF),
        ]
    scratch = weights + [
        pltpu.VMEM((micro, CHIPS, tok, width), BF),
        pltpu.VMEM((micro, CHIPS, tok, width), BF),
        pltpu.VMEM((micro, CHIPS, tok, width), BF),
        pltpu.VMEM((micro, CHIPS, tok, width), BF),
        pltpu.VMEM((micro, rows, ff_own), BF),
        pltpu.VMEM((micro, rows, ff_own), BF),
        pltpu.VMEM((micro, OWN_HEADS, rows, HD), BF),
        pltpu.VMEM((micro, 2, OWN_HEADS, CORES, rows, HD), BF),
        pltpu.VMEM((micro, OWN_HEADS, HD, rows), BF),
        pltpu.VMEM((micro, OWN_HEADS, 1, rows), F32),
        pltpu.VMEM((OWN_HEADS, rows, HD), BF),
        pltpu.VMEM((OWN_HEADS, rows, HD), BF),
        pltpu.VMEM((micro, 2, OWN_HEADS, rows, HD), BF),
        pltpu.VMEM((micro, CHIPS, tok, width), BF),
        pltpu.VMEM((micro, CHIPS, tok, width), BF),
        pltpu.VMEM((micro, CHIPS - 1, tok, width), BF),
        pltpu.VMEM((micro, CHIPS - 1, tok, width), BF),
        pltpu.VMEM((micro, tok, width), F32),
        pltpu.VMEM((micro, tok, width), F32),
        pltpu.VMEM((8, width), F32),
        pltpu.VMEM((1, ff_own), F32),
        pltpu.VMEM((1, QKV_WIDTH), F32),
        pltpu.VMEM((1, ff_own), F32),
        pltpu.VMEM((1, QKV_WIDTH), F32),
        pltpu.VMEM((8, width), F32),
    ]
    if fused:
        scratch += [
            pltpu.VMEM((planes, share, width), BF),
            pltpu.VMEM((planes, share, width), BF),
            pltpu.VMEM((5, share, width), BF),
            pltpu.VMEM((CHIPS, share, QKV_WIDTH), BF),
            pltpu.VMEM((CHIPS, share, ff_own), BF),
            pltpu.VMEM((CHIPS, share, QKV_WIDTH), BF),
            pltpu.VMEM((CHIPS, share, ff_own), BF),
        ]
        scratch += [
            pltpu.VMEM((planes, 8, 256), F32),
            pltpu.VMEM((CORES, CHIPS, planes, 8, 256), F32),
        ]
        for lines in (8, 2):
            scratch += [pltpu.VMEM((lines, width), F32) for _ in range(3)]
            scratch += [pltpu.VMEM((planes - 1, lines, width), F32), pltpu.VMEM((CHIPS - 1, lines, width), F32)]
            scratch.append(pltpu.VMEM((lines, width), F32))
        scratch += [pltpu.SemaphoreType.REGULAR((2,)) for _ in range(3)]
    scratch += [
        pltpu.SemaphoreType.DMA((SEND_SEMS,)),
        pltpu.SemaphoreType.DMA((RECV_SEMS,)),
        pltpu.SemaphoreType.DMA((LOCAL_SEMS,)),
    ]
    return pl.pallas_call(
        partial(block_kernel, fused, planes, micro, tok, width, ff_own, share, ff_share),
        out_shape=[out for out, _ in outs],
        in_specs=[vmem, vmem, smem] + [vmem] * len(vectors) + [anywhere] * len(weights_in),
        out_specs=[spec for _, spec in outs],
        scratch_shapes=scratch,
        compiler_params=pltpu.CompilerParams(
            collective_id=0, has_side_effects=True, vmem_limit_bytes=63 * 1000 * 1000
        ),
    )(x, dy, lengths, *vectors, *weights_in)


def finish_kernel(planes, share, ff_share, bo, ig, vo, vt, gq, ge, go, gs, *refs):
    device = lax.axis_index("fsdp")
    c, _, e = place(device)
    outs, (blocks_q, blocks_e, lines, last_lines, sems) = refs[:17], refs[17:]
    moves = [(vo, lines), (vt, last_lines), (gq, blocks_q), (ge, blocks_e)]
    moves += [(bo, outs[0]), (ig, outs[1]), (go, outs[6]), (gs, outs[7])]
    copies = [pltpu.make_async_copy(src, dst, sems.at[i]) for i, (src, dst) in enumerate(moves)]
    for copy in copies:
        copy.start()
    for copy in copies[:4]:
        copy.wait()
    part = ge.shape[2] // planes
    for n in range(planes):
        for j in range(CHIPS):
            at = (n * CHIPS + j) * part
            outs[5][:, at:at + part] = blocks_e[j][:, n * part:(n + 1) * part]
    for i, out in enumerate(outs[2:5]):
        first = i * OWN_FEATURES
        out[...] = jnp.concatenate(
            [blocks_q[j][:, first + n * HD:first + (n + 1) * HD] for n in range(planes) for j in range(CHIPS)], 1
        )
    vo, vt = lines, last_lines
    width = vo.shape[1]

    def own(lines, start, size):
        return pltpu.roll(lines, lax.rem(width - start, width), 1)[:, 0:size]

    early = own(vo[...], device * share, share)
    late = own(jnp.concatenate([vt[...], vo[2:8, :]], 0), device * share, share)
    expand = own(vo[...], (2 * c + e) * ff_share, ff_share)
    query = own(vo[...], (2 * c + e) * share, share)
    value = own(vo[...], 2 * OWN_FEATURES + (2 * c + e) * share, share)
    for out, line in zip(
        outs[8:],
        [late[0:1], late[1:2]] + [early[i:i + 1] for i in range(2, 6)] + [expand[6:7], query[7:8], value[7:8]],
        strict=True,
    ):
        out[...] = line
    for copy in copies[4:]:
        copy.wait()


def finish_block(planes, share, ff_share, results):
    shapes = [results[0], results[1]] + [jax.ShapeDtypeStruct((share, results[2].shape[1]), F32)] * 3
    shapes += [jax.ShapeDtypeStruct((share, CHIPS * results[5].shape[2]), F32), results[6], results[7]]
    shapes = [jax.ShapeDtypeStruct(s.shape, s.dtype) for s in shapes]
    shapes += [jax.ShapeDtypeStruct((1, share), F32)] * 6
    shapes += [jax.ShapeDtypeStruct((1, size), F32) for size in (ff_share, share, share)]
    vmem = pl.BlockSpec(memory_space=pltpu.VMEM)
    anywhere = pl.BlockSpec(memory_space=pl.ANY)
    held = [results[4], results[5], results[2], results[3]]
    return pl.pallas_call(
        partial(finish_kernel, planes, share, ff_share),
        out_shape=shapes,
        in_specs=[anywhere] * 8,
        out_specs=[vmem] * 17,
        scratch_shapes=[pltpu.VMEM(a.shape, a.dtype) for a in held] + [pltpu.SemaphoreType.DMA((8,))],
        compiler_params=pltpu.CompilerParams(vmem_limit_bytes=60 * 1000 * 1000),
    )(*results)


def by_chip(matrix, part):
    rows = matrix.shape[0]
    return matrix.reshape(rows, -1, CHIPS, part).transpose(2, 0, 1, 3).reshape(CHIPS, rows, -1)


def from_chips(blocks, part):
    rows = blocks.shape[1]
    return blocks.reshape(CHIPS, rows, -1, part).transpose(1, 2, 0, 3).reshape(rows, -1)


def body(
    inputs, cotangent, lengths, first_gain, first_shift, query_weight, query_bias, key_weight,
    value_weight, value_bias, output_weight, output_bias, second_gain, second_shift,
    expand_weight, expand_bias, shrink_weight, shrink_bias,
):
    device = lax.axis_index("fsdp")
    count = lax.axis_size("fsdp")
    c, k, e = place(device)
    planes = count // DEV_CLIP
    width = inputs.shape[2]
    share = query_weight.shape[0]
    ff_share = shrink_weight.shape[0]
    ff_part = width // 4
    fused = planes == 4 and share * 2 == HD and ff_share * 2 == ff_part
    plain = (first_gain, first_shift, second_gain, second_shift, output_bias, shrink_bias)
    matrices = (query_weight, key_weight, value_weight, expand_weight, output_weight, shrink_weight)
    if fused:
        vectors = [v.reshape(1, -1) for v in plain + (expand_bias, query_bias, value_bias)]
        got = run_block(True, planes, inputs, cotangent, lengths, vectors, matrices, share, ff_share)
        done = finish_block(planes, share, ff_share, got[:8])
        block_out, input_grad, grad_query_w, grad_key_w, grad_value_w, grad_expand_w, grad_output_w, grad_shrink_w = done[:8]
        owned = [line[0] for line in done[8:14]]
        grad_expand_b, grad_query_b, grad_value_b = (line[0] for line in done[14:])
    else:

        def whole(array):
            return lax.all_gather(array, "fsdp", axis=0, tiled=True)

        def mine(blocks):
            return lax.dynamic_index_in_dim(blocks, k, 0, keepdims=False)

        full = [whole(w.astype(BF)) for w in matrices]
        pieces = [mine(by_chip(w, HD)) for w in full[:3]]
        pieces.append(jnp.zeros((width, QKV_WIDTH - 3 * OWN_FEATURES), BF))
        wq = jnp.concatenate(pieces, 1)
        we = mine(by_chip(full[3], ff_part))
        wo = mine(by_chip(full[4].T, HD)).T
        ws = mine(by_chip(full[5].T, ff_part)).T
        bias_e = mine(by_chip(whole(expand_bias)[None], ff_part))
        bias_q = mine(by_chip(whole(query_bias)[None], HD))
        bias_v = mine(by_chip(whole(value_bias)[None], HD))
        blank = jnp.zeros((1, width - 3 * OWN_FEATURES), F32)
        bias_row = jnp.concatenate([bias_q, jnp.zeros_like(bias_q), bias_v, blank], 1)
        vec = jnp.concatenate([jnp.stack([whole(v) for v in plain]), bias_e, bias_row])
        got = run_block(False, planes, inputs, cotangent, lengths, (vec,), (wq, we, wo, ws), share, ff_share)
        block_out, input_grad, sums, late, gq, ge, go, gs = got[:8]

        def spread(block, part):
            places = lax.broadcasted_iota(jnp.int32, (CHIPS, 1, 1), 0) == k
            return from_chips(jnp.where(places, block.astype(F32)[None], 0.0), part)

        def owned_sum(array):
            return lax.psum_scatter(array, "fsdp", scatter_dimension=0, tiled=True)

        grad_query_w, grad_key_w, grad_value_w = (
            owned_sum(spread(gq[:, i * OWN_FEATURES:(i + 1) * OWN_FEATURES], HD)) for i in range(3)
        )
        grad_expand_w = owned_sum(spread(ge, ff_part))
        grad_output_w = owned_sum(spread(go.T, HD).T)
        grad_shrink_w = owned_sum(spread(gs.T, ff_part).T)
        owned = [owned_sum(late[i]) for i in range(2)] + [owned_sum(sums[i]) for i in range(2, len(plain))]
        line_q, line_v = sums[7:8, :OWN_FEATURES], sums[7:8, 2 * OWN_FEATURES:3 * OWN_FEATURES]
        grad_expand_b = owned_sum(spread(sums[6:7], ff_part)[0])
        grad_query_b = owned_sum(spread(line_q, HD)[0])
        grad_value_b = owned_sum(spread(line_v, HD)[0])
    return (
        block_out,
        input_grad,
        owned[0],
        owned[1],
        grad_query_w,
        grad_query_b,
        grad_key_w,
        grad_value_w,
        grad_value_b,
        grad_output_w,
        owned[4],
        owned[2],
        owned[3],
        grad_expand_w,
        grad_expand_b,
        grad_shrink_w,
        owned[5],
    )


def solution(mesh):
    rows, matrix, vector = P(None, "fsdp", None), P("fsdp", None), P("fsdp")
    in_specs = (
        rows, rows, P(), vector, vector, matrix, vector, matrix, matrix, vector, matrix, vector,
        vector, vector, matrix, vector, matrix, vector,
    )
    out_specs = (
        rows, rows, vector, vector, matrix, vector, matrix, matrix, vector, matrix, vector,
        vector, vector, matrix, vector, matrix, vector,
    )
    return jax.shard_map(body, mesh=mesh, in_specs=in_specs, out_specs=out_specs, check_vma=False)
```
